32 devices in a mesh: groups: 2 (over y), depth: 4 (over z), probe: 2 (over x), lat: 2 (over core).
Axes of the slice: x: 2, y: 2, z: 4, core: 2. Of those that a mesh axis runs over, the one named last changes fastest.
Arguments:
- specimen: float32 [2, 16, 768, 768], P(None, ('groups', 'depth'), 'lat'), parts along dimension 1, may hold values from -1 to 1, as said below
- illumination: float32 [2, 128, 128], replicated, may hold values from -5 to 5
- positions: int32 [1024, 2], P('groups'), parts along dimension 0, may hold values from 0 to 640
- scan_index: int32 [32, 4], P('groups', ('probe', 'lat')), parts along dimension 0, may hold values from 0 to 511
- frames: float32 [32, 4, 128, 128], P('groups', ('probe', 'lat')), parts along dimension 0, may hold values from 0 to 2
Outputs:
- specimen_grad: float32 [2, 16, 768, 768], P(None, ('groups', 'depth'), ('probe', 'lat')), parts along dimension 1
The draws below stay inside these ranges and needn't reach their ends.
There are 2 independent parts, one for each index of `groups`. The reference program is written for one: setup_inputs(seed, part) draws one part's arguments, and reference() takes and returns one part's arrays. A program takes and returns all parts, laid end to end along the dimension named above; an argument that names none is the same for every part. Nothing has to cross between parts.
Inputs may be any that keep to these rules, and one draw needn't show every extreme that they name: `specimen`: every pixel's complex transmission has a magnitude of 0.99 to 1.
All inputs are finite; a program needn't handle non-finite values.
Results may differ from the reference program's by a relative error of at most 0.00055.
Values sent between devices are 32-bit elements; how exact they have to be, the bound alone decides.
No kernel may reach another device: no remote copies, remote signals or barrier semaphores. Data moves between devices by JAX's collectives and lax.ppermute only.
A program may use at most 128 MiB of HBM per device.

```python
import math
import jax
import jax.numpy as jnp
from jax import lax

W = 128
OBJ = 768
MB = 16
NPOS = 512
NSL = 8
BATCH = 4


def draw_specimen(key, part):
    key = jax.random.fold_in(key, 5)
    key_amp, key_phase = jax.random.split(key)
    array_shape = (NSL, OBJ, OBJ)
    amplitude = jax.random.uniform(key_amp, array_shape, jnp.float32, 0.995, 1.0)
    phase_angle = jax.random.uniform(key_phase, array_shape, jnp.float32, -0.6, 0.6)
    return jnp.stack([amplitude * jnp.cos(phase_angle), amplitude * jnp.sin(phase_angle)], axis=0)


def plant(entries, rng, least, top_value):
    index_at = [jax.random.randint(jax.random.fold_in(rng, axis), (), 0, length) for axis, length in enumerate(entries.shape)]
    widest = entries.shape.index(max(entries.shape))
    beside = index_at[:widest] + [(index_at[widest] + 1) % entries.shape[widest]] + index_at[widest + 1:]
    return entries.at[tuple(index_at)].set(least).at[tuple(beside)].set(top_value)


def steps_of(stream_key, dims, pieces, least, largest):
    def one(axis_at, parts):
        heights = jax.random.uniform(jax.random.fold_in(jax.random.fold_in(stream_key, 6), axis_at), (parts,), jnp.float32, least / len(pieces), largest / len(pieces))
        return jnp.repeat(jnp.exp(heights), dims[axis_at] // parts).reshape((-1,) + (1,) * (len(dims) - axis_at - 1))

    factor_of = one(*pieces[0])
    for cut in pieces[1:]:
        factor_of = factor_of * one(*cut)
    return factor_of


def centred(rng, shape, scale, most, kind=jnp.bfloat16):
    drawn = jax.random.normal(rng, shape, jnp.float32) * scale
    return jnp.minimum(jnp.maximum(drawn, -most), most).astype(kind)


def setup_inputs(seed: int = 0, part: int = 0) -> dict:
    key_of = jax.random.split(jax.random.key(seed), 6)
    own_keys = jax.random.split(jax.random.fold_in(key_of[5], part), 6)
    specimen = draw_specimen(jax.random.fold_in(jax.random.fold_in(key_of[5], part), 71), part)
    illumination = centred(key_of[1], (2, W, W), 0.7, 5.0, jnp.float32)
    positions = plant(jax.random.randint(own_keys[2], (NPOS, 2), 0, OBJ - W + 1), jax.random.fold_in(own_keys[2], 1), 0, OBJ - W).astype(jnp.int32)
    scan_index = plant(jax.random.randint(own_keys[3], (MB, BATCH), 0, NPOS), jax.random.fold_in(own_keys[3], 1), 0, NPOS - 1).astype(jnp.int32)
    frames = jnp.clip(2.0 * jax.random.uniform(own_keys[4], (MB, BATCH, W, W), jnp.float32) ** steps_of(own_keys[4], (MB, BATCH, W, W), ((1, 4),), -0.2, 0.2), 0.0, 2.0)
    return dict(specimen=specimen, illumination=illumination, positions=positions, scan_index=scan_index, frames=frames)


PRECISE = lax.Precision.HIGHEST
FRESNEL = 8.0

def make_tables(pixels):
    index_all = jnp.arange(pixels, dtype=jnp.int32)
    freq_all = jnp.where(index_all < pixels // 2, index_all, index_all - pixels).astype(jnp.float32) / pixels
    spread = (index_all[:, None] - index_all[None, :]).astype(jnp.float32)
    phase_all = 2.0 * math.pi * freq_all[None, None, :] * spread[:, :, None] - math.pi * FRESNEL * freq_all * freq_all
    propagator = (lax.optimization_barrier(jnp.mean(jnp.cos(phase_all), axis=-1)), lax.optimization_barrier(jnp.mean(jnp.sin(phase_all), axis=-1)))
    turns = (index_all[:, None] * index_all[None, :] % pixels).astype(jnp.float32)
    angle_all = -2.0 * math.pi * turns / pixels
    norm_factor = 1.0 / math.sqrt(pixels)
    fourier = (jnp.cos(angle_all) * norm_factor, jnp.sin(angle_all) * norm_factor)
    return (propagator, fourier)

def complex_apply(pattern, matrix, fields):
    mat_real, mat_imag = matrix
    wave_real, wave_imag = (fields[:, 0], fields[:, 1])
    out_real = jnp.einsum(pattern, mat_real, wave_real, precision=PRECISE) - jnp.einsum(pattern, mat_imag, wave_imag, precision=PRECISE)
    out_imag = jnp.einsum(pattern, mat_real, wave_imag, precision=PRECISE) + jnp.einsum(pattern, mat_imag, wave_real, precision=PRECISE)
    return jnp.stack([out_real, out_imag], axis=1)

def apply_left(matrix, fields):
    return complex_apply('ab,nbc->nac', matrix, fields)

def apply_right(matrix, fields):
    return complex_apply('cb,nab->nac', matrix, fields)

def propagate(propagator, fields):
    return apply_right(propagator, apply_left(propagator, fields))

def complex_product(left_term, right_term):
    out_real = left_term[:, 0] * right_term[:, 0] - left_term[:, 1] * right_term[:, 1]
    out_imag = left_term[:, 0] * right_term[:, 1] + left_term[:, 1] * right_term[:, 0]
    return jnp.stack([out_real, out_imag], axis=1)

def reference(specimen, illumination, positions, scan_index, frames):
    propagator, fourier = make_tables(W)
    corners_all = positions[scan_index.reshape(-1)].astype(jnp.int32)
    measured = frames.reshape((-1, W, W))
    start_wave = jnp.broadcast_to(illumination, (corners_all.shape[0], 2, W, W))

    def loss_of(specimen_now):

        def layer_step(current, layer_slab):

            def cut_one(corner):
                return lax.dynamic_slice(layer_slab, (jnp.int32(0), corner[0], corner[1]), (2, W, W))
            patches = jax.vmap(cut_one)(corners_all)
            return (propagate(propagator, complex_product(patches, current)), None)
        exit_wave, unused = lax.scan(layer_step, start_wave, jnp.moveaxis(specimen_now, 1, 0))
        far_field = apply_right(fourier, apply_left(fourier, exit_wave))
        misfit = far_field[:, 0] * far_field[:, 0] + far_field[:, 1] * far_field[:, 1] - measured
        return 0.25 * jnp.sum(misfit * misfit)
    loss_value, pullback = jax.vjp(loss_of, specimen)
    return pullback(jnp.ones_like(loss_value))[0]
```

```python
import functools
import math

import jax
import jax.numpy as jnp
import ml_dtypes
import numpy as np
from jax import lax
from jax.experimental import pallas as pl
from jax.experimental.pallas import tpu as pltpu
from jax.sharding import PartitionSpec as P

FRESNEL = 8.0
LAG = 1
F32 = jnp.float32
BF16 = jnp.bfloat16
HBM = pl.BlockSpec(memory_space=pl.ANY)


def real_blocks(matrix):
    real, imag = matrix.real, matrix.imag
    left = np.block([[real, -imag], [imag, real]])
    right = np.block([[real, imag], [-imag, real]])
    return np.stack([left, right])


@functools.lru_cache(maxsize=None)
def make_tables(pixels):
    index = np.arange(pixels)
    freq = np.where(index < pixels // 2, index, index - pixels) / pixels
    spread = index[:, None] - index[None, :]
    phase = 2.0 * math.pi * freq * spread[:, :, None] - math.pi * FRESNEL * freq * freq
    propagator = np.mean(np.exp(1j * phase), axis=-1)
    turns = index[:, None] * index[None, :] % pixels
    fourier = np.exp(-2j * math.pi * turns / pixels) / math.sqrt(pixels)
    blocks = np.stack([real_blocks(propagator), real_blocks(fourier)]).astype(np.float32)
    high = blocks.astype(ml_dtypes.bfloat16)
    low = (blocks - high.astype(np.float32)).astype(ml_dtypes.bfloat16)
    return np.stack([high, low], axis=2)


def halves(x):
    high = x.astype(BF16)
    return high, (x - high.astype(F32)).astype(BF16)


def dot(a, b):
    return jnp.dot(a, b, preferred_element_type=F32)


def transform(left, right, fields):
    size = fields[0][0].shape[0]
    stacked = jnp.concatenate(
        [
            jnp.concatenate([real for real, _ in fields], axis=1),
            jnp.concatenate([imag for _, imag in fields], axis=1),
        ],
        axis=0,
    )
    high, low = halves(stacked)
    mid = dot(left[0], high) + (dot(left[1], high) + dot(left[0], low))
    rows = jnp.concatenate(
        [
            jnp.concatenate(
                [mid[:size, i * size : (i + 1) * size], mid[size:, i * size : (i + 1) * size]], axis=1
            )
            for i in range(len(fields))
        ],
        axis=0,
    )
    high, low = halves(rows)
    out = dot(high, right[0]) + (dot(high, right[1]) + dot(low, right[0]))
    return [
        (out[i * size : (i + 1) * size, :size], out[i * size : (i + 1) * size, size:])
        for i in range(len(fields))
    ]


def times(a, b):
    return a[0] * b[0] - a[1] * b[1], a[0] * b[1] + a[1] * b[0]


def times_conj(a, b):
    return a[0] * b[0] + a[1] * b[1], a[1] * b[0] - a[0] * b[1]


def cut_kernel(pixels, corners, lat, own, other, out, window, sems):
    half = own.shape[2]
    width = own.shape[3]
    tall = pixels + 8
    step = pl.program_id(0)
    steps = pl.num_programs(0)

    def places(probe):
        row = corners[2 * probe]
        column = corners[2 * probe + 1]
        row0 = jnp.minimum(row // 8 * 8, 2 * half - tall)
        col0 = jnp.minimum(column // pixels * pixels, width - 2 * pixels)
        top = row0 < half
        bottom = row0 + tall > half
        top_from = jnp.minimum(row0, half - tall)
        bottom_from = jnp.clip(row0 - half, 0, half - tall)
        offset = jnp.where(top, row0 - top_from, tall)
        return top, bottom, top_from, bottom_from, offset, row - row0, col0, column - col0

    def copies(probe, slot, act):
        top, bottom, top_from, bottom_from, _, _, col0, _ = places(probe)
        own_top = lat[0] == 0
        col0 = pl.multiple_of(col0, pixels)
        for source, is_top, sem in ((own, own_top, 0), (other, jnp.logical_not(own_top), 1)):
            start = pl.multiple_of(jnp.where(is_top, top_from, bottom_from), 8)
            to = pl.multiple_of(jnp.where(is_top, 0, tall), 8)

            @pl.when(jnp.where(is_top, top, bottom))
            def _(source=source, start=start, to=to, sem=sem):
                act(
                    pltpu.make_async_copy(
                        source.at[:, :, pl.ds(start, tall), pl.ds(col0, 2 * pixels)],
                        window.at[slot, :, :, pl.ds(to, tall), :],
                        sems.at[slot, sem],
                    )
                )

    slot = step % 2

    @pl.when(step == 0)
    def _():
        copies(0, 0, lambda copy: copy.start())

    @pl.when(step + 1 < steps)
    def _():
        copies(step + 1, 1 - slot, lambda copy: copy.start())

    copies(step, slot, lambda copy: copy.wait())
    *_, offset, down, _, shift = places(step)
    offset = pl.multiple_of(offset, 8)
    turn = (pixels - shift) % pixels
    lane = lax.broadcasted_iota(jnp.int32, (tall, pixels), 1)
    for part in range(own.shape[0]):
        for layer in range(own.shape[1]):
            near = window[slot, part, layer, pl.ds(offset, tall), pl.ds(0, pixels)]
            far = window[slot, part, layer, pl.ds(offset, tall), pl.ds(pixels, pixels)]
            near = pltpu.roll(near, turn, 1)
            far = pltpu.roll(far, turn, 1)
            patch = jnp.where(lane < pixels - shift, near, far)
            out[0, layer, part] = pltpu.roll(patch, (tall - down) % tall, 0)[:pixels]


def cut_patches(own, other, corners, lat, pixels):
    count = corners.shape[0]
    parts, layers = own.shape[:2]
    return pl.pallas_call(
        functools.partial(cut_kernel, pixels),
        grid_spec=pltpu.PrefetchScalarGridSpec(
            num_scalar_prefetch=2,
            grid=(count,),
            in_specs=[HBM, HBM],
            out_specs=pl.BlockSpec((1, layers, parts, pixels, pixels), lambda i, *_: (i, 0, 0, 0, 0)),
            scratch_shapes=[
                pltpu.VMEM((2, parts, layers, 2 * (pixels + 8), 2 * pixels), F32),
                pltpu.SemaphoreType.DMA((2, 2)),
            ],
        ),
        out_shape=jax.ShapeDtypeStruct((count, layers, parts, pixels, pixels), F32),
        compiler_params=pltpu.CompilerParams(vmem_limit_bytes=16 << 20),
        cost_estimate=pl.CostEstimate(
            flops=count * layers * parts * pixels * pixels * 4,
            bytes_accessed=count * layers * parts * pixels * pixels * 12,
            transcendentals=0,
        ),
        name="cut_patches",
    )(corners.reshape(-1), lat.reshape(1), own, other)


def forward_kernel(
    scalars, patches, arrived, start_wave, frames, prop, last, unused, leave, seen
):
    _, _, active, first, final = (scalars[i] for i in range(5))
    count, layers = patches.shape[1:3]

    @pl.when(active == 1)
    def _():
        wave = [
            tuple(jnp.where(first == 1, start_wave[part], arrived[i, part]) for part in range(2))
            for i in range(count)
        ]
        for layer in range(layers):
            chi = []
            for i in range(count):
                for part in range(2):
                    seen[0, i, layer, part] = wave[i][part]
                here = patches[0, i, layer, 0], patches[0, i, layer, 1]
                chi.append(times(here, wave[i]))
            table = last if layer == layers - 1 else prop
            wave = transform(
                (table[0, 0, 0], table[0, 0, 1]), (table[0, 1, 0], table[0, 1, 1]), chi
            )
        for i in range(count):
            real, imag = wave[i]
            misfit = real * real + imag * imag - frames[0, i]
            factor = jnp.where(final == 1, misfit, 1.0)
            leave[i, 0] = real * factor
            leave[i, 1] = imag * factor


def backward_kernel(scalars, patches, arrived, own, seen, prop, last, unused, leave, grads):
    _, _, active, _, final = (scalars[i] for i in range(5))
    count, layers = patches.shape[1:3]

    @pl.when(active == 1)
    def _():
        wave = [
            tuple(jnp.where(final == 1, own[i, part], arrived[i, part]) for part in range(2))
            for i in range(count)
        ]
        for layer in reversed(range(layers)):
            table = last if layer == layers - 1 else prop
            chi = transform(
                (table[0, 1, 0], table[0, 1, 1]), (table[0, 0, 0], table[0, 0, 1]), wave
            )
            wave = []
            for i in range(count):
                before = seen[0, i, layer, 0], seen[0, i, layer, 1]
                here = patches[0, i, layer, 0], patches[0, i, layer, 1]
                real, imag = times_conj(chi[i], before)
                grads[0, i, layer, 0] = real
                grads[0, i, layer, 1] = imag
                wave.append(times_conj(chi[i], here))
        for i in range(count):
            leave[i, 0] = wave[i][0]
            leave[i, 1] = wave[i][1]


def section_specs(count, layers, pixels):
    whole = lambda shape: pl.BlockSpec(shape, lambda g, s: (0,) * len(shape))
    at_group = lambda shape: pl.BlockSpec((1,) + shape, lambda g, s: (s[0],) + (0,) * len(shape))
    at_slot = lambda shape: pl.BlockSpec((1,) + shape, lambda g, s: (s[1],) + (0,) * len(shape))
    stack = (count, layers, 2, pixels, pixels)
    wave = (count, 2, pixels, pixels)
    table = (1, 2, 2, 2 * pixels, 2 * pixels)
    prop = pl.BlockSpec(table, lambda g, s: (0, 0, 0, 0, 0))
    last = pl.BlockSpec(table, lambda g, s: (s[4], 0, 0, 0, 0))
    return whole, at_group, at_slot, stack, wave, prop, last


def cost(count, layers, pixels):
    return pl.CostEstimate(
        flops=count * layers * 2 * 3 * 8 * pixels**3,
        bytes_accessed=count * (layers * 4 + 4) * pixels * pixels * 4,
        transcendentals=0,
    )


def run_forward(scalars, patches, arrived, start_wave, frames, tables, store):
    _, count, layers, _, pixels, _ = patches.shape
    whole, at_group, at_slot, stack, wave, prop, last = section_specs(count, layers, pixels)
    return pl.pallas_call(
        forward_kernel,
        grid_spec=pltpu.PrefetchScalarGridSpec(
            num_scalar_prefetch=1,
            grid=(1,),
            in_specs=[
                at_group(stack),
                whole(wave),
                whole((2, pixels, pixels)),
                at_group((count, pixels, pixels)),
                prop,
                last,
                HBM,
            ],
            out_specs=[whole(wave), at_slot(stack)],
        ),
        out_shape=[
            jax.ShapeDtypeStruct(wave, F32),
            jax.ShapeDtypeStruct(store.shape, F32),
        ],
        input_output_aliases={7: 1},
        compiler_params=pltpu.CompilerParams(vmem_limit_bytes=24 << 20),
        cost_estimate=cost(count, layers, pixels),
        name="forward_section",
    )(scalars, patches, arrived, start_wave, frames, tables, tables, store)


def run_backward(scalars, patches, arrived, own, seen, tables, store):
    _, count, layers, _, pixels, _ = patches.shape
    whole, at_group, at_slot, stack, wave, prop, last = section_specs(count, layers, pixels)
    return pl.pallas_call(
        backward_kernel,
        grid_spec=pltpu.PrefetchScalarGridSpec(
            num_scalar_prefetch=1,
            grid=(1,),
            in_specs=[
                at_group(stack),
                whole(wave),
                whole(wave),
                at_group(stack),
                prop,
                last,
                HBM,
            ],
            out_specs=[whole(wave), at_slot(stack)],
        ),
        out_shape=[
            jax.ShapeDtypeStruct(wave, F32),
            jax.ShapeDtypeStruct(store.shape, F32),
        ],
        input_output_aliases={7: 1},
        compiler_params=pltpu.CompilerParams(vmem_limit_bytes=24 << 20),
        cost_estimate=cost(count, layers, pixels),
        name="backward_section",
    )(scalars, patches, arrived, own, seen, tables, tables, store)


def deposit_kernel(pixels, owners, corners, lat, grads, keep, send, total, sems):
    step = pl.program_id(0)
    height, width = total.shape[2:]
    rows = height // (2 * owners)

    @pl.when(step == 0)
    def _():
        total[...] = jnp.zeros(total.shape, F32)

    tall = pixels + 8
    lane = lax.broadcasted_iota(jnp.int32, (tall, pixels), 1)
    row = corners[2 * step]
    column = corners[2 * step + 1]
    row0 = pl.multiple_of(jnp.minimum(row // 8 * 8, height - tall), 8)
    col0 = jnp.minimum(column // pixels * pixels, width - 2 * pixels)
    shift = column - col0
    near_at = pl.multiple_of(col0, pixels)
    far_at = pl.multiple_of(col0 + pixels, pixels)
    blank = jnp.zeros((8, pixels), F32)
    for layer in range(total.shape[1]):
        for part in range(2):
            padded = jnp.concatenate([grads[0, layer, part], blank], axis=0)
            turned = pltpu.roll(pltpu.roll(padded, row - row0, 0), shift % pixels, 1)
            near = jnp.where(lane >= shift, turned, 0.0)
            far = jnp.where(lane >= shift, 0.0, turned)
            total[part, layer, pl.ds(row0, tall), pl.ds(near_at, pixels)] += near
            total[part, layer, pl.ds(row0, tall), pl.ds(far_at, pixels)] += far

    @pl.when(step == pl.num_programs(0) - 1)
    def _():
        copies = []
        for owner in range(owners):
            for kind, target in ((lat[0], keep), (1 - lat[0], send)):
                start = pl.multiple_of((2 * owner + kind) * rows, 8)
                copies.append(
                    pltpu.make_async_copy(
                        total.at[:, :, pl.ds(start, rows), :],
                        target.at[:, :, owner],
                        sems.at[len(copies)],
                    )
                )
        for copy in copies:
            copy.start()
        for copy in copies:
            copy.wait()


def deposit(grads, corners, lat, owners, height, width):
    count = corners.shape[0]
    _, layers, parts, pixels, _ = grads.shape
    half = jax.ShapeDtypeStruct((parts, layers, owners, height // (2 * owners), width), F32)
    return pl.pallas_call(
        functools.partial(deposit_kernel, pixels, owners),
        grid_spec=pltpu.PrefetchScalarGridSpec(
            num_scalar_prefetch=2,
            grid=(count,),
            in_specs=[
                pl.BlockSpec((1, layers, parts, pixels, pixels), lambda i, *_: (i, 0, 0, 0, 0))
            ],
            out_specs=[HBM, HBM],
            scratch_shapes=[
                pltpu.VMEM((parts, layers, height, width), F32),
                pltpu.SemaphoreType.DMA((2 * owners,)),
            ],
        ),
        out_shape=[half, half],
        compiler_params=pltpu.CompilerParams(vmem_limit_bytes=32 << 20),
        cost_estimate=pl.CostEstimate(
            flops=count * layers * parts * pixels * pixels * 8,
            bytes_accessed=grads.size * 4 + parts * layers * height * width * 4,
            transcendentals=0,
        ),
        name="deposit_patches",
    )(corners.reshape(-1), lat.reshape(1), grads)


def swap(shard, axis):
    return lax.ppermute(shard, axis, [(0, 1), (1, 0)])


def local(specimen, illumination, positions, scan_index, frames):
    pixels = illumination.shape[-1]
    parts, layers, half, width = specimen.shape
    tables = jnp.asarray(make_tables(pixels))
    section = lax.axis_index("depth")
    sections = lax.axis_size("depth")
    lat = lax.axis_index("lat")
    owners = lax.axis_size("probe")

    other = swap(specimen, "lat")
    corners = positions[scan_index.reshape(-1)]
    probes = corners.shape[0]
    count = 2 if probes % 2 == 0 else 1
    groups = probes // count
    stack = (count, layers, parts, pixels, pixels)
    wave = (count, parts, pixels, pixels)
    patches = cut_patches(specimen, other, corners, lat, pixels).reshape((groups,) + stack)
    measured = frames.reshape((groups, count, pixels, pixels))

    is_first = (section == 0).astype(jnp.int32)
    is_last = (section == sections - 1).astype(jnp.int32)

    def scalars_of(group):
        active = (group >= 0) & (group < groups)
        at = jnp.clip(group, 0, groups - 1)
        slot = jnp.where(active, group, groups)
        return jnp.stack([at, slot, active.astype(jnp.int32), is_first, is_last]).astype(jnp.int32)

    def pairs_of(tick, by):
        pairs = []
        for source in range(sections):
            delay = source if by > 0 else 2 * (sections - 1) - source
            if 0 <= source + by < sections and 0 <= tick - LAG * delay < groups:
                pairs.append((source, source + by))
        return pairs

    seen = jnp.zeros((groups + 1,) + stack, F32)
    grads = jnp.zeros((groups + 1,) + stack, F32)
    nothing = jnp.zeros(wave, F32)
    down, up = {}, {}
    depth = LAG * (sections - 1)
    for tick in range(groups + 2 * depth):
        leaving = nothing
        if tick < groups + depth:
            scalars = scalars_of(tick - LAG * section)
            leaving, seen = run_forward(
                scalars, patches, down.pop(tick - LAG, nothing), illumination, measured, tables, seen
            )
            pairs = pairs_of(tick, 1)
            if pairs:
                down[tick] = lax.ppermute(leaving, "depth", pairs)
        if tick >= depth:
            scalars = scalars_of(tick - LAG * (2 * (sections - 1) - section))
            rising, grads = run_backward(
                scalars, patches, up.pop(tick - LAG, nothing), leaving, seen, tables, grads
            )
            pairs = pairs_of(tick, -1)
            if pairs:
                up[tick] = lax.ppermute(rising, "depth", pairs)

    flat = grads.reshape((-1,) + stack[1:])
    keep, send = deposit(flat, corners, lat, owners, 2 * half, width)
    halved = keep + swap(send, "lat")
    if owners == 2:
        probe = lax.axis_index("probe")
        mine = lax.dynamic_index_in_dim(halved, probe, 2, keepdims=False)
        theirs = lax.dynamic_index_in_dim(halved, 1 - probe, 2, keepdims=False)
        return mine + swap(theirs, "probe")
    return lax.psum_scatter(halved, "probe", scatter_dimension=2, tiled=False)


def solution(mesh):
    return jax.shard_map(
        local,
        mesh=mesh,
        in_specs=(
            P(None, ("groups", "depth"), "lat", None),
            P(),
            P("groups", None),
            P("groups", ("probe", "lat")),
            P("groups", ("probe", "lat"), None, None),
        ),
        out_specs=P(None, ("groups", "depth"), ("probe", "lat"), None),
        check_vma=False,
    )
```

```python
import functools
import math

import jax
import jax.numpy as jnp
import ml_dtypes
import numpy as np
from jax import lax
from jax.experimental import pallas as pl
from jax.experimental.pallas import tpu as pltpu
from jax.sharding import PartitionSpec as P

FRESNEL = 8.0
LAG = 1
SCOPED = 16 << 20
F32 = jnp.float32
BF16 = jnp.bfloat16
HBM = pl.BlockSpec(memory_space=pl.ANY)
VMEM = pl.BlockSpec(memory_space=pltpu.VMEM)
SMEM = pl.BlockSpec(memory_space=pltpu.SMEM)


def in_hbm(x):
    return pltpu.with_memory_space_constraint(x, pltpu.HBM)


def in_vmem(x):
    return pltpu.with_memory_space_constraint(x, pltpu.VMEM)


def real_blocks(matrix):
    real, imag = matrix.real, matrix.imag
    left = np.block([[real, -imag], [imag, real]])
    right = np.block([[real, imag], [-imag, real]])
    return np.stack([left, right])


@functools.lru_cache(maxsize=None)
def make_tables(pixels):
    index = np.arange(pixels)
    freq = np.where(index < pixels // 2, index, index - pixels) / pixels
    spread = index[:, None] - index[None, :]
    phase = 2.0 * math.pi * freq * spread[:, :, None] - math.pi * FRESNEL * freq * freq
    propagator = np.mean(np.exp(1j * phase), axis=-1)
    turns = index[:, None] * index[None, :] % pixels
    fourier = np.exp(-2j * math.pi * turns / pixels) / math.sqrt(pixels)
    blocks = np.stack([real_blocks(propagator), real_blocks(fourier)]).astype(np.float32)
    high = blocks.astype(ml_dtypes.bfloat16)
    low = (blocks - high.astype(np.float32)).astype(ml_dtypes.bfloat16)
    return np.stack([high, low], axis=2)


def halves(x):
    high = x.astype(BF16)
    return high, (x - high.astype(F32)).astype(BF16)


def dot(a, b):
    return jnp.dot(a, b, preferred_element_type=F32)


def transform(left, right, fields):
    size = fields[0][0].shape[0]
    stacked = jnp.concatenate(
        [
            jnp.concatenate([real for real, _ in fields], axis=1),
            jnp.concatenate([imag for _, imag in fields], axis=1),
        ],
        axis=0,
    )
    high, low = halves(stacked)
    mid = dot(left[0], high) + (dot(left[1], high) + dot(left[0], low))
    rows = jnp.concatenate(
        [
            jnp.concatenate(
                [mid[:size, i * size : (i + 1) * size], mid[size:, i * size : (i + 1) * size]], axis=1
            )
            for i in range(len(fields))
        ],
        axis=0,
    )
    high, low = halves(rows)
    out = dot(high, right[0]) + (dot(high, right[1]) + dot(low, right[0]))
    return [
        (out[i * size : (i + 1) * size, :size], out[i * size : (i + 1) * size, size:])
        for i in range(len(fields))
    ]


def times(a, b):
    return a[0] * b[0] - a[1] * b[1], a[0] * b[1] + a[1] * b[0]


def times_conj(a, b):
    return a[0] * b[0] + a[1] * b[1], a[1] * b[0] - a[0] * b[1]


def cut_kernel(pixels, corners, lat, own, other, out, seen, window, sems):
    half = own.shape[2]
    width = own.shape[3]
    tall = pixels + 8
    step = pl.program_id(0)
    steps = pl.num_programs(0)

    def places(probe):
        row = corners[2 * probe]
        column = corners[2 * probe + 1]
        row0 = jnp.minimum(row // 8 * 8, 2 * half - tall)
        col0 = jnp.minimum(column // pixels * pixels, width - 2 * pixels)
        top = row0 < half
        bottom = row0 + tall > half
        top_from = jnp.minimum(row0, half - tall)
        bottom_from = jnp.clip(row0 - half, 0, half - tall)
        offset = jnp.where(top, row0 - top_from, tall)
        return top, bottom, top_from, bottom_from, offset, row - row0, col0, column - col0

    def copies(probe, slot, act):
        top, bottom, top_from, bottom_from, _, _, col0, _ = places(probe)
        own_top = lat[0] == 0
        col0 = pl.multiple_of(col0, pixels)
        for source, is_top, sem in ((own, own_top, 0), (other, jnp.logical_not(own_top), 1)):
            start = pl.multiple_of(jnp.where(is_top, top_from, bottom_from), 8)
            to = pl.multiple_of(jnp.where(is_top, 0, tall), 8)

            @pl.when(jnp.where(is_top, top, bottom))
            def _(source=source, start=start, to=to, sem=sem):
                act(
                    pltpu.make_async_copy(
                        source.at[:, :, pl.ds(start, tall), pl.ds(col0, 2 * pixels)],
                        window.at[slot, :, :, pl.ds(to, tall), :],
                        sems.at[slot, sem],
                    )
                )

    slot = step % 2

    @pl.when(step == 0)
    def _():
        copies(0, 0, lambda copy: copy.start())

    @pl.when(step + 1 < steps)
    def _():
        copies(step + 1, 1 - slot, lambda copy: copy.start())

    copies(step, slot, lambda copy: copy.wait())
    *_, offset, down, _, shift = places(step)
    offset = pl.multiple_of(offset, 8)
    turn = (pixels - shift) % pixels
    lane = lax.broadcasted_iota(jnp.int32, (tall, pixels), 1)
    for part in range(own.shape[0]):
        for layer in range(own.shape[1]):
            near = window[slot, part, layer, pl.ds(offset, tall), pl.ds(0, pixels)]
            far = window[slot, part, layer, pl.ds(offset, tall), pl.ds(pixels, pixels)]
            near = pltpu.roll(near, turn, 1)
            far = pltpu.roll(far, turn, 1)
            patch = jnp.where(lane < pixels - shift, near, far)
            out[step // out.shape[1], step % out.shape[1], layer, part] = pltpu.roll(patch, (tall - down) % tall, 0)[:pixels]


def cut_patches(own, other, corners, lat, pixels, count):
    probes = corners.shape[0]
    parts, layers = own.shape[:2]
    groups = probes // count
    stack = (count, layers, parts, pixels, pixels)
    return pl.pallas_call(
        functools.partial(cut_kernel, pixels),
        grid_spec=pltpu.PrefetchScalarGridSpec(
            num_scalar_prefetch=2,
            grid=(probes,),
            in_specs=[HBM, HBM],
            out_specs=[VMEM, VMEM],
            scratch_shapes=[
                pltpu.VMEM((2, parts, layers, 2 * (pixels + 8), 2 * pixels), F32),
                pltpu.SemaphoreType.DMA((2, 2)),
            ],
        ),
        out_shape=[pltpu.VMEM((groups,) + stack, F32), pltpu.VMEM((groups,) + stack, F32)],
        compiler_params=pltpu.CompilerParams(vmem_limit_bytes=16 << 20),
        cost_estimate=pl.CostEstimate(
            flops=probes * layers * parts * pixels * pixels * 4,
            bytes_accessed=probes * layers * parts * pixels * pixels * 12,
            transcendentals=0,
        ),
        name="cut_patches",
    )(corners.reshape(-1), lat.reshape(1), in_hbm(own), in_hbm(other))


def forward_kernel(scalars, patches, arrived, start_wave, frames, tables, unused, leave, seen):
    group, active, first, final = (scalars[i] for i in range(4))
    count, layers = patches.shape[1:3]

    @pl.when(active == 1)
    def _():
        wave = [
            tuple(jnp.where(first == 1, start_wave[part], arrived[i, part]) for part in range(2))
            for i in range(count)
        ]
        for layer in range(layers):
            chi = []
            for i in range(count):
                for part in range(2):
                    seen[group, i, layer, part] = wave[i][part]
                here = patches[group, i, layer, 0], patches[group, i, layer, 1]
                chi.append(times(here, wave[i]))
            at = final if layer == layers - 1 else 0
            wave = transform((tables[at, 0, 0], tables[at, 0, 1]), (tables[at, 1, 0], tables[at, 1, 1]), chi)
        for i in range(count):
            real, imag = wave[i]
            misfit = real * real + imag * imag - frames[group, i]
            factor = jnp.where(final == 1, misfit, 1.0)
            leave[i, 0] = real * factor
            leave[i, 1] = imag * factor


def backward_kernel(scalars, patches, arrived, own, seen, tables, leave, grads):
    group, active, _, final = (scalars[i] for i in range(4))
    count, layers = patches.shape[1:3]

    @pl.when(active == 1)
    def _():
        wave = [
            tuple(jnp.where(final == 1, own[i, part], arrived[i, part]) for part in range(2))
            for i in range(count)
        ]
        for layer in reversed(range(layers)):
            at = final if layer == layers - 1 else 0
            chi = transform((tables[at, 1, 0], tables[at, 1, 1]), (tables[at, 0, 0], tables[at, 0, 1]), wave)
            wave = []
            for i in range(count):
                before = seen[group, i, layer, 0], seen[group, i, layer, 1]
                here = patches[group, i, layer, 0], patches[group, i, layer, 1]
                real, imag = times_conj(chi[i], before)
                grads[i, layer, 0] = real
                grads[i, layer, 1] = imag
                wave.append(times_conj(chi[i], here))
        for i in range(count):
            leave[i, 0] = wave[i][0]
            leave[i, 1] = wave[i][1]


def cost(count, layers, pixels):
    return pl.CostEstimate(
        flops=count * layers * 2 * 3 * 8 * pixels**3,
        bytes_accessed=count * (layers * 4 + 4) * pixels * pixels * 4,
        transcendentals=0,
    )


def run_forward(scalars, patches, arrived, start_wave, frames, tables, store):
    _, count, layers, _, pixels, _ = patches.shape
    return pl.pallas_call(
        forward_kernel,
        in_specs=[SMEM] + [VMEM] * 6,
        out_specs=[VMEM] * 2,
        out_shape=[pltpu.VMEM(arrived.shape, F32), pltpu.VMEM(store.shape, F32)],
        input_output_aliases={6: 1},
        compiler_params=pltpu.CompilerParams(vmem_limit_bytes=SCOPED),
        cost_estimate=cost(count, layers, pixels),
        name="forward_section",
    )(scalars, *map(in_vmem, (patches, arrived, start_wave, frames, tables, store)))


def run_backward(scalars, patches, arrived, own, seen, tables):
    _, count, layers, _, pixels, _ = patches.shape
    return pl.pallas_call(
        backward_kernel,
        in_specs=[SMEM] + [VMEM] * 5,
        out_specs=[VMEM] * 2,
        out_shape=[pltpu.VMEM(arrived.shape, F32), pltpu.VMEM(patches.shape[1:], F32)],
        compiler_params=pltpu.CompilerParams(vmem_limit_bytes=SCOPED),
        cost_estimate=cost(count, layers, pixels),
        name="backward_section",
    )(scalars, *map(in_vmem, (patches, arrived, own, seen, tables)))


def clear_kernel(total):
    total[...] = jnp.zeros(total.shape, F32)


def blank_total(parts, layers, rows, width, pixels):
    return pl.pallas_call(
        clear_kernel,
        out_specs=VMEM,
        out_shape=pltpu.VMEM((parts, layers, rows + 2 * (pixels + 8), width), F32),
        compiler_params=pltpu.CompilerParams(vmem_limit_bytes=SCOPED),
        name="blank_total",
    )()


def deposit_kernel(height, scalars, corners, sources, unused, total):
    pixels = sources[0].shape[-1]
    tall = pixels + 8
    width = total.shape[3]
    rows = total.shape[2] - 2 * tall
    lane = lax.broadcasted_iota(jnp.int32, (tall, pixels), 1)
    blank = jnp.zeros((8, pixels), F32)
    for which, grads in enumerate(sources):
        group, active = scalars[1 + 2 * which], scalars[2 + 2 * which]
        for i in range(grads.shape[0]):
            row = corners[which, group * grads.shape[0] + i, 0]
            column = corners[which, group * grads.shape[0] + i, 1]
            row0 = jnp.minimum(row // 8 * 8, height - tall)
            col0 = jnp.minimum(column // pixels * pixels, width - 2 * pixels)
            shift = column - col0
            near_at = pl.multiple_of(col0, pixels)
            far_at = pl.multiple_of(col0 + pixels, pixels)
            start = row0 - scalars[0] + tall

            @pl.when((active == 1) & (start > 0) & (start < rows + tall))
            def _(grads=grads, i=i, start=start, down=row - row0, shift=shift, near_at=near_at, far_at=far_at):
                at = pl.ds(pl.multiple_of(start, 8), tall)
                for layer in range(total.shape[1]):
                    for part in range(2):
                        padded = jnp.concatenate([grads[i, layer, part], blank], axis=0)
                        turned = pltpu.roll(pltpu.roll(padded, down, 0), shift % pixels, 1)
                        near = jnp.where(lane >= shift, turned, 0.0)
                        far = jnp.where(lane >= shift, 0.0, turned)
                        total[part, layer, at, pl.ds(near_at, pixels)] += near
                        total[part, layer, at, pl.ds(far_at, pixels)] += far


def deposit(scalars, corners, sources, total, height):
    n = len(sources)

    def body(scalars, corners, *refs):
        deposit_kernel(height, scalars, corners, refs[:n], *refs[n:])

    size = sum(source.size for source in sources)
    return pl.pallas_call(
        body,
        in_specs=[SMEM] * 2 + [VMEM] * (n + 1),
        out_specs=VMEM,
        out_shape=pltpu.VMEM(total.shape, F32),
        input_output_aliases={n + 2: 0},
        compiler_params=pltpu.CompilerParams(vmem_limit_bytes=SCOPED),
        cost_estimate=pl.CostEstimate(flops=size * 8, bytes_accessed=size * 12, transcendentals=0),
        name="deposit_patches",
    )(scalars, corners, *map(in_vmem, (*sources, total)))


def split_kernel(margin, lat, total, keep, send, sems):
    owners, rows = keep.shape[2:4]
    copies = []
    for owner in range(owners):
        for kind, target in ((lat[0], keep), (1 - lat[0], send)):
            start = pl.multiple_of(margin + (2 * owner + kind) * rows, 8)
            copies.append(
                pltpu.make_async_copy(
                    total.at[:, :, pl.ds(start, rows), :], target.at[:, :, owner], sems.at[len(copies)]
                )
            )
    for copy in copies:
        copy.start()
    for copy in copies:
        copy.wait()


def split_rows(total, lat, owners, margin):
    parts, layers, height, width = total.shape
    rows = (height - 2 * margin) // (2 * owners)
    half = jax.ShapeDtypeStruct((parts, layers, owners, rows, width), F32)
    return pl.pallas_call(
        functools.partial(split_kernel, margin),
        in_specs=[SMEM, VMEM],
        out_specs=[HBM, HBM],
        out_shape=[half, half],
        scratch_shapes=[pltpu.SemaphoreType.DMA((2 * owners,))],
        compiler_params=pltpu.CompilerParams(vmem_limit_bytes=SCOPED),
        name="split_rows",
    )(lat.reshape(1), in_vmem(total))


def swap(shard, axis):
    return lax.ppermute(shard, axis, [(0, 1), (1, 0)])


def local(specimen, illumination, positions, scan_index, frames):
    pixels = illumination.shape[-1]
    parts, layers, half, width = specimen.shape
    height = 2 * half
    tables = jnp.asarray(make_tables(pixels))
    section = lax.axis_index("depth")
    sections = lax.axis_size("depth")
    lat = lax.axis_index("lat")
    owners = lax.axis_size("probe")
    paired = owners == 2

    other = swap(specimen, "lat")
    corners = positions[scan_index.reshape(-1)]
    probes = corners.shape[0]
    count = 2 if probes % 2 == 0 else 1
    groups = probes // count
    wave = (count, parts, pixels, pixels)
    patches, seen = cut_patches(specimen, other, corners, lat, pixels, count)
    measured = frames.reshape((groups, count, pixels, pixels))
    if paired:
        both = jnp.stack([corners, swap(corners, "probe")])
        base = lax.axis_index("probe") * (height // 2)
        total = blank_total(parts, layers, height // 2, width, pixels)
    else:
        both = corners[None]
        base = jnp.int32(0)
        total = blank_total(parts, layers, height, width, pixels)

    is_first = (section == 0).astype(jnp.int32)
    is_last = (section == sections - 1).astype(jnp.int32)

    def scalars_of(group):
        active = ((group >= 0) & (group < groups)).astype(jnp.int32)
        return jnp.stack([jnp.clip(group, 0, groups - 1), active, is_first, is_last])

    def pairs_of(tick, by):
        pairs = []
        for source in range(sections):
            delay = source if by > 0 else 2 * (sections - 1) - source
            if 0 <= source + by < sections and 0 <= tick - LAG * delay < groups:
                pairs.append((source, source + by))
        return pairs

    nothing = jnp.zeros(wave, F32)
    down, up, across = {}, {}, None
    depth = LAG * (sections - 1)
    for tick in range(groups + 2 * depth):
        leaving = nothing
        if tick < groups + depth:
            scalars = scalars_of(tick - LAG * section)
            leaving, seen = run_forward(
                scalars, patches, down.pop(tick - LAG, nothing), illumination, measured, tables, seen
            )
            pairs = pairs_of(tick, 1)
            if pairs:
                down[tick] = lax.ppermute(leaving, "depth", pairs)
        if tick >= depth:
            scalars = scalars_of(tick - LAG * (2 * (sections - 1) - section))
            rising, grads = run_backward(
                scalars, patches, up.pop(tick - LAG, nothing), leaving, seen, tables
            )
            pairs = pairs_of(tick, -1)
            if pairs:
                up[tick] = lax.ppermute(rising, "depth", pairs)
            sources = [grads]
            ats = [scalars[:2]]
            if paired:
                if across is not None:
                    sources.append(across[0])
                    ats.append(across[1])
                across = (swap(grads, "probe"), scalars[:2])
            total = deposit(jnp.concatenate([base[None], *ats]), both, sources, total, height)
    if paired:
        scalars = jnp.concatenate([base[None], across[1]])
        total = deposit(scalars, both[1:], [across[0]], total, height)
        keep, send = split_rows(total, lat, 1, pixels + 8)
        return keep[:, :, 0] + swap(send[:, :, 0], "lat")
    keep, send = split_rows(total, lat, owners, pixels + 8)
    return lax.psum_scatter(keep + swap(send, "lat"), "probe", scatter_dimension=2, tiled=False)


def solution(mesh):
    return jax.shard_map(
        local,
        mesh=mesh,
        in_specs=(
            P(None, ("groups", "depth"), "lat", None),
            P(),
            P("groups", None),
            P("groups", ("probe", "lat")),
            P("groups", ("probe", "lat"), None, None),
        ),
        out_specs=P(None, ("groups", "depth"), ("probe", "lat"), None),
        check_vma=False,
    )
```

```python
import functools
import math

import jax
import jax.numpy as jnp
import ml_dtypes
import numpy as np
from jax import lax
from jax.experimental import pallas as pl
from jax.experimental.pallas import tpu as pltpu
from jax.sharding import PartitionSpec as P

FRESNEL = 8.0
LAG = 1
SCOPED = 4 << 20
F32 = jnp.float32
BF16 = jnp.bfloat16
HBM = pl.BlockSpec(memory_space=pl.ANY)
VMEM = pl.BlockSpec(memory_space=pltpu.VMEM)
SMEM = pl.BlockSpec(memory_space=pltpu.SMEM)


def in_hbm(x):
    return pltpu.with_memory_space_constraint(x, pltpu.HBM)


def in_vmem(x):
    return pltpu.with_memory_space_constraint(x, pltpu.VMEM)


def real_blocks(matrix):
    real, imag = matrix.real, matrix.imag
    left = np.block([[real, -imag], [imag, real]])
    right = np.block([[real, imag], [-imag, real]])
    return np.stack([left, right])


@functools.lru_cache(maxsize=None)
def make_tables(pixels):
    index = np.arange(pixels)
    freq = np.where(index < pixels // 2, index, index - pixels) / pixels
    spread = index[:, None] - index[None, :]
    phase = 2.0 * math.pi * freq * spread[:, :, None] - math.pi * FRESNEL * freq * freq
    propagator = np.mean(np.exp(1j * phase), axis=-1)
    turns = index[:, None] * index[None, :] % pixels
    fourier = np.exp(-2j * math.pi * turns / pixels) / math.sqrt(pixels)
    blocks = np.stack([real_blocks(propagator), real_blocks(fourier)]).astype(np.float32)
    high = blocks.astype(ml_dtypes.bfloat16)
    low = (blocks - high.astype(np.float32)).astype(ml_dtypes.bfloat16)
    return np.stack([high, low], axis=2)


def halves(x):
    high = x.astype(BF16)
    return high, (x - high.astype(F32)).astype(BF16)


def dot(a, b):
    return jnp.dot(a, b, preferred_element_type=F32)


def transform(left, right, fields):
    size = fields[0][0].shape[0]
    stacked = jnp.concatenate(
        [
            jnp.concatenate([real for real, _ in fields], axis=1),
            jnp.concatenate([imag for _, imag in fields], axis=1),
        ],
        axis=0,
    )
    high, low = halves(stacked)
    mid = dot(left[0], high) + (dot(left[1], high) + dot(left[0], low))
    rows = jnp.concatenate(
        [
            jnp.concatenate(
                [mid[:size, i * size : (i + 1) * size], mid[size:, i * size : (i + 1) * size]], axis=1
            )
            for i in range(len(fields))
        ],
        axis=0,
    )
    high, low = halves(rows)
    out = dot(high, right[0]) + (dot(high, right[1]) + dot(low, right[0]))
    return [
        (out[i * size : (i + 1) * size, :size], out[i * size : (i + 1) * size, size:])
        for i in range(len(fields))
    ]


def times(a, b):
    return a[0] * b[0] - a[1] * b[1], a[0] * b[1] + a[1] * b[0]


def times_conj(a, b):
    return a[0] * b[0] + a[1] * b[1], a[1] * b[0] - a[0] * b[1]


def cut_kernel(pixels, begin, corners, lat, own, other, unused, out, window, sems):
    half = own.shape[2]
    width = own.shape[3]
    tall = pixels + 8
    step = pl.program_id(0)
    steps = pl.num_programs(0)

    def places(step):
        probe = begin + step
        row = corners[2 * probe]
        column = corners[2 * probe + 1]
        row0 = jnp.minimum(row // 8 * 8, 2 * half - tall)
        col0 = jnp.minimum(column // pixels * pixels, width - 2 * pixels)
        top = row0 < half
        bottom = row0 + tall > half
        top_from = jnp.minimum(row0, half - tall)
        bottom_from = jnp.clip(row0 - half, 0, half - tall)
        offset = jnp.where(top, row0 - top_from, tall)
        return top, bottom, top_from, bottom_from, offset, row - row0, col0, column - col0

    def copies(step, slot, act):
        top, bottom, top_from, bottom_from, _, _, col0, _ = places(step)
        own_top = lat[0] == 0
        col0 = pl.multiple_of(col0, pixels)
        for source, is_top, sem in ((own, own_top, 0), (other, jnp.logical_not(own_top), 1)):
            start = pl.multiple_of(jnp.where(is_top, top_from, bottom_from), 8)
            to = pl.multiple_of(jnp.where(is_top, 0, tall), 8)

            @pl.when(jnp.where(is_top, top, bottom))
            def _(source=source, start=start, to=to, sem=sem):
                act(
                    pltpu.make_async_copy(
                        source.at[:, :, pl.ds(start, tall), pl.ds(col0, 2 * pixels)],
                        window.at[slot, :, :, pl.ds(to, tall), :],
                        sems.at[slot, sem],
                    )
                )

    slot = step % 2

    @pl.when(step == 0)
    def _():
        copies(0, 0, lambda copy: copy.start())

    @pl.when(step + 1 < steps)
    def _():
        copies(step + 1, 1 - slot, lambda copy: copy.start())

    copies(step, slot, lambda copy: copy.wait())
    *_, offset, down, _, shift = places(step)
    offset = pl.multiple_of(offset, 8)
    turn = (pixels - shift) % pixels
    probe = begin + step
    lane = lax.broadcasted_iota(jnp.int32, (tall, pixels), 1)
    for part in range(own.shape[0]):
        for layer in range(own.shape[1]):
            near = window[slot, part, layer, pl.ds(offset, tall), pl.ds(0, pixels)]
            far = window[slot, part, layer, pl.ds(offset, tall), pl.ds(pixels, pixels)]
            near = pltpu.roll(near, turn, 1)
            far = pltpu.roll(far, turn, 1)
            patch = jnp.where(lane < pixels - shift, near, far)
            out[probe // out.shape[1], probe % out.shape[1], layer, part] = pltpu.roll(patch, (tall - down) % tall, 0)[:pixels]


def cut_patches(own, other, corners, lat, patches, begin, end):
    _, _, layers, parts, pixels, _ = patches.shape
    size = (end - begin) * layers * parts * pixels * pixels
    return pl.pallas_call(
        functools.partial(cut_kernel, pixels, begin),
        grid_spec=pltpu.PrefetchScalarGridSpec(
            num_scalar_prefetch=2,
            grid=(end - begin,),
            in_specs=[HBM, HBM, VMEM],
            out_specs=VMEM,
            scratch_shapes=[
                pltpu.VMEM((2, parts, layers, 2 * (pixels + 8), 2 * pixels), F32),
                pltpu.SemaphoreType.DMA((2, 2)),
            ],
        ),
        out_shape=pltpu.VMEM(patches.shape, F32),
        input_output_aliases={4: 0},
        compiler_params=pltpu.CompilerParams(vmem_limit_bytes=8 << 20),
        cost_estimate=pl.CostEstimate(flops=size * 4, bytes_accessed=size * 12, transcendentals=0),
        name="cut_patches",
    )(corners.reshape(-1), lat.reshape(1), in_hbm(own), in_hbm(other), in_vmem(patches))


def rooms_kernel(patches, seen, total):
    total[...] = jnp.zeros(total.shape, F32)


def make_rooms(stack, total):
    return pl.pallas_call(
        rooms_kernel,
        out_specs=[VMEM] * 3,
        out_shape=[pltpu.VMEM(stack, F32), pltpu.VMEM(stack, F32), pltpu.VMEM(total, F32)],
        compiler_params=pltpu.CompilerParams(vmem_limit_bytes=SCOPED),
        name="make_rooms",
    )()


def forward_kernel(scalars, patches, arrived, start_wave, frames, tables, unused, leave, seen):
    group, active, first, final = (scalars[i] for i in range(4))
    count, layers = patches.shape[1:3]

    @pl.when(active == 1)
    def _():
        wave = [
            tuple(jnp.where(first == 1, start_wave[part], arrived[i, part]) for part in range(2))
            for i in range(count)
        ]
        for layer in range(layers):
            chi = []
            for i in range(count):
                for part in range(2):
                    seen[group, i, layer, part] = wave[i][part]
                here = patches[group, i, layer, 0], patches[group, i, layer, 1]
                chi.append(times(here, wave[i]))
            at = final if layer == layers - 1 else 0
            wave = transform((tables[at, 0, 0], tables[at, 0, 1]), (tables[at, 1, 0], tables[at, 1, 1]), chi)
        for i in range(count):
            real, imag = wave[i]
            misfit = real * real + imag * imag - frames[group, i]
            factor = jnp.where(final == 1, misfit, 1.0)
            leave[i, 0] = real * factor
            leave[i, 1] = imag * factor


def backward_kernel(scalars, patches, arrived, own, seen, tables, leave, grads):
    group, active, _, final = (scalars[i] for i in range(4))
    count, layers = patches.shape[1:3]

    @pl.when(active == 1)
    def _():
        wave = [
            tuple(jnp.where(final == 1, own[i, part], arrived[i, part]) for part in range(2))
            for i in range(count)
        ]
        for layer in reversed(range(layers)):
            at = final if layer == layers - 1 else 0
            chi = transform((tables[at, 1, 0], tables[at, 1, 1]), (tables[at, 0, 0], tables[at, 0, 1]), wave)
            wave = []
            for i in range(count):
                before = seen[group, i, layer, 0], seen[group, i, layer, 1]
                here = patches[group, i, layer, 0], patches[group, i, layer, 1]
                real, imag = times_conj(chi[i], before)
                grads[i, layer, 0] = real
                grads[i, layer, 1] = imag
                wave.append(times_conj(chi[i], here))
        for i in range(count):
            leave[i, 0] = wave[i][0]
            leave[i, 1] = wave[i][1]


def cost(count, layers, pixels):
    return pl.CostEstimate(
        flops=count * layers * 2 * 3 * 8 * pixels**3,
        bytes_accessed=count * (layers * 4 + 4) * pixels * pixels * 4,
        transcendentals=0,
    )


def run_forward(scalars, patches, arrived, start_wave, frames, tables, store):
    _, count, layers, _, pixels, _ = patches.shape
    return pl.pallas_call(
        forward_kernel,
        in_specs=[SMEM] + [VMEM] * 6,
        out_specs=[VMEM] * 2,
        out_shape=[pltpu.VMEM(arrived.shape, F32), pltpu.VMEM(store.shape, F32)],
        input_output_aliases={6: 1},
        compiler_params=pltpu.CompilerParams(vmem_limit_bytes=SCOPED),
        cost_estimate=cost(count, layers, pixels),
        name="forward_section",
    )(scalars, *map(in_vmem, (patches, arrived, start_wave, frames, tables, store)))


def run_backward(scalars, patches, arrived, own, seen, tables):
    _, count, layers, _, pixels, _ = patches.shape
    return pl.pallas_call(
        backward_kernel,
        in_specs=[SMEM] + [VMEM] * 5,
        out_specs=[VMEM] * 2,
        out_shape=[pltpu.VMEM(arrived.shape, F32), pltpu.VMEM(patches.shape[1:], F32)],
        compiler_params=pltpu.CompilerParams(vmem_limit_bytes=SCOPED),
        cost_estimate=cost(count, layers, pixels),
        name="backward_section",
    )(scalars, *map(in_vmem, (patches, arrived, own, seen, tables)))


def deposit_kernel(height, scalars, corners, sources, unused, total):
    pixels = sources[0].shape[-1]
    tall = pixels + 8
    width = total.shape[3]
    rows = total.shape[2] - 2 * tall
    lane = lax.broadcasted_iota(jnp.int32, (tall, pixels), 1)
    blank = jnp.zeros((8, pixels), F32)
    for which, grads in enumerate(sources):
        group, active = scalars[1 + 2 * which], scalars[2 + 2 * which]
        for i in range(grads.shape[0]):
            row = corners[which, group * grads.shape[0] + i, 0]
            column = corners[which, group * grads.shape[0] + i, 1]
            row0 = jnp.minimum(row // 8 * 8, height - tall)
            col0 = jnp.minimum(column // pixels * pixels, width - 2 * pixels)
            shift = column - col0
            near_at = pl.multiple_of(col0, pixels)
            far_at = pl.multiple_of(col0 + pixels, pixels)
            start = row0 - scalars[0] + tall

            @pl.when((active == 1) & (start > 0) & (start < rows + tall))
            def _(grads=grads, i=i, start=start, down=row - row0, shift=shift, near_at=near_at, far_at=far_at):
                at = pl.ds(pl.multiple_of(start, 8), tall)
                for layer in range(total.shape[1]):
                    for part in range(2):
                        padded = jnp.concatenate([grads[i, layer, part], blank], axis=0)
                        turned = pltpu.roll(pltpu.roll(padded, down, 0), shift % pixels, 1)
                        near = jnp.where(lane >= shift, turned, 0.0)
                        far = jnp.where(lane >= shift, 0.0, turned)
                        total[part, layer, at, pl.ds(near_at, pixels)] += near
                        total[part, layer, at, pl.ds(far_at, pixels)] += far


def deposit(scalars, corners, sources, total, height):
    n = len(sources)

    def body(scalars, corners, *refs):
        deposit_kernel(height, scalars, corners, refs[:n], *refs[n:])

    size = sum(source.size for source in sources)
    return pl.pallas_call(
        body,
        in_specs=[SMEM] * 2 + [VMEM] * (n + 1),
        out_specs=VMEM,
        out_shape=pltpu.VMEM(total.shape, F32),
        input_output_aliases={n + 2: 0},
        compiler_params=pltpu.CompilerParams(vmem_limit_bytes=SCOPED),
        cost_estimate=pl.CostEstimate(flops=size * 8, bytes_accessed=size * 12, transcendentals=0),
        name="deposit_patches",
    )(scalars, corners, *map(in_vmem, (*sources, total)))


def split_kernel(margin, lat, total, keep, send, sems):
    owners, rows = keep.shape[2:4]
    copies = []
    for owner in range(owners):
        for kind, target in ((lat[0], keep), (1 - lat[0], send)):
            start = pl.multiple_of(margin + (2 * owner + kind) * rows, 8)
            copies.append(
                pltpu.make_async_copy(
                    total.at[:, :, pl.ds(start, rows), :], target.at[:, :, owner], sems.at[len(copies)]
                )
            )
    for copy in copies:
        copy.start()
    for copy in copies:
        copy.wait()


def split_rows(total, lat, owners, margin):
    parts, layers, height, width = total.shape
    rows = (height - 2 * margin) // (2 * owners)
    half = jax.ShapeDtypeStruct((parts, layers, owners, rows, width), F32)
    return pl.pallas_call(
        functools.partial(split_kernel, margin),
        in_specs=[SMEM, VMEM],
        out_specs=[HBM, HBM],
        out_shape=[half, half],
        scratch_shapes=[pltpu.SemaphoreType.DMA((2 * owners,))],
        compiler_params=pltpu.CompilerParams(vmem_limit_bytes=SCOPED),
        name="split_rows",
    )(lat.reshape(1), in_vmem(total))


def swap(shard, axis):
    return lax.ppermute(shard, axis, [(0, 1), (1, 0)])


def local(specimen, illumination, positions, scan_index, frames):
    pixels = illumination.shape[-1]
    parts, layers, half, width = specimen.shape
    height = 2 * half
    tables = jnp.asarray(make_tables(pixels))
    section = lax.axis_index("depth")
    sections = lax.axis_size("depth")
    lat = lax.axis_index("lat")
    owners = lax.axis_size("probe")
    paired = owners == 2

    other = swap(specimen, "lat")
    corners = positions[scan_index.reshape(-1)]
    probes = corners.shape[0]
    count = 2 if probes % 2 == 0 else 1
    groups = probes // count
    wave = (count, parts, pixels, pixels)
    measured = frames.reshape((groups, count, pixels, pixels))
    if paired:
        both = jnp.stack([corners, swap(corners, "probe")])
        base = lax.axis_index("probe") * (height // 2)
    else:
        both = corners[None]
        base = jnp.int32(0)
    rows = height // 2 if paired else height
    patches, seen, total = make_rooms(
        (groups, count, layers, parts, pixels, pixels), (parts, layers, rows + 2 * (pixels + 8), width)
    )
    patches = cut_patches(specimen, other, corners, lat, patches, 0, count)

    is_first = (section == 0).astype(jnp.int32)
    is_last = (section == sections - 1).astype(jnp.int32)

    def scalars_of(group):
        active = ((group >= 0) & (group < groups)).astype(jnp.int32)
        return jnp.stack([jnp.clip(group, 0, groups - 1), active, is_first, is_last])

    def pairs_of(tick, by):
        pairs = []
        for source in range(sections):
            delay = source if by > 0 else 2 * (sections - 1) - source
            if 0 <= source + by < sections and 0 <= tick - LAG * delay < groups:
                pairs.append((source, source + by))
        return pairs

    nothing = jnp.zeros(wave, F32)
    down, up, across = {}, {}, None
    depth = LAG * (sections - 1)
    for tick in range(groups + 2 * depth):
        leaving = nothing
        if tick < groups + depth:
            scalars = scalars_of(tick - LAG * section)
            leaving, seen = run_forward(
                scalars, patches, down.pop(tick - LAG, nothing), illumination, measured, tables, seen
            )
            pairs = pairs_of(tick, 1)
            if pairs:
                down[tick] = lax.ppermute(leaving, "depth", pairs)
            if tick == 0:
                patches = cut_patches(specimen, other, corners, lat, patches, count, probes)
        if tick >= depth:
            scalars = scalars_of(tick - LAG * (2 * (sections - 1) - section))
            rising, grads = run_backward(
                scalars, patches, up.pop(tick - LAG, nothing), leaving, seen, tables
            )
            pairs = pairs_of(tick, -1)
            if pairs:
                up[tick] = lax.ppermute(rising, "depth", pairs)
            sources = [grads]
            ats = [scalars[:2]]
            if paired:
                if across is not None:
                    sources.append(across[0])
                    ats.append(across[1])
                across = (swap(grads, "probe"), scalars[:2])
            total = deposit(jnp.concatenate([base[None], *ats]), both, sources, total, height)
            if tick in down:
                total, down[tick] = lax.optimization_barrier((total, down[tick]))
            elif tick in up:
                total, up[tick] = lax.optimization_barrier((total, up[tick]))
    if paired:
        scalars = jnp.concatenate([base[None], across[1]])
        total = deposit(scalars, both[1:], [across[0]], total, height)
        keep, send = split_rows(total, lat, 1, pixels + 8)
        return keep[:, :, 0] + swap(send[:, :, 0], "lat")
    keep, send = split_rows(total, lat, owners, pixels + 8)
    return lax.psum_scatter(keep + swap(send, "lat"), "probe", scatter_dimension=2, tiled=False)


def solution(mesh):
    return jax.shard_map(
        local,
        mesh=mesh,
        in_specs=(
            P(None, ("groups", "depth"), "lat", None),
            P(),
            P("groups", None),
            P("groups", ("probe", "lat")),
            P("groups", ("probe", "lat"), None, None),
        ),
        out_specs=P(None, ("groups", "depth"), ("probe", "lat"), None),
        check_vma=False,
    )
```

```python
import functools
import math

import jax
import jax.numpy as jnp
import ml_dtypes
import numpy as np
from jax import lax
from jax.experimental import pallas as pl
from jax.experimental.pallas import tpu as pltpu
from jax.sharding import PartitionSpec as P

FRESNEL = 8.0
CROSSING = 2
F32 = jnp.float32
BF16 = jnp.bfloat16
HBM = pl.BlockSpec(memory_space=pl.ANY)
VMEM = pl.BlockSpec(memory_space=pltpu.VMEM)
SMEM = pl.BlockSpec(memory_space=pltpu.SMEM)


def in_hbm(x):
    return pltpu.with_memory_space_constraint(x, pltpu.HBM)


def in_vmem(x):
    return pltpu.with_memory_space_constraint(x, pltpu.VMEM)


def real_blocks(matrix):
    real, imag = matrix.real, matrix.imag
    left = np.block([[real, -imag], [imag, real]])
    right = np.block([[real, imag], [-imag, real]])
    return np.stack([left, right])


@functools.lru_cache(maxsize=None)
def make_tables(pixels):
    index = np.arange(pixels)
    freq = np.where(index < pixels // 2, index, index - pixels) / pixels
    spread = index[:, None] - index[None, :]
    phase = 2.0 * math.pi * freq * spread[:, :, None] - math.pi * FRESNEL * freq * freq
    propagator = np.mean(np.exp(1j * phase), axis=-1)
    turns = index[:, None] * index[None, :] % pixels
    fourier = np.exp(-2j * math.pi * turns / pixels) / math.sqrt(pixels)
    blocks = np.stack([real_blocks(propagator), real_blocks(fourier)]).astype(np.float32)
    high = blocks.astype(ml_dtypes.bfloat16)
    low = (blocks - high.astype(np.float32)).astype(ml_dtypes.bfloat16)
    return np.stack([high, low], axis=2)


def halves(x):
    high = x.astype(BF16)
    return high, (x - high.astype(F32)).astype(BF16)


def dot(a, b):
    return jnp.dot(a, b, preferred_element_type=F32)


def transform(left, right, fields):
    size = fields[0][0].shape[0]
    stacked = jnp.concatenate(
        [
            jnp.concatenate([real for real, _ in fields], axis=1),
            jnp.concatenate([imag for _, imag in fields], axis=1),
        ],
        axis=0,
    )
    high, low = halves(stacked)
    mid = dot(left[0], high) + (dot(left[1], high) + dot(left[0], low))
    rows = jnp.concatenate(
        [
            jnp.concatenate(
                [mid[:size, i * size : (i + 1) * size], mid[size:, i * size : (i + 1) * size]], axis=1
            )
            for i in range(len(fields))
        ],
        axis=0,
    )
    high, low = halves(rows)
    out = dot(high, right[0]) + (dot(high, right[1]) + dot(low, right[0]))
    return [
        (out[i * size : (i + 1) * size, :size], out[i * size : (i + 1) * size, size:])
        for i in range(len(fields))
    ]


def times(a, b):
    return a[0] * b[0] - a[1] * b[1], a[0] * b[1] + a[1] * b[0]


def times_conj(a, b):
    return a[0] * b[0] + a[1] * b[1], a[1] * b[0] - a[0] * b[1]


class Layout:
    def __init__(self, probes, count, layers, pixels, rows, width):
        self.probes, self.count, self.layers, self.pixels = probes, count, layers, pixels
        self.groups = probes // count
        self.tall = pixels + 8
        self.rows, self.width = rows, width
        self.blocks = width // pixels
        self.deep = rows + 2 * self.tall
        stack = probes * layers * 2 * pixels
        self.seen_from = stack
        self.frames_from = 2 * stack
        self.total_from = self.frames_from + probes * pixels
        self.shape = (self.total_from + 2 * layers * self.blocks * self.deep, pixels)

    def stacked(self, group, i, layer, part):
        probe = group * self.count + i
        return ((probe * self.layers + layer) * 2 + part) * self.pixels

    def tile(self, start):
        return pl.ds(pl.multiple_of(start, 8), self.pixels)

    def patch(self, group, i, layer, part):
        return self.tile(self.stacked(group, i, layer, part))

    def seen(self, group, i, layer, part):
        return self.tile(self.seen_from + self.stacked(group, i, layer, part))

    def frame(self, group, i):
        return self.tile(self.frames_from + (group * self.count + i) * self.pixels)

    def total(self, part, layer, block, row):
        block = (part * self.layers + layer) * self.blocks + block
        return self.total_from + block * self.deep + row

    def window(self, corners, probe):
        row, column = corners[2 * probe], corners[2 * probe + 1]
        row0 = jnp.minimum(row // 8 * 8, self.height - self.tall)
        block = jnp.minimum(column // self.pixels, self.blocks - 2)
        return row0, row - row0, block, column - block * self.pixels


def call(lay, body, state, before, outs, scratch=(), grid=(), prefetch=(), limit=4, flops=0, moved=0, name=None):
    spaces = {"hbm": (HBM, in_hbm), "vmem": (VMEM, in_vmem), "smem": (SMEM, lambda x: x)}
    specs = [spaces[kind][0] for kind, _ in before]
    operands = [spaces[kind][1](x) for kind, x in before]
    at = len(prefetch) + len(before)

    def kernel(*refs):
        body(*refs[:at], *refs[at + 1 :])

    return pl.pallas_call(
        kernel,
        grid_spec=pltpu.PrefetchScalarGridSpec(
            num_scalar_prefetch=len(prefetch),
            grid=grid,
            in_specs=[*specs, VMEM],
            out_specs=[VMEM] * (1 + len(outs)),
            scratch_shapes=list(scratch),
        ),
        out_shape=[pltpu.VMEM(shape, F32) for shape in (lay.shape, *outs)],
        input_output_aliases={at: 0},
        compiler_params=pltpu.CompilerParams(vmem_limit_bytes=limit << 20),
        cost_estimate=pl.CostEstimate(flops=flops, bytes_accessed=moved, transcendentals=0),
        name=name,
    )(*prefetch, *operands, in_vmem(state))


def make_state(lay, frames):
    start = lay.total_from

    def body(frames, state, sem):
        copy = pltpu.make_async_copy(
            frames, state.at[pl.ds(lay.frames_from, lay.probes * lay.pixels), :], sem
        )
        copy.start()
        state[pl.ds(start, lay.shape[0] - start), :] = jnp.zeros((lay.shape[0] - start, lay.pixels), F32)
        copy.wait()

    return pl.pallas_call(
        body,
        in_specs=[HBM],
        out_specs=VMEM,
        out_shape=pltpu.VMEM(lay.shape, F32),
        scratch_shapes=[pltpu.SemaphoreType.DMA(())],
        compiler_params=pltpu.CompilerParams(vmem_limit_bytes=4 << 20),
        name="make_state",
    )(in_hbm(frames.reshape((-1, lay.pixels))))


def cut_patches(lay, info, own, other, state, begin, end):
    half = own.shape[2]
    tall, pixels = lay.tall, lay.pixels

    def body(info, own, other, state, window, sems):
        step = pl.program_id(0)
        steps = pl.num_programs(0)

        def copies(step, slot, act):
            row0, _, block, _ = lay.window(info.at[pl.ds(3, 2 * lay.probes)], begin + step)
            own_top = info[1] == 0
            for source, is_top, sem in ((own, own_top, 0), (other, jnp.logical_not(own_top), 1)):
                start = jnp.clip(row0 - jnp.where(is_top, 0, half), 0, half - tall)
                to = jnp.where(is_top, 0, tall)

                @pl.when(jnp.where(is_top, row0 < half, row0 + tall > half))
                def _(source=source, start=start, to=to, sem=sem):
                    act(
                        pltpu.make_async_copy(
                            source.at[
                                :,
                                :,
                                pl.ds(pl.multiple_of(start, 8), tall),
                                pl.ds(pl.multiple_of(block * pixels, pixels), 2 * pixels),
                            ],
                            window.at[slot, :, :, pl.ds(pl.multiple_of(to, 8), tall), :],
                            sems.at[slot, sem],
                        )
                    )

        slot = step % 2

        @pl.when(step == 0)
        def _():
            copies(0, 0, lambda copy: copy.start())

        @pl.when(step + 1 < steps)
        def _():
            copies(step + 1, 1 - slot, lambda copy: copy.start())

        copies(step, slot, lambda copy: copy.wait())
        row0, down, _, shift = lay.window(info.at[pl.ds(3, 2 * lay.probes)], begin + step)
        offset = jnp.where(row0 < half, jnp.maximum(row0 - (half - tall), 0), tall)
        offset = pl.multiple_of(offset, 8)
        turn = (pixels - shift) % pixels
        lane = lax.broadcasted_iota(jnp.int32, (tall, pixels), 1)
        for part in range(2):
            for layer in range(lay.layers):
                near = window[slot, part, layer, pl.ds(offset, tall), pl.ds(0, pixels)]
                far = window[slot, part, layer, pl.ds(offset, tall), pl.ds(pixels, pixels)]
                near = pltpu.roll(near, turn, 1)
                far = pltpu.roll(far, turn, 1)
                patch = jnp.where(lane < pixels - shift, near, far)
                patch = pltpu.roll(patch, (tall - down) % tall, 0)[:pixels]
                state[lay.patch(0, begin + step, layer, part), :] = patch

    size = (end - begin) * lay.layers * 2 * pixels * pixels
    return call(
        lay,
        body,
        state,
        [("hbm", own), ("hbm", other)],
        [],
        scratch=[
            pltpu.VMEM((2, 2, lay.layers, 2 * tall, 2 * pixels), F32),
            pltpu.SemaphoreType.DMA((2, 2)),
        ],
        grid=(end - begin,),
        prefetch=(info,),
        limit=8,
        flops=size * 4,
        moved=size * 12,
        name="cut_patches",
    )[0]


def section_cost(lay):
    size = lay.count * lay.pixels**2
    return dict(flops=lay.layers * 2 * 3 * 8 * size * lay.pixels, moved=(lay.layers * 2 + 4) * 8 * size)


def pair(ref, at):
    return ref[at(0), :], ref[at(1), :]


def run_forward(lay, tick, sections, info, tables, state, arrived, start_wave):
    def body(info, tables, *refs):
        arrived_ref = refs[0] if arrived is not None else None
        start_ref = refs[-3] if start_wave is not None else None
        state, leave = refs[-2:]
        section = info[0]
        group = tick - section
        final = (section == sections - 1).astype(jnp.int32)

        @pl.when((group >= 0) & (group < lay.groups))
        def _():
            wave = []
            for i in range(lay.count):
                if arrived is None:
                    wave.append((start_ref[0], start_ref[1]))
                elif start_wave is None:
                    wave.append((arrived_ref[i, 0], arrived_ref[i, 1]))
                else:
                    wave.append(
                        tuple(jnp.where(section == 0, start_ref[p], arrived_ref[i, p]) for p in range(2))
                    )
            for layer in range(lay.layers):
                chi = []
                for i in range(lay.count):
                    for part in range(2):
                        state[lay.seen(group, i, layer, part), :] = wave[i][part]
                    chi.append(times(pair(state, functools.partial(lay.patch, group, i, layer)), wave[i]))
                at = final if layer == lay.layers - 1 else 0
                wave = transform((tables[at, 0, 0], tables[at, 0, 1]), (tables[at, 1, 0], tables[at, 1, 1]), chi)
            for i in range(lay.count):
                real, imag = wave[i]
                misfit = real * real + imag * imag - state[lay.frame(group, i), :]
                factor = jnp.where(final == 1, misfit, 1.0)
                leave[i, 0] = real * factor
                leave[i, 1] = imag * factor

    waves = [("vmem", x) for x in (arrived, start_wave) if x is not None]
    return call(
        lay,
        body,
        state,
        [("smem", info), ("vmem", tables), *waves],
        [(lay.count, 2, lay.pixels, lay.pixels)],
        name="forward_section",
        **section_cost(lay),
    )


def run_backward(lay, tick, sections, info, tables, state, arrived, own):
    def body(info, tables, *refs):
        arrived_ref = refs[0] if arrived is not None else None
        own_ref = refs[-4] if own is not None else None
        state, leave, grads = refs[-3:]
        section = info[0]
        group = tick - (2 * (sections - 1) - section)
        final = (section == sections - 1).astype(jnp.int32)

        @pl.when((group >= 0) & (group < lay.groups))
        def _():
            wave = []
            for i in range(lay.count):
                if arrived is None:
                    wave.append((own_ref[i, 0], own_ref[i, 1]))
                elif own is None:
                    wave.append((arrived_ref[i, 0], arrived_ref[i, 1]))
                else:
                    wave.append(
                        tuple(jnp.where(final == 1, own_ref[i, p], arrived_ref[i, p]) for p in range(2))
                    )
            for layer in reversed(range(lay.layers)):
                at = final if layer == lay.layers - 1 else 0
                chi = transform((tables[at, 1, 0], tables[at, 1, 1]), (tables[at, 0, 0], tables[at, 0, 1]), wave)
                wave = []
                for i in range(lay.count):
                    real, imag = times_conj(chi[i], pair(state, functools.partial(lay.seen, group, i, layer)))
                    grads[i, layer, 0] = real
                    grads[i, layer, 1] = imag
                    wave.append(times_conj(chi[i], pair(state, functools.partial(lay.patch, group, i, layer))))
            for i in range(lay.count):
                leave[i, 0] = wave[i][0]
                leave[i, 1] = wave[i][1]

    waves = [("vmem", x) for x in (arrived, own) if x is not None]
    return call(
        lay,
        body,
        state,
        [("smem", info), ("vmem", tables), *waves],
        [
            (lay.count, 2, lay.pixels, lay.pixels),
            (lay.count, lay.layers, 2, lay.pixels, lay.pixels),
        ],
        name="backward_section",
        **section_cost(lay),
    )


def deposit(lay, sections, info, sources, state):
    n = len(sources)
    pixels, tall = lay.pixels, lay.tall

    def body(info, *refs):
        state = refs[2 * n]
        lane = lax.broadcasted_iota(jnp.int32, (tall, pixels), 1)
        blank = jnp.zeros((8, pixels), F32)
        for which, (tick, _, _) in enumerate(sources):
            corners, grads = refs[which], refs[n + which]
            group = tick - (2 * (sections - 1) - info[0])
            active = (group >= 0) & (group < lay.groups)
            for i in range(lay.count):
                probe = jnp.clip(group, 0, lay.groups - 1) * lay.count + i
                row0, down, block, shift = lay.window(corners, probe)
                start = row0 - info[2] + tall

                @pl.when(active & (start > 0) & (start < lay.rows + tall))
                def _(grads=grads, i=i, start=start, down=down, block=block, shift=shift):
                    for layer in range(lay.layers):
                        for part in range(2):
                            padded = jnp.concatenate([grads[i, layer, part], blank], axis=0)
                            turned = pltpu.roll(pltpu.roll(padded, down, 0), shift % pixels, 1)
                            near = pl.ds(pl.multiple_of(lay.total(part, layer, block, start), 8), tall)
                            far = pl.ds(pl.multiple_of(lay.total(part, layer, block + 1, start), 8), tall)
                            state[near, :] += jnp.where(lane >= shift, turned, 0.0)
                            state[far, :] += jnp.where(lane >= shift, 0.0, turned)

    size = sum(grads.size for *_, grads in sources)
    return call(
        lay,
        body,
        state,
        [("smem", info)]
        + [("smem", corners) for _, corners, _ in sources]
        + [("vmem", grads) for *_, grads in sources],
        [],
        flops=size * 8,
        moved=size * 12,
        name="deposit_patches",
    )[0]


def split_rows(lay, info, state, owners):
    rows = lay.rows // (2 * owners)

    def body(info, state, keep, send, sems):
        copies = []
        for owner in range(owners):
            for kind, target in ((info[1], keep), (1 - info[1], send)):
                for part in range(2):
                    for layer in range(lay.layers):
                        for block in range(lay.blocks):
                            start = lay.total(part, layer, block, lay.tall + (2 * owner + kind) * rows)
                            copies.append(
                                pltpu.make_async_copy(
                                    state.at[pl.ds(pl.multiple_of(start, 8), rows), :],
                                    target.at[part, layer, owner, :, pl.ds(block * lay.pixels, lay.pixels)],
                                    sems.at[len(copies)],
                                )
                            )
        for copy in copies:
            copy.start()
        for copy in copies:
            copy.wait()

    half = (2, lay.layers, owners, rows, lay.width)
    return pl.pallas_call(
        body,
        in_specs=[SMEM, VMEM],
        out_specs=[VMEM, VMEM],
        out_shape=[pltpu.VMEM(half, F32), pltpu.VMEM(half, F32)],
        scratch_shapes=[pltpu.SemaphoreType.DMA((4 * owners * lay.layers * lay.blocks,))],
        compiler_params=pltpu.CompilerParams(vmem_limit_bytes=4 << 20),
        name="split_rows",
    )(info, in_vmem(state))


def swap(shard, axis):
    return lax.ppermute(shard, axis, [(0, 1), (1, 0)])


def local(specimen, illumination, positions, scan_index, frames):
    pixels = illumination.shape[-1]
    _, layers, half, width = specimen.shape
    height = 2 * half
    tables = jnp.asarray(make_tables(pixels))
    section = lax.axis_index("depth")
    sections = lax.axis_size("depth")
    owners = lax.axis_size("probe")
    paired = owners == 2

    other = swap(specimen, "lat")
    corners = positions[scan_index.reshape(-1)].reshape(-1)
    probes = corners.shape[0] // 2
    count = 2 if probes % 2 == 0 else 1
    base = lax.axis_index("probe") * half if paired else 0
    lay = Layout(probes, count, layers, pixels, half if paired else height, width)
    lay.height = height
    info = jnp.concatenate([jnp.stack([section, lax.axis_index("lat"), jnp.int32(base)]), corners])
    partner = swap(corners, "probe") if paired else corners
    state = make_state(lay, frames)
    state = cut_patches(lay, info, specimen, other, state, 0, count)

    def busy(tick, source, by):
        delay = source if by > 0 else 2 * (sections - 1) - source
        return 0 <= tick - delay < lay.groups

    def pass_on(wave, tick, by):
        pairs = [
            (source, source + by)
            for source in range(sections)
            if 0 <= source + by < sections and busy(tick, source, by)
        ]
        return lax.ppermute(wave, "depth", pairs) if pairs else None

    def cross(grads, tick):
        pairs = [
            (2 * source + side, 2 * source + 1 - side)
            for source in range(sections)
            for side in range(2)
            if busy(tick, source, -1)
        ]
        return lax.ppermute(grads, ("depth", "probe"), pairs)

    down = up = None
    crossing = []
    last_tick = lay.groups + 2 * (sections - 1) - 1
    for tick in range(last_tick + 1):
        own = None
        if tick < lay.groups + sections - 1:
            start_wave = illumination if tick < lay.groups else None
            state, own = run_forward(lay, tick, sections, info, tables, state, down, start_wave)
            down = pass_on(own, tick, 1)
            if tick == 0:
                state = cut_patches(lay, info, specimen, other, state, count, probes)
        if tick >= sections - 1:
            state, rising, grads = run_backward(lay, tick, sections, info, tables, state, up, own)
            up = pass_on(rising, tick, -1)
            sources = [(tick, corners, grads)]
            if paired:
                crossing.append((tick, partner, cross(grads, tick)))
                if len(crossing) > CROSSING:
                    sources.append(crossing.pop(0))
            state = deposit(lay, sections, info, sources, state)
    for source in crossing:
        state = deposit(lay, sections, info, [source], state)
    if paired:
        keep, send = split_rows(lay, info, state, 1)
        return keep[:, :, 0] + swap(send[:, :, 0], "lat")
    keep, send = split_rows(lay, info, state, owners)
    return lax.psum_scatter(keep + swap(send, "lat"), "probe", scatter_dimension=2, tiled=False)


def solution(mesh):
    return jax.shard_map(
        local,
        mesh=mesh,
        in_specs=(
            P(None, ("groups", "depth"), "lat", None),
            P(),
            P("groups", None),
            P("groups", ("probe", "lat")),
            P("groups", ("probe", "lat"), None, None),
        ),
        out_specs=P(None, ("groups", "depth"), ("probe", "lat"), None),
        check_vma=False,
    )
```

```python
import functools
import math

import jax
import jax.numpy as jnp
import ml_dtypes
import numpy as np
from jax import lax
from jax.experimental import pallas as pl
from jax.experimental.pallas import tpu as pltpu
from jax.sharding import PartitionSpec as P

FRESNEL = 8.0
SCOPED = 8 << 20
CROSSING = 2
F32 = jnp.float32
BF16 = jnp.bfloat16
HBM = pl.BlockSpec(memory_space=pl.ANY)
VMEM = pl.BlockSpec(memory_space=pltpu.VMEM)
SMEM = pl.BlockSpec(memory_space=pltpu.SMEM)


def in_hbm(x):
    return pltpu.with_memory_space_constraint(x, pltpu.HBM)


def in_vmem(x):
    return pltpu.with_memory_space_constraint(x, pltpu.VMEM)


def real_blocks(matrix):
    real, imag = matrix.real, matrix.imag
    left = np.block([[real, -imag], [imag, real]])
    right = np.block([[real, imag], [-imag, real]])
    return np.stack([left, right])


@functools.lru_cache(maxsize=None)
def make_tables(pixels):
    index = np.arange(pixels)
    freq = np.where(index < pixels // 2, index, index - pixels) / pixels
    spread = index[:, None] - index[None, :]
    phase = 2.0 * math.pi * freq * spread[:, :, None] - math.pi * FRESNEL * freq * freq
    propagator = np.mean(np.exp(1j * phase), axis=-1)
    turns = index[:, None] * index[None, :] % pixels
    fourier = np.exp(-2j * math.pi * turns / pixels) / math.sqrt(pixels)
    blocks = np.stack([real_blocks(propagator), real_blocks(fourier)]).astype(np.float32)
    high = blocks.astype(ml_dtypes.bfloat16)
    low = (blocks - high.astype(np.float32)).astype(ml_dtypes.bfloat16)
    return np.stack([high, low], axis=2)


def halves(x):
    high = x.astype(BF16)
    return high, (x - high.astype(F32)).astype(BF16)


def dot(a, b):
    return jnp.dot(a, b, preferred_element_type=F32)


def transform(left, right, fields):
    size = fields[0][0].shape[0]
    stacked = jnp.concatenate(
        [
            jnp.concatenate([real for real, _ in fields], axis=1),
            jnp.concatenate([imag for _, imag in fields], axis=1),
        ],
        axis=0,
    )
    high, low = halves(stacked)
    mid = dot(left[0], high) + (dot(left[1], high) + dot(left[0], low))
    rows = jnp.concatenate(
        [
            jnp.concatenate(
                [mid[:size, i * size : (i + 1) * size], mid[size:, i * size : (i + 1) * size]], axis=1
            )
            for i in range(len(fields))
        ],
        axis=0,
    )
    high, low = halves(rows)
    out = dot(high, right[0]) + (dot(high, right[1]) + dot(low, right[0]))
    return [
        (out[i * size : (i + 1) * size, :size], out[i * size : (i + 1) * size, size:])
        for i in range(len(fields))
    ]


def times(a, b):
    return a[0] * b[0] - a[1] * b[1], a[0] * b[1] + a[1] * b[0]


def times_conj(a, b):
    return a[0] * b[0] + a[1] * b[1], a[1] * b[0] - a[0] * b[1]


class Layout:
    def __init__(self, probes, count, layers, pixels, rows, width):
        self.probes, self.count, self.layers, self.pixels = probes, count, layers, pixels
        self.groups = probes // count
        self.tall = pixels + 8
        self.rows, self.width = rows, width
        self.blocks = width // pixels
        self.deep = rows + 2 * self.tall
        stack = probes * layers * 2 * pixels
        self.seen_from = stack
        self.frames_from = 2 * stack
        self.total_from = self.frames_from + probes * pixels
        self.shape = (self.total_from + 2 * layers * self.blocks * self.deep, pixels)

    def stacked(self, group, i, layer, part):
        probe = group * self.count + i
        return ((probe * self.layers + layer) * 2 + part) * self.pixels

    def tile(self, start):
        return pl.ds(pl.multiple_of(start, 8), self.pixels)

    def patch(self, group, i, layer, part):
        return self.tile(self.stacked(group, i, layer, part))

    def seen(self, group, i, layer, part):
        return self.tile(self.seen_from + self.stacked(group, i, layer, part))

    def frame(self, group, i):
        return self.tile(self.frames_from + (group * self.count + i) * self.pixels)

    def total(self, part, layer, block, row):
        block = (part * self.layers + layer) * self.blocks + block
        return self.total_from + block * self.deep + row

    def window(self, info, probe, partner=False):
        at = 3 + 2 * (probe + partner * self.probes)
        row, column = info[at], info[at + 1]
        row0 = jnp.minimum(row // 8 * 8, self.height - self.tall)
        block = jnp.minimum(column // self.pixels, self.blocks - 2)
        return row0, row - row0, block, column - block * self.pixels


def call(lay, body, state, before, outs, scratch=(), grid=(), prefetch=(), flops=0, moved=0, name=None):
    spaces = {"hbm": (HBM, in_hbm), "vmem": (VMEM, in_vmem), "smem": (SMEM, lambda x: x)}
    specs = [spaces[kind][0] for kind, _ in before]
    operands = [spaces[kind][1](x) for kind, x in before]
    at = len(prefetch) + len(before)

    def kernel(*refs):
        body(*refs[:at], *refs[at + 1 :])

    return pl.pallas_call(
        kernel,
        grid_spec=pltpu.PrefetchScalarGridSpec(
            num_scalar_prefetch=len(prefetch),
            grid=grid,
            in_specs=[*specs, VMEM],
            out_specs=[VMEM] * (1 + len(outs)),
            scratch_shapes=list(scratch),
        ),
        out_shape=[pltpu.VMEM(shape, F32) for shape in (lay.shape, *outs)],
        input_output_aliases={at: 0},
        compiler_params=pltpu.CompilerParams(vmem_limit_bytes=SCOPED),
        cost_estimate=pl.CostEstimate(flops=flops, bytes_accessed=moved, transcendentals=0),
        name=name,
    )(*prefetch, *operands, in_vmem(state))


def make_state(lay, frames):
    start = lay.total_from

    def body(frames, state, sem):
        copy = pltpu.make_async_copy(
            frames, state.at[pl.ds(lay.frames_from, lay.probes * lay.pixels), :], sem
        )
        copy.start()
        state[pl.ds(start, lay.shape[0] - start), :] = jnp.zeros((lay.shape[0] - start, lay.pixels), F32)
        copy.wait()

    return pl.pallas_call(
        body,
        in_specs=[HBM],
        out_specs=VMEM,
        out_shape=pltpu.VMEM(lay.shape, F32),
        scratch_shapes=[pltpu.SemaphoreType.DMA(())],
        compiler_params=pltpu.CompilerParams(vmem_limit_bytes=SCOPED),
        name="make_state",
    )(in_hbm(frames.reshape((-1, lay.pixels))))


def cut_patches(lay, info, own, other, state, begin, end):
    half = own.shape[2]
    tall, pixels = lay.tall, lay.pixels

    def body(info, own, other, state, window, sems):
        step = pl.program_id(0)
        steps = pl.num_programs(0)

        def copies(step, slot, act):
            row0, _, block, _ = lay.window(info, begin + step)
            own_top = info[1] == 0
            for source, is_top, sem in ((own, own_top, 0), (other, jnp.logical_not(own_top), 1)):
                start = jnp.clip(row0 - jnp.where(is_top, 0, half), 0, half - tall)
                to = jnp.where(is_top, 0, tall)

                @pl.when(jnp.where(is_top, row0 < half, row0 + tall > half))
                def _(source=source, start=start, to=to, sem=sem):
                    act(
                        pltpu.make_async_copy(
                            source.at[
                                :,
                                :,
                                pl.ds(pl.multiple_of(start, 8), tall),
                                pl.ds(pl.multiple_of(block * pixels, pixels), 2 * pixels),
                            ],
                            window.at[slot, :, :, pl.ds(pl.multiple_of(to, 8), tall), :],
                            sems.at[slot, sem],
                        )
                    )

        slot = step % 2

        @pl.when(step == 0)
        def _():
            copies(0, 0, lambda copy: copy.start())

        @pl.when(step + 1 < steps)
        def _():
            copies(step + 1, 1 - slot, lambda copy: copy.start())

        copies(step, slot, lambda copy: copy.wait())
        row0, down, _, shift = lay.window(info, begin + step)
        offset = jnp.where(row0 < half, jnp.maximum(row0 - (half - tall), 0), tall)
        offset = pl.multiple_of(offset, 8)
        turn = (pixels - shift) % pixels
        lane = lax.broadcasted_iota(jnp.int32, (tall, pixels), 1)
        for part in range(2):
            for layer in range(lay.layers):
                near = window[slot, part, layer, pl.ds(offset, tall), pl.ds(0, pixels)]
                far = window[slot, part, layer, pl.ds(offset, tall), pl.ds(pixels, pixels)]
                near = pltpu.roll(near, turn, 1)
                far = pltpu.roll(far, turn, 1)
                patch = jnp.where(lane < pixels - shift, near, far)
                patch = pltpu.roll(patch, (tall - down) % tall, 0)[:pixels]
                state[lay.patch(0, begin + step, layer, part), :] = patch

    size = (end - begin) * lay.layers * 2 * pixels * pixels
    return call(
        lay,
        body,
        state,
        [("hbm", own), ("vmem", other)],
        [],
        scratch=[
            pltpu.VMEM((2, 2, lay.layers, 2 * tall, 2 * pixels), F32),
            pltpu.SemaphoreType.DMA((2, 2)),
        ],
        grid=(end - begin,),
        prefetch=(info,),
        flops=size * 4,
        moved=size * 12,
        name="cut_patches",
    )[0]


def section_cost(lay):
    size = lay.count * lay.pixels**2
    return dict(flops=lay.layers * 2 * 3 * 8 * size * lay.pixels, moved=(lay.layers * 2 + 4) * 8 * size)


def pair(ref, at):
    return ref[at(0), :], ref[at(1), :]


def run_forward(lay, tick, sections, info, tables, state, arrived, start_wave):
    def body(info, tables, *refs):
        arrived_ref = refs[0] if arrived is not None else None
        start_ref = refs[-3] if start_wave is not None else None
        state, leave = refs[-2:]
        section = info[0]
        group = tick - section
        final = (section == sections - 1).astype(jnp.int32)

        @pl.when((group >= 0) & (group < lay.groups))
        def _():
            wave = []
            for i in range(lay.count):
                if arrived is None:
                    wave.append((start_ref[0], start_ref[1]))
                elif start_wave is None:
                    wave.append((arrived_ref[i, 0], arrived_ref[i, 1]))
                else:
                    wave.append(
                        tuple(jnp.where(section == 0, start_ref[p], arrived_ref[i, p]) for p in range(2))
                    )
            for layer in range(lay.layers):
                chi = []
                for i in range(lay.count):
                    for part in range(2):
                        state[lay.seen(group, i, layer, part), :] = wave[i][part]
                    chi.append(times(pair(state, functools.partial(lay.patch, group, i, layer)), wave[i]))
                at = final if layer == lay.layers - 1 else 0
                wave = transform((tables[at, 0, 0], tables[at, 0, 1]), (tables[at, 1, 0], tables[at, 1, 1]), chi)
            for i in range(lay.count):
                real, imag = wave[i]
                misfit = real * real + imag * imag - state[lay.frame(group, i), :]
                factor = jnp.where(final == 1, misfit, 1.0)
                leave[i, 0] = real * factor
                leave[i, 1] = imag * factor

    waves = [("vmem", x) for x in (arrived, start_wave) if x is not None]
    return call(
        lay,
        body,
        state,
        [("smem", info), ("vmem", tables), *waves],
        [(lay.count, 2, lay.pixels, lay.pixels)],
        name="forward_section",
        **section_cost(lay),
    )


def run_backward(lay, tick, sections, info, tables, state, arrived, own):
    def body(info, tables, *refs):
        arrived_ref = refs[0] if arrived is not None else None
        own_ref = refs[-4] if own is not None else None
        state, leave, grads = refs[-3:]
        section = info[0]
        group = tick - (2 * (sections - 1) - section)
        final = (section == sections - 1).astype(jnp.int32)

        @pl.when((group >= 0) & (group < lay.groups))
        def _():
            wave = []
            for i in range(lay.count):
                if arrived is None:
                    wave.append((own_ref[i, 0], own_ref[i, 1]))
                elif own is None:
                    wave.append((arrived_ref[i, 0], arrived_ref[i, 1]))
                else:
                    wave.append(
                        tuple(jnp.where(final == 1, own_ref[i, p], arrived_ref[i, p]) for p in range(2))
                    )
            for layer in reversed(range(lay.layers)):
                at = final if layer == lay.layers - 1 else 0
                chi = transform((tables[at, 1, 0], tables[at, 1, 1]), (tables[at, 0, 0], tables[at, 0, 1]), wave)
                wave = []
                for i in range(lay.count):
                    real, imag = times_conj(chi[i], pair(state, functools.partial(lay.seen, group, i, layer)))
                    grads[i, layer, 0] = real
                    grads[i, layer, 1] = imag
                    wave.append(times_conj(chi[i], pair(state, functools.partial(lay.patch, group, i, layer))))
            for i in range(lay.count):
                leave[i, 0] = wave[i][0]
                leave[i, 1] = wave[i][1]

    waves = [("vmem", x) for x in (arrived, own) if x is not None]
    return call(
        lay,
        body,
        state,
        [("smem", info), ("vmem", tables), *waves],
        [
            (lay.count, 2, lay.pixels, lay.pixels),
            (lay.count, lay.layers, 2, lay.pixels, lay.pixels),
        ],
        name="backward_section",
        **section_cost(lay),
    )


def deposit(lay, sections, info, sources, state):
    n = len(sources)
    pixels, tall = lay.pixels, lay.tall

    def body(info, *refs):
        state = refs[n]
        lane = lax.broadcasted_iota(jnp.int32, (tall, pixels), 1)
        blank = jnp.zeros((8, pixels), F32)
        for grads, (tick, partner, _) in zip(refs, sources):
            group = tick - (2 * (sections - 1) - info[0])
            active = (group >= 0) & (group < lay.groups)
            for i in range(lay.count):
                probe = jnp.clip(group, 0, lay.groups - 1) * lay.count + i
                row0, down, block, shift = lay.window(info, probe, partner)
                start = row0 - info[2] + tall

                @pl.when(active & (start > 0) & (start < lay.rows + tall))
                def _(grads=grads, i=i, start=start, down=down, block=block, shift=shift):
                    for layer in range(lay.layers):
                        for part in range(2):
                            padded = jnp.concatenate([grads[i, layer, part], blank], axis=0)
                            turned = pltpu.roll(pltpu.roll(padded, down, 0), shift % pixels, 1)
                            near = pl.ds(pl.multiple_of(lay.total(part, layer, block, start), 8), tall)
                            far = pl.ds(pl.multiple_of(lay.total(part, layer, block + 1, start), 8), tall)
                            state[near, :] += jnp.where(lane >= shift, turned, 0.0)
                            state[far, :] += jnp.where(lane >= shift, 0.0, turned)

    size = sum(grads.size for *_, grads in sources)
    return call(
        lay,
        body,
        state,
        [("smem", info)] + [("vmem", grads) for *_, grads in sources],
        [],
        flops=size * 8,
        moved=size * 12,
        name="deposit_patches",
    )[0]


def split_rows(lay, info, state, owners):
    rows = lay.rows // (2 * owners)

    def body(info, state, keep, send, sems):
        copies = []
        for owner in range(owners):
            for kind, target in ((info[1], keep), (1 - info[1], send)):
                for part in range(2):
                    for layer in range(lay.layers):
                        for block in range(lay.blocks):
                            start = lay.total(part, layer, block, lay.tall + (2 * owner + kind) * rows)
                            copies.append(
                                pltpu.make_async_copy(
                                    state.at[pl.ds(pl.multiple_of(start, 8), rows), :],
                                    target.at[part, layer, owner, :, pl.ds(block * lay.pixels, lay.pixels)],
                                    sems.at[len(copies)],
                                )
                            )
        for copy in copies:
            copy.start()
        for copy in copies:
            copy.wait()

    half = (2, lay.layers, owners, rows, lay.width)
    return pl.pallas_call(
        body,
        in_specs=[SMEM, VMEM],
        out_specs=[VMEM, VMEM],
        out_shape=[pltpu.VMEM(half, F32), pltpu.VMEM(half, F32)],
        scratch_shapes=[pltpu.SemaphoreType.DMA((4 * owners * lay.layers * lay.blocks,))],
        compiler_params=pltpu.CompilerParams(vmem_limit_bytes=SCOPED),
        name="split_rows",
    )(info, in_vmem(state))


def swap(shard, axis):
    return lax.ppermute(shard, axis, [(0, 1), (1, 0)])


def local(specimen, illumination, positions, scan_index, frames):
    pixels = illumination.shape[-1]
    _, layers, half, width = specimen.shape
    height = 2 * half
    tables = jnp.asarray(make_tables(pixels))
    section = lax.axis_index("depth")
    sections = lax.axis_size("depth")
    owners = lax.axis_size("probe")
    paired = owners == 2

    other = swap(specimen, "lat")
    corners = positions[scan_index.reshape(-1)].reshape(-1)
    probes = corners.shape[0] // 2
    count = 2 if probes % 2 == 0 else 1
    base = lax.axis_index("probe") * half if paired else 0
    lay = Layout(probes, count, layers, pixels, half if paired else height, width)
    lay.height = height
    partner = swap(corners, "probe") if paired else corners
    place = jnp.stack([section, lax.axis_index("lat"), jnp.int32(base)])
    info = jnp.concatenate([place, corners, partner])
    state = make_state(lay, frames)
    state = cut_patches(lay, info, specimen, other, state, 0, count)

    def busy(tick, source, by):
        delay = source if by > 0 else 2 * (sections - 1) - source
        return 0 <= tick - delay < lay.groups

    def pass_on(wave, tick, by):
        pairs = [
            (source, source + by)
            for source in range(sections)
            if 0 <= source + by < sections and busy(tick, source, by)
        ]
        return lax.ppermute(wave, "depth", pairs) if pairs else None

    def cross(grads, tick):
        pairs = [
            (2 * source + side, 2 * source + 1 - side)
            for source in range(sections)
            for side in range(2)
            if busy(tick, source, -1)
        ]
        return lax.ppermute(grads, ("depth", "probe"), pairs)

    down = up = None
    crossing = []
    last_tick = lay.groups + 2 * (sections - 1) - 1
    for tick in range(last_tick + 1):
        own = None
        if tick < lay.groups + sections - 1:
            start_wave = illumination if tick < lay.groups else None
            state, own = run_forward(lay, tick, sections, info, tables, state, down, start_wave)
            down = pass_on(own, tick, 1)
            if tick == 0:
                state = cut_patches(lay, info, specimen, other, state, count, probes)
        if tick >= sections - 1:
            state, rising, grads = run_backward(lay, tick, sections, info, tables, state, up, own)
            up = pass_on(rising, tick, -1)
            sources = [(tick, False, grads)]
            if paired:
                crossing.append((tick, True, cross(grads, tick)))
                if len(crossing) > CROSSING:
                    sources.append(crossing.pop(0))
            state = deposit(lay, sections, info, sources, state)
    for source in crossing:
        state = deposit(lay, sections, info, [source], state)
    if paired:
        keep, send = split_rows(lay, info, state, 1)
        return keep[:, :, 0] + swap(send[:, :, 0], "lat")
    keep, send = split_rows(lay, info, state, owners)
    return lax.psum_scatter(keep + swap(send, "lat"), "probe", scatter_dimension=2, tiled=False)


def solution(mesh):
    return jax.shard_map(
        local,
        mesh=mesh,
        in_specs=(
            P(None, ("groups", "depth"), "lat", None),
            P(),
            P("groups", None),
            P("groups", ("probe", "lat")),
            P("groups", ("probe", "lat"), None, None),
        ),
        out_specs=P(None, ("groups", "depth"), ("probe", "lat"), None),
        check_vma=False,
    )
```

```python
import functools
import math

import jax
import jax.numpy as jnp
import ml_dtypes
import numpy as np
from jax import lax
from jax.experimental import pallas as pl
from jax.experimental.pallas import tpu as pltpu
from jax.sharding import PartitionSpec as P

FRESNEL = 8.0
SCOPED = 8 << 20
CROSSING = 3
F32 = jnp.float32
BF16 = jnp.bfloat16
HBM = pl.BlockSpec(memory_space=pl.ANY)
VMEM = pl.BlockSpec(memory_space=pltpu.VMEM)
SMEM = pl.BlockSpec(memory_space=pltpu.SMEM)


def in_hbm(x):
    return pltpu.with_memory_space_constraint(x, pltpu.HBM)


def in_vmem(x):
    return pltpu.with_memory_space_constraint(x, pltpu.VMEM)


def real_blocks(matrix):
    real, imag = matrix.real, matrix.imag
    left = np.block([[real, -imag], [imag, real]])
    right = np.block([[real, imag], [-imag, real]])
    return np.stack([left, right])


@functools.lru_cache(maxsize=None)
def make_tables(pixels):
    index = np.arange(pixels)
    freq = np.where(index < pixels // 2, index, index - pixels) / pixels
    spread = index[:, None] - index[None, :]
    phase = 2.0 * math.pi * freq * spread[:, :, None] - math.pi * FRESNEL * freq * freq
    propagator = np.mean(np.exp(1j * phase), axis=-1)
    turns = index[:, None] * index[None, :] % pixels
    fourier = np.exp(-2j * math.pi * turns / pixels) / math.sqrt(pixels)
    blocks = np.stack([real_blocks(propagator), real_blocks(fourier)]).astype(np.float32)
    high = blocks.astype(ml_dtypes.bfloat16)
    low = (blocks - high.astype(np.float32)).astype(ml_dtypes.bfloat16)
    return np.stack([high, low], axis=2)


def halves(x):
    high = x.astype(BF16)
    return high, (x - high.astype(F32)).astype(BF16)


def dot(a, b):
    return jnp.dot(a, b, preferred_element_type=F32)


def transform(left, right, fields):
    size = fields[0][0].shape[0]
    stacked = jnp.concatenate(
        [
            jnp.concatenate([real for real, _ in fields], axis=1),
            jnp.concatenate([imag for _, imag in fields], axis=1),
        ],
        axis=0,
    )
    high, low = halves(stacked)
    mid = dot(left[0], high) + (dot(left[1], high) + dot(left[0], low))
    rows = jnp.concatenate(
        [
            jnp.concatenate(
                [mid[:size, i * size : (i + 1) * size], mid[size:, i * size : (i + 1) * size]], axis=1
            )
            for i in range(len(fields))
        ],
        axis=0,
    )
    high, low = halves(rows)
    out = dot(high, right[0]) + (dot(high, right[1]) + dot(low, right[0]))
    return [
        (out[i * size : (i + 1) * size, :size], out[i * size : (i + 1) * size, size:])
        for i in range(len(fields))
    ]


def times(a, b):
    return a[0] * b[0] - a[1] * b[1], a[0] * b[1] + a[1] * b[0]


def times_conj(a, b):
    return a[0] * b[0] + a[1] * b[1], a[1] * b[0] - a[0] * b[1]


class Layout:
    def __init__(self, probes, count, layers, pixels, rows, height, width, only_sums=False):
        self.probes, self.count, self.layers, self.pixels = probes, count, layers, pixels
        self.groups = probes // count
        self.tall = pixels + 8
        self.rows, self.height, self.width = rows, height, width
        self.blocks = width // pixels
        self.deep = rows + 2 * self.tall
        self.column_bits = (width - 1).bit_length()
        self.name_bits = (4 * probes - 1).bit_length()
        self.stack = probes * layers * 2 * pixels
        self.seen_from = self.stack
        self.grads_from = 2 * self.stack
        self.frames_from = 3 * self.stack
        self.total_from = 0 if only_sums else self.frames_from + probes * pixels
        self.shape = (self.total_from + 2 * layers * self.blocks * self.deep, pixels)

    def stacked(self, group, i, layer, part):
        probe = group * self.count + i
        return ((probe * self.layers + layer) * 2 + part) * self.pixels

    def tile(self, start):
        return pl.ds(pl.multiple_of(start, 8), self.pixels)

    def patch(self, group, i, layer, part):
        return self.tile(self.stacked(group, i, layer, part))

    def seen(self, group, i, layer, part):
        return self.tile(self.seen_from + self.stacked(group, i, layer, part))

    def grad(self, group, i, layer, part):
        return self.tile(self.grads_from + self.stacked(group, i, layer, part))

    def grads_of(self, begin, end):
        each = self.stack // self.groups
        return self.grads_from + begin * each, self.grads_from + end * each

    def frame(self, group, i):
        return self.tile(self.frames_from + (group * self.count + i) * self.pixels)

    def total(self, part, layer, block, row):
        block = (part * self.layers + layer) * self.blocks + block
        return self.total_from + block * self.deep + row

    def pack(self, row, column, name):
        return (((row << self.column_bits) + column) << self.name_bits) + name

    def row(self, key):
        return key >> (self.column_bits + self.name_bits)

    def window(self, info, probe, partner=False):
        key = info[0, probe + partner * self.probes]
        row = self.row(key)
        column = (key >> self.name_bits) & ((1 << self.column_bits) - 1)
        row0 = jnp.minimum(row // 8 * 8, self.height - self.tall)
        block = jnp.minimum(column // self.pixels, self.blocks - 2)
        return row0, row - row0, block, column - block * self.pixels


def call(lay, body, state, before, outs, scratch=(), grid=(), flops=0, moved=0, name=None):
    spaces = {"hbm": (HBM, in_hbm), "vmem": (VMEM, in_vmem), "smem": (SMEM, lambda x: x)}
    specs = [spaces[kind][0] for kind, _ in before]
    operands = [spaces[kind][1](x) for kind, x in before]
    at = len(before)
    aliases = {}
    if state is not None:
        specs.append(VMEM)
        operands.append(in_vmem(state))
        aliases = {at: 0}

    def kernel(*refs):
        body(*refs[:at], *refs[at + len(aliases) :])

    return pl.pallas_call(
        kernel,
        grid=grid,
        in_specs=specs,
        out_specs=[VMEM] * (1 + len(outs)),
        out_shape=[pltpu.VMEM(shape, F32) for shape in (lay.shape, *outs)],
        scratch_shapes=list(scratch),
        input_output_aliases=aliases,
        compiler_params=pltpu.CompilerParams(vmem_limit_bytes=SCOPED),
        cost_estimate=pl.CostEstimate(flops=flops, bytes_accessed=moved, transcendentals=0),
        name=name,
    )(*operands)


def clear_total(lay, state):
    start = lay.total_from

    def body(state):
        state[pl.ds(start, lay.shape[0] - start), :] = jnp.zeros((lay.shape[0] - start, lay.pixels), F32)

    return call(lay, body, state, [], [], name="clear_total")[0]


def place_frames(lay, info, pools, state):
    def body(info, *refs):
        *pools, state, sems = refs
        lat, side = lax.axis_index("lat"), lax.axis_index("probe")
        for act in ("start", "wait"):
            for probe in range(lay.probes):
                name = info[0, probe] & ((1 << lay.name_bits) - 1)
                owner = name // lay.probes
                slot = name % lay.probes
                if len(pools) > 1:
                    slot += ((owner // 2) ^ side) * lay.probes + ((owner % 2) ^ lat) * 2 * lay.probes
                first = 0
                for pool in pools:
                    size = pool.shape[0] // lay.pixels

                    @pl.when((slot >= first) & (slot < first + size))
                    def _(pool=pool, first=first, probe=probe, slot=slot):
                        copy = pltpu.make_async_copy(
                            pool.at[lay.tile((slot - first) * lay.pixels), :],
                            state.at[lay.frame(0, probe), :],
                            sems.at[probe],
                        )
                        getattr(copy, act)()

                    first += size

    pools = [("hbm", pool.reshape((-1, lay.pixels))) for pool in pools]
    return call(
        lay,
        body,
        state,
        [("smem", info), *pools],
        [],
        scratch=[pltpu.SemaphoreType.DMA((lay.probes,))],
        moved=lay.probes * lay.pixels**2 * 8,
        name="place_frames",
    )[0]


def cut_patches(lay, info, own, other, state, begin, end):
    half = own.shape[2]
    tall, pixels = lay.tall, lay.pixels

    def body(info, own, other, state, window):
        probe = begin + pl.program_id(0)
        row0, down, block, shift = lay.window(info, probe)
        own_top = lax.axis_index("lat") == 0
        near_at = pl.ds(pl.multiple_of(block * pixels, pixels), pixels)
        far_at = pl.ds(pl.multiple_of((block + 1) * pixels, pixels), pixels)
        for source, is_top in ((own, own_top), (other, jnp.logical_not(own_top))):
            start = jnp.clip(row0 - jnp.where(is_top, 0, half), 0, half - tall)
            to = pl.ds(pl.multiple_of(jnp.where(is_top, 0, tall), 8), tall)
            rows = pl.ds(pl.multiple_of(start, 8), tall)

            @pl.when(jnp.where(is_top, row0 < half, row0 + tall > half))
            def _(source=source, rows=rows, to=to):
                for part in range(2):
                    for layer in range(lay.layers):
                        window[part, layer, to, 0:pixels] = source[part, layer, rows, near_at]
                        window[part, layer, to, pixels : 2 * pixels] = source[part, layer, rows, far_at]

        offset = jnp.where(row0 < half, jnp.maximum(row0 - (half - tall), 0), tall)
        rows = pl.ds(pl.multiple_of(offset, 8), tall)
        turn = (pixels - shift) % pixels
        lane = lax.broadcasted_iota(jnp.int32, (tall, pixels), 1)
        for part in range(2):
            for layer in range(lay.layers):
                near = pltpu.roll(window[part, layer, rows, 0:pixels], turn, 1)
                far = pltpu.roll(window[part, layer, rows, pixels : 2 * pixels], turn, 1)
                patch = jnp.where(lane < pixels - shift, near, far)
                patch = pltpu.roll(patch, (tall - down) % tall, 0)[:pixels]
                state[lay.patch(0, probe, layer, part), :] = patch

    size = (end - begin) * lay.layers * 2 * pixels * pixels
    return call(
        lay,
        body,
        state,
        [("smem", info), ("vmem", own), ("vmem", other)],
        [],
        scratch=[pltpu.VMEM((2, lay.layers, 2 * tall, 2 * pixels), F32)],
        grid=(end - begin,),
        flops=size * 4,
        moved=size * 12,
        name="cut_patches",
    )[0]


def section_cost(lay):
    size = lay.count * lay.pixels**2
    return dict(flops=lay.layers * 2 * 3 * 8 * size * lay.pixels, moved=(lay.layers * 2 + 4) * 8 * size)


def pair(ref, at):
    return ref[at(0), :], ref[at(1), :]


def run_forward(lay, tick, sections, tables, state, arrived, start_wave):
    def body(tables, *refs):
        arrived_ref = refs[0] if arrived is not None else None
        start_ref = refs[-3] if start_wave is not None else None
        state, leave = refs[-2:]
        section = lax.axis_index("depth")
        group = tick - section
        final = (section == sections - 1).astype(jnp.int32)

        @pl.when((group >= 0) & (group < lay.groups))
        def _():
            wave = []
            for i in range(lay.count):
                if arrived is None:
                    wave.append((start_ref[0], start_ref[1]))
                elif start_wave is None:
                    wave.append((arrived_ref[i, 0], arrived_ref[i, 1]))
                else:
                    wave.append(
                        tuple(jnp.where(section == 0, start_ref[p], arrived_ref[i, p]) for p in range(2))
                    )
            for layer in range(lay.layers):
                chi = []
                for i in range(lay.count):
                    for part in range(2):
                        state[lay.seen(group, i, layer, part), :] = wave[i][part]
                    chi.append(times(pair(state, functools.partial(lay.patch, group, i, layer)), wave[i]))
                at = final if layer == lay.layers - 1 else 0
                wave = transform((tables[at, 0, 0], tables[at, 0, 1]), (tables[at, 1, 0], tables[at, 1, 1]), chi)
            for i in range(lay.count):
                real, imag = wave[i]
                misfit = real * real + imag * imag - state[lay.frame(group, i), :]
                factor = jnp.where(final == 1, misfit, 1.0)
                leave[i, 0] = real * factor
                leave[i, 1] = imag * factor

    waves = [("vmem", x) for x in (arrived, start_wave) if x is not None]
    return call(
        lay,
        body,
        state,
        [("vmem", tables), *waves],
        [(lay.count, 2, lay.pixels, lay.pixels)],
        name="forward_section",
        **section_cost(lay),
    )


def run_backward(lay, tick, sections, tables, state, arrived, own):
    def body(tables, *refs):
        arrived_ref = refs[0] if arrived is not None else None
        own_ref = refs[-3] if own is not None else None
        state, leave = refs[-2:]
        section = lax.axis_index("depth")
        group = tick - (2 * (sections - 1) - section)
        final = (section == sections - 1).astype(jnp.int32)

        @pl.when((group >= 0) & (group < lay.groups))
        def _():
            wave = []
            for i in range(lay.count):
                if arrived is None:
                    wave.append((own_ref[i, 0], own_ref[i, 1]))
                elif own is None:
                    wave.append((arrived_ref[i, 0], arrived_ref[i, 1]))
                else:
                    wave.append(
                        tuple(jnp.where(final == 1, own_ref[i, p], arrived_ref[i, p]) for p in range(2))
                    )
            for layer in reversed(range(lay.layers)):
                at = final if layer == lay.layers - 1 else 0
                chi = transform((tables[at, 1, 0], tables[at, 1, 1]), (tables[at, 0, 0], tables[at, 0, 1]), wave)
                wave = []
                for i in range(lay.count):
                    real, imag = times_conj(chi[i], pair(state, functools.partial(lay.seen, group, i, layer)))
                    state[lay.grad(group, i, layer, 0), :] = real
                    state[lay.grad(group, i, layer, 1), :] = imag
                    wave.append(times_conj(chi[i], pair(state, functools.partial(lay.patch, group, i, layer))))
            for i in range(lay.count):
                leave[i, 0] = wave[i][0]
                leave[i, 1] = wave[i][1]

    waves = [("vmem", x) for x in (arrived, own) if x is not None]
    return call(
        lay,
        body,
        state,
        [("vmem", tables), *waves],
        [(lay.count, 2, lay.pixels, lay.pixels)],
        name="backward_section",
        **section_cost(lay),
    )


def deposit(lay, tick, sections, info, received, state):
    pixels, tall = lay.pixels, lay.tall

    def body(info, *refs):
        state = refs[-1]
        lane = lax.broadcasted_iota(jnp.int32, (tall, pixels), 1)
        blank = jnp.zeros((8, pixels), F32)
        base = lax.axis_index("probe") * lay.rows if lay.rows < lay.height else 0

        def add(probe, partner, active, load):
            row0, down, block, shift = lay.window(info, probe, partner)
            start = row0 - base + tall

            @pl.when(active & (start > 0) & (start < lay.rows + tall))
            def _():
                for layer in range(lay.layers):
                    for part in range(2):
                        padded = jnp.concatenate([load(layer, part), blank], axis=0)
                        turned = pltpu.roll(pltpu.roll(padded, down, 0), shift % pixels, 1)
                        near = pl.ds(pl.multiple_of(lay.total(part, layer, block, start), 8), tall)
                        far = pl.ds(pl.multiple_of(lay.total(part, layer, block + 1, start), 8), tall)
                        state[near, :] += jnp.where(lane >= shift, turned, 0.0)
                        state[far, :] += jnp.where(lane >= shift, 0.0, turned)

        if tick is not None:
            group = tick - (2 * (sections - 1) - lax.axis_index("depth"))
            active = (group >= 0) & (group < lay.groups)
            group = jnp.clip(group, 0, lay.groups - 1)
            for i in range(lay.count):
                add(
                    group * lay.count + i,
                    False,
                    active,
                    lambda layer, part, i=i: state[lay.grad(group, i, layer, part), :],
                )
        for ref, (first, grads) in zip(refs, received):

            def one(i, _, ref=ref, first=first):
                add(
                    first * lay.count + i,
                    True,
                    True,
                    lambda layer, part: ref[lay.patch(0, i, layer, part), :],
                )
                return 0

            lax.fori_loop(0, grads.shape[0] // (lay.layers * 2 * pixels), one, 0)

    size = lay.count * lay.layers * 2 * pixels**2 + sum(grads.size for _, grads in received)
    return call(
        lay,
        body,
        state,
        [("smem", info)] + [("vmem", grads) for _, grads in received],
        [],
        flops=size * 8,
        moved=size * 12,
        name="deposit_patches",
    )[0]


def split_rows(lay, state, owners):
    rows = lay.rows // (2 * owners)

    def body(state, keep, send, sems):
        lat = lax.axis_index("lat")
        copies = []
        for owner in range(owners):
            for kind, target in ((lat, keep), (1 - lat, send)):
                for part in range(2):
                    for layer in range(lay.layers):
                        for block in range(lay.blocks):
                            start = lay.total(part, layer, block, lay.tall + (2 * owner + kind) * rows)
                            copies.append(
                                pltpu.make_async_copy(
                                    state.at[pl.ds(pl.multiple_of(start, 8), rows), :],
                                    target.at[part, layer, owner, :, pl.ds(block * lay.pixels, lay.pixels)],
                                    sems.at[len(copies)],
                                )
                            )
        for copy in copies:
            copy.start()
        for copy in copies:
            copy.wait()

    half = (2, lay.layers, owners, rows, lay.width)
    return pl.pallas_call(
        body,
        in_specs=[VMEM],
        out_specs=[VMEM, VMEM],
        out_shape=[pltpu.VMEM(half, F32), pltpu.VMEM(half, F32)],
        scratch_shapes=[pltpu.SemaphoreType.DMA((4 * owners * lay.layers * lay.blocks,))],
        compiler_params=pltpu.CompilerParams(vmem_limit_bytes=SCOPED),
        name="split_rows",
    )(in_vmem(state))


def swap(shard, axis):
    return lax.ppermute(shard, axis, [(0, 1), (1, 0)])


def sort_probes(lay, early, positions, indices, specimen):
    n = lay.probes
    total = 4 * n

    def body(positions, *refs):
        *scans, specimen, info, brought, sem = refs
        copy = pltpu.make_async_copy(specimen, brought, sem)
        copy.start()
        lat, side = lax.axis_index("lat"), lax.axis_index("probe")
        lane = lax.broadcasted_iota(jnp.int32, (1, 128), 1)
        at = lax.broadcasted_iota(jnp.int32, (total, 128), 0)
        across = jnp.full((1, 128), jnp.iinfo(jnp.int32).max, jnp.int32)
        down = jnp.zeros((total, 128), jnp.int32)
        for which, scan in enumerate(scans):
            owner = (side ^ (which % 2)) * 2 + (lat ^ (which // 2))
            for i in range(n):
                place = scan[i]
                key = lay.pack(positions[0, place], positions[1, place], owner * n + i)
                across = jnp.where(lane == which * n + i, key, across)
                down = jnp.where(at == which * n + i, key, down)
        rank = jnp.sum((across < down).astype(jnp.int32), axis=1, keepdims=True)
        partner = lane // n
        order = 2 * (lane % n) + lat
        wanted = jnp.where((side ^ partner) == 0, 2 * n - 1 - order, 2 * n + order)
        reach = 2 * early * lay.count
        wanted = jnp.where(lane == 2 * n, 2 * n - 1 - reach, wanted)
        wanted = jnp.where(lane == 2 * n + 1, 2 * n + reach, wanted)
        wanted = jnp.where(lane > 2 * n + 1, -1, wanted)
        info[...] = jnp.sum(jnp.where(rank == wanted, down, 0), axis=0, keepdims=True)
        copy.wait()

    return pl.pallas_call(
        body,
        in_specs=[SMEM] * 5 + [HBM],
        out_specs=[VMEM, VMEM],
        out_shape=[jax.ShapeDtypeStruct((1, 128), jnp.int32), pltpu.VMEM(specimen.shape, F32)],
        scratch_shapes=[pltpu.SemaphoreType.DMA(())],
        compiler_params=pltpu.CompilerParams(vmem_limit_bytes=SCOPED),
        name="sort_probes",
    )(positions.T, *indices, in_hbm(specimen))


def local(specimen, illumination, positions, scan_index, frames):
    pixels = illumination.shape[-1]
    _, layers, half, width = specimen.shape
    height = 2 * half
    tables = jnp.asarray(make_tables(pixels))
    sections = lax.axis_size("depth")
    owners = lax.axis_size("probe")
    paired = owners == 2 and lax.axis_size("groups") <= 2
    probes = scan_index.size
    count = 2 if probes % 4 == 0 else 1
    lay = Layout(probes, count, layers, pixels, half if paired else height, height, width)
    early = lay.groups // 2

    other = swap(specimen, "lat")
    if paired:
        scan = scan_index.reshape(-1)
        others = [scan, swap(scan, "probe"), swap(scan, "lat")]
        others.append(lax.ppermute(scan, ("probe", "lat"), [(i, 3 - i) for i in range(4)]))
        info, specimen = sort_probes(lay, early, positions, others, specimen)
        measured, _ = lax.optimization_barrier((frames, info))
        end = sections - 1
        ends = [(2 * end, 2 * end + 1), (2 * end + 1, 2 * end)]
        mine = lax.ppermute(measured, ("depth", "probe"), ends)
        crossed = lax.ppermute(jnp.concatenate([frames, mine]), ("depth", "lat"), ends)
        pools = [frames, mine, crossed]
        everyone = swap(info, "groups") if lax.axis_size("groups") == 2 else info
    else:
        corners = positions[scan_index.reshape(-1)]
        info = lay.pack(corners[:, 0], corners[:, 1], jnp.arange(probes, dtype=jnp.int32))
        info = jnp.pad(info, (0, -probes % 128))[None]
        pools = [frames]
    state = cut_patches(lay, info, specimen, other, None, 0, count)

    def busy(tick, source, by):
        delay = source if by > 0 else 2 * (sections - 1) - source
        return 0 <= tick - delay < lay.groups

    def pass_on(wave, tick, by):
        pairs = [
            (source, source + by)
            for source in range(sections)
            if 0 <= source + by < sections and busy(tick, source, by)
        ]
        return lax.ppermute(wave, "depth", pairs) if pairs else None

    def grads_of(state, begin, end):
        begin, end = lay.grads_of(begin, end)
        return lax.slice_in_dim(state, begin, end)

    fill = sections - 1
    portion = -(-(lay.groups - 1) // fill) * count
    parts = [(0, early // 2), (early // 2, early)] if paired else []
    crossing = {}
    down = up = None
    cut = count
    for tick in range(lay.groups + 2 * fill):
        own = None
        if tick < lay.groups + fill:
            start_wave = illumination if tick < lay.groups else None
            state, own = run_forward(lay, tick, sections, tables, state, down, start_wave)
            down = pass_on(own, tick, 1)
            if cut < probes:
                state = cut_patches(lay, info, specimen, other, state, cut, min(cut + portion, probes))
                cut += portion
            if tick == 0:
                state = clear_total(lay, state)
            if tick == fill - 1:
                if paired:
                    state, everyone = lax.optimization_barrier((state, everyone))
                state = place_frames(lay, info, pools, state)
        if tick >= fill:
            state, rising = run_backward(lay, tick, sections, tables, state, up, own)
            up = pass_on(rising, tick, -1)
            received = crossing.pop(tick, [])
            for begin, end in parts:
                if tick == end - 1 + 2 * fill:
                    due = min(tick + CROSSING, lay.groups + 2 * fill - 1)
                    crossing.setdefault(due, []).append((begin, swap(grads_of(state, begin, end), "probe")))
            state = deposit(lay, tick, sections, info, received, state)
    if not paired:
        keep, send = split_rows(lay, state, owners)
        return lax.psum_scatter(keep + swap(send, "lat"), "probe", scatter_dimension=2, tiled=False)

    keep, send = split_rows(lay, state, 1)
    late_grads = grads_of(state, early, lay.groups)

    def reaches(info):
        nearest = lay.row(info[0, 2 * probes : 2 * probes + 2])
        return (nearest[0] + pixels > half) | (nearest[1] < half)

    def as_they_are(keep, received, grads):
        return keep + received

    def with_partners(keep, received, grads):
        sums = Layout(probes, count, layers, pixels, half, height, width, only_sums=True)
        state = clear_total(sums, None)
        state = deposit(sums, None, sections, info, [(early, swap(grads, "probe"))], state)
        more, send = split_rows(sums, state, 1)
        return (keep + received) + (more + swap(send, "lat"))

    late = reaches(info) | reaches(everyone)
    result = lax.cond(late, with_partners, as_they_are, keep, swap(send, "lat"), late_grads)
    return result[:, :, 0]


def solution(mesh):
    return jax.shard_map(
        local,
        mesh=mesh,
        in_specs=(
            P(None, ("groups", "depth"), "lat", None),
            P(),
            P("groups", None),
            P("groups", ("probe", "lat")),
            P("groups", ("probe", "lat"), None, None),
        ),
        out_specs=P(None, ("groups", "depth"), ("probe", "lat"), None),
        check_vma=False,
    )
```

```python
import functools
import math

import jax
import jax.numpy as jnp
import ml_dtypes
import numpy as np
from jax import lax
from jax.experimental import pallas as pl
from jax.experimental.pallas import tpu as pltpu
from jax.sharding import PartitionSpec as P

FRESNEL = 8.0
SCOPED = 8 << 20
CROSSING = 3
F32 = jnp.float32
BF16 = jnp.bfloat16
HBM = pl.BlockSpec(memory_space=pl.ANY)
VMEM = pl.BlockSpec(memory_space=pltpu.VMEM)
SMEM = pl.BlockSpec(memory_space=pltpu.SMEM)


def in_hbm(x):
    return pltpu.with_memory_space_constraint(x, pltpu.HBM)


def in_vmem(x):
    return pltpu.with_memory_space_constraint(x, pltpu.VMEM)


def real_blocks(matrix):
    real, imag = matrix.real, matrix.imag
    left = np.block([[real, -imag], [imag, real]])
    right = np.block([[real, imag], [-imag, real]])
    return np.stack([left, right])


@functools.lru_cache(maxsize=None)
def make_tables(pixels):
    index = np.arange(pixels)
    freq = np.where(index < pixels // 2, index, index - pixels) / pixels
    spread = index[:, None] - index[None, :]
    phase = 2.0 * math.pi * freq * spread[:, :, None] - math.pi * FRESNEL * freq * freq
    propagator = np.mean(np.exp(1j * phase), axis=-1)
    turns = index[:, None] * index[None, :] % pixels
    fourier = np.exp(-2j * math.pi * turns / pixels) / math.sqrt(pixels)
    blocks = np.stack([real_blocks(propagator), real_blocks(fourier)]).astype(np.float32)
    high = blocks.astype(ml_dtypes.bfloat16)
    low = (blocks - high.astype(np.float32)).astype(ml_dtypes.bfloat16)
    return np.stack([high, low], axis=2)


def halves(x):
    high = x.astype(BF16)
    return high, (x - high.astype(F32)).astype(BF16)


def dot(a, b):
    return jnp.dot(a, b, preferred_element_type=F32)


def transform(left, right, fields):
    size = fields[0][0].shape[0]
    stacked = jnp.concatenate(
        [
            jnp.concatenate([real for real, _ in fields], axis=1),
            jnp.concatenate([imag for _, imag in fields], axis=1),
        ],
        axis=0,
    )
    high, low = halves(stacked)
    mid = dot(left[0], high) + (dot(left[1], high) + dot(left[0], low))
    rows = jnp.concatenate(
        [
            jnp.concatenate(
                [mid[:size, i * size : (i + 1) * size], mid[size:, i * size : (i + 1) * size]], axis=1
            )
            for i in range(len(fields))
        ],
        axis=0,
    )
    high, low = halves(rows)
    out = dot(high, right[0]) + (dot(high, right[1]) + dot(low, right[0]))
    return [
        (out[i * size : (i + 1) * size, :size], out[i * size : (i + 1) * size, size:])
        for i in range(len(fields))
    ]


def times(a, b):
    return a[0] * b[0] - a[1] * b[1], a[0] * b[1] + a[1] * b[0]


def times_conj(a, b):
    return a[0] * b[0] + a[1] * b[1], a[1] * b[0] - a[0] * b[1]


class Layout:
    def __init__(self, probes, count, layers, pixels, rows, height, width, only_sums=False):
        self.probes, self.count, self.layers, self.pixels = probes, count, layers, pixels
        self.groups = probes // count
        self.tall = pixels + 8
        self.rows, self.height, self.width = rows, height, width
        self.blocks = width // pixels
        self.deep = rows + 2 * self.tall
        self.column_bits = (width - 1).bit_length()
        self.name_bits = (4 * probes - 1).bit_length()
        self.stack = probes * layers * 2 * pixels
        self.seen_from = self.stack
        self.grads_from = 2 * self.stack
        self.frames_from = 3 * self.stack
        self.total_from = 0 if only_sums else self.frames_from + probes * pixels
        self.shape = (self.total_from + 2 * layers * self.blocks * self.deep, pixels)

    def stacked(self, group, i, layer, part):
        probe = group * self.count + i
        return ((probe * self.layers + layer) * 2 + part) * self.pixels

    def tile(self, start):
        return pl.ds(pl.multiple_of(start, 8), self.pixels)

    def patch(self, group, i, layer, part):
        return self.tile(self.stacked(group, i, layer, part))

    def seen(self, group, i, layer, part):
        return self.tile(self.seen_from + self.stacked(group, i, layer, part))

    def grad(self, group, i, layer, part):
        return self.tile(self.grads_from + self.stacked(group, i, layer, part))

    def grads_of(self, begin, end):
        each = self.stack // self.groups
        return self.grads_from + begin * each, self.grads_from + end * each

    def frame(self, group, i):
        return self.tile(self.frames_from + (group * self.count + i) * self.pixels)

    def total(self, part, layer, block, row):
        block = (part * self.layers + layer) * self.blocks + block
        return self.total_from + block * self.deep + row

    def pack(self, row, column, name):
        return (((row << self.column_bits) + column) << self.name_bits) + name

    def row(self, key):
        return key >> (self.column_bits + self.name_bits)

    def window(self, info, probe, partner=False):
        key = info[0, probe + partner * self.probes]
        row = self.row(key)
        column = (key >> self.name_bits) & ((1 << self.column_bits) - 1)
        row0 = jnp.minimum(row // 8 * 8, self.height - self.tall)
        block = jnp.minimum(column // self.pixels, self.blocks - 2)
        return row0, row - row0, block, column - block * self.pixels


def call(lay, body, state, before, outs, scratch=(), grid=(), flops=1000, moved=1000, name=None):
    spaces = {"hbm": (HBM, in_hbm), "vmem": (VMEM, in_vmem), "smem": (SMEM, lambda x: x)}
    specs = [spaces[kind][0] for kind, _ in before]
    operands = [spaces[kind][1](x) for kind, x in before]
    at = len(before)
    aliases = {}
    if state is not None:
        specs.append(VMEM)
        operands.append(in_vmem(state))
        aliases = {at: 0}

    def kernel(*refs):
        body(*refs[:at], *refs[at + len(aliases) :])

    return pl.pallas_call(
        kernel,
        grid=grid,
        in_specs=specs,
        out_specs=[VMEM] * (1 + len(outs)),
        out_shape=[pltpu.VMEM(shape, F32) for shape in (lay.shape, *outs)],
        scratch_shapes=list(scratch),
        input_output_aliases=aliases,
        compiler_params=pltpu.CompilerParams(vmem_limit_bytes=SCOPED),
        cost_estimate=pl.CostEstimate(flops=flops, bytes_accessed=moved, transcendentals=0),
        name=name,
    )(*operands)


def clear_total(lay, state):
    start = lay.total_from

    def body(state):
        state[pl.ds(start, lay.shape[0] - start), :] = jnp.zeros((lay.shape[0] - start, lay.pixels), F32)

    return call(lay, body, state, [], [], name="clear_total")[0]


def place_frames(lay, sections, info, pools, state):
    def body(info, *refs):
        *pools, state, sems = refs
        lat, side = lax.axis_index("lat"), lax.axis_index("probe")
        section = lax.axis_index("depth")
        for act in ("start", "wait"):
            for probe in range(lay.probes):
                name = info[0, probe] & ((1 << lay.name_bits) - 1)
                owner = name // lay.probes
                slot = name % lay.probes
                if len(pools) > 1:
                    slot += ((owner // 2) ^ side) * lay.probes + ((owner % 2) ^ lat) * 2 * lay.probes
                first = 0
                for pool in pools:
                    size = pool.shape[0] // lay.pixels

                    @pl.when((section == sections - 1) & (slot >= first) & (slot < first + size))
                    def _(pool=pool, first=first, probe=probe, slot=slot):
                        copy = pltpu.make_async_copy(
                            pool.at[lay.tile((slot - first) * lay.pixels), :],
                            state.at[lay.frame(0, probe), :],
                            sems.at[probe],
                        )
                        getattr(copy, act)()

                    first += size

    pools = [("hbm", pool.reshape((-1, lay.pixels))) for pool in pools]
    return call(
        lay,
        body,
        state,
        [("smem", info), *pools],
        [],
        scratch=[pltpu.SemaphoreType.DMA((lay.probes,))],
        name="place_frames",
    )[0]


def cut_patches(lay, info, own, other, state, begin, end, core=None):
    half = own.shape[2]
    tall, pixels = lay.tall, lay.pixels

    def one(probe, info, own, other, state, window):
        row0, down, block, shift = lay.window(info, probe)
        own_top = lax.axis_index("lat") == 0
        near_at = pl.ds(pl.multiple_of(block * pixels, pixels), pixels)
        far_at = pl.ds(pl.multiple_of((block + 1) * pixels, pixels), pixels)
        for source, is_top in ((own, own_top), (other, jnp.logical_not(own_top))):
            start = jnp.clip(row0 - jnp.where(is_top, 0, half), 0, half - tall)
            to = pl.ds(pl.multiple_of(jnp.where(is_top, 0, tall), 8), tall)
            rows = pl.ds(pl.multiple_of(start, 8), tall)

            @pl.when(jnp.where(is_top, row0 < half, row0 + tall > half))
            def _(source=source, rows=rows, to=to):
                for part in range(2):
                    for layer in range(lay.layers):
                        window[part, layer, to, 0:pixels] = source[part, layer, rows, near_at]
                        window[part, layer, to, pixels : 2 * pixels] = source[part, layer, rows, far_at]

        offset = jnp.where(row0 < half, jnp.maximum(row0 - (half - tall), 0), tall)
        rows = pl.ds(pl.multiple_of(offset, 8), tall)
        turn = (pixels - shift) % pixels
        lane = lax.broadcasted_iota(jnp.int32, (tall, pixels), 1)
        for part in range(2):
            for layer in range(lay.layers):
                near = pltpu.roll(window[part, layer, rows, 0:pixels], turn, 1)
                far = pltpu.roll(window[part, layer, rows, pixels : 2 * pixels], turn, 1)
                patch = jnp.where(lane < pixels - shift, near, far)
                patch = pltpu.roll(patch, (tall - down) % tall, 0)[:pixels]
                state[lay.patch(0, probe, layer, part), :] = patch

    def body(info, *refs):
        @pl.when(core is None or lax.axis_index("lat") == core)
        def _():
            lax.fori_loop(begin, end, lambda probe, _: one(probe, info, *refs) or 0, 0)

    return call(
        lay,
        body,
        state,
        [("smem", info), ("vmem", own), ("vmem", other)],
        [],
        scratch=[pltpu.VMEM((2, lay.layers, 2 * tall, 2 * pixels), F32)],
        name="cut_patches",
    )[0]


def section_cost(lay):
    size = lay.count * lay.pixels**2
    return dict(flops=lay.layers * 2 * 3 * 8 * size * lay.pixels, moved=(lay.layers * 2 + 4) * 8 * size)


def pair(ref, at):
    return ref[at(0), :], ref[at(1), :]


def run_forward(lay, tick, sections, tables, state, arrived, start_wave):
    def body(tables, *refs):
        arrived_ref = refs[0] if arrived is not None else None
        start_ref = refs[-3] if start_wave is not None else None
        state, leave = refs[-2:]
        section = lax.axis_index("depth")
        group = tick - section
        final = (section == sections - 1).astype(jnp.int32)

        @pl.when((group >= 0) & (group < lay.groups))
        def _():
            wave = []
            for i in range(lay.count):
                if arrived is None:
                    wave.append((start_ref[0], start_ref[1]))
                elif start_wave is None:
                    wave.append((arrived_ref[i, 0], arrived_ref[i, 1]))
                else:
                    wave.append(
                        tuple(jnp.where(section == 0, start_ref[p], arrived_ref[i, p]) for p in range(2))
                    )
            for layer in range(lay.layers):
                chi = []
                for i in range(lay.count):
                    for part in range(2):
                        state[lay.seen(group, i, layer, part), :] = wave[i][part]
                    chi.append(times(pair(state, functools.partial(lay.patch, group, i, layer)), wave[i]))
                at = final if layer == lay.layers - 1 else 0
                wave = transform((tables[at, 0, 0], tables[at, 0, 1]), (tables[at, 1, 0], tables[at, 1, 1]), chi)
            for i in range(lay.count):
                real, imag = wave[i]
                misfit = real * real + imag * imag - state[lay.frame(group, i), :]
                factor = jnp.where(final == 1, misfit, 1.0)
                leave[i, 0] = real * factor
                leave[i, 1] = imag * factor

    waves = [("vmem", x) for x in (arrived, start_wave) if x is not None]
    return call(
        lay,
        body,
        state,
        [("vmem", tables), *waves],
        [(lay.count, 2, lay.pixels, lay.pixels)],
        name="forward_section",
        **section_cost(lay),
    )


def run_backward(lay, tick, sections, tables, state, arrived, own):
    def body(tables, *refs):
        arrived_ref = refs[0] if arrived is not None else None
        own_ref = refs[-3] if own is not None else None
        state, leave = refs[-2:]
        section = lax.axis_index("depth")
        group = tick - (2 * (sections - 1) - section)
        final = (section == sections - 1).astype(jnp.int32)

        @pl.when((group >= 0) & (group < lay.groups))
        def _():
            wave = []
            for i in range(lay.count):
                if arrived is None:
                    wave.append((own_ref[i, 0], own_ref[i, 1]))
                elif own is None:
                    wave.append((arrived_ref[i, 0], arrived_ref[i, 1]))
                else:
                    wave.append(
                        tuple(jnp.where(final == 1, own_ref[i, p], arrived_ref[i, p]) for p in range(2))
                    )
            for layer in reversed(range(lay.layers)):
                at = final if layer == lay.layers - 1 else 0
                chi = transform((tables[at, 1, 0], tables[at, 1, 1]), (tables[at, 0, 0], tables[at, 0, 1]), wave)
                wave = []
                for i in range(lay.count):
                    real, imag = times_conj(chi[i], pair(state, functools.partial(lay.seen, group, i, layer)))
                    state[lay.grad(group, i, layer, 0), :] = real
                    state[lay.grad(group, i, layer, 1), :] = imag
                    wave.append(times_conj(chi[i], pair(state, functools.partial(lay.patch, group, i, layer))))
            for i in range(lay.count):
                leave[i, 0] = wave[i][0]
                leave[i, 1] = wave[i][1]

    waves = [("vmem", x) for x in (arrived, own) if x is not None]
    return call(
        lay,
        body,
        state,
        [("vmem", tables), *waves],
        [(lay.count, 2, lay.pixels, lay.pixels)],
        name="backward_section",
        **section_cost(lay),
    )


def deposit(lay, tick, sections, info, received, state):
    pixels, tall = lay.pixels, lay.tall

    def body(info, *refs):
        state = refs[-1]
        lane = lax.broadcasted_iota(jnp.int32, (tall, pixels), 1)
        blank = jnp.zeros((8, pixels), F32)
        base = lax.axis_index("probe") * lay.rows if lay.rows < lay.height else 0

        def add(probe, partner, active, load):
            row0, down, block, shift = lay.window(info, probe, partner)
            start = row0 - base + tall

            @pl.when(active & (start > 0) & (start < lay.rows + tall))
            def _():
                for layer in range(lay.layers):
                    for part in range(2):
                        padded = jnp.concatenate([load(layer, part), blank], axis=0)
                        turned = pltpu.roll(pltpu.roll(padded, down, 0), shift % pixels, 1)
                        near = pl.ds(pl.multiple_of(lay.total(part, layer, block, start), 8), tall)
                        far = pl.ds(pl.multiple_of(lay.total(part, layer, block + 1, start), 8), tall)
                        state[near, :] += jnp.where(lane >= shift, turned, 0.0)
                        state[far, :] += jnp.where(lane >= shift, 0.0, turned)

        if tick is not None:
            group = tick - (2 * (sections - 1) - lax.axis_index("depth"))
            active = (group >= 0) & (group < lay.groups)
            group = jnp.clip(group, 0, lay.groups - 1)
            for i in range(lay.count):
                add(
                    group * lay.count + i,
                    False,
                    active,
                    lambda layer, part, i=i: state[lay.grad(group, i, layer, part), :],
                )
        for ref, (first, grads) in zip(refs, received):

            def one(i, _, ref=ref, first=first):
                add(
                    first * lay.count + i,
                    True,
                    True,
                    lambda layer, part: ref[lay.patch(0, i, layer, part), :],
                )
                return 0

            lax.fori_loop(0, grads.shape[0] // (lay.layers * 2 * pixels), one, 0)

    return call(
        lay,
        body,
        state,
        [("smem", info)] + [("vmem", grads) for _, grads in received],
        [],
        name="deposit_patches",
    )[0]


def split_rows(lay, state, owners):
    rows = lay.rows // (2 * owners)

    def body(state, keep, send, sems):
        lat = lax.axis_index("lat")
        copies = []
        for owner in range(owners):
            for kind, target in ((lat, keep), (1 - lat, send)):
                for part in range(2):
                    for layer in range(lay.layers):
                        for block in range(lay.blocks):
                            start = lay.total(part, layer, block, lay.tall + (2 * owner + kind) * rows)
                            copies.append(
                                pltpu.make_async_copy(
                                    state.at[pl.ds(pl.multiple_of(start, 8), rows), :],
                                    target.at[part, layer, owner, :, pl.ds(block * lay.pixels, lay.pixels)],
                                    sems.at[len(copies)],
                                )
                            )
        for copy in copies:
            copy.start()
        for copy in copies:
            copy.wait()

    half = (2, lay.layers, owners, rows, lay.width)
    return pl.pallas_call(
        body,
        in_specs=[VMEM],
        out_specs=[VMEM, VMEM],
        out_shape=[pltpu.VMEM(half, F32), pltpu.VMEM(half, F32)],
        scratch_shapes=[pltpu.SemaphoreType.DMA((4 * owners * lay.layers * lay.blocks,))],
        compiler_params=pltpu.CompilerParams(vmem_limit_bytes=SCOPED),
        name="split_rows",
    )(in_vmem(state))


def swap(shard, axis):
    return lax.ppermute(shard, axis, [(0, 1), (1, 0)])


def sort_probes(lay, early, positions, indices, specimen):
    n = lay.probes
    total = 4 * n

    def body(positions, *refs):
        *scans, specimen, info, brought, sem = refs
        copy = pltpu.make_async_copy(specimen, brought, sem)
        copy.start()
        lat, side = lax.axis_index("lat"), lax.axis_index("probe")
        lane = lax.broadcasted_iota(jnp.int32, (1, 128), 1)
        at = lax.broadcasted_iota(jnp.int32, (total, 128), 0)
        across = jnp.full((1, 128), jnp.iinfo(jnp.int32).max, jnp.int32)
        down = jnp.zeros((total, 128), jnp.int32)
        for which, scan in enumerate(scans):
            owner = (side ^ (which % 2)) * 2 + (lat ^ (which // 2))
            for i in range(n):
                place = scan[i]
                key = lay.pack(positions[0, place], positions[1, place], owner * n + i)
                across = jnp.where(lane == which * n + i, key, across)
                down = jnp.where(at == which * n + i, key, down)
        rank = jnp.sum((across < down).astype(jnp.int32), axis=1, keepdims=True)
        partner = lane // n
        order = 2 * (lane % n) + lat
        wanted = jnp.where((side ^ partner) == 0, 2 * n - 1 - order, 2 * n + order)
        reach = 2 * early * lay.count
        wanted = jnp.where(lane == 2 * n, 2 * n - 1 - reach, wanted)
        wanted = jnp.where(lane == 2 * n + 1, 2 * n + reach, wanted)
        wanted = jnp.where(lane > 2 * n + 1, -1, wanted)
        info[...] = jnp.sum(jnp.where(rank == wanted, down, 0), axis=0, keepdims=True)
        copy.wait()

    return pl.pallas_call(
        body,
        in_specs=[SMEM] * 5 + [HBM],
        out_specs=[VMEM, VMEM],
        out_shape=[jax.ShapeDtypeStruct((1, 128), jnp.int32), pltpu.VMEM(specimen.shape, F32)],
        scratch_shapes=[pltpu.SemaphoreType.DMA(())],
        compiler_params=pltpu.CompilerParams(vmem_limit_bytes=SCOPED),
        name="sort_probes",
    )(positions.T, *indices, in_hbm(specimen))


def local(specimen, illumination, positions, scan_index, frames):
    pixels = illumination.shape[-1]
    _, layers, half, width = specimen.shape
    height = 2 * half
    tables = jnp.asarray(make_tables(pixels))
    sections = lax.axis_size("depth")
    owners = lax.axis_size("probe")
    paired = owners == 2 and lax.axis_size("groups") <= 2
    probes = scan_index.size
    count = 2 if probes % 4 == 0 else 1
    lay = Layout(probes, count, layers, pixels, half if paired else height, height, width)
    early = lay.groups // 2

    everyone = mine = None
    if paired:
        scan = scan_index.reshape(-1)
        beside = swap(scan, "lat")
        half_rows, beside = lax.optimization_barrier((specimen, beside))
        other = swap(half_rows, "lat")
        indices = [scan, swap(scan, "probe"), beside, swap(beside, "probe")]
        info, specimen = sort_probes(lay, early, positions, indices, specimen)
        measured, _ = lax.optimization_barrier((frames, info))
        end = sections - 1
        ends = [(2 * end, 2 * end + 1), (2 * end + 1, 2 * end)]
        mine = lax.ppermute(measured, ("depth", "probe"), ends)
        everyone = swap(info, "groups") if lax.axis_size("groups") == 2 else info
    else:
        other = swap(specimen, "lat")
        corners = positions[scan_index.reshape(-1)]
        info = lay.pack(corners[:, 0], corners[:, 1], jnp.arange(probes, dtype=jnp.int32))
        info = jnp.pad(info, (0, -probes % 128))[None]
    state = cut_patches(lay, info, specimen, other, None, 0, count)
    portion = -(-(lay.groups - 1) // (sections - 1)) * count
    behind = min(count + portion, probes)
    state = cut_patches(lay, info, specimen, other, state, count, behind, 1)

    def reaches(info):
        nearest = lay.row(info[0, 2 * probes : 2 * probes + 2])
        return (nearest[0] + pixels > half) | (nearest[1] < half)

    def busy(tick, source, by):
        delay = source if by > 0 else 2 * (sections - 1) - source
        return 0 <= tick - delay < lay.groups

    def pass_on(wave, tick, by):
        pairs = [
            (source, source + by)
            for source in range(sections)
            if 0 <= source + by < sections and busy(tick, source, by)
        ]
        return lax.ppermute(wave, "depth", pairs) if pairs else None

    def grads_of(state, begin, end):
        begin, end = lay.grads_of(begin, end)
        return lax.slice_in_dim(state, begin, end)

    fill = sections - 1
    parts = [(0, early // 2), (early // 2, early)] if paired else []
    crossing = {}
    down = up = None
    cut = count
    for tick in range(lay.groups + 2 * fill):
        own = None
        if paired and tick == fill - 1:
            down, mine, everyone = lax.optimization_barrier((down, mine, everyone))
            crossed = [lax.ppermute(x, ("depth", "lat"), ends) for x in (frames, mine)]
            late = reaches(info) | reaches(everyone)
        if tick < lay.groups + fill:
            start_wave = illumination if tick < lay.groups else None
            state, own = run_forward(lay, tick, sections, tables, state, down, start_wave)
            down = pass_on(own, tick, 1)
            if cut < probes:
                core = 0 if tick == 0 else None
                state = cut_patches(lay, info, specimen, other, state, cut, min(cut + portion, probes), core)
                cut += portion
            if tick == 0:
                state = clear_total(lay, state)
            if tick == fill - 1:
                if paired:
                    state, late = lax.optimization_barrier((state, late))
                pools = [frames, mine, *crossed] if paired else [frames]
                state = place_frames(lay, sections, info, pools, state)
        if tick >= fill:
            state, rising = run_backward(lay, tick, sections, tables, state, up, own)
            up = pass_on(rising, tick, -1)
            received = crossing.pop(tick, [])
            for begin, end in parts:
                if tick == end - 1 + 2 * fill:
                    due = min(tick + CROSSING, lay.groups + 2 * fill - 1)
                    crossing.setdefault(due, []).append((begin, swap(grads_of(state, begin, end), "probe")))
            state = deposit(lay, tick, sections, info, received, state)
    if not paired:
        keep, send = split_rows(lay, state, owners)
        return lax.psum_scatter(keep + swap(send, "lat"), "probe", scatter_dimension=2, tiled=False)

    keep, send = split_rows(lay, state, 1)
    late_grads = grads_of(state, early, lay.groups)

    def as_they_are(keep, received, grads):
        return keep + received

    def with_partners(keep, received, grads):
        sums = Layout(probes, count, layers, pixels, half, height, width, only_sums=True)
        state = clear_total(sums, None)
        state = deposit(sums, None, sections, info, [(early, swap(grads, "probe"))], state)
        more, send = split_rows(sums, state, 1)
        return (keep + received) + (more + swap(send, "lat"))

    result = lax.cond(late, with_partners, as_they_are, keep, swap(send, "lat"), late_grads)
    return result[:, :, 0]


def solution(mesh):
    return jax.shard_map(
        local,
        mesh=mesh,
        in_specs=(
            P(None, ("groups", "depth"), "lat", None),
            P(),
            P("groups", None),
            P("groups", ("probe", "lat")),
            P("groups", ("probe", "lat"), None, None),
        ),
        out_specs=P(None, ("groups", "depth"), ("probe", "lat"), None),
        check_vma=False,
    )
```

```python
import functools
import math

import jax
import jax.numpy as jnp
import ml_dtypes
import numpy as np
from jax import lax
from jax.experimental import pallas as pl
from jax.experimental.pallas import tpu as pltpu
from jax.sharding import PartitionSpec as P

FRESNEL = 8.0
SCOPED = 8 << 20
CROSSING = 3
F32 = jnp.float32
BF16 = jnp.bfloat16
HBM = pl.BlockSpec(memory_space=pl.ANY)
VMEM = pl.BlockSpec(memory_space=pltpu.VMEM)
SMEM = pl.BlockSpec(memory_space=pltpu.SMEM)


def in_hbm(x):
    return pltpu.with_memory_space_constraint(x, pltpu.HBM)


def in_vmem(x):
    return pltpu.with_memory_space_constraint(x, pltpu.VMEM)


def real_blocks(matrix):
    real, imag = matrix.real, matrix.imag
    left = np.block([[real, -imag], [imag, real]])
    right = np.block([[real, imag], [-imag, real]])
    return np.stack([left, right])


@functools.lru_cache(maxsize=None)
def make_tables(pixels):
    index = np.arange(pixels)
    freq = np.where(index < pixels // 2, index, index - pixels) / pixels
    spread = index[:, None] - index[None, :]
    phase = 2.0 * math.pi * freq * spread[:, :, None] - math.pi * FRESNEL * freq * freq
    propagator = np.mean(np.exp(1j * phase), axis=-1)
    turns = index[:, None] * index[None, :] % pixels
    fourier = np.exp(-2j * math.pi * turns / pixels) / math.sqrt(pixels)
    blocks = np.stack([real_blocks(propagator), real_blocks(fourier)]).astype(np.float32)
    high = blocks.astype(ml_dtypes.bfloat16)
    low = (blocks - high.astype(np.float32)).astype(ml_dtypes.bfloat16)
    return np.stack([high, low], axis=2)


def halves(x):
    high = x.astype(BF16)
    return high, (x - high.astype(F32)).astype(BF16)


def dot(a, b):
    return jnp.dot(a, b, preferred_element_type=F32)


def transform(left, right, fields):
    size = fields[0][0].shape[0]
    stacked = jnp.concatenate(
        [
            jnp.concatenate([real for real, _ in fields], axis=1),
            jnp.concatenate([imag for _, imag in fields], axis=1),
        ],
        axis=0,
    )
    high, low = halves(stacked)
    mid = dot(left[0], high) + (dot(left[1], high) + dot(left[0], low))
    rows = jnp.concatenate(
        [
            jnp.concatenate(
                [mid[:size, i * size : (i + 1) * size], mid[size:, i * size : (i + 1) * size]], axis=1
            )
            for i in range(len(fields))
        ],
        axis=0,
    )
    high, low = halves(rows)
    out = dot(high, right[0]) + (dot(high, right[1]) + dot(low, right[0]))
    return [
        (out[i * size : (i + 1) * size, :size], out[i * size : (i + 1) * size, size:])
        for i in range(len(fields))
    ]


def times(a, b):
    return a[0] * b[0] - a[1] * b[1], a[0] * b[1] + a[1] * b[0]


def times_conj(a, b):
    return a[0] * b[0] + a[1] * b[1], a[1] * b[0] - a[0] * b[1]


class Layout:
    def __init__(self, probes, count, layers, pixels, rows, height, width, only_sums=False):
        self.probes, self.count, self.layers, self.pixels = probes, count, layers, pixels
        self.groups = probes // count
        self.tall = pixels + 8
        self.rows, self.height, self.width = rows, height, width
        self.blocks = width // pixels
        self.deep = rows + 2 * self.tall
        self.column_bits = (width - 1).bit_length()
        self.name_bits = (4 * probes - 1).bit_length()
        self.stack = probes * layers * 2 * pixels
        self.seen_from = self.stack
        self.grads_from = 2 * self.stack
        self.frames_from = 3 * self.stack
        self.total_from = 0 if only_sums else self.frames_from + probes * pixels
        self.shape = (self.total_from + 2 * layers * self.blocks * self.deep, pixels)

    def stacked(self, group, i, layer, part):
        probe = group * self.count + i
        return ((probe * self.layers + layer) * 2 + part) * self.pixels

    def tile(self, start):
        return pl.ds(pl.multiple_of(start, 8), self.pixels)

    def patch(self, group, i, layer, part):
        return self.tile(self.stacked(group, i, layer, part))

    def seen(self, group, i, layer, part):
        return self.tile(self.seen_from + self.stacked(group, i, layer, part))

    def grad(self, group, i, layer, part):
        return self.tile(self.grads_from + self.stacked(group, i, layer, part))

    def grads_of(self, begin, end):
        each = self.stack // self.groups
        return self.grads_from + begin * each, self.grads_from + end * each

    def frame(self, group, i):
        return self.tile(self.frames_from + (group * self.count + i) * self.pixels)

    def total(self, part, layer, block, row):
        block = (part * self.layers + layer) * self.blocks + block
        return self.total_from + block * self.deep + row

    def pack(self, row, column, name):
        return (((row << self.column_bits) + column) << self.name_bits) + name

    def row(self, key):
        return key >> (self.column_bits + self.name_bits)

    def window(self, info, probe, partner=False):
        key = info[0, probe + partner * self.probes]
        row = self.row(key)
        column = (key >> self.name_bits) & ((1 << self.column_bits) - 1)
        row0 = jnp.minimum(row // 8 * 8, self.height - self.tall)
        block = jnp.minimum(column // self.pixels, self.blocks - 2)
        return row0, row - row0, block, column - block * self.pixels


def call(lay, body, state, before, outs, scratch=(), grid=(), flops=1000, moved=1000, name=None):
    spaces = {"hbm": (HBM, in_hbm), "vmem": (VMEM, in_vmem), "smem": (SMEM, lambda x: x)}
    specs = [spaces[kind][0] for kind, _ in before]
    operands = [spaces[kind][1](x) for kind, x in before]
    at = len(before)
    aliases = {}
    if state is not None:
        specs.append(VMEM)
        operands.append(in_vmem(state))
        aliases = {at: 0}

    def kernel(*refs):
        body(*refs[:at], *refs[at + len(aliases) :])

    return pl.pallas_call(
        kernel,
        grid=grid,
        in_specs=specs,
        out_specs=[VMEM] * (1 + len(outs)),
        out_shape=[pltpu.VMEM(shape, F32) for shape in (lay.shape, *outs)],
        scratch_shapes=list(scratch),
        input_output_aliases=aliases,
        compiler_params=pltpu.CompilerParams(vmem_limit_bytes=SCOPED),
        cost_estimate=pl.CostEstimate(flops=flops, bytes_accessed=moved, transcendentals=0),
        name=name,
    )(*operands)


def clear_total(lay, state):
    start = lay.total_from

    def body(state):
        state[pl.ds(start, lay.shape[0] - start), :] = jnp.zeros((lay.shape[0] - start, lay.pixels), F32)

    return call(lay, body, state, [], [], name="clear_total")[0]


def place_frames(lay, sections, info, pools, state):
    def body(info, *refs):
        *pools, state, sems = refs
        lat, side = lax.axis_index("lat"), lax.axis_index("probe")
        section = lax.axis_index("depth")
        for act in ("start", "wait"):
            for probe in range(lay.probes):
                name = info[0, probe] & ((1 << lay.name_bits) - 1)
                owner = name // lay.probes
                slot = name % lay.probes
                if len(pools) > 1:
                    slot += ((owner // 2) ^ side) * lay.probes + ((owner % 2) ^ lat) * 2 * lay.probes
                first = 0
                for pool in pools:
                    size = pool.shape[0] // lay.pixels

                    @pl.when((section == sections - 1) & (slot >= first) & (slot < first + size))
                    def _(pool=pool, first=first, probe=probe, slot=slot):
                        copy = pltpu.make_async_copy(
                            pool.at[lay.tile((slot - first) * lay.pixels), :],
                            state.at[lay.frame(0, probe), :],
                            sems.at[probe],
                        )
                        getattr(copy, act)()

                    first += size

    pools = [("hbm", pool.reshape((-1, lay.pixels))) for pool in pools]
    return call(
        lay,
        body,
        state,
        [("smem", info), *pools],
        [],
        scratch=[pltpu.SemaphoreType.DMA((lay.probes,))],
        name="place_frames",
    )[0]


def cut_patches(lay, info, own, other, state, begin, end):
    half = own.shape[2]
    tall, pixels = lay.tall, lay.pixels

    def one(probe, info, own, other, state, window):
        row0, down, block, shift = lay.window(info, probe)
        own_top = lax.axis_index("lat") == 0
        near_at = pl.ds(pl.multiple_of(block * pixels, pixels), pixels)
        far_at = pl.ds(pl.multiple_of((block + 1) * pixels, pixels), pixels)
        for source, is_top in ((own, own_top), (other, jnp.logical_not(own_top))):
            start = jnp.clip(row0 - jnp.where(is_top, 0, half), 0, half - tall)
            to = pl.ds(pl.multiple_of(jnp.where(is_top, 0, tall), 8), tall)
            rows = pl.ds(pl.multiple_of(start, 8), tall)

            @pl.when(jnp.where(is_top, row0 < half, row0 + tall > half))
            def _(source=source, rows=rows, to=to):
                for part in range(2):
                    for layer in range(lay.layers):
                        window[part, layer, to, 0:pixels] = source[part, layer, rows, near_at]
                        window[part, layer, to, pixels : 2 * pixels] = source[part, layer, rows, far_at]

        offset = jnp.where(row0 < half, jnp.maximum(row0 - (half - tall), 0), tall)
        rows = pl.ds(pl.multiple_of(offset, 8), tall)
        turn = (pixels - shift) % pixels
        lane = lax.broadcasted_iota(jnp.int32, (tall, pixels), 1)
        for part in range(2):
            for layer in range(lay.layers):
                near = pltpu.roll(window[part, layer, rows, 0:pixels], turn, 1)
                far = pltpu.roll(window[part, layer, rows, pixels : 2 * pixels], turn, 1)
                patch = jnp.where(lane < pixels - shift, near, far)
                patch = pltpu.roll(patch, (tall - down) % tall, 0)[:pixels]
                state[lay.patch(0, probe, layer, part), :] = patch

    def body(info, *refs):
        lax.fori_loop(begin, end, lambda probe, _: one(probe, info, *refs) or 0, 0)

    return call(
        lay,
        body,
        state,
        [("smem", info), ("vmem", own), ("vmem", other)],
        [],
        scratch=[pltpu.VMEM((2, lay.layers, 2 * tall, 2 * pixels), F32)],
        name="cut_patches",
    )[0]


def section_cost(lay):
    size = lay.count * lay.pixels**2
    return dict(flops=lay.layers * 2 * 3 * 8 * size * lay.pixels, moved=(lay.layers * 2 + 4) * 8 * size)


def pair(ref, at):
    return ref[at(0), :], ref[at(1), :]


def run_section(lay, tick, sections, tables, state, arrived, start_wave):
    shape = (lay.count, 2, lay.pixels, lay.pixels)
    came = [x for x in arrived if x is not None]
    depth = sections - 1

    def body(tables, *refs):
        state, *leave, turned = refs[-4:]
        start_ref = refs[len(came)] if start_wave is not None else None
        section = lax.axis_index("depth")
        even = section % 2 == 0
        final = section == depth
        last = final.astype(jnp.int32)

        def came_over(odd_for_even, i, part):
            if len(came) == 1:
                return refs[0][i, part]
            first, second = (refs[1], refs[0]) if odd_for_even else (refs[0], refs[1])
            return jnp.where(even, first[i, part], second[i, part])

        def send(wave, odd_for_even):
            for link in range(2):

                @pl.when(even == ((link == 1) == odd_for_even))
                def _(link=link):
                    for i in range(lay.count):
                        leave[link][i, 0], leave[link][i, 1] = wave[i]

        group = tick - section

        @pl.when((group >= 0) & (group < lay.groups))
        def _():
            wave = []
            for i in range(lay.count):
                if not came:
                    wave.append((start_ref[0], start_ref[1]))
                elif start_wave is None:
                    wave.append(tuple(came_over(True, i, p) for p in range(2)))
                else:
                    wave.append(
                        tuple(jnp.where(section == 0, start_ref[p], came_over(True, i, p)) for p in range(2))
                    )
            for layer in range(lay.layers):
                chi = []
                for i in range(lay.count):
                    for part in range(2):
                        state[lay.seen(group, i, layer, part), :] = wave[i][part]
                    chi.append(times(pair(state, functools.partial(lay.patch, group, i, layer)), wave[i]))
                at = last if layer == lay.layers - 1 else 0
                wave = transform((tables[at, 0, 0], tables[at, 0, 1]), (tables[at, 1, 0], tables[at, 1, 1]), chi)
            if tick < depth:
                send(wave, False)
            else:

                @pl.when(final)
                def _():
                    for i in range(lay.count):
                        real, imag = wave[i]
                        misfit = real * real + imag * imag - state[lay.frame(group, i), :]
                        turned[i, 0] = real * misfit
                        turned[i, 1] = imag * misfit

                @pl.when(jnp.logical_not(final))
                def _():
                    send(wave, False)

        group_up = tick - (2 * depth - section)

        @pl.when((group_up >= 0) & (group_up < lay.groups))
        def _():
            wave = []
            for i in range(lay.count):
                if not came:
                    wave.append((turned[i, 0], turned[i, 1]))
                else:
                    wave.append(
                        tuple(jnp.where(final, turned[i, p], came_over(False, i, p)) for p in range(2))
                    )
            for layer in reversed(range(lay.layers)):
                at = last if layer == lay.layers - 1 else 0
                chi = transform((tables[at, 1, 0], tables[at, 1, 1]), (tables[at, 0, 0], tables[at, 0, 1]), wave)
                wave = []
                for i in range(lay.count):
                    before = pair(state, functools.partial(lay.seen, group_up, i, layer))
                    real, imag = times_conj(chi[i], before)
                    state[lay.grad(group_up, i, layer, 0), :] = real
                    state[lay.grad(group_up, i, layer, 1), :] = imag
                    here = pair(state, functools.partial(lay.patch, group_up, i, layer))
                    wave.append(times_conj(chi[i], here))
            send(wave, True)

    waves = [("vmem", x) for x in (*came, start_wave) if x is not None]
    return call(
        lay,
        body,
        state,
        [("vmem", tables), *waves],
        [shape, shape],
        scratch=[pltpu.VMEM(shape, F32)],
        name="section",
        **section_cost(lay),
    )


def deposit(lay, tick, sections, info, received, state):
    pixels, tall = lay.pixels, lay.tall

    def body(info, *refs):
        state = refs[-1]
        lane = lax.broadcasted_iota(jnp.int32, (tall, pixels), 1)
        blank = jnp.zeros((8, pixels), F32)
        base = lax.axis_index("probe") * lay.rows if lay.rows < lay.height else 0

        def add(probe, partner, active, load):
            row0, down, block, shift = lay.window(info, probe, partner)
            start = row0 - base + tall

            @pl.when(active & (start > 0) & (start < lay.rows + tall))
            def _():
                for layer in range(lay.layers):
                    for part in range(2):
                        padded = jnp.concatenate([load(layer, part), blank], axis=0)
                        turned = pltpu.roll(pltpu.roll(padded, down, 0), shift % pixels, 1)
                        near = pl.ds(pl.multiple_of(lay.total(part, layer, block, start), 8), tall)
                        far = pl.ds(pl.multiple_of(lay.total(part, layer, block + 1, start), 8), tall)
                        state[near, :] += jnp.where(lane >= shift, turned, 0.0)
                        state[far, :] += jnp.where(lane >= shift, 0.0, turned)

        if tick is not None:
            group = tick - (2 * (sections - 1) - lax.axis_index("depth"))
            active = (group >= 0) & (group < lay.groups)
            group = jnp.clip(group, 0, lay.groups - 1)
            for i in range(lay.count):
                add(
                    group * lay.count + i,
                    False,
                    active,
                    lambda layer, part, i=i: state[lay.grad(group, i, layer, part), :],
                )
        for ref, (first, grads) in zip(refs, received):

            def one(i, _, ref=ref, first=first):
                add(
                    first * lay.count + i,
                    True,
                    True,
                    lambda layer, part: ref[lay.patch(0, i, layer, part), :],
                )
                return 0

            lax.fori_loop(0, grads.shape[0] // (lay.layers * 2 * pixels), one, 0)

    return call(
        lay,
        body,
        state,
        [("smem", info)] + [("vmem", grads) for _, grads in received],
        [],
        name="deposit_patches",
    )[0]


def split_rows(lay, state, owners, taken=(0, 8)):
    rows = lay.rows // (2 * owners)
    pieces = 4 * owners * lay.layers * lay.blocks

    def body(state, keep, send, rest, sems):
        lat = lax.axis_index("lat")
        copies = [pltpu.make_async_copy(state.at[pl.ds(taken[0], taken[1] - taken[0]), :], rest, sems.at[pieces])]
        for owner in range(owners):
            for kind, target in ((lat, keep), (1 - lat, send)):
                for part in range(2):
                    for layer in range(lay.layers):
                        for block in range(lay.blocks):
                            start = lay.total(part, layer, block, lay.tall + (2 * owner + kind) * rows)
                            copies.append(
                                pltpu.make_async_copy(
                                    state.at[pl.ds(pl.multiple_of(start, 8), rows), :],
                                    target.at[part, layer, owner, :, pl.ds(block * lay.pixels, lay.pixels)],
                                    sems.at[len(copies) - 1],
                                )
                            )
        for copy in copies:
            copy.start()
        for copy in copies:
            copy.wait()

    half = (2, lay.layers, owners, rows, lay.width)
    return pl.pallas_call(
        body,
        in_specs=[VMEM],
        out_specs=[VMEM, VMEM, HBM],
        out_shape=[
            pltpu.VMEM(half, F32),
            pltpu.VMEM(half, F32),
            pltpu.HBM((taken[1] - taken[0], lay.pixels), F32),
        ],
        scratch_shapes=[pltpu.SemaphoreType.DMA((pieces + 1,))],
        compiler_params=pltpu.CompilerParams(vmem_limit_bytes=SCOPED),
        name="split_rows",
    )(in_vmem(state))


def swap(shard, axis):
    return lax.ppermute(shard, axis, [(0, 1), (1, 0)])


def sort_probes(lay, early, positions, indices, specimen):
    n = lay.probes
    total = 4 * n

    def body(positions, *refs):
        *scans, specimen, info, brought, sem = refs
        copy = pltpu.make_async_copy(specimen, brought, sem)
        copy.start()
        lat, side = lax.axis_index("lat"), lax.axis_index("probe")
        lane = lax.broadcasted_iota(jnp.int32, (1, 128), 1)
        at = lax.broadcasted_iota(jnp.int32, (total, 128), 0)
        across = jnp.full((1, 128), jnp.iinfo(jnp.int32).max, jnp.int32)
        down = jnp.zeros((total, 128), jnp.int32)
        for which, scan in enumerate(scans):
            owner = (side ^ (which % 2)) * 2 + (lat ^ (which // 2))
            for i in range(n):
                place = scan[i]
                key = lay.pack(positions[0, place], positions[1, place], owner * n + i)
                across = jnp.where(lane == which * n + i, key, across)
                down = jnp.where(at == which * n + i, key, down)
        rank = jnp.sum((across < down).astype(jnp.int32), axis=1, keepdims=True)
        partner = lane // n
        order = 2 * (lane % n) + lat
        wanted = jnp.where((side ^ partner) == 0, 2 * n - 1 - order, 2 * n + order)
        reach = 2 * early * lay.count
        wanted = jnp.where(lane == 2 * n, 2 * n - 1 - reach, wanted)
        wanted = jnp.where(lane == 2 * n + 1, 2 * n + reach, wanted)
        wanted = jnp.where(lane > 2 * n + 1, -1, wanted)
        info[...] = jnp.sum(jnp.where(rank == wanted, down, 0), axis=0, keepdims=True)
        copy.wait()

    return pl.pallas_call(
        body,
        in_specs=[SMEM] * 5 + [HBM],
        out_specs=[VMEM, VMEM],
        out_shape=[jax.ShapeDtypeStruct((1, 128), jnp.int32), pltpu.VMEM(specimen.shape, F32)],
        scratch_shapes=[pltpu.SemaphoreType.DMA(())],
        compiler_params=pltpu.CompilerParams(vmem_limit_bytes=SCOPED),
        name="sort_probes",
    )(positions.T, *indices, in_hbm(specimen))


def local(specimen, illumination, positions, scan_index, frames):
    pixels = illumination.shape[-1]
    _, layers, half, width = specimen.shape
    height = 2 * half
    tables = jnp.asarray(make_tables(pixels))
    sections = lax.axis_size("depth")
    owners = lax.axis_size("probe")
    paired = owners == 2 and lax.axis_size("groups") <= 2
    probes = scan_index.size
    count = 2 if probes % 4 == 0 else 1
    lay = Layout(probes, count, layers, pixels, half if paired else height, height, width)
    early = lay.groups // 2

    everyone = mine = None
    if paired:
        scan = scan_index.reshape(-1)
        beside = swap(scan, "lat")
        half_rows, beside = lax.optimization_barrier((specimen, beside))
        other = swap(half_rows, "lat")
        indices = [scan, swap(scan, "probe"), beside, swap(beside, "probe")]
        info, specimen = sort_probes(lay, early, positions, indices, specimen)
        measured, _ = lax.optimization_barrier((frames, info))
        end = sections - 1
        ends = [(2 * end, 2 * end + 1), (2 * end + 1, 2 * end)]
        mine = lax.ppermute(measured, ("depth", "probe"), ends)
        everyone = swap(info, "groups") if lax.axis_size("groups") == 2 else info
    else:
        other = swap(specimen, "lat")
        corners = positions[scan_index.reshape(-1)]
        info = lay.pack(corners[:, 0], corners[:, 1], jnp.arange(probes, dtype=jnp.int32))
        info = jnp.pad(info, (0, -probes % 128))[None]
    state = cut_patches(lay, info, specimen, other, None, 0, count)
    portion = -(-(lay.groups - 1) // (sections - 1)) * count

    def reaches(info):
        nearest = lay.row(info[0, 2 * probes : 2 * probes + 2])
        return (nearest[0] + pixels > half) | (nearest[1] < half)

    def busy(tick, source, by):
        delay = source if by > 0 else 2 * (sections - 1) - source
        return 0 <= tick - delay < lay.groups

    def pass_on(wave, tick, first):
        pairs = []
        for source in range(first, sections - 1, 2):
            if busy(tick, source, 1) or busy(tick, source + 1, -1):
                pairs += [(source, source + 1), (source + 1, source)]
        return lax.ppermute(wave, "depth", pairs) if pairs else None

    def grads_of(state, begin, end):
        begin, end = lay.grads_of(begin, end)
        return lax.slice_in_dim(state, begin, end)

    fill = sections - 1
    parts = [(0, early // 2), (early // 2, early)] if paired else []
    crossing = {}
    arrived = [None, None]
    cut = count
    for tick in range(lay.groups + 2 * fill):
        if paired and tick == fill - 1:
            arrived[0], mine, everyone = lax.optimization_barrier((arrived[0], mine, everyone))
            crossed = [lax.ppermute(x, ("depth", "lat"), ends) for x in (frames, mine)]
            late = reaches(info) | reaches(everyone)
        start_wave = illumination if tick < lay.groups else None
        state, *leaving = run_section(lay, tick, sections, tables, state, arrived, start_wave)
        arrived = [pass_on(wave, tick, first) for first, wave in enumerate(leaving)]
        if cut < probes:
            state = cut_patches(lay, info, specimen, other, state, cut, min(cut + portion, probes))
            cut += portion
        if tick == 0:
            state = clear_total(lay, state)
        if tick == fill - 1:
            if paired:
                state, late = lax.optimization_barrier((state, late))
            pools = [frames, mine, *crossed] if paired else [frames]
            state = place_frames(lay, sections, info, pools, state)
        if tick >= fill:
            received = crossing.pop(tick, [])
            for begin, end in parts:
                if tick == end - 1 + 2 * fill:
                    due = min(tick + CROSSING, lay.groups + 2 * fill - 1)
                    crossing.setdefault(due, []).append((begin, swap(grads_of(state, begin, end), "probe")))
            state = deposit(lay, tick, sections, info, received, state)
    if not paired:
        keep, send, _ = split_rows(lay, state, owners)
        return lax.psum_scatter(keep + swap(send, "lat"), "probe", scatter_dimension=2, tiled=False)

    keep, send, late_grads = split_rows(lay, state, 1, lay.grads_of(early, lay.groups))

    def as_they_are(keep, received, grads):
        return keep + received

    def with_partners(keep, received, grads):
        sums = Layout(probes, count, layers, pixels, half, height, width, only_sums=True)
        state = clear_total(sums, None)
        state = deposit(sums, None, sections, info, [(early, swap(grads, "probe"))], state)
        more, send, _ = split_rows(sums, state, 1)
        return (keep + received) + (more + swap(send, "lat"))

    result = lax.cond(late, with_partners, as_they_are, keep, swap(send, "lat"), late_grads)
    return result[:, :, 0]


def solution(mesh):
    return jax.shard_map(
        local,
        mesh=mesh,
        in_specs=(
            P(None, ("groups", "depth"), "lat", None),
            P(),
            P("groups", None),
            P("groups", ("probe", "lat")),
            P("groups", ("probe", "lat"), None, None),
        ),
        out_specs=P(None, ("groups", "depth"), ("probe", "lat"), None),
        check_vma=False,
    )
```

```python
import functools
import math

import jax
import jax.numpy as jnp
import ml_dtypes
import numpy as np
from jax import lax
from jax.experimental import pallas as pl
from jax.experimental.pallas import tpu as pltpu
from jax.sharding import PartitionSpec as P

FRESNEL = 8.0
SCOPED = 8 << 20
CROSSING = 3
F32 = jnp.float32
BF16 = jnp.bfloat16
HBM = pl.BlockSpec(memory_space=pl.ANY)
VMEM = pl.BlockSpec(memory_space=pltpu.VMEM)
SMEM = pl.BlockSpec(memory_space=pltpu.SMEM)


def in_hbm(x):
    return pltpu.with_memory_space_constraint(x, pltpu.HBM)


def in_vmem(x):
    return pltpu.with_memory_space_constraint(x, pltpu.VMEM)


def real_blocks(matrix):
    real, imag = matrix.real, matrix.imag
    left = np.block([[real, -imag], [imag, real]])
    right = np.block([[real, imag], [-imag, real]])
    return np.stack([left, right])


@functools.lru_cache(maxsize=None)
def make_tables(pixels):
    index = np.arange(pixels)
    freq = np.where(index < pixels // 2, index, index - pixels) / pixels
    spread = index[:, None] - index[None, :]
    phase = 2.0 * math.pi * freq * spread[:, :, None] - math.pi * FRESNEL * freq * freq
    propagator = np.mean(np.exp(1j * phase), axis=-1)
    turns = index[:, None] * index[None, :] % pixels
    fourier = np.exp(-2j * math.pi * turns / pixels) / math.sqrt(pixels)
    blocks = np.stack([real_blocks(propagator), real_blocks(fourier)]).astype(np.float32)
    high = blocks.astype(ml_dtypes.bfloat16)
    low = (blocks - high.astype(np.float32)).astype(ml_dtypes.bfloat16)
    return np.stack([high, low], axis=2)


def halves(x):
    high = x.astype(BF16)
    return high, (x - high.astype(F32)).astype(BF16)


def dot(a, b):
    return jnp.dot(a, b, preferred_element_type=F32)


def transform(left, right, fields):
    size = fields[0][0].shape[0]
    stacked = jnp.concatenate(
        [
            jnp.concatenate([real for real, _ in fields], axis=1),
            jnp.concatenate([imag for _, imag in fields], axis=1),
        ],
        axis=0,
    )
    high, low = halves(stacked)
    mid = dot(left[0], high) + (dot(left[1], high) + dot(left[0], low))
    rows = jnp.concatenate(
        [
            jnp.concatenate(
                [mid[:size, i * size : (i + 1) * size], mid[size:, i * size : (i + 1) * size]], axis=1
            )
            for i in range(len(fields))
        ],
        axis=0,
    )
    high, low = halves(rows)
    out = dot(high, right[0]) + (dot(high, right[1]) + dot(low, right[0]))
    return [
        (out[i * size : (i + 1) * size, :size], out[i * size : (i + 1) * size, size:])
        for i in range(len(fields))
    ]


def times(a, b):
    return a[0] * b[0] - a[1] * b[1], a[0] * b[1] + a[1] * b[0]


def times_conj(a, b):
    return a[0] * b[0] + a[1] * b[1], a[1] * b[0] - a[0] * b[1]


class Layout:
    def __init__(self, probes, count, layers, pixels, rows, height, width, only_sums=False):
        self.probes, self.count, self.layers, self.pixels = probes, count, layers, pixels
        self.groups = probes // count
        self.tall = pixels + 8
        self.rows, self.height, self.width = rows, height, width
        self.blocks = width // pixels
        self.deep = rows + 2 * self.tall
        self.column_bits = (width - 1).bit_length()
        self.name_bits = (4 * probes - 1).bit_length()
        self.stack = probes * layers * 2 * pixels
        self.seen_from = self.stack
        self.grads_from = 2 * self.stack
        self.frames_from = 3 * self.stack
        self.total_from = 0 if only_sums else self.frames_from + probes * pixels
        self.shape = (self.total_from + 2 * layers * self.blocks * self.deep, pixels)

    def stacked(self, group, i, layer, part):
        probe = group * self.count + i
        return ((probe * self.layers + layer) * 2 + part) * self.pixels

    def tile(self, start):
        return pl.ds(pl.multiple_of(start, 8), self.pixels)

    def patch(self, group, i, layer, part):
        return self.tile(self.stacked(group, i, layer, part))

    def seen(self, group, i, layer, part):
        return self.tile(self.seen_from + self.stacked(group, i, layer, part))

    def grad(self, group, i, layer, part):
        return self.tile(self.grads_from + self.stacked(group, i, layer, part))

    def grads_of(self, begin, end):
        each = self.stack // self.groups
        return self.grads_from + begin * each, self.grads_from + end * each

    def frame(self, group, i):
        return self.tile(self.frames_from + (group * self.count + i) * self.pixels)

    def total(self, part, layer, block, row):
        block = (part * self.layers + layer) * self.blocks + block
        return self.total_from + block * self.deep + row

    def pack(self, row, column, name):
        return (((row << self.column_bits) + column) << self.name_bits) + name

    def row(self, key):
        return key >> (self.column_bits + self.name_bits)

    def window(self, info, probe, partner=False):
        lane = lax.broadcasted_iota(jnp.int32, info.shape, 1)
        key = jnp.sum(jnp.where(lane == probe + partner * self.probes, info[...], 0))
        row = self.row(key)
        column = (key >> self.name_bits) & ((1 << self.column_bits) - 1)
        row0 = jnp.minimum(row // 8 * 8, self.height - self.tall)
        block = jnp.minimum(column // self.pixels, self.blocks - 2)
        return row0, row - row0, block, column - block * self.pixels


def call(lay, body, state, before, outs, scratch=(), flag=False, flops=1000, moved=1000, name=None):
    spaces = {"hbm": (HBM, in_hbm), "vmem": (VMEM, in_vmem), "smem": (SMEM, lambda x: x)}
    specs = [spaces[kind][0] for kind, _ in before]
    operands = [spaces[kind][1](x) for kind, x in before]
    at = len(before)
    aliases = {}
    if state is not None:
        specs.append(VMEM)
        operands.append(in_vmem(state))
        aliases = {at: 0}

    def kernel(*refs):
        body(*refs[:at], *refs[at + len(aliases) :])

    return pl.pallas_call(
        kernel,
        in_specs=specs,
        out_specs=[VMEM] * (1 + len(outs)) + [SMEM] * flag,
        out_shape=[pltpu.VMEM(shape, F32) for shape in (lay.shape, *outs)]
        + [jax.ShapeDtypeStruct((1,), jnp.int32)] * flag,
        scratch_shapes=list(scratch),
        input_output_aliases=aliases,
        compiler_params=pltpu.CompilerParams(vmem_limit_bytes=SCOPED),
        cost_estimate=pl.CostEstimate(flops=flops, bytes_accessed=moved, transcendentals=0),
        name=name,
    )(*operands)


def clear_total(lay, state):
    start = lay.total_from

    def body(state):
        state[pl.ds(start, lay.shape[0] - start), :] = jnp.zeros((lay.shape[0] - start, lay.pixels), F32)

    return call(lay, body, state, [], [], name="clear_total")[0]


def place_frames(lay, sections, info, everyone, pools, state):
    def body(info, everyone, *refs):
        *pools, state, late, sems = refs
        nearest = 2 * lay.probes
        reach = jnp.bool_(False)
        for ref in (info, everyone):
            reach |= lay.row(ref[0, nearest]) + lay.pixels > lay.rows
            reach |= lay.row(ref[0, nearest + 1]) < lay.rows
        late[0] = reach.astype(jnp.int32)
        lat, side = lax.axis_index("lat"), lax.axis_index("probe")
        section = lax.axis_index("depth")
        for act in ("start", "wait"):
            for probe in range(lay.probes):
                name = info[0, probe] & ((1 << lay.name_bits) - 1)
                owner = name // lay.probes
                slot = name % lay.probes
                if len(pools) > 1:
                    slot += ((owner // 2) ^ side) * lay.probes + ((owner % 2) ^ lat) * 2 * lay.probes
                first = 0
                for pool in pools:
                    size = pool.shape[0] // lay.pixels

                    @pl.when((section == sections - 1) & (slot >= first) & (slot < first + size))
                    def _(pool=pool, first=first, probe=probe, slot=slot):
                        copy = pltpu.make_async_copy(
                            pool.at[lay.tile((slot - first) * lay.pixels), :],
                            state.at[lay.frame(0, probe), :],
                            sems.at[probe],
                        )
                        getattr(copy, act)()

                    first += size

    pools = [("hbm", pool.reshape((-1, lay.pixels))) for pool in pools]
    return call(
        lay,
        body,
        state,
        [("smem", info), ("smem", everyone), *pools],
        [],
        flag=True,
        scratch=[pltpu.SemaphoreType.DMA((lay.probes,))],
        name="place_frames",
    )


def cut_patches(lay, info, own, other, state, begin, end):
    half = own.shape[2]
    tall, pixels = lay.tall, lay.pixels

    def one(probe, info, own, other, state, window):
        row0, down, block, shift = lay.window(info, probe)
        own_top = lax.axis_index("lat") == 0
        near_at = pl.ds(pl.multiple_of(block * pixels, pixels), pixels)
        far_at = pl.ds(pl.multiple_of((block + 1) * pixels, pixels), pixels)
        for source, is_top in ((own, own_top), (other, jnp.logical_not(own_top))):
            start = jnp.clip(row0 - jnp.where(is_top, 0, half), 0, half - tall)
            to = pl.ds(pl.multiple_of(jnp.where(is_top, 0, tall), 8), tall)
            rows = pl.ds(pl.multiple_of(start, 8), tall)

            @pl.when(jnp.where(is_top, row0 < half, row0 + tall > half))
            def _(source=source, rows=rows, to=to):
                for part in range(2):
                    for layer in range(lay.layers):
                        window[part, layer, to, 0:pixels] = source[part, layer, rows, near_at]
                        window[part, layer, to, pixels : 2 * pixels] = source[part, layer, rows, far_at]

        offset = jnp.where(row0 < half, jnp.maximum(row0 - (half - tall), 0), tall)
        rows = pl.ds(pl.multiple_of(offset, 8), tall)
        turn = (pixels - shift) % pixels
        lane = lax.broadcasted_iota(jnp.int32, (tall, pixels), 1)
        for part in range(2):
            for layer in range(lay.layers):
                near = pltpu.roll(window[part, layer, rows, 0:pixels], turn, 1)
                far = pltpu.roll(window[part, layer, rows, pixels : 2 * pixels], turn, 1)
                patch = jnp.where(lane < pixels - shift, near, far)
                patch = pltpu.roll(patch, (tall - down) % tall, 0)[:pixels]
                state[lay.patch(0, probe, layer, part), :] = patch

    def body(info, *refs):
        lax.fori_loop(begin, end, lambda probe, _: one(probe, info, *refs) or 0, 0)

    return call(
        lay,
        body,
        state,
        [("vmem", info), ("vmem", own), ("vmem", other)],
        [],
        scratch=[pltpu.VMEM((2, lay.layers, 2 * tall, 2 * pixels), F32)],
        name="cut_patches",
    )[0]


def section_cost(lay):
    size = lay.count * lay.pixels**2
    return dict(flops=lay.layers * 2 * 3 * 8 * size * lay.pixels, moved=(lay.layers * 2 + 4) * 8 * size)


def pair(ref, at):
    return ref[at(0), :], ref[at(1), :]


def run_forward(lay, tick, sections, tables, state, arrived, start_wave):
    def body(tables, *refs):
        arrived_ref = refs[0] if arrived is not None else None
        start_ref = refs[-3] if start_wave is not None else None
        state, leave = refs[-2:]
        section = lax.axis_index("depth")
        group = tick - section
        final = (section == sections - 1).astype(jnp.int32)

        @pl.when((group >= 0) & (group < lay.groups))
        def _():
            wave = []
            for i in range(lay.count):
                if arrived is None:
                    wave.append((start_ref[0], start_ref[1]))
                elif start_wave is None:
                    wave.append((arrived_ref[i, 0], arrived_ref[i, 1]))
                else:
                    wave.append(
                        tuple(jnp.where(section == 0, start_ref[p], arrived_ref[i, p]) for p in range(2))
                    )
            for layer in range(lay.layers):
                chi = []
                for i in range(lay.count):
                    for part in range(2):
                        state[lay.seen(group, i, layer, part), :] = wave[i][part]
                    chi.append(times(pair(state, functools.partial(lay.patch, group, i, layer)), wave[i]))
                at = final if layer == lay.layers - 1 else 0
                wave = transform((tables[at, 0, 0], tables[at, 0, 1]), (tables[at, 1, 0], tables[at, 1, 1]), chi)
            for i in range(lay.count):
                real, imag = wave[i]
                misfit = real * real + imag * imag - state[lay.frame(group, i), :]
                factor = jnp.where(final == 1, misfit, 1.0)
                leave[i, 0] = real * factor
                leave[i, 1] = imag * factor

    waves = [("vmem", x) for x in (arrived, start_wave) if x is not None]
    return call(
        lay,
        body,
        state,
        [("vmem", tables), *waves],
        [(lay.count, 2, lay.pixels, lay.pixels)],
        name="forward_section",
        **section_cost(lay),
    )


def run_backward(lay, tick, sections, tables, state, arrived, own):
    def body(tables, *refs):
        arrived_ref = refs[0] if arrived is not None else None
        own_ref = refs[-3] if own is not None else None
        state, leave = refs[-2:]
        section = lax.axis_index("depth")
        group = tick - (2 * (sections - 1) - section)
        final = (section == sections - 1).astype(jnp.int32)

        @pl.when((group >= 0) & (group < lay.groups))
        def _():
            wave = []
            for i in range(lay.count):
                if arrived is None:
                    wave.append((own_ref[i, 0], own_ref[i, 1]))
                elif own is None:
                    wave.append((arrived_ref[i, 0], arrived_ref[i, 1]))
                else:
                    wave.append(
                        tuple(jnp.where(final == 1, own_ref[i, p], arrived_ref[i, p]) for p in range(2))
                    )
            for layer in reversed(range(lay.layers)):
                at = final if layer == lay.layers - 1 else 0
                chi = transform((tables[at, 1, 0], tables[at, 1, 1]), (tables[at, 0, 0], tables[at, 0, 1]), wave)
                wave = []
                for i in range(lay.count):
                    real, imag = times_conj(chi[i], pair(state, functools.partial(lay.seen, group, i, layer)))
                    state[lay.grad(group, i, layer, 0), :] = real
                    state[lay.grad(group, i, layer, 1), :] = imag
                    wave.append(times_conj(chi[i], pair(state, functools.partial(lay.patch, group, i, layer))))
            for i in range(lay.count):
                leave[i, 0] = wave[i][0]
                leave[i, 1] = wave[i][1]

    waves = [("vmem", x) for x in (arrived, own) if x is not None]
    return call(
        lay,
        body,
        state,
        [("vmem", tables), *waves],
        [(lay.count, 2, lay.pixels, lay.pixels)],
        name="backward_section",
        **section_cost(lay),
    )


def deposit(lay, tick, sections, info, received, state):
    pixels, tall = lay.pixels, lay.tall

    def body(info, *refs):
        state = refs[-1]
        lane = lax.broadcasted_iota(jnp.int32, (tall, pixels), 1)
        blank = jnp.zeros((8, pixels), F32)
        base = lax.axis_index("probe") * lay.rows if lay.rows < lay.height else 0

        def add(probe, partner, active, load):
            row0, down, block, shift = lay.window(info, probe, partner)
            start = row0 - base + tall

            @pl.when(active & (start > 0) & (start < lay.rows + tall))
            def _():
                for layer in range(lay.layers):
                    for part in range(2):
                        padded = jnp.concatenate([load(layer, part), blank], axis=0)
                        turned = pltpu.roll(pltpu.roll(padded, down, 0), shift % pixels, 1)
                        near = pl.ds(pl.multiple_of(lay.total(part, layer, block, start), 8), tall)
                        far = pl.ds(pl.multiple_of(lay.total(part, layer, block + 1, start), 8), tall)
                        state[near, :] += jnp.where(lane >= shift, turned, 0.0)
                        state[far, :] += jnp.where(lane >= shift, 0.0, turned)

        if tick is not None:
            group = tick - (2 * (sections - 1) - lax.axis_index("depth"))
            active = (group >= 0) & (group < lay.groups)
            group = jnp.clip(group, 0, lay.groups - 1)
            for i in range(lay.count):
                add(
                    group * lay.count + i,
                    False,
                    active,
                    lambda layer, part, i=i: state[lay.grad(group, i, layer, part), :],
                )
        for ref, (first, grads) in zip(refs, received):

            def one(i, _, ref=ref, first=first):
                add(
                    first * lay.count + i,
                    True,
                    True,
                    lambda layer, part: ref[lay.patch(0, i, layer, part), :],
                )
                return 0

            lax.fori_loop(0, grads.shape[0] // (lay.layers * 2 * pixels), one, 0)

    return call(
        lay,
        body,
        state,
        [("vmem", info)] + [("vmem", grads) for _, grads in received],
        [],
        name="deposit_patches",
    )[0]


def split_rows(lay, state, owners, taken=(0, 8)):
    rows = lay.rows // (2 * owners)
    pieces = 4 * owners * lay.layers * lay.blocks

    def body(state, keep, send, rest, sems):
        lat = lax.axis_index("lat")
        copies = [pltpu.make_async_copy(state.at[pl.ds(taken[0], taken[1] - taken[0]), :], rest, sems.at[pieces])]
        for owner in range(owners):
            for kind, target in ((lat, keep), (1 - lat, send)):
                for part in range(2):
                    for layer in range(lay.layers):
                        for block in range(lay.blocks):
                            start = lay.total(part, layer, block, lay.tall + (2 * owner + kind) * rows)
                            copies.append(
                                pltpu.make_async_copy(
                                    state.at[pl.ds(pl.multiple_of(start, 8), rows), :],
                                    target.at[part, layer, owner, :, pl.ds(block * lay.pixels, lay.pixels)],
                                    sems.at[len(copies) - 1],
                                )
                            )
        for copy in copies:
            copy.start()
        for copy in copies:
            copy.wait()

    half = (2, lay.layers, owners, rows, lay.width)
    return pl.pallas_call(
        body,
        in_specs=[VMEM],
        out_specs=[VMEM, VMEM, HBM],
        out_shape=[
            pltpu.VMEM(half, F32),
            pltpu.VMEM(half, F32),
            pltpu.HBM((taken[1] - taken[0], lay.pixels), F32),
        ],
        scratch_shapes=[pltpu.SemaphoreType.DMA((pieces + 1,))],
        compiler_params=pltpu.CompilerParams(vmem_limit_bytes=SCOPED),
        name="split_rows",
    )(in_vmem(state))


def add_up(a, b):
    each = pl.BlockSpec((1, 1, *a.shape[2:]), lambda i, j: (i, j, 0, 0, 0))

    def body(a, b, out):
        out[...] = a[...] + b[...]

    return pl.pallas_call(
        body,
        grid=a.shape[:2],
        in_specs=[each, each],
        out_specs=each,
        out_shape=pltpu.HBM(a.shape, F32),
        compiler_params=pltpu.CompilerParams(vmem_limit_bytes=SCOPED),
        name="add_up",
    )(a, b)


def swap(shard, axis):
    return lax.ppermute(shard, axis, [(0, 1), (1, 0)])


def sort_probes(lay, early, positions, indices, specimen):
    n = lay.probes
    total = 4 * n

    def body(positions, *refs):
        *scans, specimen, info, brought, sem = refs
        copy = pltpu.make_async_copy(specimen, brought, sem)
        copy.start()
        lat, side = lax.axis_index("lat"), lax.axis_index("probe")
        lane = lax.broadcasted_iota(jnp.int32, (1, 128), 1)
        at = lax.broadcasted_iota(jnp.int32, (total, 128), 0)
        across = jnp.full((1, 128), jnp.iinfo(jnp.int32).max, jnp.int32)
        down = jnp.zeros((total, 128), jnp.int32)
        for which, scan in enumerate(scans):
            owner = (side ^ (which % 2)) * 2 + (lat ^ (which // 2))
            for i in range(n):
                place = scan[i]
                key = lay.pack(positions[0, place], positions[1, place], owner * n + i)
                across = jnp.where(lane == which * n + i, key, across)
                down = jnp.where(at == which * n + i, key, down)
        rank = jnp.sum((across < down).astype(jnp.int32), axis=1, keepdims=True)
        partner = lane // n
        order = 2 * (lane % n) + lat
        wanted = jnp.where((side ^ partner) == 0, 2 * n - 1 - order, 2 * n + order)
        reach = 2 * early * lay.count
        wanted = jnp.where(lane == 2 * n, 2 * n - 1 - reach, wanted)
        wanted = jnp.where(lane == 2 * n + 1, 2 * n + reach, wanted)
        wanted = jnp.where(lane > 2 * n + 1, -1, wanted)
        info[...] = jnp.sum(jnp.where(rank == wanted, down, 0), axis=0, keepdims=True)
        copy.wait()

    return pl.pallas_call(
        body,
        in_specs=[SMEM] * 5 + [HBM],
        out_specs=[VMEM, VMEM],
        out_shape=[pltpu.VMEM((1, 128), jnp.int32), pltpu.VMEM(specimen.shape, F32)],
        scratch_shapes=[pltpu.SemaphoreType.DMA(())],
        compiler_params=pltpu.CompilerParams(vmem_limit_bytes=SCOPED),
        name="sort_probes",
    )(positions.T, *indices, in_hbm(specimen))


def local(specimen, illumination, positions, scan_index, frames):
    pixels = illumination.shape[-1]
    _, layers, half, width = specimen.shape
    height = 2 * half
    tables = jnp.asarray(make_tables(pixels))
    sections = lax.axis_size("depth")
    owners = lax.axis_size("probe")
    paired = owners == 2 and lax.axis_size("groups") <= 2
    probes = scan_index.size
    count = 2 if probes % 4 == 0 else 1
    lay = Layout(probes, count, layers, pixels, half if paired else height, height, width)
    early = lay.groups // 2

    everyone = mine = None
    if paired:
        scan = scan_index.reshape(-1)
        beside = swap(scan, "lat")
        half_rows, beside = lax.optimization_barrier((specimen, beside))
        other = swap(half_rows, "lat")
        indices = [scan, swap(scan, "probe"), beside, swap(beside, "probe")]
        measured, *indices[1:] = lax.optimization_barrier((frames, *indices[1:]))
        end = sections - 1
        ends = [(2 * end, 2 * end + 1), (2 * end + 1, 2 * end)]
        mine = lax.ppermute(measured, ("depth", "probe"), ends)
        info, specimen = sort_probes(lay, early, positions, indices, specimen)
        everyone = swap(info, "groups") if lax.axis_size("groups") == 2 else info
    else:
        other = swap(specimen, "lat")
        corners = positions[scan_index.reshape(-1)]
        info = lay.pack(corners[:, 0], corners[:, 1], jnp.arange(probes, dtype=jnp.int32))
        info = everyone = jnp.pad(info, (0, 3 * probes))[None]
    state = cut_patches(lay, info, specimen, other, None, 0, count)
    def busy(tick, source, by):
        delay = source if by > 0 else 2 * (sections - 1) - source
        return 0 <= tick - delay < lay.groups

    def pass_on(wave, tick, by):
        pairs = [
            (source, source + by)
            for source in range(sections)
            if 0 <= source + by < sections and busy(tick, source, by)
        ]
        return lax.ppermute(wave, "depth", pairs) if pairs else None

    def grads_of(state, begin, end):
        begin, end = lay.grads_of(begin, end)
        return lax.slice_in_dim(state, begin, end)

    fill = sections - 1
    parts = [(0, early // 2), (early // 2, early)] if paired else []
    crossing = {}
    down = up = None
    middle = min(1 + -(-lay.groups // 2), lay.groups) * count
    cuts = {0: (count, middle), min(fill - 1, lay.groups // 2): (middle, probes)}
    for tick in range(lay.groups + 2 * fill):
        own = None
        if paired and tick == fill - 1:
            down, mine, everyone = lax.optimization_barrier((down, mine, everyone))
            crossed = [lax.ppermute(x, ("depth", "lat"), ends) for x in (frames, mine)]
        if tick < lay.groups + fill:
            start_wave = illumination if tick < lay.groups else None
            state, own = run_forward(lay, tick, sections, tables, state, down, start_wave)
            down = pass_on(own, tick, 1)
            if tick in cuts:
                state = cut_patches(lay, info, specimen, other, state, *cuts[tick])
            if tick == 0:
                state = clear_total(lay, state)
            if tick == fill - 1:
                pools = [frames, mine, *crossed] if paired else [frames]
                state, late = place_frames(lay, sections, info, everyone, pools, state)
        if tick >= fill:
            state, rising = run_backward(lay, tick, sections, tables, state, up, own)
            up = pass_on(rising, tick, -1)
            received = crossing.pop(tick, [])
            for begin, end in parts:
                if tick == end - 1 + 2 * fill:
                    due = min(tick + CROSSING, lay.groups + 2 * fill - 1)
                    crossing.setdefault(due, []).append((begin, swap(grads_of(state, begin, end), "probe")))
            state = deposit(lay, tick, sections, info, received, state)
    if not paired:
        keep, send, _ = split_rows(lay, state, owners)
        return lax.psum_scatter(keep + swap(send, "lat"), "probe", scatter_dimension=2, tiled=False)

    keep, send, late_grads = split_rows(lay, state, 1, lay.grads_of(early, lay.groups))

    def as_they_are(keep, received, grads):
        return add_up(keep, received)

    def with_partners(keep, received, grads):
        sums = Layout(probes, count, layers, pixels, half, height, width, only_sums=True)
        state = clear_total(sums, None)
        state = deposit(sums, None, sections, info, [(early, swap(grads, "probe"))], state)
        more, send, _ = split_rows(sums, state, 1)
        return add_up(keep + more, received + swap(send, "lat"))

    result = lax.cond(late[0] > 0, with_partners, as_they_are, keep, swap(send, "lat"), late_grads)
    return result[:, :, 0]


def solution(mesh):
    return jax.shard_map(
        local,
        mesh=mesh,
        in_specs=(
            P(None, ("groups", "depth"), "lat", None),
            P(),
            P("groups", None),
            P("groups", ("probe", "lat")),
            P("groups", ("probe", "lat"), None, None),
        ),
        out_specs=P(None, ("groups", "depth"), ("probe", "lat"), None),
        check_vma=False,
    )
```

```python
import functools
import math

import jax
import jax.numpy as jnp
import ml_dtypes
import numpy as np
from jax import lax
from jax.experimental import pallas as pl
from jax.experimental.pallas import tpu as pltpu
from jax.sharding import PartitionSpec as P

FRESNEL = 8.0
SCOPED = 8 << 20
CROSSING = 3
F32 = jnp.float32
BF16 = jnp.bfloat16
HBM = pl.BlockSpec(memory_space=pl.ANY)
VMEM = pl.BlockSpec(memory_space=pltpu.VMEM)
SMEM = pl.BlockSpec(memory_space=pltpu.SMEM)


def in_hbm(x):
    return pltpu.with_memory_space_constraint(x, pltpu.HBM)


def in_vmem(x):
    return pltpu.with_memory_space_constraint(x, pltpu.VMEM)


def real_blocks(matrix):
    real, imag = matrix.real, matrix.imag
    left = np.block([[real, -imag], [imag, real]])
    right = np.block([[real, imag], [-imag, real]])
    return np.stack([left, right])


@functools.lru_cache(maxsize=None)
def make_tables(pixels):
    index = np.arange(pixels)
    freq = np.where(index < pixels // 2, index, index - pixels) / pixels
    spread = index[:, None] - index[None, :]
    phase = 2.0 * math.pi * freq * spread[:, :, None] - math.pi * FRESNEL * freq * freq
    propagator = np.mean(np.exp(1j * phase), axis=-1)
    turns = index[:, None] * index[None, :] % pixels
    fourier = np.exp(-2j * math.pi * turns / pixels) / math.sqrt(pixels)
    blocks = np.stack([real_blocks(propagator), real_blocks(fourier)]).astype(np.float32)
    high = blocks.astype(ml_dtypes.bfloat16)
    low = (blocks - high.astype(np.float32)).astype(ml_dtypes.bfloat16)
    return np.stack([high, low], axis=2)


def halves(x):
    high = x.astype(BF16)
    return high, (x - high.astype(F32)).astype(BF16)


def dot(a, b):
    return jnp.dot(a, b, preferred_element_type=F32)


def transform(left, right, fields):
    size = fields[0][0].shape[0]
    stacked = jnp.concatenate(
        [
            jnp.concatenate([real for real, _ in fields], axis=1),
            jnp.concatenate([imag for _, imag in fields], axis=1),
        ],
        axis=0,
    )
    high, low = halves(stacked)
    mid = dot(left[0], high) + (dot(left[1], high) + dot(left[0], low))
    rows = jnp.concatenate(
        [
            jnp.concatenate(
                [mid[:size, i * size : (i + 1) * size], mid[size:, i * size : (i + 1) * size]], axis=1
            )
            for i in range(len(fields))
        ],
        axis=0,
    )
    high, low = halves(rows)
    out = dot(high, right[0]) + (dot(high, right[1]) + dot(low, right[0]))
    return [
        (out[i * size : (i + 1) * size, :size], out[i * size : (i + 1) * size, size:])
        for i in range(len(fields))
    ]


def times(a, b):
    return a[0] * b[0] - a[1] * b[1], a[0] * b[1] + a[1] * b[0]


def times_conj(a, b):
    return a[0] * b[0] + a[1] * b[1], a[1] * b[0] - a[0] * b[1]


class Layout:
    def __init__(self, probes, count, layers, pixels, rows, height, width, only_sums=False):
        self.probes, self.count, self.layers, self.pixels = probes, count, layers, pixels
        self.groups = probes // count
        self.tall = pixels + 8
        self.rows, self.height, self.width = rows, height, width
        self.blocks = width // pixels
        self.deep = rows + 2 * self.tall
        self.column_bits = (width - 1).bit_length()
        self.name_bits = (4 * probes - 1).bit_length()
        self.stack = probes * layers * 2 * pixels
        self.seen_from = self.stack
        self.grads_from = 2 * self.stack
        self.frames_from = 3 * self.stack
        self.total_from = 0 if only_sums else self.frames_from + probes * pixels
        self.shape = (self.total_from + 2 * layers * self.blocks * self.deep, pixels)

    def stacked(self, group, i, layer, part):
        probe = group * self.count + i
        return ((probe * self.layers + layer) * 2 + part) * self.pixels

    def tile(self, start):
        return pl.ds(pl.multiple_of(start, 8), self.pixels)

    def patch(self, group, i, layer, part):
        return self.tile(self.stacked(group, i, layer, part))

    def seen(self, group, i, layer, part):
        return self.tile(self.seen_from + self.stacked(group, i, layer, part))

    def grad(self, group, i, layer, part):
        return self.tile(self.grads_from + self.stacked(group, i, layer, part))

    def grads_of(self, begin, end):
        each = self.stack // self.groups
        return self.grads_from + begin * each, self.grads_from + end * each

    def frame(self, group, i):
        return self.tile(self.frames_from + (group * self.count + i) * self.pixels)

    def total(self, part, layer, block, row):
        block = (part * self.layers + layer) * self.blocks + block
        return self.total_from + block * self.deep + row

    def pack(self, row, column, name):
        return (((row << self.column_bits) + column) << self.name_bits) + name

    def row(self, key):
        return key >> (self.column_bits + self.name_bits)

    def window(self, info, probe, whose=0):
        lane = lax.broadcasted_iota(jnp.int32, info.shape, 1)
        key = jnp.sum(jnp.where(lane == probe + whose * self.probes, info[...], 0))
        row = self.row(key)
        column = (key >> self.name_bits) & ((1 << self.column_bits) - 1)
        row0 = jnp.minimum(row // 8 * 8, self.height - self.tall)
        block = jnp.minimum(column // self.pixels, self.blocks - 2)
        return row0, row - row0, block, column - block * self.pixels


def call(lay, body, state, before, outs, scratch=(), flag=False, flops=1000, moved=1000, name=None):
    spaces = {"hbm": (HBM, in_hbm), "vmem": (VMEM, in_vmem), "smem": (SMEM, lambda x: x)}
    specs = [spaces[kind][0] for kind, _ in before]
    operands = [spaces[kind][1](x) for kind, x in before]
    at = len(before)
    aliases = {}
    if state is not None:
        specs.append(VMEM)
        operands.append(in_vmem(state))
        aliases = {at: 0}

    def kernel(*refs):
        body(*refs[:at], *refs[at + len(aliases) :])

    return pl.pallas_call(
        kernel,
        in_specs=specs,
        out_specs=[VMEM] * (1 + len(outs) + flag),
        out_shape=[pltpu.VMEM(shape, F32) for shape in (lay.shape, *outs)]
        + [pltpu.VMEM((1, 128), jnp.int32)] * flag,
        scratch_shapes=list(scratch),
        input_output_aliases=aliases,
        compiler_params=pltpu.CompilerParams(vmem_limit_bytes=SCOPED),
        cost_estimate=pl.CostEstimate(flops=flops, bytes_accessed=moved, transcendentals=0),
        name=name,
    )(*operands)


def clear_total(lay, state):
    start = lay.total_from

    def body(state):
        state[pl.ds(start, lay.shape[0] - start), :] = jnp.zeros((lay.shape[0] - start, lay.pixels), F32)

    return call(lay, body, state, [], [], name="clear_total")[0]


def place_frames(lay, sections, info, everyone, pools, state):
    def body(info, everyone, *refs):
        *pools, state, late, sems = refs
        nearest = 3 * lay.probes
        reach = jnp.bool_(False)
        for ref in (info, everyone):
            reach |= lay.row(ref[0, nearest]) + lay.pixels > lay.rows
            reach |= lay.row(ref[0, nearest + 1]) < lay.rows
        late[...] = jnp.full(late.shape, reach.astype(jnp.int32), jnp.int32)
        lat, side = lax.axis_index("lat"), lax.axis_index("probe")

        @pl.when(lax.axis_index("depth") == sections - 1)
        def _():
            for act in ("start", "wait"):
                for probe in range(lay.probes):
                    name = info[0, probe] & ((1 << lay.name_bits) - 1)
                    owner = name // lay.probes
                    slot = name % lay.probes
                    if len(pools) > 1:
                        slot += ((owner // 2) ^ side) * lay.probes + ((owner % 2) ^ lat) * 2 * lay.probes
                    first = 0
                    for pool in pools:
                        size = pool.shape[0] // lay.pixels

                        @pl.when((slot >= first) & (slot < first + size))
                        def _(pool=pool, first=first, probe=probe, slot=slot):
                            copy = pltpu.make_async_copy(
                                pool.at[lay.tile((slot - first) * lay.pixels), :],
                                state.at[lay.frame(0, probe), :],
                                sems.at[probe],
                            )
                            getattr(copy, act)()

                        first += size

    pools = [pool.reshape((-1, lay.pixels)) for pool in pools]
    pools = [("hbm", pools[0]), *(("vmem", pool) for pool in pools[1:])]
    return call(
        lay,
        body,
        state,
        [("smem", info), ("smem", everyone), *pools],
        [],
        flag=True,
        scratch=[pltpu.SemaphoreType.DMA((lay.probes,))],
        name="place_frames",
    )


def cut_patches(lay, info, own, other, state, begin, end):
    half = own.shape[2]
    tall, pixels = lay.tall, lay.pixels

    def one(probe, info, own, other, state, window):
        row0, down, block, shift = lay.window(info, probe)
        own_top = lax.axis_index("lat") == 0
        near_at = pl.ds(pl.multiple_of(block * pixels, pixels), pixels)
        far_at = pl.ds(pl.multiple_of((block + 1) * pixels, pixels), pixels)
        for source, is_top in ((own, own_top), (other, jnp.logical_not(own_top))):
            start = jnp.clip(row0 - jnp.where(is_top, 0, half), 0, half - tall)
            to = pl.ds(pl.multiple_of(jnp.where(is_top, 0, tall), 8), tall)
            rows = pl.ds(pl.multiple_of(start, 8), tall)

            @pl.when(jnp.where(is_top, row0 < half, row0 + tall > half))
            def _(source=source, rows=rows, to=to):
                for part in range(2):
                    for layer in range(lay.layers):
                        window[part, layer, to, 0:pixels] = source[part, layer, rows, near_at]
                        window[part, layer, to, pixels : 2 * pixels] = source[part, layer, rows, far_at]

        offset = jnp.where(row0 < half, jnp.maximum(row0 - (half - tall), 0), tall)
        rows = pl.ds(pl.multiple_of(offset, 8), tall)
        turn = (pixels - shift) % pixels
        lane = lax.broadcasted_iota(jnp.int32, (tall, pixels), 1)
        for part in range(2):
            for layer in range(lay.layers):
                near = pltpu.roll(window[part, layer, rows, 0:pixels], turn, 1)
                far = pltpu.roll(window[part, layer, rows, pixels : 2 * pixels], turn, 1)
                patch = jnp.where(lane < pixels - shift, near, far)
                patch = pltpu.roll(patch, (tall - down) % tall, 0)[:pixels]
                state[lay.patch(0, probe, layer, part), :] = patch

    def body(info, *refs):
        section = lax.axis_index("depth")
        bounds = [x(section) if callable(x) else x for x in (begin, end)]
        lax.fori_loop(*bounds, lambda probe, _: one(probe, info, *refs) or 0, 0)

    return call(
        lay,
        body,
        state,
        [("vmem", info), ("vmem", own), ("vmem", other)],
        [],
        scratch=[pltpu.VMEM((2, lay.layers, 2 * tall, 2 * pixels), F32)],
        name="cut_patches",
    )[0]


def section_cost(lay):
    size = lay.count * lay.pixels**2
    return dict(flops=lay.layers * 2 * 3 * 8 * size * lay.pixels, moved=(lay.layers * 2 + 4) * 8 * size)


def pair(ref, at):
    return ref[at(0), :], ref[at(1), :]


def run_forward(lay, tick, sections, tables, state, arrived, start_wave):
    def body(tables, *refs):
        arrived_ref = refs[0] if arrived is not None else None
        start_ref = refs[-3] if start_wave is not None else None
        state, leave = refs[-2:]
        section = lax.axis_index("depth")
        group = tick - section
        final = (section == sections - 1).astype(jnp.int32)

        @pl.when((group >= 0) & (group < lay.groups))
        def _():
            wave = []
            for i in range(lay.count):
                if arrived is None:
                    wave.append((start_ref[0], start_ref[1]))
                elif start_wave is None:
                    wave.append((arrived_ref[i, 0], arrived_ref[i, 1]))
                else:
                    wave.append(
                        tuple(jnp.where(section == 0, start_ref[p], arrived_ref[i, p]) for p in range(2))
                    )
            for layer in range(lay.layers):
                chi = []
                for i in range(lay.count):
                    for part in range(2):
                        state[lay.seen(group, i, layer, part), :] = wave[i][part]
                    chi.append(times(pair(state, functools.partial(lay.patch, group, i, layer)), wave[i]))
                at = final if layer == lay.layers - 1 else 0
                wave = transform((tables[at, 0, 0], tables[at, 0, 1]), (tables[at, 1, 0], tables[at, 1, 1]), chi)
            for i in range(lay.count):
                real, imag = wave[i]
                misfit = real * real + imag * imag - state[lay.frame(group, i), :]
                factor = jnp.where(final == 1, misfit, 1.0)
                leave[i, 0] = real * factor
                leave[i, 1] = imag * factor

    waves = [("vmem", x) for x in (arrived, start_wave) if x is not None]
    return call(
        lay,
        body,
        state,
        [("vmem", tables), *waves],
        [(lay.count, 2, lay.pixels, lay.pixels)],
        name="forward_section",
        **section_cost(lay),
    )


def run_backward(lay, tick, sections, tables, state, arrived, own, copied=False):
    def body(tables, *refs):
        arrived_ref = refs[0] if arrived is not None else None
        own_ref = refs[1 if arrived is not None else 0] if own is not None else None
        state, leave = refs[-3:-1] if copied else refs[-2:]
        section = lax.axis_index("depth")
        group = tick - (2 * (sections - 1) - section)
        final = (section == sections - 1).astype(jnp.int32)

        @pl.when((group >= 0) & (group < lay.groups))
        def _():
            wave = []
            for i in range(lay.count):
                if arrived is None:
                    wave.append((own_ref[i, 0], own_ref[i, 1]))
                elif own is None:
                    wave.append((arrived_ref[i, 0], arrived_ref[i, 1]))
                else:
                    wave.append(
                        tuple(jnp.where(final == 1, own_ref[i, p], arrived_ref[i, p]) for p in range(2))
                    )
            for layer in reversed(range(lay.layers)):
                at = final if layer == lay.layers - 1 else 0
                chi = transform((tables[at, 1, 0], tables[at, 1, 1]), (tables[at, 0, 0], tables[at, 0, 1]), wave)
                wave = []
                for i in range(lay.count):
                    real, imag = times_conj(chi[i], pair(state, functools.partial(lay.seen, group, i, layer)))
                    state[lay.grad(group, i, layer, 0), :] = real
                    state[lay.grad(group, i, layer, 1), :] = imag
                    if copied:
                        refs[-1][lay.patch(0, i, layer, 0), :] = real
                        refs[-1][lay.patch(0, i, layer, 1), :] = imag
                    wave.append(times_conj(chi[i], pair(state, functools.partial(lay.patch, group, i, layer))))
            for i in range(lay.count):
                leave[i, 0] = wave[i][0]
                leave[i, 1] = wave[i][1]

    waves = [("vmem", x) for x in (arrived, own) if x is not None]
    return call(
        lay,
        body,
        state,
        [("vmem", tables), *waves],
        [(lay.count, 2, lay.pixels, lay.pixels)] + [(lay.stack // lay.groups, lay.pixels)] * copied,
        name="backward_section",
        **section_cost(lay),
    )


def deposit(lay, tick, sections, info, received, state):
    pixels, tall = lay.pixels, lay.tall

    def body(info, *refs):
        state = refs[-1]
        lane = lax.broadcasted_iota(jnp.int32, (tall, pixels), 1)
        blank = jnp.zeros((8, pixels), F32)
        base = lax.axis_index("probe") * lay.rows if lay.rows < lay.height else 0

        def add(probe, whose, active, load):
            row0, down, block, shift = lay.window(info, probe, whose)
            start = row0 - base + tall

            @pl.when(active & (start > 0) & (start < lay.rows + tall))
            def _():
                for layer in range(lay.layers):
                    for part in range(2):
                        padded = jnp.concatenate([load(layer, part), blank], axis=0)
                        turned = pltpu.roll(pltpu.roll(padded, down, 0), shift % pixels, 1)
                        near = pl.ds(pl.multiple_of(lay.total(part, layer, block, start), 8), tall)
                        far = pl.ds(pl.multiple_of(lay.total(part, layer, block + 1, start), 8), tall)
                        state[near, :] += jnp.where(lane >= shift, turned, 0.0)
                        state[far, :] += jnp.where(lane >= shift, 0.0, turned)

        if tick is not None:
            group = tick - (2 * (sections - 1) - lax.axis_index("depth"))
            active = (group >= 0) & (group < lay.groups)
            group = jnp.clip(group, 0, lay.groups - 1)
            for i in range(lay.count):
                add(
                    group * lay.count + i,
                    0,
                    active,
                    lambda layer, part, i=i: state[lay.grad(group, i, layer, part), :],
                )
        for ref, (first, whose, grads) in zip(refs, received):

            def one(i, _, ref=ref, first=first, whose=whose):
                add(
                    first * lay.count + i,
                    whose,
                    (lax.axis_index("depth") == 0) | (whose != 2),
                    lambda layer, part: ref[lay.patch(0, i, layer, part), :],
                )
                return 0

            lax.fori_loop(0, grads.shape[0] // (lay.layers * 2 * pixels), one, 0)

    return call(
        lay,
        body,
        state,
        [("vmem", info)] + [("vmem", grads) for *_, grads in received],
        [],
        name="deposit_patches",
    )[0]


def take_rows(lay, state, owners, others):
    rows = lay.rows // (2 * owners)
    pieces = [(p, l, o, b) for p in range(2) for l in range(lay.layers) for o in range(owners) for b in range(lay.blocks)]

    def body(state, out, sems):
        core = lax.axis_index("lat")
        core = 1 - core if others else core
        for act in ("start", "wait"):
            for i, (part, layer, owner, block) in enumerate(pieces):
                start = lay.total(part, layer, block, lay.tall + (2 * owner + core) * rows)
                copy = pltpu.make_async_copy(
                    state.at[pl.ds(pl.multiple_of(start, 8), rows), :],
                    out.at[part, layer, owner, block],
                    sems.at[i],
                )
                getattr(copy, act)()

    return pl.pallas_call(
        body,
        in_specs=[VMEM],
        out_specs=VMEM,
        out_shape=pltpu.VMEM((2, lay.layers, owners, lay.blocks, rows, lay.pixels), F32),
        scratch_shapes=[pltpu.SemaphoreType.DMA((len(pieces),))],
        compiler_params=pltpu.CompilerParams(vmem_limit_bytes=SCOPED),
        cost_estimate=pl.CostEstimate(flops=1000, bytes_accessed=1000, transcendentals=0),
        name="take_rows",
    )(in_vmem(state))


def room(shape):
    return pl.pallas_call(
        lambda out: None,
        out_specs=VMEM,
        out_shape=pltpu.VMEM(shape, F32),
        compiler_params=pltpu.CompilerParams(vmem_limit_bytes=SCOPED),
        name="room",
    )()


def finish(lay, state, received, more, late):
    rows = lay.rows // 2

    def body(late, state, received, more, out):
        part, layer = pl.program_id(0), pl.program_id(1)
        is_late = jnp.max(late[...]) > 0
        for block in range(lay.blocks):
            start = lay.total(part, layer, block, lay.tall + lax.axis_index("lat") * rows)
            columns = pl.ds(block * lay.pixels, lay.pixels)
            here = state[pl.ds(pl.multiple_of(start, 8), rows), :] + received[part, layer, 0, block]
            out[0, 0, :, columns] = here

            @pl.when(is_late)
            def _(block=block, columns=columns, here=here):
                out[0, 0, :, columns] = here + more[part, layer, 0, block]

    return pl.pallas_call(
        body,
        grid=(2, lay.layers),
        in_specs=[VMEM] * 4,
        out_specs=pl.BlockSpec((1, 1, rows, lay.width), lambda i, j: (i, j, 0, 0)),
        out_shape=pltpu.HBM((2, lay.layers, rows, lay.width), F32),
        compiler_params=pltpu.CompilerParams(vmem_limit_bytes=SCOPED),
        name="finish",
    )(*map(in_vmem, (late, state, received, more)))


def swap(shard, axis):
    return lax.ppermute(shard, axis, [(0, 1), (1, 0)])


def sort_probes(lay, early, positions, indices):
    n = lay.probes
    total = 4 * n

    def body(positions, *refs):
        *scans, info = refs
        lat, side = lax.axis_index("lat"), lax.axis_index("probe")
        lane = lax.broadcasted_iota(jnp.int32, (1, 128), 1)
        at = lax.broadcasted_iota(jnp.int32, (total, 128), 0)
        across = jnp.full((1, 128), jnp.iinfo(jnp.int32).max, jnp.int32)
        down = jnp.zeros((total, 128), jnp.int32)
        for which, scan in enumerate(scans):
            owner = (side ^ (which % 2)) * 2 + (lat ^ (which // 2))
            for i in range(n):
                place = scan[i]
                key = lay.pack(positions[0, place], positions[1, place], owner * n + i)
                across = jnp.where(lane == which * n + i, key, across)
                down = jnp.where(at == which * n + i, key, down)
        rank = jnp.sum((across < down).astype(jnp.int32), axis=1, keepdims=True)
        whose = lane // n
        order = 2 * (lane % n) + jnp.where(whose == 2, 1 - lat, lat)
        wanted = jnp.where(jnp.where(whose == 1, 1 - side, side) == 0, 2 * n - 1 - order, 2 * n + order)
        reach = 2 * early * lay.count
        wanted = jnp.where(lane == 3 * n, 2 * n - 1 - reach, wanted)
        wanted = jnp.where(lane == 3 * n + 1, 2 * n + reach, wanted)
        wanted = jnp.where(lane > 3 * n + 1, -1, wanted)
        info[...] = jnp.sum(jnp.where(rank == wanted, down, 0), axis=0, keepdims=True)

    return pl.pallas_call(
        body,
        in_specs=[SMEM] * 5,
        out_specs=VMEM,
        out_shape=pltpu.VMEM((1, 128), jnp.int32),
        compiler_params=pltpu.CompilerParams(vmem_limit_bytes=SCOPED),
        name="sort_probes",
    )(positions.T, *indices)


def bring(x):
    def body(x, out, sem):
        copy = pltpu.make_async_copy(x, out, sem)
        copy.start()
        copy.wait()

    return pl.pallas_call(
        body,
        in_specs=[HBM],
        out_specs=VMEM,
        out_shape=pltpu.VMEM(x.shape, x.dtype),
        scratch_shapes=[pltpu.SemaphoreType.DMA(())],
        compiler_params=pltpu.CompilerParams(vmem_limit_bytes=SCOPED),
        cost_estimate=pl.CostEstimate(flops=0, bytes_accessed=2 * x.size * 4, transcendentals=0),
        name="bring",
    )(in_hbm(x))


def local(specimen, illumination, positions, scan_index, frames):
    pixels = illumination.shape[-1]
    _, layers, half, width = specimen.shape
    height = 2 * half
    tables = jnp.asarray(make_tables(pixels))
    sections = lax.axis_size("depth")
    owners = lax.axis_size("probe")
    paired = owners == 2 and lax.axis_size("groups") <= 2
    probes = scan_index.size
    count = 2 if probes % 4 == 0 else 1
    lay = Layout(probes, count, layers, pixels, half if paired else height, height, width)
    early = lay.groups // 2

    everyone = mine = None
    if paired:
        scan = scan_index.reshape(-1)
        beside = swap(scan, "lat")
        half_rows, beside = lax.optimization_barrier((specimen, beside))
        other = swap(half_rows, "lat")
        indices = [scan, swap(scan, "probe"), beside, swap(beside, "probe")]
        measured, *indices[1:] = lax.optimization_barrier((frames, *indices[1:]))
        end = sections - 1
        ends = [(2 * end, 2 * end + 1), (2 * end + 1, 2 * end)]
        mine = lax.ppermute(measured, ("depth", "probe"), ends)
        specimen = bring(specimen)
        info = sort_probes(lay, early, positions, indices)
        everyone = swap(info, "groups") if lax.axis_size("groups") == 2 else info
    else:
        other = swap(specimen, "lat")
        corners = positions[scan_index.reshape(-1)]
        info = lay.pack(corners[:, 0], corners[:, 1], jnp.arange(probes, dtype=jnp.int32))
        info = everyone = jnp.pad(info, (0, 3 * probes))[None]
    state = cut_patches(lay, info, specimen, other, None, 0, count)
    def busy(tick, source, by):
        delay = source if by > 0 else 2 * (sections - 1) - source
        return 0 <= tick - delay < lay.groups

    def pass_on(wave, tick, by):
        pairs = [
            (source, source + by)
            for source in range(sections)
            if 0 <= source + by < sections and busy(tick, source, by)
        ]
        return lax.ppermute(wave, "depth", pairs) if pairs else None

    def grads_of(state, begin, end):
        begin, end = lay.grads_of(begin, end)
        return lax.slice_in_dim(state, begin, end)

    fill = sections - 1
    parts = [(0, early // 2), (early // 2, early)] if paired else []
    crossing = {}
    down = up = None
    middle = min(1 + -(-lay.groups // 2), lay.groups) * count
    part = lambda section: jnp.where(section < 2, middle, probes)
    cuts = {0: (count, part), min(fill, lay.groups // 2): (part, probes)}
    last_tick = lay.groups + 2 * fill - 1
    sent = None
    for tick in range(lay.groups + 2 * fill):
        own = None
        if paired and tick == fill - 1:
            down, mine, everyone = lax.optimization_barrier((down, mine, everyone))
            crossed = [lax.ppermute(x, ("depth", "lat"), ends) for x in (frames, mine)]
        if tick < lay.groups + fill:
            start_wave = illumination if tick < lay.groups else None
            state, own = run_forward(lay, tick, sections, tables, state, down, start_wave)
            down = pass_on(own, tick, 1)
            if tick in cuts:
                state = cut_patches(lay, info, specimen, other, state, *cuts[tick])
            if tick == 0:
                state = clear_total(lay, state)
            if tick == fill - 1:
                pools = [frames, mine, *crossed] if paired else [frames]
                state, late = place_frames(lay, sections, info, everyone, pools, state)
        if tick >= fill:
            copied = paired and tick == last_tick
            state, rising, *rest = run_backward(lay, tick, sections, tables, state, up, own, copied)
            up = pass_on(rising, tick, -1)
            received = crossing.pop(tick, [])
            for begin, end in parts:
                if tick == end - 1 + 2 * fill:
                    due = min(tick + CROSSING, last_tick - 1)
                    crossing.setdefault(due, []).append((begin, 1, swap(grads_of(state, begin, end), "probe")))
            state = deposit(lay, tick, sections, info, received, state)
            if paired and tick == last_tick - 1:
                state, up = lax.optimization_barrier((state, up))
                sent = swap(take_rows(lay, state, 1, True), "lat")
    if paired:
        last = swap(rest[0], "lat")
        state = deposit(lay, None, sections, info, [(lay.groups - 1, 2, last)], state)
    if not paired:
        whole = take_rows(lay, state, owners, False) + swap(take_rows(lay, state, owners, True), "lat")
        whole = jnp.moveaxis(whole, 3, 4).reshape((2, layers, owners, -1, width))
        return lax.psum_scatter(whole, "probe", scatter_dimension=2, tiled=False)

    def nothing_more(grads):
        return room(sent.shape)

    def from_partners(grads):
        sums = Layout(probes, count, layers, pixels, half, height, width, only_sums=True)
        sums_state = clear_total(sums, None)
        sums_state = deposit(sums, None, sections, info, [(early, 1, swap(grads, "probe"))], sums_state)
        return take_rows(sums, sums_state, 1, False) + swap(take_rows(sums, sums_state, 1, True), "lat")

    more = lax.cond(late[0, 0] > 0, from_partners, nothing_more, grads_of(state, early, lay.groups))
    return finish(lay, state, sent, more, late)


def solution(mesh):
    return jax.shard_map(
        local,
        mesh=mesh,
        in_specs=(
            P(None, ("groups", "depth"), "lat", None),
            P(),
            P("groups", None),
            P("groups", ("probe", "lat")),
            P("groups", ("probe", "lat"), None, None),
        ),
        out_specs=P(None, ("groups", "depth"), ("probe", "lat"), None),
        check_vma=False,
    )
```

```python
import functools
import math

import jax
import jax.numpy as jnp
import ml_dtypes
import numpy as np
from jax import lax
from jax.experimental import pallas as pl
from jax.experimental.pallas import tpu as pltpu
from jax.sharding import PartitionSpec as P

FRESNEL = 8.0
SCOPED = 8 << 20
CROSSING = 3
F32 = jnp.float32
BF16 = jnp.bfloat16
HBM = pl.BlockSpec(memory_space=pl.ANY)
VMEM = pl.BlockSpec(memory_space=pltpu.VMEM)
SMEM = pl.BlockSpec(memory_space=pltpu.SMEM)


def in_hbm(x):
    return pltpu.with_memory_space_constraint(x, pltpu.HBM)


def in_vmem(x):
    return pltpu.with_memory_space_constraint(x, pltpu.VMEM)


def real_blocks(matrix):
    real, imag = matrix.real, matrix.imag
    left = np.block([[real, -imag], [imag, real]])
    right = np.block([[real, imag], [-imag, real]])
    return np.stack([left, right])


@functools.lru_cache(maxsize=None)
def make_tables(pixels):
    index = np.arange(pixels)
    freq = np.where(index < pixels // 2, index, index - pixels) / pixels
    spread = index[:, None] - index[None, :]
    phase = 2.0 * math.pi * freq * spread[:, :, None] - math.pi * FRESNEL * freq * freq
    propagator = np.mean(np.exp(1j * phase), axis=-1)
    turns = index[:, None] * index[None, :] % pixels
    fourier = np.exp(-2j * math.pi * turns / pixels) / math.sqrt(pixels)
    blocks = np.stack([real_blocks(propagator), real_blocks(fourier)]).astype(np.float32)
    high = blocks.astype(ml_dtypes.bfloat16)
    low = (blocks - high.astype(np.float32)).astype(ml_dtypes.bfloat16)
    return np.stack([high, low], axis=2)


def halves(x):
    high = x.astype(BF16)
    return high, (x - high.astype(F32)).astype(BF16)


def dot(a, b):
    return jnp.dot(a, b, preferred_element_type=F32)


def transform(left, right, fields):
    size = fields[0][0].shape[0]
    mids = []
    for high, low in [halves(jnp.concatenate(field, axis=0)) for field in fields]:
        both = dot(left[0], jnp.concatenate([high, low], axis=1))
        mids.append(both[:, :size] + (both[:, size:] + dot(left[1], high)))
    outs = []
    for high, low in [halves(jnp.concatenate([mid[:size], mid[size:]], axis=1)) for mid in mids]:
        both = dot(jnp.concatenate([high, low], axis=0), right[0])
        outs.append(both[:size] + (both[size:] + dot(high, right[1])))
    return [(out[:, :size], out[:, size:]) for out in outs]


def times(a, b):
    return a[0] * b[0] - a[1] * b[1], a[0] * b[1] + a[1] * b[0]


def times_conj(a, b):
    return a[0] * b[0] + a[1] * b[1], a[1] * b[0] - a[0] * b[1]


class Layout:
    def __init__(self, probes, count, layers, pixels, rows, height, width, only_sums=False):
        self.probes, self.count, self.layers, self.pixels = probes, count, layers, pixels
        self.groups = probes // count
        self.tall = pixels + 8
        self.rows, self.height, self.width = rows, height, width
        self.blocks = width // pixels
        self.deep = rows + 2 * self.tall
        self.column_bits = (width - 1).bit_length()
        self.name_bits = (4 * probes - 1).bit_length()
        self.stack = probes * layers * 2 * pixels
        self.seen_from = self.stack
        self.grads_from = 2 * self.stack
        self.frames_from = 3 * self.stack
        self.total_from = 0 if only_sums else self.frames_from + probes * pixels
        self.shape = (self.total_from + 2 * layers * self.blocks * self.deep, pixels)

    def stacked(self, group, i, layer, part):
        probe = group * self.count + i
        return ((probe * self.layers + layer) * 2 + part) * self.pixels

    def tile(self, start):
        return pl.ds(pl.multiple_of(start, 8), self.pixels)

    def patch(self, group, i, layer, part):
        return self.tile(self.stacked(group, i, layer, part))

    def seen(self, group, i, layer, part):
        return self.tile(self.seen_from + self.stacked(group, i, layer, part))

    def grad(self, group, i, layer, part):
        return self.tile(self.grads_from + self.stacked(group, i, layer, part))

    def grads_of(self, begin, end):
        each = self.stack // self.groups
        return self.grads_from + begin * each, self.grads_from + end * each

    def frame(self, group, i):
        return self.tile(self.frames_from + (group * self.count + i) * self.pixels)

    def total(self, part, layer, block, row):
        block = (part * self.layers + layer) * self.blocks + block
        return self.total_from + block * self.deep + row

    def pack(self, row, column, name):
        return (((row << self.column_bits) + column) << self.name_bits) + name

    def row(self, key):
        return key >> (self.column_bits + self.name_bits)

    def window(self, info, probe, whose=0):
        lane = lax.broadcasted_iota(jnp.int32, info.shape, 1)
        key = jnp.sum(jnp.where(lane == probe + whose * self.probes, info[...], 0))
        row = self.row(key)
        column = (key >> self.name_bits) & ((1 << self.column_bits) - 1)
        row0 = jnp.minimum(row // 8 * 8, self.height - self.tall)
        block = jnp.minimum(column // self.pixels, self.blocks - 2)
        return row0, row - row0, block, column - block * self.pixels


def call(lay, body, state, before, outs, scratch=(), flag=False, flops=1000, moved=1000, name=None):
    spaces = {"hbm": (HBM, in_hbm), "vmem": (VMEM, in_vmem), "smem": (SMEM, lambda x: x)}
    specs = [spaces[kind][0] for kind, _ in before]
    operands = [spaces[kind][1](x) for kind, x in before]
    at = len(before)
    aliases = {}
    if state is not None:
        specs.append(VMEM)
        operands.append(in_vmem(state))
        aliases = {at: 0}

    def kernel(*refs):
        body(*refs[:at], *refs[at + len(aliases) :])

    return pl.pallas_call(
        kernel,
        in_specs=specs,
        out_specs=[VMEM] * (1 + len(outs) + flag),
        out_shape=[pltpu.VMEM(shape, F32) for shape in (lay.shape, *outs)]
        + [pltpu.VMEM((1, 128), jnp.int32)] * flag,
        scratch_shapes=list(scratch),
        input_output_aliases=aliases,
        compiler_params=pltpu.CompilerParams(vmem_limit_bytes=SCOPED),
        cost_estimate=pl.CostEstimate(flops=flops, bytes_accessed=moved, transcendentals=0),
        name=name,
    )(*operands)


def clear_total(lay, state):
    start = lay.total_from

    def body(state):
        state[pl.ds(start, lay.shape[0] - start), :] = jnp.zeros((lay.shape[0] - start, lay.pixels), F32)

    return call(lay, body, state, [], [], name="clear_total")[0]


def place_frames(lay, sections, info, everyone, pools, state):
    def body(info, everyone, *refs):
        *pools, state, late, sems = refs
        nearest = 3 * lay.probes
        reach = jnp.bool_(False)
        for ref in (info, everyone):
            reach |= lay.row(ref[0, nearest]) + lay.pixels > lay.rows
            reach |= lay.row(ref[0, nearest + 1]) < lay.rows
        late[...] = jnp.full(late.shape, reach.astype(jnp.int32), jnp.int32)
        lat, side = lax.axis_index("lat"), lax.axis_index("probe")

        @pl.when(lax.axis_index("depth") == sections - 1)
        def _():
            for act in ("start", "wait"):
                for probe in range(lay.probes):
                    name = info[0, probe] & ((1 << lay.name_bits) - 1)
                    owner = name // lay.probes
                    slot = name % lay.probes
                    if len(pools) > 1:
                        slot += ((owner // 2) ^ side) * lay.probes + ((owner % 2) ^ lat) * 2 * lay.probes
                    first = 0
                    for pool in pools:
                        size = pool.shape[0] // lay.pixels

                        @pl.when((slot >= first) & (slot < first + size))
                        def _(pool=pool, first=first, probe=probe, slot=slot):
                            copy = pltpu.make_async_copy(
                                pool.at[lay.tile((slot - first) * lay.pixels), :],
                                state.at[lay.frame(0, probe), :],
                                sems.at[probe],
                            )
                            getattr(copy, act)()

                        first += size

    pools = [pool.reshape((-1, lay.pixels)) for pool in pools]
    pools = [("hbm", pools[0]), *(("vmem", pool) for pool in pools[1:])]
    return call(
        lay,
        body,
        state,
        [("smem", info), ("smem", everyone), *pools],
        [],
        flag=True,
        scratch=[pltpu.SemaphoreType.DMA((lay.probes,))],
        name="place_frames",
    )


def cut_patches(lay, info, own, other, state, begin, end, from_hbm=False):
    half = own.shape[2]
    tall, pixels = lay.tall, lay.pixels

    def one(probe, info, own, other, state, window, sem):
        row0, down, block, shift = lay.window(info, probe)
        own_top = lax.axis_index("lat") == 0
        near_at = pl.ds(pl.multiple_of(block * pixels, pixels), pixels)
        far_at = pl.ds(pl.multiple_of((block + 1) * pixels, pixels), pixels)
        for source, is_top in ((own, own_top), (other, jnp.logical_not(own_top))):
            start = jnp.clip(row0 - jnp.where(is_top, 0, half), 0, half - tall)
            to = pl.ds(pl.multiple_of(jnp.where(is_top, 0, tall), 8), tall)
            rows = pl.ds(pl.multiple_of(start, 8), tall)

            @pl.when(jnp.where(is_top, row0 < half, row0 + tall > half))
            def _(source=source, rows=rows, to=to):
                if source is own and from_hbm:
                    both = pl.ds(pl.multiple_of(block * pixels, pixels), 2 * pixels)
                    copy = pltpu.make_async_copy(source.at[:, :, rows, both], window.at[:, :, to, :], sem)
                    copy.start()
                    copy.wait()
                    return
                for part in range(2):
                    for layer in range(lay.layers):
                        window[part, layer, to, 0:pixels] = source[part, layer, rows, near_at]
                        window[part, layer, to, pixels : 2 * pixels] = source[part, layer, rows, far_at]

        offset = jnp.where(row0 < half, jnp.maximum(row0 - (half - tall), 0), tall)
        rows = pl.ds(pl.multiple_of(offset, 8), tall)
        turn = (pixels - shift) % pixels
        lane = lax.broadcasted_iota(jnp.int32, (tall, pixels), 1)
        for part in range(2):
            for layer in range(lay.layers):
                near = pltpu.roll(window[part, layer, rows, 0:pixels], turn, 1)
                far = pltpu.roll(window[part, layer, rows, pixels : 2 * pixels], turn, 1)
                patch = jnp.where(lane < pixels - shift, near, far)
                patch = pltpu.roll(patch, (tall - down) % tall, 0)[:pixels]
                state[lay.patch(0, probe, layer, part), :] = patch

    def body(info, *refs):
        section = lax.axis_index("depth")
        bounds = [x(section) if callable(x) else x for x in (begin, end)]
        lax.fori_loop(*bounds, lambda probe, _: one(probe, info, *refs) or 0, 0)

    return call(
        lay,
        body,
        state,
        [("vmem", info), ("hbm" if from_hbm else "vmem", own), ("vmem", other)],
        [],
        scratch=[pltpu.VMEM((2, lay.layers, 2 * tall, 2 * pixels), F32), pltpu.SemaphoreType.DMA(())],
        name="cut_patches",
    )[0]


def section_cost(lay):
    size = lay.count * lay.pixels**2
    return dict(flops=lay.layers * 2 * 3 * 8 * size * lay.pixels, moved=(lay.layers * 2 + 4) * 8 * size)


def pair(ref, at):
    return ref[at(0), :], ref[at(1), :]


def run_forward(lay, tick, sections, tables, state, arrived, start_wave):
    def body(tables, *refs):
        arrived_ref = refs[0] if arrived is not None else None
        start_ref = refs[-3] if start_wave is not None else None
        state, leave = refs[-2:]
        section = lax.axis_index("depth")
        group = tick - section
        final = (section == sections - 1).astype(jnp.int32)

        @pl.when((group >= 0) & (group < lay.groups))
        def _():
            wave = []
            for i in range(lay.count):
                if arrived is None:
                    wave.append((start_ref[0], start_ref[1]))
                elif start_wave is None:
                    wave.append((arrived_ref[i, 0], arrived_ref[i, 1]))
                else:
                    wave.append(
                        tuple(jnp.where(section == 0, start_ref[p], arrived_ref[i, p]) for p in range(2))
                    )
            for layer in range(lay.layers):
                chi = []
                for i in range(lay.count):
                    for part in range(2):
                        state[lay.seen(group, i, layer, part), :] = wave[i][part]
                    chi.append(times(pair(state, functools.partial(lay.patch, group, i, layer)), wave[i]))
                at = final if layer == lay.layers - 1 else 0
                wave = transform((tables[at, 0, 0], tables[at, 0, 1]), (tables[at, 1, 0], tables[at, 1, 1]), chi)
            for i in range(lay.count):
                real, imag = wave[i]
                misfit = real * real + imag * imag - state[lay.frame(group, i), :]
                factor = jnp.where(final == 1, misfit, 1.0)
                leave[i, 0] = real * factor
                leave[i, 1] = imag * factor

    waves = [("vmem", x) for x in (arrived, start_wave) if x is not None]
    return call(
        lay,
        body,
        state,
        [("vmem", tables), *waves],
        [(lay.count, 2, lay.pixels, lay.pixels)],
        name="forward_section",
        **section_cost(lay),
    )


def run_backward(lay, tick, sections, tables, state, arrived, own, copied=False):
    def body(tables, *refs):
        arrived_ref = refs[0] if arrived is not None else None
        own_ref = refs[1 if arrived is not None else 0] if own is not None else None
        state, leave = refs[-3:-1] if copied else refs[-2:]
        section = lax.axis_index("depth")
        group = tick - (2 * (sections - 1) - section)
        final = (section == sections - 1).astype(jnp.int32)

        @pl.when((group >= 0) & (group < lay.groups))
        def _():
            wave = []
            for i in range(lay.count):
                if arrived is None:
                    wave.append((own_ref[i, 0], own_ref[i, 1]))
                elif own is None:
                    wave.append((arrived_ref[i, 0], arrived_ref[i, 1]))
                else:
                    wave.append(
                        tuple(jnp.where(final == 1, own_ref[i, p], arrived_ref[i, p]) for p in range(2))
                    )
            for layer in reversed(range(lay.layers)):
                at = final if layer == lay.layers - 1 else 0
                chi = transform((tables[at, 1, 0], tables[at, 1, 1]), (tables[at, 0, 0], tables[at, 0, 1]), wave)
                wave = []
                for i in range(lay.count):
                    real, imag = times_conj(chi[i], pair(state, functools.partial(lay.seen, group, i, layer)))
                    state[lay.grad(group, i, layer, 0), :] = real
                    state[lay.grad(group, i, layer, 1), :] = imag
                    if copied:
                        refs[-1][lay.patch(0, i, layer, 0), :] = real
                        refs[-1][lay.patch(0, i, layer, 1), :] = imag
                    wave.append(times_conj(chi[i], pair(state, functools.partial(lay.patch, group, i, layer))))
            for i in range(lay.count):
                leave[i, 0] = wave[i][0]
                leave[i, 1] = wave[i][1]

    waves = [("vmem", x) for x in (arrived, own) if x is not None]
    return call(
        lay,
        body,
        state,
        [("vmem", tables), *waves],
        [(lay.count, 2, lay.pixels, lay.pixels)] + [(lay.stack // lay.groups, lay.pixels)] * copied,
        name="backward_section",
        **section_cost(lay),
    )


def deposit(lay, tick, sections, info, received, state):
    pixels, tall = lay.pixels, lay.tall

    def body(info, *refs):
        state = refs[-1]
        lane = lax.broadcasted_iota(jnp.int32, (tall, pixels), 1)
        blank = jnp.zeros((8, pixels), F32)
        base = lax.axis_index("probe") * lay.rows if lay.rows < lay.height else 0

        def add(probe, whose, active, load):
            row0, down, block, shift = lay.window(info, probe, whose)
            start = row0 - base + tall

            @pl.when(active & (start > 0) & (start < lay.rows + tall))
            def _():
                for layer in range(lay.layers):
                    for part in range(2):
                        padded = jnp.concatenate([load(layer, part), blank], axis=0)
                        turned = pltpu.roll(pltpu.roll(padded, down, 0), shift % pixels, 1)
                        near = pl.ds(pl.multiple_of(lay.total(part, layer, block, start), 8), tall)
                        far = pl.ds(pl.multiple_of(lay.total(part, layer, block + 1, start), 8), tall)
                        state[near, :] += jnp.where(lane >= shift, turned, 0.0)
                        state[far, :] += jnp.where(lane >= shift, 0.0, turned)

        if tick is not None:
            group = tick - (2 * (sections - 1) - lax.axis_index("depth"))
            active = (group >= 0) & (group < lay.groups)
            group = jnp.clip(group, 0, lay.groups - 1)
            for i in range(lay.count):
                add(
                    group * lay.count + i,
                    0,
                    active,
                    lambda layer, part, i=i: state[lay.grad(group, i, layer, part), :],
                )
        for ref, (first, whose, grads) in zip(refs, received):

            def one(i, _, ref=ref, first=first, whose=whose):
                add(
                    first * lay.count + i,
                    whose,
                    (lax.axis_index("depth") == 0) | (whose != 2),
                    lambda layer, part: ref[lay.patch(0, i, layer, part), :],
                )
                return 0

            lax.fori_loop(0, grads.shape[0] // (lay.layers * 2 * pixels), one, 0)

    return call(
        lay,
        body,
        state,
        [("vmem", info)] + [("vmem", grads) for *_, grads in received],
        [],
        name="deposit_patches",
    )[0]


def take_rows(lay, state, owners, others):
    rows = lay.rows // (2 * owners)

    def body(state, out):
        core = lax.axis_index("lat")
        core = 1 - core if others else core
        for part in range(2):
            for layer in range(lay.layers):
                for owner in range(owners):
                    for block in range(lay.blocks):
                        start = lay.total(part, layer, block, lay.tall + (2 * owner + core) * rows)
                        out[part, layer, owner, block] = state[pl.ds(pl.multiple_of(start, 8), rows), :]

    return pl.pallas_call(
        body,
        in_specs=[VMEM],
        out_specs=VMEM,
        out_shape=pltpu.VMEM((2, lay.layers, owners, lay.blocks, rows, lay.pixels), F32),
        compiler_params=pltpu.CompilerParams(vmem_limit_bytes=SCOPED),
        cost_estimate=pl.CostEstimate(flops=1000, bytes_accessed=1000, transcendentals=0),
        name="take_rows",
    )(in_vmem(state))


def put_aside(state, begin, end):
    def body(state, out, sem):
        copy = pltpu.make_async_copy(state.at[pl.ds(begin, end - begin), :], out, sem)
        copy.start()
        copy.wait()

    return pl.pallas_call(
        body,
        in_specs=[VMEM],
        out_specs=HBM,
        out_shape=pltpu.HBM((end - begin, state.shape[1]), F32),
        scratch_shapes=[pltpu.SemaphoreType.DMA(())],
        compiler_params=pltpu.CompilerParams(vmem_limit_bytes=SCOPED),
        cost_estimate=pl.CostEstimate(flops=1000, bytes_accessed=1000, transcendentals=0),
        name="put_aside",
    )(in_vmem(state))


def add_up(kept, received):
    _, layers, _, blocks, rows, pixels = kept.shape
    each = pl.BlockSpec((1, 1, 1, blocks, rows, pixels), lambda i, j: (i, j, 0, 0, 0, 0))

    def body(kept, received, out):
        for block in range(blocks):
            out[0, 0, :, pl.ds(block * pixels, pixels)] = kept[0, 0, 0, block] + received[0, 0, 0, block]

    return pl.pallas_call(
        body,
        grid=(2, layers),
        in_specs=[each, each],
        out_specs=pl.BlockSpec((1, 1, rows, blocks * pixels), lambda i, j: (i, j, 0, 0)),
        out_shape=pltpu.HBM((2, layers, rows, blocks * pixels), F32),
        compiler_params=pltpu.CompilerParams(vmem_limit_bytes=SCOPED),
        name="add_up",
    )(kept, received)


def swap(shard, axis):
    return lax.ppermute(shard, axis, [(0, 1), (1, 0)])


def sort_probes(lay, early, positions, indices):
    n = lay.probes
    total = 4 * n

    def body(listed, *refs):
        *scans, info, positions, sem = refs
        copy = pltpu.make_async_copy(listed, positions, sem)
        copy.start()
        copy.wait()
        lat, side = lax.axis_index("lat"), lax.axis_index("probe")
        lane = lax.broadcasted_iota(jnp.int32, (1, 128), 1)
        at = lax.broadcasted_iota(jnp.int32, (total, 128), 0)
        across = jnp.full((1, 128), jnp.iinfo(jnp.int32).max, jnp.int32)
        down = jnp.zeros((total, 128), jnp.int32)
        for which, scan in enumerate(scans):
            owner = (side ^ (which % 2)) * 2 + (lat ^ (which // 2))
            for i in range(n):
                place = scan[i]
                key = lay.pack(positions[0, place], positions[1, place], owner * n + i)
                across = jnp.where(lane == which * n + i, key, across)
                down = jnp.where(at == which * n + i, key, down)
        rank = jnp.sum((across < down).astype(jnp.int32), axis=1, keepdims=True)
        whose = lane // n
        order = 2 * (lane % n) + jnp.where(whose == 2, 1 - lat, lat)
        wanted = jnp.where(jnp.where(whose == 1, 1 - side, side) == 0, 2 * n - 1 - order, 2 * n + order)
        reach = 2 * early * lay.count
        wanted = jnp.where(lane == 3 * n, 2 * n - 1 - reach, wanted)
        wanted = jnp.where(lane == 3 * n + 1, 2 * n + reach, wanted)
        wanted = jnp.where(lane > 3 * n + 1, -1, wanted)
        info[...] = jnp.sum(jnp.where(rank == wanted, down, 0), axis=0, keepdims=True)

    return pl.pallas_call(
        body,
        in_specs=[HBM] + [SMEM] * 4,
        out_specs=VMEM,
        out_shape=pltpu.VMEM((1, 128), jnp.int32),
        scratch_shapes=[pltpu.SMEM(positions.T.shape, jnp.int32), pltpu.SemaphoreType.DMA(())],
        compiler_params=pltpu.CompilerParams(vmem_limit_bytes=SCOPED),
        name="sort_probes",
    )(in_hbm(positions.T), *indices)


def bring(x):
    def body(x, out, sem):
        copy = pltpu.make_async_copy(x, out, sem)
        copy.start()
        copy.wait()

    return pl.pallas_call(
        body,
        in_specs=[HBM],
        out_specs=VMEM,
        out_shape=pltpu.VMEM(x.shape, x.dtype),
        scratch_shapes=[pltpu.SemaphoreType.DMA(())],
        compiler_params=pltpu.CompilerParams(vmem_limit_bytes=SCOPED),
        cost_estimate=pl.CostEstimate(flops=1000, bytes_accessed=1000, transcendentals=0),
        name="bring",
    )(in_hbm(x))


def local(specimen, illumination, positions, scan_index, frames):
    pixels = illumination.shape[-1]
    _, layers, half, width = specimen.shape
    height = 2 * half
    tables = jnp.asarray(make_tables(pixels))
    sections = lax.axis_size("depth")
    owners = lax.axis_size("probe")
    paired = owners == 2 and lax.axis_size("groups") <= 2
    probes = scan_index.size
    count = 2 if probes % 4 == 0 else 1
    lay = Layout(probes, count, layers, pixels, half if paired else height, height, width)
    early = lay.groups // 2

    everyone = mine = None
    if paired:
        scan = scan_index.reshape(-1)
        beside = swap(scan, "lat")
        half_rows, beside = lax.optimization_barrier((specimen, beside))
        other = swap(half_rows, "lat")
        indices = [scan, swap(scan, "probe"), beside, swap(beside, "probe")]
        measured, *indices[1:] = lax.optimization_barrier((frames, *indices[1:]))
        end = sections - 1
        ends = [(2 * end, 2 * end + 1), (2 * end + 1, 2 * end)]
        mine = lax.ppermute(measured, ("depth", "probe"), ends)
        info = sort_probes(lay, early, positions, indices)
        everyone = swap(info, "groups") if lax.axis_size("groups") == 2 else info
    else:
        other = swap(specimen, "lat")
        corners = positions[scan_index.reshape(-1)]
        info = lay.pack(corners[:, 0], corners[:, 1], jnp.arange(probes, dtype=jnp.int32))
        info = everyone = jnp.pad(info, (0, 3 * probes))[None]
    state = cut_patches(lay, info, specimen, other, None, 0, count, from_hbm=True)
    def busy(tick, source, by):
        delay = source if by > 0 else 2 * (sections - 1) - source
        return 0 <= tick - delay < lay.groups

    def pass_on(wave, tick, by):
        pairs = [
            (source, source + by)
            for source in range(sections)
            if 0 <= source + by < sections and busy(tick, source, by)
        ]
        return lax.ppermute(wave, "depth", pairs) if pairs else None

    def grads_of(state, begin, end):
        begin, end = lay.grads_of(begin, end)
        return lax.slice_in_dim(state, begin, end)

    fill = sections - 1
    parts = [(0, early // 2), (early // 2, early)] if paired else []
    crossing = {}
    down = up = None
    def upto(group):
        early_sections = min(group, lay.groups) * count
        return lambda section: jnp.where(section < 2, early_sections, probes)

    cuts = {0: (count, upto(3)), 2: (upto(3), upto(5)), 3: (upto(5), probes)}
    last_tick = lay.groups + 2 * fill - 1
    sent = None
    for tick in range(lay.groups + 2 * fill):
        own = None
        if paired and tick == fill - 1:
            down, mine, everyone = lax.optimization_barrier((down, mine, everyone))
            crossed = [lax.ppermute(x, ("depth", "lat"), ends) for x in (frames, mine)]
        if tick < lay.groups + fill:
            start_wave = illumination if tick < lay.groups else None
            state, own = run_forward(lay, tick, sections, tables, state, down, start_wave)
            if tick == 0:
                own, specimen = lax.optimization_barrier((own, specimen))
                brought = bring(specimen)
            down = pass_on(own, tick, 1)
            if tick in cuts:
                state = cut_patches(lay, info, brought, other, state, *cuts[tick])
            if tick == 0:
                state = clear_total(lay, state)
            if tick == fill - 1:
                pools = [frames, mine, *crossed] if paired else [frames]
                state, late = place_frames(lay, sections, info, everyone, pools, state)
        if tick >= fill:
            copied = paired and tick == last_tick
            state, rising, *rest = run_backward(lay, tick, sections, tables, state, up, own, copied)
            up = pass_on(rising, tick, -1)
            received = crossing.pop(tick, [])
            for begin, end in parts:
                if tick == end - 1 + 2 * fill:
                    due = min(tick + CROSSING, last_tick - 1)
                    crossing.setdefault(due, []).append((begin, 1, swap(grads_of(state, begin, end), "probe")))
            state = deposit(lay, tick, sections, info, received, state)
            if paired and tick == last_tick - 1:
                aside = put_aside(state, *lay.grads_of(early, lay.groups))
                going = take_rows(lay, state, 1, True)
                going, aside, up = lax.optimization_barrier((going, aside, up))
                sent = swap(going, "lat")
    if paired:
        last = swap(rest[0], "lat")
        state = deposit(lay, None, sections, info, [(lay.groups - 1, 2, last)], state)
    if not paired:
        whole = take_rows(lay, state, owners, False) + swap(take_rows(lay, state, owners, True), "lat")
        whole = jnp.moveaxis(whole, 3, 4).reshape((2, layers, owners, -1, width))
        return lax.psum_scatter(whole, "probe", scatter_dimension=2, tiled=False)

    def as_they_are(kept, received, grads, last):
        return add_up(kept, received)

    def with_partners(kept, received, grads, last):
        each = grads.shape[0] // (lay.groups - early)
        last = jnp.where(section == 0, last, grads[-each:])
        grads = swap(jnp.concatenate([grads[:-each], last]), "probe")
        sums = Layout(probes, count, layers, pixels, half, height, width, only_sums=True)
        state = clear_total(sums, None)
        state = deposit(sums, None, sections, info, [(early, 1, grads)], state)
        kept = kept + take_rows(sums, state, 1, False)
        return add_up(kept, received + swap(take_rows(sums, state, 1, True), "lat"))

    section = lax.axis_index("depth")
    kept = take_rows(lay, state, 1, False)
    return lax.cond(late[0, 0] > 0, with_partners, as_they_are, kept, sent, aside, rest[0])


def solution(mesh):
    return jax.shard_map(
        local,
        mesh=mesh,
        in_specs=(
            P(None, ("groups", "depth"), "lat", None),
            P(),
            P("groups", None),
            P("groups", ("probe", "lat")),
            P("groups", ("probe", "lat"), None, None),
        ),
        out_specs=P(None, ("groups", "depth"), ("probe", "lat"), None),
        check_vma=False,
    )
```

```python
import functools
import math

import jax
import jax.numpy as jnp
import ml_dtypes
import numpy as np
from jax import lax
from jax.experimental import pallas as pl
from jax.experimental.pallas import tpu as pltpu
from jax.sharding import PartitionSpec as P

FRESNEL = 8.0
SCOPED = 8 << 20
CROSSING = 3
F32 = jnp.float32
BF16 = jnp.bfloat16
HBM = pl.BlockSpec(memory_space=pl.ANY)
VMEM = pl.BlockSpec(memory_space=pltpu.VMEM)
SMEM = pl.BlockSpec(memory_space=pltpu.SMEM)


def in_hbm(x):
    return pltpu.with_memory_space_constraint(x, pltpu.HBM)


def in_vmem(x):
    return pltpu.with_memory_space_constraint(x, pltpu.VMEM)


def real_blocks(matrix):
    real, imag = matrix.real, matrix.imag
    left = np.block([[real, -imag], [imag, real]])
    right = np.block([[real, imag], [-imag, real]])
    return np.stack([left, right])


@functools.lru_cache(maxsize=None)
def make_tables(pixels):
    index = np.arange(pixels)
    freq = np.where(index < pixels // 2, index, index - pixels) / pixels
    spread = index[:, None] - index[None, :]
    phase = 2.0 * math.pi * freq * spread[:, :, None] - math.pi * FRESNEL * freq * freq
    propagator = np.mean(np.exp(1j * phase), axis=-1)
    turns = index[:, None] * index[None, :] % pixels
    fourier = np.exp(-2j * math.pi * turns / pixels) / math.sqrt(pixels)
    blocks = np.stack([real_blocks(propagator), real_blocks(fourier)]).astype(np.float32)
    high = blocks.astype(ml_dtypes.bfloat16)
    low = (blocks - high.astype(np.float32)).astype(ml_dtypes.bfloat16)
    return np.stack([high, low], axis=2)


def halves(x):
    high = x.astype(BF16)
    return high, (x - high.astype(F32)).astype(BF16)


def dot(a, b):
    return jnp.dot(a, b, preferred_element_type=F32)


def transform(left, right, fields):
    size = fields[0][0].shape[0]
    mids = []
    for high, low in [halves(jnp.concatenate(field, axis=0)) for field in fields]:
        both = dot(left[0], jnp.concatenate([high, low], axis=1))
        mids.append(both[:, :size] + (both[:, size:] + dot(left[1], high)))
    outs = []
    for high, low in [halves(jnp.concatenate([mid[:size], mid[size:]], axis=1)) for mid in mids]:
        both = dot(jnp.concatenate([high, low], axis=0), right[0])
        outs.append(both[:size] + (both[size:] + dot(high, right[1])))
    return [(out[:, :size], out[:, size:]) for out in outs]


def times(a, b):
    return a[0] * b[0] - a[1] * b[1], a[0] * b[1] + a[1] * b[0]


def times_conj(a, b):
    return a[0] * b[0] + a[1] * b[1], a[1] * b[0] - a[0] * b[1]


class Layout:
    def __init__(self, probes, count, layers, pixels, rows, height, width, only_sums=False):
        self.probes, self.count, self.layers, self.pixels = probes, count, layers, pixels
        self.groups = probes // count
        self.tall = pixels + 8
        self.rows, self.height, self.width = rows, height, width
        self.blocks = width // pixels
        self.deep = rows + 2 * self.tall
        self.column_bits = (width - 1).bit_length()
        self.name_bits = (4 * probes - 1).bit_length()
        self.stack = probes * layers * 2 * pixels
        self.seen_from = self.stack
        self.grads_from = 2 * self.stack
        self.frames_from = 3 * self.stack
        self.total_from = 0 if only_sums else self.frames_from + probes * pixels
        self.shape = (self.total_from + 2 * layers * self.blocks * self.deep, pixels)

    def stacked(self, group, i, layer, part):
        probe = group * self.count + i
        return ((probe * self.layers + layer) * 2 + part) * self.pixels

    def tile(self, start):
        return pl.ds(pl.multiple_of(start, 8), self.pixels)

    def patch(self, group, i, layer, part):
        return self.tile(self.stacked(group, i, layer, part))

    def seen(self, group, i, layer, part):
        return self.tile(self.seen_from + self.stacked(group, i, layer, part))

    def grad(self, group, i, layer, part):
        return self.tile(self.grads_from + self.stacked(group, i, layer, part))

    def grads_of(self, begin, end):
        each = self.stack // self.groups
        return self.grads_from + begin * each, self.grads_from + end * each

    def frame(self, group, i):
        return self.tile(self.frames_from + (group * self.count + i) * self.pixels)

    def total(self, part, layer, block, row):
        block = (part * self.layers + layer) * self.blocks + block
        return self.total_from + block * self.deep + row

    def pack(self, row, column, name):
        return (((row << self.column_bits) + column) << self.name_bits) + name

    def row(self, key):
        return key >> (self.column_bits + self.name_bits)

    def window(self, info, probe, whose=0):
        lane = lax.broadcasted_iota(jnp.int32, info.shape, 1)
        key = jnp.sum(jnp.where(lane == probe + whose * self.probes, info[...], 0))
        row = self.row(key)
        column = (key >> self.name_bits) & ((1 << self.column_bits) - 1)
        row0 = jnp.minimum(row // 8 * 8, self.height - self.tall)
        block = jnp.minimum(column // self.pixels, self.blocks - 2)
        return row0, row - row0, block, column - block * self.pixels


def call(lay, body, state, before, outs, scratch=(), flag=False, flops=1000, moved=1000, name=None):
    spaces = {"hbm": (HBM, in_hbm), "vmem": (VMEM, in_vmem), "smem": (SMEM, lambda x: x)}
    specs = [spaces[kind][0] for kind, _ in before]
    operands = [spaces[kind][1](x) for kind, x in before]
    at = len(before)
    aliases = {}
    if state is not None:
        specs.append(VMEM)
        operands.append(in_vmem(state))
        aliases = {at: 0}

    def kernel(*refs):
        body(*refs[:at], *refs[at + len(aliases) :])

    return pl.pallas_call(
        kernel,
        in_specs=specs,
        out_specs=[VMEM] * (1 + len(outs) + flag),
        out_shape=[pltpu.VMEM(shape, F32) for shape in (lay.shape, *outs)]
        + [pltpu.VMEM((1, 128), jnp.int32)] * flag,
        scratch_shapes=list(scratch),
        input_output_aliases=aliases,
        compiler_params=pltpu.CompilerParams(vmem_limit_bytes=SCOPED),
        cost_estimate=pl.CostEstimate(flops=flops, bytes_accessed=moved, transcendentals=0),
        name=name,
    )(*operands)


def clear_total(lay, state):
    start = lay.total_from

    def body(state):
        state[pl.ds(start, lay.shape[0] - start), :] = jnp.zeros((lay.shape[0] - start, lay.pixels), F32)

    return call(lay, body, state, [], [], name="clear_total")[0]


def place_frames(lay, sections, info, everyone, pools, state):
    def body(info, everyone, *refs):
        *pools, state, late, sems = refs
        nearest = 3 * lay.probes
        reach = jnp.bool_(False)
        for ref in (info, everyone):
            reach |= lay.row(ref[0, nearest]) + lay.pixels > lay.rows
            reach |= lay.row(ref[0, nearest + 1]) < lay.rows
        late[...] = jnp.full(late.shape, reach.astype(jnp.int32), jnp.int32)
        lat, side = lax.axis_index("lat"), lax.axis_index("probe")

        @pl.when(lax.axis_index("depth") == sections - 1)
        def _():
            for act in ("start", "wait"):
                for probe in range(lay.probes):
                    name = info[0, probe] & ((1 << lay.name_bits) - 1)
                    owner = name // lay.probes
                    slot = name % lay.probes
                    if len(pools) > 1:
                        slot += ((owner // 2) ^ side) * lay.probes + ((owner % 2) ^ lat) * 2 * lay.probes
                    first = 0
                    for pool in pools:
                        size = pool.shape[0] // lay.pixels

                        @pl.when((slot >= first) & (slot < first + size))
                        def _(pool=pool, first=first, probe=probe, slot=slot):
                            copy = pltpu.make_async_copy(
                                pool.at[lay.tile((slot - first) * lay.pixels), :],
                                state.at[lay.frame(0, probe), :],
                                sems.at[probe],
                            )
                            getattr(copy, act)()

                        first += size

    pools = [pool.reshape((-1, lay.pixels)) for pool in pools]
    pools = [("hbm", pools[0]), *(("vmem", pool) for pool in pools[1:])]
    return call(
        lay,
        body,
        state,
        [("smem", info), ("smem", everyone), *pools],
        [],
        flag=True,
        scratch=[pltpu.SemaphoreType.DMA((lay.probes,))],
        name="place_frames",
    )


def cut_patches(lay, info, own, other, state, begin, end, from_hbm=False):
    half = own.shape[2]
    tall, pixels = lay.tall, lay.pixels

    def one(probe, info, own, other, state, window, sem):
        row0, down, block, shift = lay.window(info, probe)
        own_top = lax.axis_index("lat") == 0
        near_at = pl.ds(pl.multiple_of(block * pixels, pixels), pixels)
        far_at = pl.ds(pl.multiple_of((block + 1) * pixels, pixels), pixels)
        for source, is_top in ((own, own_top), (other, jnp.logical_not(own_top))):
            start = jnp.clip(row0 - jnp.where(is_top, 0, half), 0, half - tall)
            to = pl.ds(pl.multiple_of(jnp.where(is_top, 0, tall), 8), tall)
            rows = pl.ds(pl.multiple_of(start, 8), tall)

            @pl.when(jnp.where(is_top, row0 < half, row0 + tall > half))
            def _(source=source, rows=rows, to=to):
                if source is own and from_hbm:
                    both = pl.ds(pl.multiple_of(block * pixels, pixels), 2 * pixels)
                    copy = pltpu.make_async_copy(source.at[:, :, rows, both], window.at[:, :, to, :], sem)
                    copy.start()
                    copy.wait()
                    return
                for part in range(2):
                    for layer in range(lay.layers):
                        window[part, layer, to, 0:pixels] = source[part, layer, rows, near_at]
                        window[part, layer, to, pixels : 2 * pixels] = source[part, layer, rows, far_at]

        offset = jnp.where(row0 < half, jnp.maximum(row0 - (half - tall), 0), tall)
        rows = pl.ds(pl.multiple_of(offset, 8), tall)
        turn = (pixels - shift) % pixels
        lane = lax.broadcasted_iota(jnp.int32, (tall, pixels), 1)
        for part in range(2):
            for layer in range(lay.layers):
                near = pltpu.roll(window[part, layer, rows, 0:pixels], turn, 1)
                far = pltpu.roll(window[part, layer, rows, pixels : 2 * pixels], turn, 1)
                patch = jnp.where(lane < pixels - shift, near, far)
                patch = pltpu.roll(patch, (tall - down) % tall, 0)[:pixels]
                state[lay.patch(0, probe, layer, part), :] = patch

    def body(info, *refs):
        section = lax.axis_index("depth")
        bounds = [x(section) if callable(x) else x for x in (begin, end)]
        lax.fori_loop(*bounds, lambda probe, _: one(probe, info, *refs) or 0, 0)

    return call(
        lay,
        body,
        state,
        [("vmem", info), ("hbm" if from_hbm else "vmem", own), ("vmem", other)],
        [],
        scratch=[pltpu.VMEM((2, lay.layers, 2 * tall, 2 * pixels), F32), pltpu.SemaphoreType.DMA(())],
        name="cut_patches",
    )[0]


def section_cost(lay):
    size = lay.count * lay.pixels**2
    return dict(flops=lay.layers * 2 * 3 * 8 * size * lay.pixels, moved=(lay.layers * 2 + 4) * 8 * size)


def pair(ref, at):
    return ref[at(0), :], ref[at(1), :]


def run_forward(lay, tick, sections, tables, state, arrived, start_wave):
    def body(tables, *refs):
        arrived_ref = refs[0] if arrived is not None else None
        start_ref = refs[-3] if start_wave is not None else None
        state, leave = refs[-2:]
        section = lax.axis_index("depth")
        group = tick - section
        final = (section == sections - 1).astype(jnp.int32)

        @pl.when((group >= 0) & (group < lay.groups))
        def _():
            wave = []
            for i in range(lay.count):
                if arrived is None:
                    wave.append((start_ref[0], start_ref[1]))
                elif start_wave is None:
                    wave.append((arrived_ref[i, 0], arrived_ref[i, 1]))
                else:
                    wave.append(
                        tuple(jnp.where(section == 0, start_ref[p], arrived_ref[i, p]) for p in range(2))
                    )
            for layer in range(lay.layers):
                chi = []
                for i in range(lay.count):
                    for part in range(2):
                        state[lay.seen(group, i, layer, part), :] = wave[i][part]
                    chi.append(times(pair(state, functools.partial(lay.patch, group, i, layer)), wave[i]))
                at = final if layer == lay.layers - 1 else 0
                wave = transform((tables[at, 0, 0], tables[at, 0, 1]), (tables[at, 1, 0], tables[at, 1, 1]), chi)
            for i in range(lay.count):
                real, imag = wave[i]
                misfit = real * real + imag * imag - state[lay.frame(group, i), :]
                factor = jnp.where(final == 1, misfit, 1.0)
                leave[i, 0] = real * factor
                leave[i, 1] = imag * factor

    waves = [("vmem", x) for x in (arrived, start_wave) if x is not None]
    return call(
        lay,
        body,
        state,
        [("vmem", tables), *waves],
        [(lay.count, 2, lay.pixels, lay.pixels)],
        name="forward_section",
        **section_cost(lay),
    )


def run_backward(lay, tick, sections, tables, state, arrived, own):
    def body(tables, *refs):
        arrived_ref = refs[0] if arrived is not None else None
        own_ref = refs[1 if arrived is not None else 0] if own is not None else None
        state, leave = refs[-2:]
        section = lax.axis_index("depth")
        group = tick - (2 * (sections - 1) - section)
        final = (section == sections - 1).astype(jnp.int32)

        @pl.when((group >= 0) & (group < lay.groups))
        def _():
            wave = []
            for i in range(lay.count):
                if arrived is None:
                    wave.append((own_ref[i, 0], own_ref[i, 1]))
                elif own is None:
                    wave.append((arrived_ref[i, 0], arrived_ref[i, 1]))
                else:
                    wave.append(
                        tuple(jnp.where(final == 1, own_ref[i, p], arrived_ref[i, p]) for p in range(2))
                    )
            for layer in reversed(range(lay.layers)):
                at = final if layer == lay.layers - 1 else 0
                chi = transform((tables[at, 1, 0], tables[at, 1, 1]), (tables[at, 0, 0], tables[at, 0, 1]), wave)
                wave = []
                for i in range(lay.count):
                    real, imag = times_conj(chi[i], pair(state, functools.partial(lay.seen, group, i, layer)))
                    state[lay.grad(group, i, layer, 0), :] = real
                    state[lay.grad(group, i, layer, 1), :] = imag
                    wave.append(times_conj(chi[i], pair(state, functools.partial(lay.patch, group, i, layer))))
            for i in range(lay.count):
                leave[i, 0] = wave[i][0]
                leave[i, 1] = wave[i][1]

    waves = [("vmem", x) for x in (arrived, own) if x is not None]
    return call(
        lay,
        body,
        state,
        [("vmem", tables), *waves],
        [(lay.count, 2, lay.pixels, lay.pixels)],
        name="backward_section",
        **section_cost(lay),
    )


def deposit(lay, tick, sections, info, received, state):
    pixels, tall = lay.pixels, lay.tall

    def body(info, *refs):
        state = refs[-1]
        lane = lax.broadcasted_iota(jnp.int32, (tall, pixels), 1)
        blank = jnp.zeros((8, pixels), F32)
        base = lax.axis_index("probe") * lay.rows if lay.rows < lay.height else 0

        def add(probe, whose, active, load):
            row0, down, block, shift = lay.window(info, probe, whose)
            start = row0 - base + tall

            @pl.when(active & (start > 0) & (start < lay.rows + tall))
            def _():
                for layer in range(lay.layers):
                    for part in range(2):
                        padded = jnp.concatenate([load(layer, part), blank], axis=0)
                        turned = pltpu.roll(pltpu.roll(padded, down, 0), shift % pixels, 1)
                        near = pl.ds(pl.multiple_of(lay.total(part, layer, block, start), 8), tall)
                        far = pl.ds(pl.multiple_of(lay.total(part, layer, block + 1, start), 8), tall)
                        state[near, :] += jnp.where(lane >= shift, turned, 0.0)
                        state[far, :] += jnp.where(lane >= shift, 0.0, turned)

        if tick is not None:
            group = tick - (2 * (sections - 1) - lax.axis_index("depth"))
            active = (group >= 0) & (group < lay.groups)
            group = jnp.clip(group, 0, lay.groups - 1)
            for i in range(lay.count):
                add(
                    group * lay.count + i,
                    0,
                    active,
                    lambda layer, part, i=i: state[lay.grad(group, i, layer, part), :],
                )
        for ref, (first, whose, grads) in zip(refs, received):

            def one(i, _, ref=ref, first=first, whose=whose):
                add(
                    first * lay.count + i,
                    whose,
                    True,
                    lambda layer, part: ref[lay.patch(0, i, layer, part), :],
                )
                return 0

            lax.fori_loop(0, grads.shape[0] // (lay.layers * 2 * pixels), one, 0)

    return call(
        lay,
        body,
        state,
        [("vmem", info)] + [("vmem", grads) for *_, grads in received],
        [],
        name="deposit_patches",
    )[0]


def split_rows(lay, state, owners, taken=(0, 8)):
    rows = lay.rows // (2 * owners)
    pieces = 4 * owners * lay.layers * lay.blocks

    def body(state, keep, send, rest, sems):
        lat = lax.axis_index("lat")
        copies = [pltpu.make_async_copy(state.at[pl.ds(taken[0], taken[1] - taken[0]), :], rest, sems.at[pieces])]
        for owner in range(owners):
            for kind, target in ((lat, keep), (1 - lat, send)):
                for part in range(2):
                    for layer in range(lay.layers):
                        for block in range(lay.blocks):
                            start = lay.total(part, layer, block, lay.tall + (2 * owner + kind) * rows)
                            copies.append(
                                pltpu.make_async_copy(
                                    state.at[pl.ds(pl.multiple_of(start, 8), rows), :],
                                    target.at[part, layer, owner, :, pl.ds(block * lay.pixels, lay.pixels)],
                                    sems.at[len(copies) - 1],
                                )
                            )
        for copy in copies:
            copy.start()
        for copy in copies:
            copy.wait()

    half = (2, lay.layers, owners, rows, lay.width)
    return pl.pallas_call(
        body,
        in_specs=[VMEM],
        out_specs=[VMEM, VMEM, HBM],
        out_shape=[
            pltpu.VMEM(half, F32),
            pltpu.VMEM(half, F32),
            pltpu.HBM((taken[1] - taken[0], lay.pixels), F32),
        ],
        scratch_shapes=[pltpu.SemaphoreType.DMA((pieces + 1,))],
        compiler_params=pltpu.CompilerParams(vmem_limit_bytes=SCOPED),
        name="split_rows",
    )(in_vmem(state))


def add_up(a, b):
    each = pl.BlockSpec((1, 1, *a.shape[2:]), lambda i, j: (i, j, 0, 0, 0))

    def body(a, b, out):
        out[...] = a[...] + b[...]

    return pl.pallas_call(
        body,
        grid=a.shape[:2],
        in_specs=[each, each],
        out_specs=each,
        out_shape=pltpu.HBM(a.shape, F32),
        compiler_params=pltpu.CompilerParams(vmem_limit_bytes=SCOPED),
        name="add_up",
    )(a, b)


def swap(shard, axis):
    return lax.ppermute(shard, axis, [(0, 1), (1, 0)])


def sort_probes(lay, early, positions, indices):
    n = lay.probes
    total = 4 * n

    def body(listed, *refs):
        *scans, info, positions, sem = refs
        copy = pltpu.make_async_copy(listed, positions, sem)
        copy.start()
        copy.wait()
        lat, side = lax.axis_index("lat"), lax.axis_index("probe")
        lane = lax.broadcasted_iota(jnp.int32, (1, 128), 1)
        at = lax.broadcasted_iota(jnp.int32, (total, 128), 0)
        across = jnp.full((1, 128), jnp.iinfo(jnp.int32).max, jnp.int32)
        down = jnp.zeros((total, 128), jnp.int32)
        for which, scan in enumerate(scans):
            owner = (side ^ (which % 2)) * 2 + (lat ^ (which // 2))
            for i in range(n):
                place = scan[i]
                key = lay.pack(positions[0, place], positions[1, place], owner * n + i)
                across = jnp.where(lane == which * n + i, key, across)
                down = jnp.where(at == which * n + i, key, down)
        rank = jnp.sum((across < down).astype(jnp.int32), axis=1, keepdims=True)
        whose = lane // n
        order = 2 * (lane % n) + jnp.where(whose == 2, 1 - lat, lat)
        wanted = jnp.where(jnp.where(whose == 1, 1 - side, side) == 0, 2 * n - 1 - order, 2 * n + order)
        reach = 2 * early * lay.count
        wanted = jnp.where(lane == 3 * n, 2 * n - 1 - reach, wanted)
        wanted = jnp.where(lane == 3 * n + 1, 2 * n + reach, wanted)
        wanted = jnp.where(lane > 3 * n + 1, -1, wanted)
        info[...] = jnp.sum(jnp.where(rank == wanted, down, 0), axis=0, keepdims=True)

    return pl.pallas_call(
        body,
        in_specs=[HBM] + [SMEM] * 4,
        out_specs=VMEM,
        out_shape=pltpu.VMEM((1, 128), jnp.int32),
        scratch_shapes=[pltpu.SMEM(positions.T.shape, jnp.int32), pltpu.SemaphoreType.DMA(())],
        compiler_params=pltpu.CompilerParams(vmem_limit_bytes=SCOPED),
        name="sort_probes",
    )(in_hbm(positions.T), *indices)


def bring(x):
    def body(x, out, sem):
        copy = pltpu.make_async_copy(x, out, sem)
        copy.start()
        copy.wait()

    return pl.pallas_call(
        body,
        in_specs=[HBM],
        out_specs=VMEM,
        out_shape=pltpu.VMEM(x.shape, x.dtype),
        scratch_shapes=[pltpu.SemaphoreType.DMA(())],
        compiler_params=pltpu.CompilerParams(vmem_limit_bytes=SCOPED),
        cost_estimate=pl.CostEstimate(flops=1000, bytes_accessed=1000, transcendentals=0),
        name="bring",
    )(in_hbm(x))


def local(specimen, illumination, positions, scan_index, frames):
    pixels = illumination.shape[-1]
    _, layers, half, width = specimen.shape
    height = 2 * half
    tables = jnp.asarray(make_tables(pixels))
    sections = lax.axis_size("depth")
    owners = lax.axis_size("probe")
    paired = owners == 2 and lax.axis_size("groups") <= 2
    probes = scan_index.size
    count = 2 if probes % 4 == 0 else 1
    lay = Layout(probes, count, layers, pixels, half if paired else height, height, width)
    early = lay.groups // 2

    everyone = mine = None
    if paired:
        scan = scan_index.reshape(-1)
        beside = swap(scan, "lat")
        half_rows, beside = lax.optimization_barrier((specimen, beside))
        other = swap(half_rows, "lat")
        indices = [scan, swap(scan, "probe"), beside, swap(beside, "probe")]
        measured, *indices[1:] = lax.optimization_barrier((frames, *indices[1:]))
        end = sections - 1
        ends = [(2 * end, 2 * end + 1), (2 * end + 1, 2 * end)]
        mine = lax.ppermute(measured, ("depth", "probe"), ends)
        info = sort_probes(lay, early, positions, indices)
        everyone = swap(info, "groups") if lax.axis_size("groups") == 2 else info
    else:
        other = swap(specimen, "lat")
        corners = positions[scan_index.reshape(-1)]
        info = lay.pack(corners[:, 0], corners[:, 1], jnp.arange(probes, dtype=jnp.int32))
        info = everyone = jnp.pad(info, (0, 3 * probes))[None]
    state = cut_patches(lay, info, specimen, other, None, 0, count, from_hbm=True)
    def busy(tick, source, by):
        delay = source if by > 0 else 2 * (sections - 1) - source
        return 0 <= tick - delay < lay.groups

    def pass_on(wave, tick, by):
        pairs = [
            (source, source + by)
            for source in range(sections)
            if 0 <= source + by < sections and busy(tick, source, by)
        ]
        return lax.ppermute(wave, "depth", pairs) if pairs else None

    def grads_of(state, begin, end):
        begin, end = lay.grads_of(begin, end)
        return lax.slice_in_dim(state, begin, end)

    fill = sections - 1
    parts = [(0, early // 2), (early // 2, early)] if paired else []
    crossing = {}
    down = up = None
    def upto(group):
        early_sections = min(group, lay.groups) * count
        return lambda section: jnp.where(section < 2, early_sections, probes)

    cuts = {0: (count, upto(3)), 2: (upto(3), upto(5)), 3: (upto(5), probes)}
    last_tick = lay.groups + 2 * fill - 1
    for tick in range(lay.groups + 2 * fill):
        own = None
        if paired and tick == fill - 1:
            down, mine, everyone = lax.optimization_barrier((down, mine, everyone))
            crossed = [lax.ppermute(x, ("depth", "lat"), ends) for x in (frames, mine)]
        if tick < lay.groups + fill:
            start_wave = illumination if tick < lay.groups else None
            state, own = run_forward(lay, tick, sections, tables, state, down, start_wave)
            if tick == 0:
                own, specimen = lax.optimization_barrier((own, specimen))
                brought = bring(specimen)
            down = pass_on(own, tick, 1)
            if tick in cuts:
                state = cut_patches(lay, info, brought, other, state, *cuts[tick])
            if tick == 0:
                state = clear_total(lay, state)
            if tick == fill - 1:
                pools = [frames, mine, *crossed] if paired else [frames]
                state, late = place_frames(lay, sections, info, everyone, pools, state)
        if tick >= fill:
            state, rising = run_backward(lay, tick, sections, tables, state, up, own)
            up = pass_on(rising, tick, -1)
            received = crossing.pop(tick, [])
            for begin, end in parts:
                if tick == end - 1 + 2 * fill:
                    due = min(tick + CROSSING, last_tick - 1)
                    crossing.setdefault(due, []).append((begin, 1, swap(grads_of(state, begin, end), "probe")))
            state = deposit(lay, tick, sections, info, received, state)
    if not paired:
        keep, send, _ = split_rows(lay, state, owners)
        return lax.psum_scatter(keep + swap(send, "lat"), "probe", scatter_dimension=2, tiled=False)

    keep, send, late_grads = split_rows(lay, state, 1, lay.grads_of(early, lay.groups))

    def as_they_are(keep, received, grads):
        return add_up(keep, received)

    def with_partners(keep, received, grads):
        sums = Layout(probes, count, layers, pixels, half, height, width, only_sums=True)
        state = clear_total(sums, None)
        state = deposit(sums, None, sections, info, [(early, 1, swap(grads, "probe"))], state)
        more, send, _ = split_rows(sums, state, 1)
        return add_up(keep + more, received + swap(send, "lat"))

    result = lax.cond(late[0, 0] > 0, with_partners, as_they_are, keep, swap(send, "lat"), late_grads)
    return result[:, :, 0]


def solution(mesh):
    return jax.shard_map(
        local,
        mesh=mesh,
        in_specs=(
            P(None, ("groups", "depth"), "lat", None),
            P(),
            P("groups", None),
            P("groups", ("probe", "lat")),
            P("groups", ("probe", "lat"), None, None),
        ),
        out_specs=P(None, ("groups", "depth"), ("probe", "lat"), None),
        check_vma=False,
    )
```

```python
import functools
import math

import jax
import jax.numpy as jnp
import ml_dtypes
import numpy as np
from jax import lax
from jax.experimental import pallas as pl
from jax.experimental.pallas import tpu as pltpu
from jax.sharding import PartitionSpec as P

FRESNEL = 8.0
SCOPED = 8 << 20
CROSSING = 3
F32 = jnp.float32
BF16 = jnp.bfloat16
HBM = pl.BlockSpec(memory_space=pl.ANY)
VMEM = pl.BlockSpec(memory_space=pltpu.VMEM)
SMEM = pl.BlockSpec(memory_space=pltpu.SMEM)


def in_hbm(x):
    return pltpu.with_memory_space_constraint(x, pltpu.HBM)


def in_vmem(x):
    return pltpu.with_memory_space_constraint(x, pltpu.VMEM)


def real_blocks(matrix):
    real, imag = matrix.real, matrix.imag
    left = np.block([[real, -imag], [imag, real]])
    right = np.block([[real, imag], [-imag, real]])
    return np.stack([left, right])


@functools.lru_cache(maxsize=None)
def make_tables(pixels):
    index = np.arange(pixels)
    freq = np.where(index < pixels // 2, index, index - pixels) / pixels
    spread = index[:, None] - index[None, :]
    phase = 2.0 * math.pi * freq * spread[:, :, None] - math.pi * FRESNEL * freq * freq
    propagator = np.mean(np.exp(1j * phase), axis=-1)
    turns = index[:, None] * index[None, :] % pixels
    fourier = np.exp(-2j * math.pi * turns / pixels) / math.sqrt(pixels)
    blocks = np.stack([real_blocks(propagator), real_blocks(fourier)]).astype(np.float32)
    high = blocks.astype(ml_dtypes.bfloat16)
    low = (blocks - high.astype(np.float32)).astype(ml_dtypes.bfloat16)
    return np.stack([high, low], axis=2)


def halves(x):
    high = x.astype(BF16)
    return high, (x - high.astype(F32)).astype(BF16)


def dot(a, b):
    return jnp.dot(a, b, preferred_element_type=F32)


def transform(left, right, fields):
    size = fields[0][0].shape[0]
    mids = []
    for high, low in [halves(jnp.concatenate(field, axis=0)) for field in fields]:
        both = dot(left[0], jnp.concatenate([high, low], axis=1))
        mids.append(both[:, :size] + (both[:, size:] + dot(left[1], high)))
    outs = []
    for high, low in [halves(jnp.concatenate([mid[:size], mid[size:]], axis=1)) for mid in mids]:
        both = dot(jnp.concatenate([high, low], axis=0), right[0])
        outs.append(both[:size] + (both[size:] + dot(high, right[1])))
    return [(out[:, :size], out[:, size:]) for out in outs]


def times(a, b):
    return a[0] * b[0] - a[1] * b[1], a[0] * b[1] + a[1] * b[0]


def times_conj(a, b):
    return a[0] * b[0] + a[1] * b[1], a[1] * b[0] - a[0] * b[1]


def chosen(info):
    near, far = info
    return jnp.where(lax.axis_index("depth") == lax.axis_size("depth") - 1, far[...], near[...])


class Layout:
    def __init__(self, probes, count, layers, pixels, rows, height, width, only_sums=False):
        self.probes, self.count, self.layers, self.pixels = probes, count, layers, pixels
        self.groups = probes // count
        self.tall = pixels + 8
        self.rows, self.height, self.width = rows, height, width
        self.blocks = width // pixels
        self.deep = rows + 2 * self.tall
        self.column_bits = (width - 1).bit_length()
        self.name_bits = (4 * probes - 1).bit_length()
        self.stack = probes * layers * 2 * pixels
        self.seen_from = self.stack
        self.grads_from = 2 * self.stack
        self.frames_from = 3 * self.stack
        self.total_from = 0 if only_sums else self.frames_from + probes * pixels
        self.shape = (self.total_from + 2 * layers * self.blocks * self.deep, pixels)

    def stacked(self, group, i, layer, part):
        probe = group * self.count + i
        return ((probe * self.layers + layer) * 2 + part) * self.pixels

    def tile(self, start):
        return pl.ds(pl.multiple_of(start, 8), self.pixels)

    def patch(self, group, i, layer, part):
        return self.tile(self.stacked(group, i, layer, part))

    def seen(self, group, i, layer, part):
        return self.tile(self.seen_from + self.stacked(group, i, layer, part))

    def grad(self, group, i, layer, part):
        return self.tile(self.grads_from + self.stacked(group, i, layer, part))

    def grads_of(self, begin, end):
        each = self.stack // self.groups
        return self.grads_from + begin * each, self.grads_from + end * each

    def frame(self, group, i):
        return self.tile(self.frames_from + (group * self.count + i) * self.pixels)

    def total(self, part, layer, block, row):
        block = (part * self.layers + layer) * self.blocks + block
        return self.total_from + block * self.deep + row

    def pack(self, row, column, name):
        return (((row << self.column_bits) + column) << self.name_bits) + name

    def row(self, key):
        return key >> (self.column_bits + self.name_bits)

    def window(self, info, probe, whose=0):
        info = chosen(info)
        lane = lax.broadcasted_iota(jnp.int32, info.shape, 1)
        key = jnp.sum(jnp.where(lane == probe + whose * self.probes, info, 0))
        row = self.row(key)
        column = (key >> self.name_bits) & ((1 << self.column_bits) - 1)
        row0 = jnp.minimum(row // 8 * 8, self.height - self.tall)
        block = jnp.minimum(column // self.pixels, self.blocks - 2)
        return row0, row - row0, block, column - block * self.pixels


def call(lay, body, state, before, outs, scratch=(), flag=False, flops=1000, moved=1000, name=None):
    spaces = {"hbm": (HBM, in_hbm), "vmem": (VMEM, in_vmem), "smem": (SMEM, lambda x: x)}
    specs = [spaces[kind][0] for kind, _ in before]
    operands = [spaces[kind][1](x) for kind, x in before]
    at = len(before)
    aliases = {}
    if state is not None:
        specs.append(VMEM)
        operands.append(in_vmem(state))
        aliases = {at: 0}

    def kernel(*refs):
        body(*refs[:at], *refs[at + len(aliases) :])

    return pl.pallas_call(
        kernel,
        in_specs=specs,
        out_specs=[VMEM] * (1 + len(outs) + flag),
        out_shape=[pltpu.VMEM(shape, F32) for shape in (lay.shape, *outs)]
        + [pltpu.VMEM((1, 128), jnp.int32)] * flag,
        scratch_shapes=list(scratch),
        input_output_aliases=aliases,
        compiler_params=pltpu.CompilerParams(vmem_limit_bytes=SCOPED),
        cost_estimate=pl.CostEstimate(flops=flops, bytes_accessed=moved, transcendentals=0),
        name=name,
    )(*operands)


def clear_total(lay, state):
    start = lay.total_from

    def body(state):
        state[pl.ds(start, lay.shape[0] - start), :] = jnp.zeros((lay.shape[0] - start, lay.pixels), F32)

    return call(lay, body, state, [], [], name="clear_total")[0]


def place_frames(lay, sections, info, everyone, pools, state):
    def body(info, everyone, *refs):
        *pools, state, late, sems = refs
        nearest = 3 * lay.probes
        reach = jnp.bool_(False)
        for ref in (info, everyone):
            reach |= lay.row(ref[0, nearest]) + lay.pixels > lay.rows
            reach |= lay.row(ref[0, nearest + 1]) < lay.rows
        late[...] = jnp.full(late.shape, reach.astype(jnp.int32), jnp.int32)
        lat, side = lax.axis_index("lat"), lax.axis_index("probe")

        @pl.when(lax.axis_index("depth") == sections - 1)
        def _():
            for act in ("start", "wait"):
                for probe in range(lay.probes):
                    name = info[0, probe] & ((1 << lay.name_bits) - 1)
                    owner = name // lay.probes
                    slot = name % lay.probes
                    if len(pools) > 1:
                        slot += ((owner // 2) ^ side) * lay.probes + ((owner % 2) ^ lat) * 2 * lay.probes
                    first = 0
                    for pool in pools:
                        size = pool.shape[0] // lay.pixels

                        @pl.when((slot >= first) & (slot < first + size))
                        def _(pool=pool, first=first, probe=probe, slot=slot):
                            copy = pltpu.make_async_copy(
                                pool.at[lay.tile((slot - first) * lay.pixels), :],
                                state.at[lay.frame(0, probe), :],
                                sems.at[probe],
                            )
                            getattr(copy, act)()

                        first += size

    pools = [pool.reshape((-1, lay.pixels)) for pool in pools]
    pools = [("hbm", pools[0]), *(("vmem", pool) for pool in pools[1:])]
    return call(
        lay,
        body,
        state,
        [("smem", info), ("smem", everyone), *pools],
        [],
        flag=True,
        scratch=[pltpu.SemaphoreType.DMA((lay.probes,))],
        name="place_frames",
    )


def cut_patches(lay, info, own, other, state, begin, end, from_hbm=False):
    half = own.shape[2]
    tall, pixels = lay.tall, lay.pixels

    def one(probe, near, far, own, other, state, window, sem):
        info = near, far
        row0, down, block, shift = lay.window(info, probe)
        own_top = lax.axis_index("lat") == 0
        near_at = pl.ds(pl.multiple_of(block * pixels, pixels), pixels)
        far_at = pl.ds(pl.multiple_of((block + 1) * pixels, pixels), pixels)
        for source, is_top in ((own, own_top), (other, jnp.logical_not(own_top))):
            start = jnp.clip(row0 - jnp.where(is_top, 0, half), 0, half - tall)
            to = pl.ds(pl.multiple_of(jnp.where(is_top, 0, tall), 8), tall)
            rows = pl.ds(pl.multiple_of(start, 8), tall)

            @pl.when(jnp.where(is_top, row0 < half, row0 + tall > half))
            def _(source=source, rows=rows, to=to):
                if source is own and from_hbm:
                    both = pl.ds(pl.multiple_of(block * pixels, pixels), 2 * pixels)
                    copy = pltpu.make_async_copy(source.at[:, :, rows, both], window.at[:, :, to, :], sem)
                    copy.start()
                    copy.wait()
                    return
                for part in range(2):
                    for layer in range(lay.layers):
                        window[part, layer, to, 0:pixels] = source[part, layer, rows, near_at]
                        window[part, layer, to, pixels : 2 * pixels] = source[part, layer, rows, far_at]

        offset = jnp.where(row0 < half, jnp.maximum(row0 - (half - tall), 0), tall)
        rows = pl.ds(pl.multiple_of(offset, 8), tall)
        turn = (pixels - shift) % pixels
        lane = lax.broadcasted_iota(jnp.int32, (tall, pixels), 1)
        for part in range(2):
            for layer in range(lay.layers):
                near = pltpu.roll(window[part, layer, rows, 0:pixels], turn, 1)
                far = pltpu.roll(window[part, layer, rows, pixels : 2 * pixels], turn, 1)
                patch = jnp.where(lane < pixels - shift, near, far)
                patch = pltpu.roll(patch, (tall - down) % tall, 0)[:pixels]
                state[lay.patch(0, probe, layer, part), :] = patch

    def body(*refs):
        section = lax.axis_index("depth")
        bounds = [x(section) if callable(x) else x for x in (begin, end)]
        lax.fori_loop(*bounds, lambda probe, _: one(probe, *refs) or 0, 0)

    return call(
        lay,
        body,
        state,
        [*(("vmem", x) for x in info), ("hbm" if from_hbm else "vmem", own), ("vmem", other)],
        [],
        scratch=[pltpu.VMEM((2, lay.layers, 2 * tall, 2 * pixels), F32), pltpu.SemaphoreType.DMA(())],
        name="cut_patches",
    )[0]


def section_cost(lay):
    size = lay.count * lay.pixels**2
    return dict(flops=lay.layers * 2 * 3 * 8 * size * lay.pixels, moved=(lay.layers * 2 + 4) * 8 * size)


def pair(ref, at):
    return ref[at(0), :], ref[at(1), :]


def run_forward(lay, tick, sections, tables, state, arrived, start_wave):
    def body(tables, *refs):
        arrived_ref = refs[0] if arrived is not None else None
        start_ref = refs[-3] if start_wave is not None else None
        state, leave = refs[-2:]
        section = lax.axis_index("depth")
        group = tick - section
        final = (section == sections - 1).astype(jnp.int32)

        @pl.when((group >= 0) & (group < lay.groups))
        def _():
            wave = []
            for i in range(lay.count):
                if arrived is None:
                    wave.append((start_ref[0], start_ref[1]))
                elif start_wave is None:
                    wave.append((arrived_ref[i, 0], arrived_ref[i, 1]))
                else:
                    wave.append(
                        tuple(jnp.where(section == 0, start_ref[p], arrived_ref[i, p]) for p in range(2))
                    )
            for layer in range(lay.layers):
                chi = []
                for i in range(lay.count):
                    for part in range(2):
                        state[lay.seen(group, i, layer, part), :] = wave[i][part]
                    chi.append(times(pair(state, functools.partial(lay.patch, group, i, layer)), wave[i]))
                at = final if layer == lay.layers - 1 else 0
                wave = transform((tables[at, 0, 0], tables[at, 0, 1]), (tables[at, 1, 0], tables[at, 1, 1]), chi)
            for i in range(lay.count):
                real, imag = wave[i]
                misfit = real * real + imag * imag - state[lay.frame(group, i), :]
                factor = jnp.where(final == 1, misfit, 1.0)
                leave[i, 0] = real * factor
                leave[i, 1] = imag * factor

    waves = [("vmem", x) for x in (arrived, start_wave) if x is not None]
    return call(
        lay,
        body,
        state,
        [("vmem", tables), *waves],
        [(lay.count, 2, lay.pixels, lay.pixels)],
        name="forward_section",
        **section_cost(lay),
    )


def run_backward(lay, tick, sections, tables, state, arrived, own):
    def body(tables, *refs):
        arrived_ref = refs[0] if arrived is not None else None
        own_ref = refs[1 if arrived is not None else 0] if own is not None else None
        state, leave = refs[-2:]
        section = lax.axis_index("depth")
        group = tick - (2 * (sections - 1) - section)
        final = (section == sections - 1).astype(jnp.int32)

        @pl.when((group >= 0) & (group < lay.groups))
        def _():
            wave = []
            for i in range(lay.count):
                if arrived is None:
                    wave.append((own_ref[i, 0], own_ref[i, 1]))
                elif own is None:
                    wave.append((arrived_ref[i, 0], arrived_ref[i, 1]))
                else:
                    wave.append(
                        tuple(jnp.where(final == 1, own_ref[i, p], arrived_ref[i, p]) for p in range(2))
                    )
            for layer in reversed(range(lay.layers)):
                at = final if layer == lay.layers - 1 else 0
                chi = transform((tables[at, 1, 0], tables[at, 1, 1]), (tables[at, 0, 0], tables[at, 0, 1]), wave)
                wave = []
                for i in range(lay.count):
                    real, imag = times_conj(chi[i], pair(state, functools.partial(lay.seen, group, i, layer)))
                    state[lay.grad(group, i, layer, 0), :] = real
                    state[lay.grad(group, i, layer, 1), :] = imag
                    wave.append(times_conj(chi[i], pair(state, functools.partial(lay.patch, group, i, layer))))
            for i in range(lay.count):
                leave[i, 0] = wave[i][0]
                leave[i, 1] = wave[i][1]

    waves = [("vmem", x) for x in (arrived, own) if x is not None]
    return call(
        lay,
        body,
        state,
        [("vmem", tables), *waves],
        [(lay.count, 2, lay.pixels, lay.pixels)],
        name="backward_section",
        **section_cost(lay),
    )


def deposit(lay, tick, sections, info, received, state):
    pixels, tall = lay.pixels, lay.tall

    def body(near, far, *refs):
        info = near, far
        state = refs[-1]
        lane = lax.broadcasted_iota(jnp.int32, (tall, pixels), 1)
        blank = jnp.zeros((8, pixels), F32)
        base = lax.axis_index("probe") * lay.rows if lay.rows < lay.height else 0

        def add(probe, whose, active, load):
            row0, down, block, shift = lay.window(info, probe, whose)
            start = row0 - base + tall

            @pl.when(active & (start > 0) & (start < lay.rows + tall))
            def _():
                for layer in range(lay.layers):
                    for part in range(2):
                        padded = jnp.concatenate([load(layer, part), blank], axis=0)
                        turned = pltpu.roll(pltpu.roll(padded, down, 0), shift % pixels, 1)
                        near = pl.ds(pl.multiple_of(lay.total(part, layer, block, start), 8), tall)
                        far = pl.ds(pl.multiple_of(lay.total(part, layer, block + 1, start), 8), tall)
                        state[near, :] += jnp.where(lane >= shift, turned, 0.0)
                        state[far, :] += jnp.where(lane >= shift, 0.0, turned)

        if tick is not None:
            group = tick - (2 * (sections - 1) - lax.axis_index("depth"))
            active = (group >= 0) & (group < lay.groups)
            group = jnp.clip(group, 0, lay.groups - 1)
            for i in range(lay.count):
                add(
                    group * lay.count + i,
                    0,
                    active,
                    lambda layer, part, i=i: state[lay.grad(group, i, layer, part), :],
                )
        for ref, (first, whose, grads) in zip(refs, received):

            def one(i, _, ref=ref, first=first, whose=whose):
                add(
                    first * lay.count + i,
                    whose,
                    True,
                    lambda layer, part: ref[lay.patch(0, i, layer, part), :],
                )
                return 0

            lax.fori_loop(0, grads.shape[0] // (lay.layers * 2 * pixels), one, 0)

    return call(
        lay,
        body,
        state,
        [("vmem", x) for x in info] + [("vmem", grads) for *_, grads in received],
        [],
        name="deposit_patches",
    )[0]


def split_rows(lay, state, owners, taken=(0, 8)):
    rows = lay.rows // (2 * owners)
    pieces = 4 * owners * lay.layers * lay.blocks

    def body(state, keep, send, rest, sems):
        lat = lax.axis_index("lat")
        copies = [pltpu.make_async_copy(state.at[pl.ds(taken[0], taken[1] - taken[0]), :], rest, sems.at[pieces])]
        for owner in range(owners):
            for kind, target in ((lat, keep), (1 - lat, send)):
                for part in range(2):
                    for layer in range(lay.layers):
                        for block in range(lay.blocks):
                            start = lay.total(part, layer, block, lay.tall + (2 * owner + kind) * rows)
                            copies.append(
                                pltpu.make_async_copy(
                                    state.at[pl.ds(pl.multiple_of(start, 8), rows), :],
                                    target.at[part, layer, owner, :, pl.ds(block * lay.pixels, lay.pixels)],
                                    sems.at[len(copies) - 1],
                                )
                            )
        for copy in copies:
            copy.start()
        for copy in copies:
            copy.wait()

    half = (2, lay.layers, owners, rows, lay.width)
    return pl.pallas_call(
        body,
        in_specs=[VMEM],
        out_specs=[VMEM, VMEM, HBM],
        out_shape=[
            pltpu.VMEM(half, F32),
            pltpu.VMEM(half, F32),
            pltpu.HBM((taken[1] - taken[0], lay.pixels), F32),
        ],
        scratch_shapes=[pltpu.SemaphoreType.DMA((pieces + 1,))],
        compiler_params=pltpu.CompilerParams(vmem_limit_bytes=SCOPED),
        name="split_rows",
    )(in_vmem(state))


def add_up(a, b):
    each = pl.BlockSpec((1, 1, *a.shape[2:]), lambda i, j: (i, j, 0, 0, 0))

    def body(a, b, out):
        out[...] = a[...] + b[...]

    return pl.pallas_call(
        body,
        grid=a.shape[:2],
        in_specs=[each, each],
        out_specs=each,
        out_shape=pltpu.HBM(a.shape, F32),
        compiler_params=pltpu.CompilerParams(vmem_limit_bytes=SCOPED),
        name="add_up",
    )(a, b)


def swap(shard, axis):
    return lax.ppermute(shard, axis, [(0, 1), (1, 0)])


def sort_probes(lay, early, positions, indices):
    n = lay.probes
    total = 4 * n

    def body(listed, *refs):
        *scans, info, positions, sem = refs
        copy = pltpu.make_async_copy(listed, positions, sem)
        copy.start()
        copy.wait()
        lat, side = lax.axis_index("lat"), lax.axis_index("probe")
        lane = lax.broadcasted_iota(jnp.int32, (1, 128), 1)
        at = lax.broadcasted_iota(jnp.int32, (total, 128), 0)
        across = jnp.full((1, 128), jnp.iinfo(jnp.int32).max, jnp.int32)
        down = jnp.zeros((total, 128), jnp.int32)
        for which, scan in enumerate(scans):
            owner = (side ^ (which % 2)) * 2 + (lat ^ (which // 2))
            for i in range(n):
                place = scan[i]
                key = lay.pack(positions[0, place], positions[1, place], owner * n + i)
                across = jnp.where(lane == which * n + i, key, across)
                down = jnp.where(at == which * n + i, key, down)
        rank = jnp.sum((across < down).astype(jnp.int32), axis=1, keepdims=True)
        whose = lane // n
        order = 2 * (lane % n) + jnp.where(whose == 2, 1 - lat, lat)
        wanted = jnp.where(jnp.where(whose == 1, 1 - side, side) == 0, 2 * n - 1 - order, 2 * n + order)
        reach = 2 * early * lay.count
        wanted = jnp.where(lane == 3 * n, 2 * n - 1 - reach, wanted)
        wanted = jnp.where(lane == 3 * n + 1, 2 * n + reach, wanted)
        wanted = jnp.where(lane > 3 * n + 1, -1, wanted)
        info[...] = jnp.sum(jnp.where(rank == wanted, down, 0), axis=0, keepdims=True)

    return pl.pallas_call(
        body,
        in_specs=[HBM] + [SMEM] * 4,
        out_specs=VMEM,
        out_shape=pltpu.VMEM((1, 128), jnp.int32),
        scratch_shapes=[pltpu.SMEM(positions.T.shape, jnp.int32), pltpu.SemaphoreType.DMA(())],
        compiler_params=pltpu.CompilerParams(vmem_limit_bytes=SCOPED),
        name="sort_probes",
    )(in_hbm(positions.T), *indices)


def bring(x):
    def body(x, out, sem):
        copy = pltpu.make_async_copy(x, out, sem)
        copy.start()
        copy.wait()

    return pl.pallas_call(
        body,
        in_specs=[HBM],
        out_specs=VMEM,
        out_shape=pltpu.VMEM(x.shape, x.dtype),
        scratch_shapes=[pltpu.SemaphoreType.DMA(())],
        compiler_params=pltpu.CompilerParams(vmem_limit_bytes=SCOPED),
        cost_estimate=pl.CostEstimate(flops=1000, bytes_accessed=1000, transcendentals=0),
        name="bring",
    )(in_hbm(x))


def local(specimen, illumination, positions, scan_index, frames):
    pixels = illumination.shape[-1]
    _, layers, half, width = specimen.shape
    height = 2 * half
    tables = jnp.asarray(make_tables(pixels))
    sections = lax.axis_size("depth")
    owners = lax.axis_size("probe")
    paired = owners == 2 and lax.axis_size("groups") <= 2
    probes = scan_index.size
    count = 2 if probes % 4 == 0 else 1
    lay = Layout(probes, count, layers, pixels, half if paired else height, height, width)
    early = lay.groups // 2

    everyone = mine = None
    if paired:
        scan = scan_index.reshape(-1)
        beside = swap(scan, "lat")
        half_rows, beside = lax.optimization_barrier((specimen, beside))
        other = swap(half_rows, "lat")
        end = sections - 1
        ends = [(2 * end, 2 * end + 1), (2 * end + 1, 2 * end)]
        mine = lax.ppermute(frames, ("depth", "probe"), ends)
        above = [(i, i ^ 1) for i in range(2 * end)]
        cross_above = lambda x: lax.ppermute(x, ("depth", "probe"), above)
        indices = [scan, cross_above(scan), beside, cross_above(beside)]
        info = sort_probes(lay, early, positions, indices)
    else:
        other = swap(specimen, "lat")
        corners = positions[scan_index.reshape(-1)]
        info = lay.pack(corners[:, 0], corners[:, 1], jnp.arange(probes, dtype=jnp.int32))
        info = ranking = everyone = far = jnp.pad(info, (0, 3 * probes))[None]
    state = cut_patches(lay, (info, info), specimen, other, None, 0, count, from_hbm=True)
    def busy(tick, source, by):
        delay = source if by > 0 else 2 * (sections - 1) - source
        return 0 <= tick - delay < lay.groups

    def pass_on(wave, tick, by):
        pairs = [
            (source, source + by)
            for source in range(sections)
            if 0 <= source + by < sections and busy(tick, source, by)
        ]
        return lax.ppermute(wave, "depth", pairs) if pairs else None

    def grads_of(state, begin, end):
        begin, end = lay.grads_of(begin, end)
        return lax.slice_in_dim(state, begin, end)

    fill = sections - 1
    parts = [(0, early // 2), (early // 2, early)] if paired else []
    crossing = {}
    down = up = None
    def upto(group):
        early_sections = min(group, lay.groups) * count
        return lambda section: jnp.where(section < 2, early_sections, probes)

    begin = lambda section: jnp.where(section == fill, 0, count)
    cuts = {0: (begin, upto(3)), 2: (upto(3), upto(5)), 3: (upto(5), probes)}
    last_tick = lay.groups + 2 * fill - 1
    for tick in range(lay.groups + 2 * fill):
        own = None
        if paired and tick == fill - 1:
            down, mine, near, far = lax.optimization_barrier((down, mine, *info))
            ranking = jnp.where(lax.axis_index("depth") == fill, far, near)
            everyone = swap(ranking, "groups") if lax.axis_size("groups") == 2 else ranking
            crossed = [lax.ppermute(x, ("depth", "lat"), ends) for x in (frames, mine)]
        if tick < lay.groups + fill:
            start_wave = illumination if tick < lay.groups else None
            state, own = run_forward(lay, tick, sections, tables, state, down, start_wave)
            if tick == 0:
                if paired:
                    own, near = lax.optimization_barrier((own, info))
                    far = lax.ppermute(near, "depth", [(fill - 1, fill)])
                info = info, far
                own, specimen = lax.optimization_barrier((own, specimen))
                brought = bring(specimen)
            down = pass_on(own, tick, 1)
            if tick in cuts:
                state = cut_patches(lay, info, brought, other, state, *cuts[tick])
            if tick == 0:
                state = clear_total(lay, state)
            if tick == fill - 1:
                pools = [frames, mine, *crossed] if paired else [frames]
                state, late = place_frames(lay, sections, ranking, everyone, pools, state)
        if tick >= fill:
            state, rising = run_backward(lay, tick, sections, tables, state, up, own)
            up = pass_on(rising, tick, -1)
            received = crossing.pop(tick, [])
            for begin, end in parts:
                if tick == end - 1 + 2 * fill:
                    due = min(tick + CROSSING, last_tick - 1)
                    crossing.setdefault(due, []).append((begin, 1, swap(grads_of(state, begin, end), "probe")))
            state = deposit(lay, tick, sections, info, received, state)
    if not paired:
        keep, send, _ = split_rows(lay, state, owners)
        return lax.psum_scatter(keep + swap(send, "lat"), "probe", scatter_dimension=2, tiled=False)

    keep, send, late_grads = split_rows(lay, state, 1, lay.grads_of(early, lay.groups))

    def as_they_are(keep, received, grads):
        return add_up(keep, received)

    def with_partners(keep, received, grads):
        sums = Layout(probes, count, layers, pixels, half, height, width, only_sums=True)
        state = clear_total(sums, None)
        state = deposit(sums, None, sections, info, [(early, 1, swap(grads, "probe"))], state)
        more, send, _ = split_rows(sums, state, 1)
        return add_up(keep + more, received + swap(send, "lat"))

    result = lax.cond(late[0, 0] > 0, with_partners, as_they_are, keep, swap(send, "lat"), late_grads)
    return result[:, :, 0]


def solution(mesh):
    return jax.shard_map(
        local,
        mesh=mesh,
        in_specs=(
            P(None, ("groups", "depth"), "lat", None),
            P(),
            P("groups", None),
            P("groups", ("probe", "lat")),
            P("groups", ("probe", "lat"), None, None),
        ),
        out_specs=P(None, ("groups", "depth"), ("probe", "lat"), None),
        check_vma=False,
    )
```

```python
import functools
import math

import jax
import jax.numpy as jnp
import ml_dtypes
import numpy as np
from jax import lax
from jax.experimental import pallas as pl
from jax.experimental.pallas import tpu as pltpu
from jax.sharding import PartitionSpec as P

FRESNEL = 8.0
SCOPED = 5 << 20
CROSSING = 3
F32 = jnp.float32
BF16 = jnp.bfloat16
HBM = pl.BlockSpec(memory_space=pl.ANY)
VMEM = pl.BlockSpec(memory_space=pltpu.VMEM)
SMEM = pl.BlockSpec(memory_space=pltpu.SMEM)


def in_hbm(x):
    return pltpu.with_memory_space_constraint(x, pltpu.HBM)


def in_vmem(x):
    return pltpu.with_memory_space_constraint(x, pltpu.VMEM)


def real_blocks(matrix):
    real, imag = matrix.real, matrix.imag
    left = np.block([[real, -imag], [imag, real]])
    right = np.block([[real, imag], [-imag, real]])
    return np.stack([left, right])


@functools.lru_cache(maxsize=None)
def make_tables(pixels):
    index = np.arange(pixels)
    freq = np.where(index < pixels // 2, index, index - pixels) / pixels
    spread = index[:, None] - index[None, :]
    phase = 2.0 * math.pi * freq * spread[:, :, None] - math.pi * FRESNEL * freq * freq
    propagator = np.mean(np.exp(1j * phase), axis=-1)
    turns = index[:, None] * index[None, :] % pixels
    fourier = np.exp(-2j * math.pi * turns / pixels) / math.sqrt(pixels)
    blocks = np.stack([real_blocks(propagator), real_blocks(fourier)]).astype(np.float32)
    high = blocks.astype(ml_dtypes.bfloat16)
    low = (blocks - high.astype(np.float32)).astype(ml_dtypes.bfloat16)
    return np.stack([high, low], axis=2)


def halves(x):
    high = x.astype(BF16)
    return high, (x - high.astype(F32)).astype(BF16)


def dot(a, b):
    return jnp.dot(a, b, preferred_element_type=F32)


def transform(left, right, fields):
    size = fields[0][0].shape[0]
    mids = []
    for high, low in [halves(jnp.concatenate(field, axis=0)) for field in fields]:
        both = dot(left[0], jnp.concatenate([high, low], axis=1))
        mids.append(both[:, :size] + (both[:, size:] + dot(left[1], high)))
    outs = []
    for high, low in [halves(jnp.concatenate([mid[:size], mid[size:]], axis=1)) for mid in mids]:
        both = dot(jnp.concatenate([high, low], axis=0), right[0])
        outs.append(both[:size] + (both[size:] + dot(high, right[1])))
    return [(out[:, :size], out[:, size:]) for out in outs]


def times(a, b):
    return a[0] * b[0] - a[1] * b[1], a[0] * b[1] + a[1] * b[0]


def times_conj(a, b):
    return a[0] * b[0] + a[1] * b[1], a[1] * b[0] - a[0] * b[1]


def chosen(info):
    near, far = info
    return jnp.where(lax.axis_index("depth") == lax.axis_size("depth") - 1, far[...], near[...])


class Layout:
    def __init__(self, probes, count, layers, pixels, rows, height, width, only_sums=False):
        self.probes, self.count, self.layers, self.pixels = probes, count, layers, pixels
        self.groups = probes // count
        self.tall = pixels + 8
        self.rows, self.height, self.width = rows, height, width
        self.blocks = width // pixels
        self.deep = rows + 2 * self.tall
        self.column_bits = (width - 1).bit_length()
        self.name_bits = (4 * probes - 1).bit_length()
        self.stack = probes * layers * 2 * pixels
        self.seen_from = self.stack
        self.grads_from = 2 * self.stack
        self.frames_from = 3 * self.stack
        self.total_from = 0 if only_sums else self.frames_from + probes * pixels
        self.shape = (self.total_from + 2 * layers * self.blocks * self.deep, pixels)

    def stacked(self, group, i, layer, part):
        probe = group * self.count + i
        return ((probe * self.layers + layer) * 2 + part) * self.pixels

    def tile(self, start):
        return pl.ds(pl.multiple_of(start, 8), self.pixels)

    def patch(self, group, i, layer, part):
        return self.tile(self.stacked(group, i, layer, part))

    def seen(self, group, i, layer, part):
        return self.tile(self.seen_from + self.stacked(group, i, layer, part))

    def grad(self, group, i, layer, part):
        return self.tile(self.grads_from + self.stacked(group, i, layer, part))

    def grads_of(self, begin, end):
        each = self.stack // self.groups
        return self.grads_from + begin * each, self.grads_from + end * each

    def frame(self, group, i):
        return self.tile(self.frames_from + (group * self.count + i) * self.pixels)

    def total(self, part, layer, block, row):
        block = (part * self.layers + layer) * self.blocks + block
        return self.total_from + block * self.deep + row

    def pack(self, row, column, name):
        return (((row << self.column_bits) + column) << self.name_bits) + name

    def row(self, key):
        return key >> (self.column_bits + self.name_bits)

    def window(self, info, probe, whose=0):
        info = chosen(info)
        lane = lax.broadcasted_iota(jnp.int32, info.shape, 1)
        key = jnp.sum(jnp.where(lane == probe + whose * self.probes, info, 0))
        row = self.row(key)
        column = (key >> self.name_bits) & ((1 << self.column_bits) - 1)
        row0 = jnp.minimum(row // 8 * 8, self.height - self.tall)
        block = jnp.minimum(column // self.pixels, self.blocks - 2)
        return row0, row - row0, block, column - block * self.pixels


def call(lay, body, state, before, outs, scratch=(), flag=False, flops=1000, moved=1000, name=None):
    spaces = {"hbm": (HBM, in_hbm), "vmem": (VMEM, in_vmem), "smem": (SMEM, lambda x: x)}
    specs = [spaces[kind][0] for kind, _ in before]
    operands = [spaces[kind][1](x) for kind, x in before]
    at = len(before)
    aliases = {}
    if state is not None:
        specs.append(VMEM)
        operands.append(in_vmem(state))
        aliases = {at: 0}

    def kernel(*refs):
        body(*refs[:at], *refs[at + len(aliases) :])

    return pl.pallas_call(
        kernel,
        in_specs=specs,
        out_specs=[VMEM] * (1 + len(outs) + flag),
        out_shape=[pltpu.VMEM(shape, F32) for shape in (lay.shape, *outs)]
        + [pltpu.VMEM((1, 128), jnp.int32)] * flag,
        scratch_shapes=list(scratch),
        input_output_aliases=aliases,
        compiler_params=pltpu.CompilerParams(vmem_limit_bytes=SCOPED),
        cost_estimate=pl.CostEstimate(flops=flops, bytes_accessed=moved, transcendentals=0),
        name=name,
    )(*operands)


def clear_total(lay, state):
    start = lay.total_from

    def body(state):
        state[pl.ds(start, lay.shape[0] - start), :] = jnp.zeros((lay.shape[0] - start, lay.pixels), F32)

    return call(lay, body, state, [], [], name="clear_total")[0]


def place_frames(lay, sections, info, everyone, pools, state):
    def body(info, everyone, *refs):
        *pools, state, late, sems = refs
        nearest = 3 * lay.probes
        reach = jnp.bool_(False)
        for ref in (info, everyone):
            reach |= lay.row(ref[0, nearest]) + lay.pixels > lay.rows
            reach |= lay.row(ref[0, nearest + 1]) < lay.rows
        late[...] = jnp.full(late.shape, reach.astype(jnp.int32), jnp.int32)
        lat, side = lax.axis_index("lat"), lax.axis_index("probe")

        @pl.when(lax.axis_index("depth") == sections - 1)
        def _():
            for act in ("start", "wait"):
                for probe in range(lay.probes):
                    name = info[0, probe] & ((1 << lay.name_bits) - 1)
                    owner = name // lay.probes
                    slot = name % lay.probes
                    if len(pools) > 1:
                        slot += ((owner // 2) ^ side) * lay.probes + ((owner % 2) ^ lat) * 2 * lay.probes
                    first = 0
                    for pool in pools:
                        size = pool.shape[0] // lay.pixels

                        @pl.when((slot >= first) & (slot < first + size))
                        def _(pool=pool, first=first, probe=probe, slot=slot):
                            copy = pltpu.make_async_copy(
                                pool.at[lay.tile((slot - first) * lay.pixels), :],
                                state.at[lay.frame(0, probe), :],
                                sems.at[probe],
                            )
                            getattr(copy, act)()

                        first += size

    pools = [pool.reshape((-1, lay.pixels)) for pool in pools]
    pools = [("hbm", pool) for pool in pools]
    return call(
        lay,
        body,
        state,
        [("smem", info), ("smem", everyone), *pools],
        [],
        flag=True,
        scratch=[pltpu.SemaphoreType.DMA((lay.probes,))],
        name="place_frames",
    )


def cut_patches(lay, info, own, other, state, begin, end, from_hbm=False):
    half = own.shape[2]
    tall, pixels = lay.tall, lay.pixels

    def one(probe, near, far, own, other, state, window, sem):
        info = near, far
        row0, down, block, shift = lay.window(info, probe)
        own_top = lax.axis_index("lat") == 0
        near_at = pl.ds(pl.multiple_of(block * pixels, pixels), pixels)
        far_at = pl.ds(pl.multiple_of((block + 1) * pixels, pixels), pixels)
        for source, is_top in ((own, own_top), (other, jnp.logical_not(own_top))):
            start = jnp.clip(row0 - jnp.where(is_top, 0, half), 0, half - tall)
            to = pl.ds(pl.multiple_of(jnp.where(is_top, 0, tall), 8), tall)
            rows = pl.ds(pl.multiple_of(start, 8), tall)

            @pl.when(jnp.where(is_top, row0 < half, row0 + tall > half))
            def _(source=source, rows=rows, to=to):
                if source is own and from_hbm:
                    both = pl.ds(pl.multiple_of(block * pixels, pixels), 2 * pixels)
                    copy = pltpu.make_async_copy(source.at[:, :, rows, both], window.at[:, :, to, :], sem)
                    copy.start()
                    copy.wait()
                    return
                for part in range(2):
                    for layer in range(lay.layers):
                        window[part, layer, to, 0:pixels] = source[part, layer, rows, near_at]
                        window[part, layer, to, pixels : 2 * pixels] = source[part, layer, rows, far_at]

        offset = jnp.where(row0 < half, jnp.maximum(row0 - (half - tall), 0), tall)
        rows = pl.ds(pl.multiple_of(offset, 8), tall)
        turn = (pixels - shift) % pixels
        lane = lax.broadcasted_iota(jnp.int32, (tall, pixels), 1)
        for part in range(2):
            for layer in range(lay.layers):
                near = pltpu.roll(window[part, layer, rows, 0:pixels], turn, 1)
                far = pltpu.roll(window[part, layer, rows, pixels : 2 * pixels], turn, 1)
                patch = jnp.where(lane < pixels - shift, near, far)
                patch = pltpu.roll(patch, (tall - down) % tall, 0)[:pixels]
                state[lay.patch(0, probe, layer, part), :] = patch

    def body(*refs):
        section = lax.axis_index("depth")
        bounds = [x(section) if callable(x) else x for x in (begin, end)]
        lax.fori_loop(*bounds, lambda probe, _: one(probe, *refs) or 0, 0)

    return call(
        lay,
        body,
        state,
        [*(("vmem", x) for x in info), ("hbm" if from_hbm else "vmem", own), ("vmem", other)],
        [],
        scratch=[pltpu.VMEM((2, lay.layers, 2 * tall, 2 * pixels), F32), pltpu.SemaphoreType.DMA(())],
        name="cut_patches",
    )[0]


def section_cost(lay):
    size = lay.count * lay.pixels**2
    return dict(flops=lay.layers * 2 * 3 * 8 * size * lay.pixels, moved=(lay.layers * 2 + 4) * 8 * size)


def pair(ref, at):
    return ref[at(0), :], ref[at(1), :]


def run_forward(lay, tick, sections, tables, state, arrived, start_wave):
    def body(tables, *refs):
        arrived_ref = refs[0] if arrived is not None else None
        start_ref = refs[-3] if start_wave is not None else None
        state, leave = refs[-2:]
        section = lax.axis_index("depth")
        group = tick - section
        final = (section == sections - 1).astype(jnp.int32)

        @pl.when((group >= 0) & (group < lay.groups))
        def _():
            wave = []
            for i in range(lay.count):
                if arrived is None:
                    wave.append((start_ref[0], start_ref[1]))
                elif start_wave is None:
                    wave.append((arrived_ref[i, 0], arrived_ref[i, 1]))
                else:
                    wave.append(
                        tuple(jnp.where(section == 0, start_ref[p], arrived_ref[i, p]) for p in range(2))
                    )
            for layer in range(lay.layers):
                chi = []
                for i in range(lay.count):
                    for part in range(2):
                        state[lay.seen(group, i, layer, part), :] = wave[i][part]
                    chi.append(times(pair(state, functools.partial(lay.patch, group, i, layer)), wave[i]))
                at = final if layer == lay.layers - 1 else 0
                wave = transform((tables[at, 0, 0], tables[at, 0, 1]), (tables[at, 1, 0], tables[at, 1, 1]), chi)
            for i in range(lay.count):
                real, imag = wave[i]
                misfit = real * real + imag * imag - state[lay.frame(group, i), :]
                factor = jnp.where(final == 1, misfit, 1.0)
                leave[i, 0] = real * factor
                leave[i, 1] = imag * factor

    waves = [("vmem", x) for x in (arrived, start_wave) if x is not None]
    return call(
        lay,
        body,
        state,
        [("vmem", tables), *waves],
        [(lay.count, 2, lay.pixels, lay.pixels)],
        name="forward_section",
        **section_cost(lay),
    )


def run_backward(lay, tick, sections, tables, state, arrived, own):
    def body(tables, *refs):
        arrived_ref = refs[0] if arrived is not None else None
        own_ref = refs[1 if arrived is not None else 0] if own is not None else None
        state, leave = refs[-2:]
        section = lax.axis_index("depth")
        group = tick - (2 * (sections - 1) - section)
        final = (section == sections - 1).astype(jnp.int32)

        @pl.when((group >= 0) & (group < lay.groups))
        def _():
            wave = []
            for i in range(lay.count):
                if arrived is None:
                    wave.append((own_ref[i, 0], own_ref[i, 1]))
                elif own is None:
                    wave.append((arrived_ref[i, 0], arrived_ref[i, 1]))
                else:
                    wave.append(
                        tuple(jnp.where(final == 1, own_ref[i, p], arrived_ref[i, p]) for p in range(2))
                    )
            for layer in reversed(range(lay.layers)):
                at = final if layer == lay.layers - 1 else 0
                chi = transform((tables[at, 1, 0], tables[at, 1, 1]), (tables[at, 0, 0], tables[at, 0, 1]), wave)
                wave = []
                for i in range(lay.count):
                    real, imag = times_conj(chi[i], pair(state, functools.partial(lay.seen, group, i, layer)))
                    state[lay.grad(group, i, layer, 0), :] = real
                    state[lay.grad(group, i, layer, 1), :] = imag
                    wave.append(times_conj(chi[i], pair(state, functools.partial(lay.patch, group, i, layer))))
            for i in range(lay.count):
                leave[i, 0] = wave[i][0]
                leave[i, 1] = wave[i][1]

    waves = [("vmem", x) for x in (arrived, own) if x is not None]
    return call(
        lay,
        body,
        state,
        [("vmem", tables), *waves],
        [(lay.count, 2, lay.pixels, lay.pixels)],
        name="backward_section",
        **section_cost(lay),
    )


def deposit(lay, tick, sections, info, received, state):
    pixels, tall = lay.pixels, lay.tall

    def body(near, far, *refs):
        info = near, far
        state = refs[-1]
        lane = lax.broadcasted_iota(jnp.int32, (tall, pixels), 1)
        blank = jnp.zeros((8, pixels), F32)
        base = lax.axis_index("probe") * lay.rows if lay.rows < lay.height else 0

        def add(probe, whose, active, load):
            row0, down, block, shift = lay.window(info, probe, whose)
            start = row0 - base + tall

            @pl.when(active & (start > 0) & (start < lay.rows + tall))
            def _():
                for layer in range(lay.layers):
                    for part in range(2):
                        padded = jnp.concatenate([load(layer, part), blank], axis=0)
                        turned = pltpu.roll(pltpu.roll(padded, down, 0), shift % pixels, 1)
                        near = pl.ds(pl.multiple_of(lay.total(part, layer, block, start), 8), tall)
                        far = pl.ds(pl.multiple_of(lay.total(part, layer, block + 1, start), 8), tall)
                        state[near, :] += jnp.where(lane >= shift, turned, 0.0)
                        state[far, :] += jnp.where(lane >= shift, 0.0, turned)

        if tick is not None:
            group = tick - (2 * (sections - 1) - lax.axis_index("depth"))
            active = (group >= 0) & (group < lay.groups)
            group = jnp.clip(group, 0, lay.groups - 1)
            for i in range(lay.count):
                add(
                    group * lay.count + i,
                    0,
                    active,
                    lambda layer, part, i=i: state[lay.grad(group, i, layer, part), :],
                )
        for ref, (first, whose, grads) in zip(refs, received):

            def one(i, _, ref=ref, first=first, whose=whose):
                add(
                    first * lay.count + i,
                    whose,
                    True,
                    lambda layer, part: ref[lay.patch(0, i, layer, part), :],
                )
                return 0

            lax.fori_loop(0, grads.shape[0] // (lay.layers * 2 * pixels), one, 0)

    return call(
        lay,
        body,
        state,
        [("vmem", x) for x in info] + [("vmem", grads) for *_, grads in received],
        [],
        name="deposit_patches",
    )[0]


def split_rows(lay, state, owners, taken=(0, 8)):
    rows = lay.rows // (2 * owners)
    pieces = 4 * owners * lay.layers * lay.blocks

    def body(state, keep, send, rest, sems):
        lat = lax.axis_index("lat")
        copies = [pltpu.make_async_copy(state.at[pl.ds(taken[0], taken[1] - taken[0]), :], rest, sems.at[pieces])]
        for owner in range(owners):
            for kind, target in ((lat, keep), (1 - lat, send)):
                for part in range(2):
                    for layer in range(lay.layers):
                        for block in range(lay.blocks):
                            start = lay.total(part, layer, block, lay.tall + (2 * owner + kind) * rows)
                            copies.append(
                                pltpu.make_async_copy(
                                    state.at[pl.ds(pl.multiple_of(start, 8), rows), :],
                                    target.at[part, layer, owner, :, pl.ds(block * lay.pixels, lay.pixels)],
                                    sems.at[len(copies) - 1],
                                )
                            )
        for copy in copies:
            copy.start()
        for copy in copies:
            copy.wait()

    half = (2, lay.layers, owners, rows, lay.width)
    return pl.pallas_call(
        body,
        in_specs=[VMEM],
        out_specs=[VMEM, VMEM, HBM],
        out_shape=[
            pltpu.VMEM(half, F32),
            pltpu.VMEM(half, F32),
            pltpu.HBM((taken[1] - taken[0], lay.pixels), F32),
        ],
        scratch_shapes=[pltpu.SemaphoreType.DMA((pieces + 1,))],
        compiler_params=pltpu.CompilerParams(vmem_limit_bytes=SCOPED),
        name="split_rows",
    )(in_vmem(state))


def add_up(a, b):
    each = pl.BlockSpec((1, 1, *a.shape[2:]), lambda i, j: (i, j, 0, 0, 0))

    def body(a, b, out):
        out[...] = a[...] + b[...]

    return pl.pallas_call(
        body,
        grid=a.shape[:2],
        in_specs=[each, each],
        out_specs=each,
        out_shape=pltpu.HBM(a.shape, F32),
        compiler_params=pltpu.CompilerParams(vmem_limit_bytes=SCOPED),
        name="add_up",
    )(a, b)


def swap(shard, axis):
    return lax.ppermute(shard, axis, [(0, 1), (1, 0)])


def sort_probes(lay, early, positions, indices):
    n = lay.probes
    total = 4 * n

    def body(listed, *refs):
        *scans, info, positions, sem = refs
        copy = pltpu.make_async_copy(listed, positions, sem)
        copy.start()
        copy.wait()
        lat, side = lax.axis_index("lat"), lax.axis_index("probe")
        lane = lax.broadcasted_iota(jnp.int32, (1, 128), 1)
        at = lax.broadcasted_iota(jnp.int32, (total, 128), 0)
        across = jnp.full((1, 128), jnp.iinfo(jnp.int32).max, jnp.int32)
        down = jnp.zeros((total, 128), jnp.int32)
        for which, scan in enumerate(scans):
            owner = (side ^ (which % 2)) * 2 + (lat ^ (which // 2))
            for i in range(n):
                place = scan[i]
                key = lay.pack(positions[0, place], positions[1, place], owner * n + i)
                across = jnp.where(lane == which * n + i, key, across)
                down = jnp.where(at == which * n + i, key, down)
        rank = jnp.sum((across < down).astype(jnp.int32), axis=1, keepdims=True)
        whose = lane // n
        order = 2 * (lane % n) + jnp.where(whose == 2, 1 - lat, lat)
        wanted = jnp.where(jnp.where(whose == 1, 1 - side, side) == 0, 2 * n - 1 - order, 2 * n + order)
        reach = 2 * early * lay.count
        wanted = jnp.where(lane == 3 * n, 2 * n - 1 - reach, wanted)
        wanted = jnp.where(lane == 3 * n + 1, 2 * n + reach, wanted)
        wanted = jnp.where(lane > 3 * n + 1, -1, wanted)
        info[...] = jnp.sum(jnp.where(rank == wanted, down, 0), axis=0, keepdims=True)

    return pl.pallas_call(
        body,
        in_specs=[HBM] + [SMEM] * 4,
        out_specs=VMEM,
        out_shape=pltpu.VMEM((1, 128), jnp.int32),
        scratch_shapes=[pltpu.SMEM(positions.T.shape, jnp.int32), pltpu.SemaphoreType.DMA(())],
        compiler_params=pltpu.CompilerParams(vmem_limit_bytes=SCOPED),
        name="sort_probes",
    )(in_hbm(positions.T), *indices)


def bring(x):
    def body(x, out, sem):
        copy = pltpu.make_async_copy(x, out, sem)
        copy.start()
        copy.wait()

    return pl.pallas_call(
        body,
        in_specs=[HBM],
        out_specs=VMEM,
        out_shape=pltpu.VMEM(x.shape, x.dtype),
        scratch_shapes=[pltpu.SemaphoreType.DMA(())],
        compiler_params=pltpu.CompilerParams(vmem_limit_bytes=SCOPED),
        cost_estimate=pl.CostEstimate(flops=1000, bytes_accessed=1000, transcendentals=0),
        name="bring",
    )(in_hbm(x))


def local(specimen, illumination, positions, scan_index, frames):
    pixels = illumination.shape[-1]
    _, layers, half, width = specimen.shape
    height = 2 * half
    tables = jnp.asarray(make_tables(pixels))
    sections = lax.axis_size("depth")
    owners = lax.axis_size("probe")
    paired = owners == 2 and lax.axis_size("groups") <= 2
    probes = scan_index.size
    count = 2 if probes % 4 == 0 else 1
    lay = Layout(probes, count, layers, pixels, half if paired else height, height, width)
    early = lay.groups // 2

    everyone = mine = None
    if paired:
        scan = scan_index.reshape(-1)
        beside = swap(scan, "lat")
        half_rows, beside = lax.optimization_barrier((specimen, beside))
        other = swap(half_rows, "lat")
        end = sections - 1
        ends = [(2 * end, 2 * end + 1), (2 * end + 1, 2 * end)]
        mine = lax.ppermute(frames, ("depth", "probe"), ends)
        above = [(i, i ^ 1) for i in range(2 * end)]
        cross_above = lambda x: lax.ppermute(x, ("depth", "probe"), above)
        indices = [scan, cross_above(scan), beside, cross_above(beside)]
        info = sort_probes(lay, early, positions, indices)
    else:
        other = swap(specimen, "lat")
        corners = positions[scan_index.reshape(-1)]
        info = lay.pack(corners[:, 0], corners[:, 1], jnp.arange(probes, dtype=jnp.int32))
        info = ranking = everyone = far = jnp.pad(info, (0, 3 * probes))[None]
    state = cut_patches(lay, (info, info), specimen, other, None, 0, count, from_hbm=True)
    def busy(tick, source, by):
        delay = source if by > 0 else 2 * (sections - 1) - source
        return 0 <= tick - delay < lay.groups

    def pass_on(wave, tick, by):
        pairs = [
            (source, source + by)
            for source in range(sections)
            if 0 <= source + by < sections and busy(tick, source, by)
        ]
        return lax.ppermute(wave, "depth", pairs) if pairs else None

    def grads_of(state, begin, end):
        begin, end = lay.grads_of(begin, end)
        return lax.slice_in_dim(state, begin, end)

    fill = sections - 1
    parts = [(0, early // 2), (early // 2, early)] if paired else []
    crossing = {}
    down = up = None
    def upto(group):
        early_sections = min(group, lay.groups) * count
        return lambda section: jnp.where(section < 2, early_sections, probes)

    begin = lambda section: jnp.where(section == fill, 0, count)
    cuts = {0: (begin, upto(3)), 2: (upto(3), upto(5)), 3: (upto(5), probes)}
    last_tick = lay.groups + 2 * fill - 1
    for tick in range(lay.groups + 2 * fill):
        own = None
        if paired and tick == fill - 1:
            down, mine, near, far = lax.optimization_barrier((down, mine, *info))
            ranking = jnp.where(lax.axis_index("depth") == fill, far, near)
            everyone = swap(ranking, "groups") if lax.axis_size("groups") == 2 else ranking
            crossed = [lax.ppermute(x, ("depth", "lat"), ends) for x in (frames, mine)]
        if tick < lay.groups + fill:
            start_wave = illumination if tick < lay.groups else None
            state, own = run_forward(lay, tick, sections, tables, state, down, start_wave)
            if tick == 0:
                if paired:
                    own, near = lax.optimization_barrier((own, info))
                    far = lax.ppermute(near, "depth", [(fill - 1, fill)])
                info = info, far
                own, specimen = lax.optimization_barrier((own, specimen))
                brought = bring(specimen)
            down = pass_on(own, tick, 1)
            if tick in cuts:
                state = cut_patches(lay, info, brought, other, state, *cuts[tick])
            if tick == 0:
                state = clear_total(lay, state)
            if tick == fill - 1:
                pools = [frames, mine, *crossed] if paired else [frames]
                state, late = place_frames(lay, sections, ranking, everyone, pools, state)
        if tick >= fill:
            state, rising = run_backward(lay, tick, sections, tables, state, up, own)
            up = pass_on(rising, tick, -1)
            received = crossing.pop(tick, [])
            for begin, end in parts:
                if tick == end - 1 + 2 * fill:
                    due = min(tick + CROSSING, last_tick - 1)
                    crossing.setdefault(due, []).append((begin, 1, swap(grads_of(state, begin, end), "probe")))
            state = deposit(lay, tick, sections, info, received, state)
    if not paired:
        keep, send, _ = split_rows(lay, state, owners)
        return lax.psum_scatter(keep + swap(send, "lat"), "probe", scatter_dimension=2, tiled=False)

    keep, send, late_grads = split_rows(lay, state, 1, lay.grads_of(early, lay.groups))

    def as_they_are(keep, received, grads):
        return add_up(keep, received)

    def with_partners(keep, received, grads):
        sums = Layout(probes, count, layers, pixels, half, height, width, only_sums=True)
        state = clear_total(sums, None)
        state = deposit(sums, None, sections, info, [(early, 1, swap(grads, "probe"))], state)
        more, send, _ = split_rows(sums, state, 1)
        return add_up(keep + more, received + swap(send, "lat"))

    result = lax.cond(late[0, 0] > 0, with_partners, as_they_are, keep, swap(send, "lat"), late_grads)
    return result[:, :, 0]


def solution(mesh):
    return jax.shard_map(
        local,
        mesh=mesh,
        in_specs=(
            P(None, ("groups", "depth"), "lat", None),
            P(),
            P("groups", None),
            P("groups", ("probe", "lat")),
            P("groups", ("probe", "lat"), None, None),
        ),
        out_specs=P(None, ("groups", "depth"), ("probe", "lat"), None),
        check_vma=False,
    )
```

```python
import functools
import math

import jax
import jax.numpy as jnp
import ml_dtypes
import numpy as np
from jax import lax
from jax.experimental import pallas as pl
from jax.experimental.pallas import tpu as pltpu
from jax.sharding import PartitionSpec as P

FRESNEL = 8.0
SCOPED = 8 << 20
CROSSING = 3
F32 = jnp.float32
BF16 = jnp.bfloat16
HBM = pl.BlockSpec(memory_space=pl.ANY)
VMEM = pl.BlockSpec(memory_space=pltpu.VMEM)
SMEM = pl.BlockSpec(memory_space=pltpu.SMEM)


def in_hbm(x):
    return pltpu.with_memory_space_constraint(x, pltpu.HBM)


def in_vmem(x):
    return pltpu.with_memory_space_constraint(x, pltpu.VMEM)


def real_blocks(matrix):
    real, imag = matrix.real, matrix.imag
    left = np.block([[real, -imag], [imag, real]])
    right = np.block([[real, imag], [-imag, real]])
    return np.stack([left, right])


@functools.lru_cache(maxsize=None)
def make_tables(pixels):
    index = np.arange(pixels)
    freq = np.where(index < pixels // 2, index, index - pixels) / pixels
    spread = index[:, None] - index[None, :]
    phase = 2.0 * math.pi * freq * spread[:, :, None] - math.pi * FRESNEL * freq * freq
    propagator = np.mean(np.exp(1j * phase), axis=-1)
    turns = index[:, None] * index[None, :] % pixels
    fourier = np.exp(-2j * math.pi * turns / pixels) / math.sqrt(pixels)
    blocks = np.stack([real_blocks(propagator), real_blocks(fourier)]).astype(np.float32)
    high = blocks.astype(ml_dtypes.bfloat16)
    low = (blocks - high.astype(np.float32)).astype(ml_dtypes.bfloat16)
    return np.stack([high, low], axis=2)


def halves(x):
    high = x.astype(BF16)
    return high, (x - high.astype(F32)).astype(BF16)


def dot(a, b):
    return jnp.dot(a, b, preferred_element_type=F32)


def transform(left, right, fields):
    size = fields[0][0].shape[0]
    mids = []
    for high, low in [halves(jnp.concatenate(field, axis=0)) for field in fields]:
        both = dot(left[0], jnp.concatenate([high, low], axis=1))
        mids.append(both[:, :size] + (both[:, size:] + dot(left[1], high)))
    outs = []
    for high, low in [halves(jnp.concatenate([mid[:size], mid[size:]], axis=1)) for mid in mids]:
        both = dot(jnp.concatenate([high, low], axis=0), right[0])
        outs.append(both[:size] + (both[size:] + dot(high, right[1])))
    return [(out[:, :size], out[:, size:]) for out in outs]


def times(a, b):
    return a[0] * b[0] - a[1] * b[1], a[0] * b[1] + a[1] * b[0]


def times_conj(a, b):
    return a[0] * b[0] + a[1] * b[1], a[1] * b[0] - a[0] * b[1]


class Layout:
    def __init__(self, probes, count, layers, pixels, rows, height, width, only_sums=False):
        self.probes, self.count, self.layers, self.pixels = probes, count, layers, pixels
        self.groups = probes // count
        self.tall = pixels + 8
        self.rows, self.height, self.width = rows, height, width
        self.blocks = width // pixels
        self.deep = rows + 2 * self.tall
        self.column_bits = (width - 1).bit_length()
        self.name_bits = (4 * probes - 1).bit_length()
        self.stack = probes * layers * 2 * pixels
        self.seen_from = self.stack
        self.grads_from = 2 * self.stack
        self.frames_from = 3 * self.stack
        self.total_from = 0 if only_sums else self.frames_from + probes * pixels
        self.shape = (self.total_from + 2 * layers * self.blocks * self.deep, pixels)

    def stacked(self, group, i, layer, part):
        probe = group * self.count + i
        return ((probe * self.layers + layer) * 2 + part) * self.pixels

    def tile(self, start):
        return pl.ds(pl.multiple_of(start, 8), self.pixels)

    def patch(self, group, i, layer, part):
        return self.tile(self.stacked(group, i, layer, part))

    def seen(self, group, i, layer, part):
        return self.tile(self.seen_from + self.stacked(group, i, layer, part))

    def grad(self, group, i, layer, part):
        return self.tile(self.grads_from + self.stacked(group, i, layer, part))

    def grads_of(self, begin, end):
        each = self.stack // self.groups
        return self.grads_from + begin * each, self.grads_from + end * each

    def frame(self, group, i):
        return self.tile(self.frames_from + (group * self.count + i) * self.pixels)

    def total(self, part, layer, block, row):
        block = (part * self.layers + layer) * self.blocks + block
        return self.total_from + block * self.deep + row

    def pack(self, row, column, name):
        return (((row << self.column_bits) + column) << self.name_bits) + name

    def row(self, key):
        return key >> (self.column_bits + self.name_bits)

    def window(self, info, probe, whose=0):
        lane = lax.broadcasted_iota(jnp.int32, info.shape, 1)
        key = jnp.sum(jnp.where(lane == probe + whose * self.probes, info[...], 0))
        row = self.row(key)
        column = (key >> self.name_bits) & ((1 << self.column_bits) - 1)
        row0 = jnp.minimum(row // 8 * 8, self.height - self.tall)
        block = jnp.minimum(column // self.pixels, self.blocks - 2)
        return row0, row - row0, block, column - block * self.pixels


def call(lay, body, state, before, outs, scratch=(), flag=False, flops=1000, moved=1000, name=None):
    spaces = {"hbm": (HBM, in_hbm), "vmem": (VMEM, in_vmem), "smem": (SMEM, lambda x: x)}
    specs = [spaces[kind][0] for kind, _ in before]
    operands = [spaces[kind][1](x) for kind, x in before]
    at = len(before)
    aliases = {}
    if state is not None:
        specs.append(VMEM)
        operands.append(in_vmem(state))
        aliases = {at: 0}

    def kernel(*refs):
        body(*refs[:at], *refs[at + len(aliases) :])

    return pl.pallas_call(
        kernel,
        in_specs=specs,
        out_specs=[VMEM] * (1 + len(outs) + flag),
        out_shape=[pltpu.VMEM(shape, F32) for shape in (lay.shape, *outs)]
        + [pltpu.VMEM((1, 128), jnp.int32)] * flag,
        scratch_shapes=list(scratch),
        input_output_aliases=aliases,
        compiler_params=pltpu.CompilerParams(vmem_limit_bytes=SCOPED),
        cost_estimate=pl.CostEstimate(flops=flops, bytes_accessed=moved, transcendentals=0),
        name=name,
    )(*operands)


def clear_total(lay, state):
    start = lay.total_from

    def body(state):
        state[pl.ds(start, lay.shape[0] - start), :] = jnp.zeros((lay.shape[0] - start, lay.pixels), F32)

    return call(lay, body, state, [], [], name="clear_total")[0]


def place_frames(lay, sections, info, everyone, pools, state):
    def body(info, everyone, *refs):
        *pools, state, late, sems = refs
        nearest = 3 * lay.probes
        reach = jnp.bool_(False)
        for ref in (info, everyone):
            reach |= lay.row(ref[0, nearest]) + lay.pixels > lay.rows
            reach |= lay.row(ref[0, nearest + 1]) < lay.rows
        late[...] = jnp.full(late.shape, reach.astype(jnp.int32), jnp.int32)
        lat, side = lax.axis_index("lat"), lax.axis_index("probe")

        @pl.when(lax.axis_index("depth") == sections - 1)
        def _():
            for act in ("start", "wait"):
                for probe in range(lay.probes):
                    name = info[0, probe] & ((1 << lay.name_bits) - 1)
                    owner = name // lay.probes
                    slot = name % lay.probes
                    if len(pools) > 1:
                        slot += ((owner // 2) ^ side) * lay.probes + ((owner % 2) ^ lat) * 2 * lay.probes
                    first = 0
                    for pool in pools:
                        size = pool.shape[0] // lay.pixels

                        @pl.when((slot >= first) & (slot < first + size))
                        def _(pool=pool, first=first, probe=probe, slot=slot):
                            copy = pltpu.make_async_copy(
                                pool.at[lay.tile((slot - first) * lay.pixels), :],
                                state.at[lay.frame(0, probe), :],
                                sems.at[probe],
                            )
                            getattr(copy, act)()

                        first += size

    pools = [pool.reshape((-1, lay.pixels)) for pool in pools]
    pools = [("hbm", pools[0]), *(("vmem", pool) for pool in pools[1:])]
    return call(
        lay,
        body,
        state,
        [("smem", info), ("smem", everyone), *pools],
        [],
        flag=True,
        scratch=[pltpu.SemaphoreType.DMA((lay.probes,))],
        name="place_frames",
    )


def cut_patches(lay, info, own, other, state, begin, end, from_hbm=False):
    half = own.shape[2]
    tall, pixels = lay.tall, lay.pixels

    def one(probe, info, own, other, state, window, sem):
        row0, down, block, shift = lay.window(info, probe)
        own_top = lax.axis_index("lat") == 0
        near_at = pl.ds(pl.multiple_of(block * pixels, pixels), pixels)
        far_at = pl.ds(pl.multiple_of((block + 1) * pixels, pixels), pixels)
        for source, is_top in ((own, own_top), (other, jnp.logical_not(own_top))):
            start = jnp.clip(row0 - jnp.where(is_top, 0, half), 0, half - tall)
            to = pl.ds(pl.multiple_of(jnp.where(is_top, 0, tall), 8), tall)
            rows = pl.ds(pl.multiple_of(start, 8), tall)

            @pl.when(jnp.where(is_top, row0 < half, row0 + tall > half))
            def _(source=source, rows=rows, to=to):
                if source is own and from_hbm:
                    both = pl.ds(pl.multiple_of(block * pixels, pixels), 2 * pixels)
                    copy = pltpu.make_async_copy(source.at[:, :, rows, both], window.at[:, :, to, :], sem)
                    copy.start()
                    copy.wait()
                    return
                for part in range(2):
                    for layer in range(lay.layers):
                        window[part, layer, to, 0:pixels] = source[part, layer, rows, near_at]
                        window[part, layer, to, pixels : 2 * pixels] = source[part, layer, rows, far_at]

        offset = jnp.where(row0 < half, jnp.maximum(row0 - (half - tall), 0), tall)
        rows = pl.ds(pl.multiple_of(offset, 8), tall)
        turn = (pixels - shift) % pixels
        lane = lax.broadcasted_iota(jnp.int32, (tall, pixels), 1)
        for part in range(2):
            for layer in range(lay.layers):
                near = pltpu.roll(window[part, layer, rows, 0:pixels], turn, 1)
                far = pltpu.roll(window[part, layer, rows, pixels : 2 * pixels], turn, 1)
                patch = jnp.where(lane < pixels - shift, near, far)
                patch = pltpu.roll(patch, (tall - down) % tall, 0)[:pixels]
                state[lay.patch(0, probe, layer, part), :] = patch

    def body(info, *refs):
        section = lax.axis_index("depth")
        bounds = [x(section) if callable(x) else x for x in (begin, end)]
        lax.fori_loop(*bounds, lambda probe, _: one(probe, info, *refs) or 0, 0)

    return call(
        lay,
        body,
        state,
        [("vmem", info), ("hbm" if from_hbm else "vmem", own), ("vmem", other)],
        [],
        scratch=[pltpu.VMEM((2, lay.layers, 2 * tall, 2 * pixels), F32), pltpu.SemaphoreType.DMA(())],
        name="cut_patches",
    )[0]


def section_cost(lay):
    size = lay.count * lay.pixels**2
    return dict(flops=lay.layers * 2 * 3 * 8 * size * lay.pixels, moved=(lay.layers * 2 + 4) * 8 * size)


def pair(ref, at):
    return ref[at(0), :], ref[at(1), :]


def run_forward(lay, tick, sections, tables, state, arrived, start_wave):
    def body(tables, *refs):
        arrived_ref = refs[0] if arrived is not None else None
        start_ref = refs[-3] if start_wave is not None else None
        state, leave = refs[-2:]
        section = lax.axis_index("depth")
        group = tick - section
        final = (section == sections - 1).astype(jnp.int32)

        @pl.when((group >= 0) & (group < lay.groups))
        def _():
            wave = []
            for i in range(lay.count):
                if arrived is None:
                    wave.append((start_ref[0], start_ref[1]))
                elif start_wave is None:
                    wave.append((arrived_ref[i, 0], arrived_ref[i, 1]))
                else:
                    wave.append(
                        tuple(jnp.where(section == 0, start_ref[p], arrived_ref[i, p]) for p in range(2))
                    )
            for layer in range(lay.layers):
                chi = []
                for i in range(lay.count):
                    for part in range(2):
                        state[lay.seen(group, i, layer, part), :] = wave[i][part]
                    chi.append(times(pair(state, functools.partial(lay.patch, group, i, layer)), wave[i]))
                at = final if layer == lay.layers - 1 else 0
                wave = transform((tables[at, 0, 0], tables[at, 0, 1]), (tables[at, 1, 0], tables[at, 1, 1]), chi)
            for i in range(lay.count):
                real, imag = wave[i]
                misfit = real * real + imag * imag - state[lay.frame(group, i), :]
                factor = jnp.where(final == 1, misfit, 1.0)
                leave[i, 0] = real * factor
                leave[i, 1] = imag * factor

    waves = [("vmem", x) for x in (arrived, start_wave) if x is not None]
    return call(
        lay,
        body,
        state,
        [("vmem", tables), *waves],
        [(lay.count, 2, lay.pixels, lay.pixels)],
        name="forward_section",
        **section_cost(lay),
    )


def run_backward(lay, tick, sections, tables, state, arrived, own):
    def body(tables, *refs):
        arrived_ref = refs[0] if arrived is not None else None
        own_ref = refs[1 if arrived is not None else 0] if own is not None else None
        state, leave = refs[-2:]
        section = lax.axis_index("depth")
        group = tick - (2 * (sections - 1) - section)
        final = (section == sections - 1).astype(jnp.int32)

        @pl.when((group >= 0) & (group < lay.groups))
        def _():
            wave = []
            for i in range(lay.count):
                if arrived is None:
                    wave.append((own_ref[i, 0], own_ref[i, 1]))
                elif own is None:
                    wave.append((arrived_ref[i, 0], arrived_ref[i, 1]))
                else:
                    wave.append(
                        tuple(jnp.where(final == 1, own_ref[i, p], arrived_ref[i, p]) for p in range(2))
                    )
            for layer in reversed(range(lay.layers)):
                at = final if layer == lay.layers - 1 else 0
                chi = transform((tables[at, 1, 0], tables[at, 1, 1]), (tables[at, 0, 0], tables[at, 0, 1]), wave)
                wave = []
                for i in range(lay.count):
                    real, imag = times_conj(chi[i], pair(state, functools.partial(lay.seen, group, i, layer)))
                    state[lay.grad(group, i, layer, 0), :] = real
                    state[lay.grad(group, i, layer, 1), :] = imag
                    wave.append(times_conj(chi[i], pair(state, functools.partial(lay.patch, group, i, layer))))
            for i in range(lay.count):
                leave[i, 0] = wave[i][0]
                leave[i, 1] = wave[i][1]

    waves = [("vmem", x) for x in (arrived, own) if x is not None]
    return call(
        lay,
        body,
        state,
        [("vmem", tables), *waves],
        [(lay.count, 2, lay.pixels, lay.pixels)],
        name="backward_section",
        **section_cost(lay),
    )


def deposit(lay, tick, sections, info, received, state):
    pixels, tall = lay.pixels, lay.tall

    def body(info, *refs):
        state = refs[-1]
        lane = lax.broadcasted_iota(jnp.int32, (tall, pixels), 1)
        blank = jnp.zeros((8, pixels), F32)
        base = lax.axis_index("probe") * lay.rows if lay.rows < lay.height else 0

        def add(probe, whose, active, load):
            row0, down, block, shift = lay.window(info, probe, whose)
            start = row0 - base + tall

            @pl.when(active & (start > 0) & (start < lay.rows + tall))
            def _():
                for layer in range(lay.layers):
                    for part in range(2):
                        padded = jnp.concatenate([load(layer, part), blank], axis=0)
                        turned = pltpu.roll(pltpu.roll(padded, down, 0), shift % pixels, 1)
                        near = pl.ds(pl.multiple_of(lay.total(part, layer, block, start), 8), tall)
                        far = pl.ds(pl.multiple_of(lay.total(part, layer, block + 1, start), 8), tall)
                        state[near, :] += jnp.where(lane >= shift, turned, 0.0)
                        state[far, :] += jnp.where(lane >= shift, 0.0, turned)

        if tick is not None:
            group = tick - (2 * (sections - 1) - lax.axis_index("depth"))
            active = (group >= 0) & (group < lay.groups)
            group = jnp.clip(group, 0, lay.groups - 1)
            for i in range(lay.count):
                add(
                    group * lay.count + i,
                    0,
                    active,
                    lambda layer, part, i=i: state[lay.grad(group, i, layer, part), :],
                )
        for ref, (first, whose, grads) in zip(refs, received):

            def one(i, _, ref=ref, first=first, whose=whose):
                add(
                    first * lay.count + i,
                    whose,
                    True,
                    lambda layer, part: ref[lay.patch(0, i, layer, part), :],
                )
                return 0

            lax.fori_loop(0, grads.shape[0] // (lay.layers * 2 * pixels), one, 0)

    return call(
        lay,
        body,
        state,
        [("vmem", info)] + [("vmem", grads) for *_, grads in received],
        [],
        name="deposit_patches",
    )[0]


def split_rows(lay, state, owners, taken=(0, 8)):
    rows = lay.rows // (2 * owners)
    pieces = 4 * owners * lay.layers * lay.blocks

    def body(state, keep, send, rest, sems):
        lat = lax.axis_index("lat")
        copies = [pltpu.make_async_copy(state.at[pl.ds(taken[0], taken[1] - taken[0]), :], rest, sems.at[pieces])]
        for owner in range(owners):
            for kind, target in ((lat, keep), (1 - lat, send)):
                for part in range(2):
                    for layer in range(lay.layers):
                        for block in range(lay.blocks):
                            start = lay.total(part, layer, block, lay.tall + (2 * owner + kind) * rows)
                            copies.append(
                                pltpu.make_async_copy(
                                    state.at[pl.ds(pl.multiple_of(start, 8), rows), :],
                                    target.at[part, layer, owner, :, pl.ds(block * lay.pixels, lay.pixels)],
                                    sems.at[len(copies) - 1],
                                )
                            )
        for copy in copies:
            copy.start()
        for copy in copies:
            copy.wait()

    half = (2, lay.layers, owners, rows, lay.width)
    return pl.pallas_call(
        body,
        in_specs=[VMEM],
        out_specs=[VMEM, VMEM, HBM],
        out_shape=[
            pltpu.VMEM(half, F32),
            pltpu.VMEM(half, F32),
            pltpu.HBM((taken[1] - taken[0], lay.pixels), F32),
        ],
        scratch_shapes=[pltpu.SemaphoreType.DMA((pieces + 1,))],
        compiler_params=pltpu.CompilerParams(vmem_limit_bytes=SCOPED),
        name="split_rows",
    )(in_vmem(state))


def add_up(a, b):
    each = pl.BlockSpec((1, 1, *a.shape[2:]), lambda i, j: (i, j, 0, 0, 0))

    def body(a, b, out):
        out[...] = a[...] + b[...]

    return pl.pallas_call(
        body,
        grid=a.shape[:2],
        in_specs=[each, each],
        out_specs=each,
        out_shape=pltpu.HBM(a.shape, F32),
        compiler_params=pltpu.CompilerParams(vmem_limit_bytes=SCOPED),
        name="add_up",
    )(a, b)


def swap(shard, axis):
    return lax.ppermute(shard, axis, [(0, 1), (1, 0)])


def sort_probes(lay, early, positions, indices):
    n = lay.probes
    total = 4 * n

    def body(listed, *refs):
        *scans, info, positions, sem = refs
        copy = pltpu.make_async_copy(listed, positions, sem)
        copy.start()
        copy.wait()
        lat, side = lax.axis_index("lat"), lax.axis_index("probe")
        lane = lax.broadcasted_iota(jnp.int32, (1, 128), 1)
        at = lax.broadcasted_iota(jnp.int32, (total, 128), 0)
        across = jnp.full((1, 128), jnp.iinfo(jnp.int32).max, jnp.int32)
        down = jnp.zeros((total, 128), jnp.int32)
        for which, scan in enumerate(scans):
            owner = (side ^ (which % 2)) * 2 + (lat ^ (which // 2))
            for i in range(n):
                place = scan[i]
                key = lay.pack(positions[0, place], positions[1, place], owner * n + i)
                across = jnp.where(lane == which * n + i, key, across)
                down = jnp.where(at == which * n + i, key, down)
        rank = jnp.sum((across < down).astype(jnp.int32), axis=1, keepdims=True)
        whose = lane // n
        order = 2 * (lane % n) + jnp.where(whose == 2, 1 - lat, lat)
        wanted = jnp.where(jnp.where(whose == 1, 1 - side, side) == 0, 2 * n - 1 - order, 2 * n + order)
        reach = 2 * early * lay.count
        wanted = jnp.where(lane == 3 * n, 2 * n - 1 - reach, wanted)
        wanted = jnp.where(lane == 3 * n + 1, 2 * n + reach, wanted)
        wanted = jnp.where(lane > 3 * n + 1, -1, wanted)
        info[...] = jnp.sum(jnp.where(rank == wanted, down, 0), axis=0, keepdims=True)

    return pl.pallas_call(
        body,
        in_specs=[HBM] + [SMEM] * 4,
        out_specs=VMEM,
        out_shape=pltpu.VMEM((1, 128), jnp.int32),
        scratch_shapes=[pltpu.SMEM(positions.T.shape, jnp.int32), pltpu.SemaphoreType.DMA(())],
        compiler_params=pltpu.CompilerParams(vmem_limit_bytes=SCOPED),
        name="sort_probes",
    )(in_hbm(positions.T), *indices)


def bring(x):
    def body(x, out, sem):
        copy = pltpu.make_async_copy(x, out, sem)
        copy.start()
        copy.wait()

    return pl.pallas_call(
        body,
        in_specs=[HBM],
        out_specs=VMEM,
        out_shape=pltpu.VMEM(x.shape, x.dtype),
        scratch_shapes=[pltpu.SemaphoreType.DMA(())],
        compiler_params=pltpu.CompilerParams(vmem_limit_bytes=SCOPED),
        cost_estimate=pl.CostEstimate(flops=1000, bytes_accessed=1000, transcendentals=0),
        name="bring",
    )(in_hbm(x))


def local(specimen, illumination, positions, scan_index, frames):
    pixels = illumination.shape[-1]
    _, layers, half, width = specimen.shape
    height = 2 * half
    tables = jnp.asarray(make_tables(pixels))
    sections = lax.axis_size("depth")
    owners = lax.axis_size("probe")
    paired = owners == 2 and lax.axis_size("groups") <= 2
    probes = scan_index.size
    count = 2 if probes % 4 == 0 else 1
    lay = Layout(probes, count, layers, pixels, half if paired else height, height, width)
    early = lay.groups // 2

    everyone = mine = None
    if paired:
        scan = scan_index.reshape(-1)
        beside = swap(scan, "lat")
        half_rows, beside = lax.optimization_barrier((specimen, beside))
        other = swap(half_rows, "lat")
        indices = [scan, swap(scan, "probe"), beside, swap(beside, "probe")]
        measured, *indices[1:] = lax.optimization_barrier((frames, *indices[1:]))
        end = sections - 1
        ends = [(2 * end, 2 * end + 1), (2 * end + 1, 2 * end)]
        mine = lax.ppermute(measured, ("depth", "probe"), ends)
        info = sort_probes(lay, early, positions, indices)
        everyone = swap(info, "groups") if lax.axis_size("groups") == 2 else info
    else:
        other = swap(specimen, "lat")
        corners = positions[scan_index.reshape(-1)]
        info = lay.pack(corners[:, 0], corners[:, 1], jnp.arange(probes, dtype=jnp.int32))
        info = everyone = jnp.pad(info, (0, 3 * probes))[None]
    state = cut_patches(lay, info, specimen, other, None, 0, count, from_hbm=True)
    def busy(tick, source, by):
        delay = source if by > 0 else 2 * (sections - 1) - source
        return 0 <= tick - delay < lay.groups

    def pass_on(wave, tick, by):
        pairs = [
            (source, source + by)
            for source in range(sections)
            if 0 <= source + by < sections and busy(tick, source, by)
        ]
        return lax.ppermute(wave, "depth", pairs) if pairs else None

    def grads_of(state, begin, end):
        begin, end = lay.grads_of(begin, end)
        return lax.slice_in_dim(state, begin, end)

    fill = sections - 1
    parts = [(0, early // 2), (early // 2, early)] if paired else []
    crossing = {}
    down = up = None
    def upto(group):
        early_sections = min(group, lay.groups) * count
        return lambda section: jnp.where(section < 2, early_sections, probes)

    cuts = {0: (count, upto(3)), 2: (upto(3), upto(5)), 4: (upto(5), probes)}
    last_tick = lay.groups + 2 * fill - 1
    for tick in range(lay.groups + 2 * fill):
        own = None
        if paired and tick == fill - 1:
            down, mine, everyone = lax.optimization_barrier((down, mine, everyone))
            crossed = [lax.ppermute(x, ("depth", "lat"), ends) for x in (frames, mine)]
        if tick < lay.groups + fill:
            start_wave = illumination if tick < lay.groups else None
            state, own = run_forward(lay, tick, sections, tables, state, down, start_wave)
            if tick == 0:
                own, specimen = lax.optimization_barrier((own, specimen))
                brought = bring(specimen)
            down = pass_on(own, tick, 1)
            if tick in cuts:
                state = cut_patches(lay, info, brought, other, state, *cuts[tick])
            if tick == 0:
                state = clear_total(lay, state)
            if tick == fill - 1:
                pools = [frames, mine, *crossed] if paired else [frames]
                state, late = place_frames(lay, sections, info, everyone, pools, state)
        if tick >= fill:
            state, rising = run_backward(lay, tick, sections, tables, state, up, own)
            up = pass_on(rising, tick, -1)
            received = crossing.pop(tick, [])
            for begin, end in parts:
                if tick == end - 1 + 2 * fill:
                    due = min(tick + CROSSING, last_tick - 1)
                    crossing.setdefault(due, []).append((begin, 1, swap(grads_of(state, begin, end), "probe")))
            state = deposit(lay, tick, sections, info, received, state)
    if not paired:
        keep, send, _ = split_rows(lay, state, owners)
        return lax.psum_scatter(keep + swap(send, "lat"), "probe", scatter_dimension=2, tiled=False)

    keep, send, late_grads = split_rows(lay, state, 1, lay.grads_of(early, lay.groups))

    def as_they_are(keep, received, grads):
        return add_up(keep, received)

    def with_partners(keep, received, grads):
        sums = Layout(probes, count, layers, pixels, half, height, width, only_sums=True)
        state = clear_total(sums, None)
        state = deposit(sums, None, sections, info, [(early, 1, swap(grads, "probe"))], state)
        more, send, _ = split_rows(sums, state, 1)
        return add_up(keep + more, received + swap(send, "lat"))

    result = lax.cond(late[0, 0] > 0, with_partners, as_they_are, keep, swap(send, "lat"), late_grads)
    return result[:, :, 0]


def solution(mesh):
    return jax.shard_map(
        local,
        mesh=mesh,
        in_specs=(
            P(None, ("groups", "depth"), "lat", None),
            P(),
            P("groups", None),
            P("groups", ("probe", "lat")),
            P("groups", ("probe", "lat"), None, None),
        ),
        out_specs=P(None, ("groups", "depth"), ("probe", "lat"), None),
        check_vma=False,
    )
```

```python
import functools
import math

import jax
import jax.numpy as jnp
import ml_dtypes
import numpy as np
from jax import lax
from jax.experimental import pallas as pl
from jax.experimental.pallas import tpu as pltpu
from jax.sharding import PartitionSpec as P

FRESNEL = 8.0
SCOPED = 8 << 20
CROSSING = 3
F32 = jnp.float32
BF16 = jnp.bfloat16
HBM = pl.BlockSpec(memory_space=pl.ANY)
VMEM = pl.BlockSpec(memory_space=pltpu.VMEM)
SMEM = pl.BlockSpec(memory_space=pltpu.SMEM)


def in_hbm(x):
    return pltpu.with_memory_space_constraint(x, pltpu.HBM)


def in_vmem(x):
    return pltpu.with_memory_space_constraint(x, pltpu.VMEM)


def real_blocks(matrix):
    real, imag = matrix.real, matrix.imag
    left = np.block([[real, -imag], [imag, real]])
    right = np.block([[real, imag], [-imag, real]])
    return np.stack([left, right])


@functools.lru_cache(maxsize=None)
def make_tables(pixels):
    index = np.arange(pixels)
    freq = np.where(index < pixels // 2, index, index - pixels) / pixels
    spread = index[:, None] - index[None, :]
    phase = 2.0 * math.pi * freq * spread[:, :, None] - math.pi * FRESNEL * freq * freq
    propagator = np.mean(np.exp(1j * phase), axis=-1)
    turns = index[:, None] * index[None, :] % pixels
    fourier = np.exp(-2j * math.pi * turns / pixels) / math.sqrt(pixels)
    blocks = np.stack([real_blocks(propagator), real_blocks(fourier)]).astype(np.float32)
    high = blocks.astype(ml_dtypes.bfloat16)
    low = (blocks - high.astype(np.float32)).astype(ml_dtypes.bfloat16)
    return np.stack([high, low], axis=2)


def halves(x):
    high = x.astype(BF16)
    return high, (x - high.astype(F32)).astype(BF16)


def dot(a, b):
    return jnp.dot(a, b, preferred_element_type=F32)


def transform(left, right, fields):
    size = fields[0][0].shape[0]
    mids = []
    for high, low in [halves(jnp.concatenate(field, axis=0)) for field in fields]:
        both = dot(left[0], jnp.concatenate([high, low], axis=1))
        mids.append(both[:, :size] + (both[:, size:] + dot(left[1], high)))
    outs = []
    for high, low in [halves(jnp.concatenate([mid[:size], mid[size:]], axis=1)) for mid in mids]:
        both = dot(jnp.concatenate([high, low], axis=0), right[0])
        outs.append(both[:size] + (both[size:] + dot(high, right[1])))
    return [(out[:, :size], out[:, size:]) for out in outs]


def times(a, b):
    return a[0] * b[0] - a[1] * b[1], a[0] * b[1] + a[1] * b[0]


def times_conj(a, b):
    return a[0] * b[0] + a[1] * b[1], a[1] * b[0] - a[0] * b[1]


class Layout:
    def __init__(self, probes, count, layers, pixels, rows, height, width, only_sums=False):
        self.probes, self.count, self.layers, self.pixels = probes, count, layers, pixels
        self.groups = probes // count
        self.tall = pixels + 8
        self.rows, self.height, self.width = rows, height, width
        self.blocks = width // pixels
        self.deep = rows + 2 * self.tall
        self.column_bits = (width - 1).bit_length()
        self.name_bits = (4 * probes - 1).bit_length()
        self.stack = probes * layers * 2 * pixels
        self.seen_from = self.stack
        self.grads_from = 2 * self.stack
        self.frames_from = 3 * self.stack
        self.total_from = 0 if only_sums else self.frames_from + probes * pixels
        self.shape = (self.total_from + 2 * layers * self.blocks * self.deep, pixels)

    def stacked(self, group, i, layer, part):
        probe = group * self.count + i
        return ((probe * self.layers + layer) * 2 + part) * self.pixels

    def tile(self, start):
        return pl.ds(pl.multiple_of(start, 8), self.pixels)

    def patch(self, group, i, layer, part):
        return self.tile(self.stacked(group, i, layer, part))

    def seen(self, group, i, layer, part):
        return self.tile(self.seen_from + self.stacked(group, i, layer, part))

    def grad(self, group, i, layer, part):
        return self.tile(self.grads_from + self.stacked(group, i, layer, part))

    def grads_of(self, begin, end):
        each = self.stack // self.groups
        return self.grads_from + begin * each, self.grads_from + end * each

    def frame(self, group, i):
        return self.tile(self.frames_from + (group * self.count + i) * self.pixels)

    def total(self, part, layer, block, row):
        block = (part * self.layers + layer) * self.blocks + block
        return self.total_from + block * self.deep + row

    def pack(self, row, column, name):
        return (((row << self.column_bits) + column) << self.name_bits) + name

    def row(self, key):
        return key >> (self.column_bits + self.name_bits)

    def window(self, info, probe, whose=0):
        lane = lax.broadcasted_iota(jnp.int32, info.shape, 1)
        key = jnp.sum(jnp.where(lane == probe + whose * self.probes, info[...], 0))
        row = self.row(key)
        column = (key >> self.name_bits) & ((1 << self.column_bits) - 1)
        row0 = jnp.minimum(row // 8 * 8, self.height - self.tall)
        block = jnp.minimum(column // self.pixels, self.blocks - 2)
        return row0, row - row0, block, column - block * self.pixels


def call(lay, body, state, before, outs, scratch=(), flag=False, flops=1000, moved=1000, name=None):
    spaces = {"hbm": (HBM, in_hbm), "vmem": (VMEM, in_vmem), "smem": (SMEM, lambda x: x)}
    specs = [spaces[kind][0] for kind, _ in before]
    operands = [spaces[kind][1](x) for kind, x in before]
    at = len(before)
    aliases = {}
    if state is not None:
        specs.append(VMEM)
        operands.append(in_vmem(state))
        aliases = {at: 0}

    def kernel(*refs):
        body(*refs[:at], *refs[at + len(aliases) :])

    return pl.pallas_call(
        kernel,
        in_specs=specs,
        out_specs=[VMEM] * (1 + len(outs) + flag),
        out_shape=[pltpu.VMEM(shape, F32) for shape in (lay.shape, *outs)]
        + [pltpu.VMEM((1, 128), jnp.int32)] * flag,
        scratch_shapes=list(scratch),
        input_output_aliases=aliases,
        compiler_params=pltpu.CompilerParams(vmem_limit_bytes=SCOPED),
        cost_estimate=pl.CostEstimate(flops=flops, bytes_accessed=moved, transcendentals=0),
        name=name,
    )(*operands)


def clear_total(lay, state):
    start = lay.total_from

    def body(state):
        state[pl.ds(start, lay.shape[0] - start), :] = jnp.zeros((lay.shape[0] - start, lay.pixels), F32)

    return call(lay, body, state, [], [], name="clear_total")[0]


def place_frames(lay, sections, info, everyone, pools, state):
    def body(info, everyone, *refs):
        *pools, state, late, sems = refs
        nearest = 3 * lay.probes
        reach = jnp.bool_(False)
        for ref in (info, everyone):
            reach |= lay.row(ref[0, nearest]) + lay.pixels > lay.rows
            reach |= lay.row(ref[0, nearest + 1]) < lay.rows
        late[...] = jnp.full(late.shape, reach.astype(jnp.int32), jnp.int32)
        lat, side = lax.axis_index("lat"), lax.axis_index("probe")

        @pl.when(lax.axis_index("depth") == sections - 1)
        def _():
            for act in ("start", "wait"):
                for probe in range(lay.probes):
                    name = info[0, probe] & ((1 << lay.name_bits) - 1)
                    owner = name // lay.probes
                    slot = name % lay.probes
                    if len(pools) > 1:
                        slot += ((owner // 2) ^ side) * lay.probes + ((owner % 2) ^ lat) * 2 * lay.probes
                    first = 0
                    for pool in pools:
                        size = pool.shape[0] // lay.pixels

                        @pl.when((slot >= first) & (slot < first + size))
                        def _(pool=pool, first=first, probe=probe, slot=slot):
                            copy = pltpu.make_async_copy(
                                pool.at[lay.tile((slot - first) * lay.pixels), :],
                                state.at[lay.frame(0, probe), :],
                                sems.at[probe],
                            )
                            getattr(copy, act)()

                        first += size

    pools = [pool.reshape((-1, lay.pixels)) for pool in pools]
    pools = [("hbm", pools[0]), *(("vmem", pool) for pool in pools[1:])]
    return call(
        lay,
        body,
        state,
        [("smem", info), ("smem", everyone), *pools],
        [],
        flag=True,
        scratch=[pltpu.SemaphoreType.DMA((lay.probes,))],
        name="place_frames",
    )


def cut_patches(lay, info, own, other, state, begin, end, from_hbm=False):
    half = own.shape[2]
    tall, pixels = lay.tall, lay.pixels

    def one(probe, info, own, other, state, window, sem):
        row0, down, block, shift = lay.window(info, probe)
        own_top = lax.axis_index("lat") == 0
        near_at = pl.ds(pl.multiple_of(block * pixels, pixels), pixels)
        far_at = pl.ds(pl.multiple_of((block + 1) * pixels, pixels), pixels)
        for source, is_top in ((own, own_top), (other, jnp.logical_not(own_top))):
            start = jnp.clip(row0 - jnp.where(is_top, 0, half), 0, half - tall)
            to = pl.ds(pl.multiple_of(jnp.where(is_top, 0, tall), 8), tall)
            rows = pl.ds(pl.multiple_of(start, 8), tall)

            @pl.when(jnp.where(is_top, row0 < half, row0 + tall > half))
            def _(source=source, rows=rows, to=to):
                if source is own and from_hbm:
                    both = pl.ds(pl.multiple_of(block * pixels, pixels), 2 * pixels)
                    copy = pltpu.make_async_copy(source.at[:, :, rows, both], window.at[:, :, to, :], sem)
                    copy.start()
                    copy.wait()
                    return
                for part in range(2):
                    for layer in range(lay.layers):
                        window[part, layer, to, 0:pixels] = source[part, layer, rows, near_at]
                        window[part, layer, to, pixels : 2 * pixels] = source[part, layer, rows, far_at]

        offset = jnp.where(row0 < half, jnp.maximum(row0 - (half - tall), 0), tall)
        rows = pl.ds(pl.multiple_of(offset, 8), tall)
        turn = (pixels - shift) % pixels
        lane = lax.broadcasted_iota(jnp.int32, (tall, pixels), 1)
        for part in range(2):
            for layer in range(lay.layers):
                near = pltpu.roll(window[part, layer, rows, 0:pixels], turn, 1)
                far = pltpu.roll(window[part, layer, rows, pixels : 2 * pixels], turn, 1)
                patch = jnp.where(lane < pixels - shift, near, far)
                patch = pltpu.roll(patch, (tall - down) % tall, 0)[:pixels]
                state[lay.patch(0, probe, layer, part), :] = patch

    def body(info, *refs):
        section = lax.axis_index("depth")
        bounds = [x(section) if callable(x) else x for x in (begin, end)]
        lax.fori_loop(*bounds, lambda probe, _: one(probe, info, *refs) or 0, 0)

    return call(
        lay,
        body,
        state,
        [("vmem", info), ("hbm" if from_hbm else "vmem", own), ("vmem", other)],
        [],
        scratch=[pltpu.VMEM((2, lay.layers, 2 * tall, 2 * pixels), F32), pltpu.SemaphoreType.DMA(())],
        name="cut_patches",
    )[0]


def section_cost(lay):
    size = lay.count * lay.pixels**2
    return dict(flops=lay.layers * 2 * 3 * 8 * size * lay.pixels, moved=(lay.layers * 2 + 4) * 8 * size)


def pair(ref, at):
    return ref[at(0), :], ref[at(1), :]


def run_forward(lay, tick, sections, tables, state, arrived, start_wave):
    def body(tables, *refs):
        arrived_ref = refs[0] if arrived is not None else None
        start_ref = refs[-3] if start_wave is not None else None
        state, leave = refs[-2:]
        section = lax.axis_index("depth")
        group = tick - section
        final = (section == sections - 1).astype(jnp.int32)

        @pl.when((group >= 0) & (group < lay.groups))
        def _():
            wave = []
            for i in range(lay.count):
                if arrived is None:
                    wave.append((start_ref[0], start_ref[1]))
                elif start_wave is None:
                    wave.append((arrived_ref[i, 0], arrived_ref[i, 1]))
                else:
                    wave.append(
                        tuple(jnp.where(section == 0, start_ref[p], arrived_ref[i, p]) for p in range(2))
                    )
            for layer in range(lay.layers):
                chi = []
                for i in range(lay.count):
                    for part in range(2):
                        state[lay.seen(group, i, layer, part), :] = wave[i][part]
                    chi.append(times(pair(state, functools.partial(lay.patch, group, i, layer)), wave[i]))
                at = final if layer == lay.layers - 1 else 0
                wave = transform((tables[at, 0, 0], tables[at, 0, 1]), (tables[at, 1, 0], tables[at, 1, 1]), chi)
            for i in range(lay.count):
                real, imag = wave[i]
                misfit = real * real + imag * imag - state[lay.frame(group, i), :]
                factor = jnp.where(final == 1, misfit, 1.0)
                leave[i, 0] = real * factor
                leave[i, 1] = imag * factor

    waves = [("vmem", x) for x in (arrived, start_wave) if x is not None]
    return call(
        lay,
        body,
        state,
        [("vmem", tables), *waves],
        [(lay.count, 2, lay.pixels, lay.pixels)],
        name="forward_section",
        **section_cost(lay),
    )


def run_backward(lay, tick, sections, tables, state, arrived, own, passes_on=True):
    def body(tables, *refs):
        arrived_ref = refs[0] if arrived is not None else None
        own_ref = refs[1 if arrived is not None else 0] if own is not None else None
        state, leave = refs[-2:] if passes_on else (refs[-1], None)
        section = lax.axis_index("depth")
        group = tick - (2 * (sections - 1) - section)
        final = (section == sections - 1).astype(jnp.int32)

        @pl.when((group >= 0) & (group < lay.groups))
        def _():
            wave = []
            for i in range(lay.count):
                if arrived is None:
                    wave.append((own_ref[i, 0], own_ref[i, 1]))
                elif own is None:
                    wave.append((arrived_ref[i, 0], arrived_ref[i, 1]))
                else:
                    wave.append(
                        tuple(jnp.where(final == 1, own_ref[i, p], arrived_ref[i, p]) for p in range(2))
                    )
            for layer in reversed(range(lay.layers)):
                at = final if layer == lay.layers - 1 else 0
                chi = transform((tables[at, 1, 0], tables[at, 1, 1]), (tables[at, 0, 0], tables[at, 0, 1]), wave)
                wave = []
                for i in range(lay.count):
                    real, imag = times_conj(chi[i], pair(state, functools.partial(lay.seen, group, i, layer)))
                    state[lay.grad(group, i, layer, 0), :] = real
                    state[lay.grad(group, i, layer, 1), :] = imag
                    wave.append(times_conj(chi[i], pair(state, functools.partial(lay.patch, group, i, layer))))
            for i in range(lay.count if passes_on else 0):
                leave[i, 0] = wave[i][0]
                leave[i, 1] = wave[i][1]

    waves = [("vmem", x) for x in (arrived, own) if x is not None]
    return call(
        lay,
        body,
        state,
        [("vmem", tables), *waves],
        [(lay.count, 2, lay.pixels, lay.pixels)] * passes_on,
        name="backward_section",
        **section_cost(lay),
    )


def deposit(lay, tick, sections, info, received, state):
    pixels, tall = lay.pixels, lay.tall

    def body(info, *refs):
        state = refs[-1]
        lane = lax.broadcasted_iota(jnp.int32, (tall, pixels), 1)
        blank = jnp.zeros((8, pixels), F32)
        base = lax.axis_index("probe") * lay.rows if lay.rows < lay.height else 0

        def add(probe, whose, active, load):
            row0, down, block, shift = lay.window(info, probe, whose)
            start = row0 - base + tall

            @pl.when(active & (start > 0) & (start < lay.rows + tall))
            def _():
                for layer in range(lay.layers):
                    for part in range(2):
                        padded = jnp.concatenate([load(layer, part), blank], axis=0)
                        turned = pltpu.roll(pltpu.roll(padded, down, 0), shift % pixels, 1)
                        near = pl.ds(pl.multiple_of(lay.total(part, layer, block, start), 8), tall)
                        far = pl.ds(pl.multiple_of(lay.total(part, layer, block + 1, start), 8), tall)
                        state[near, :] += jnp.where(lane >= shift, turned, 0.0)
                        state[far, :] += jnp.where(lane >= shift, 0.0, turned)

        if tick is not None:
            group = tick - (2 * (sections - 1) - lax.axis_index("depth"))
            active = (group >= 0) & (group < lay.groups)
            group = jnp.clip(group, 0, lay.groups - 1)
            for i in range(lay.count):
                add(
                    group * lay.count + i,
                    0,
                    active,
                    lambda layer, part, i=i: state[lay.grad(group, i, layer, part), :],
                )
        for ref, (first, whose, grads) in zip(refs, received):

            def one(i, _, ref=ref, first=first, whose=whose):
                add(
                    first * lay.count + i,
                    whose,
                    True,
                    lambda layer, part: ref[lay.patch(0, i, layer, part), :],
                )
                return 0

            lax.fori_loop(0, grads.shape[0] // (lay.layers * 2 * pixels), one, 0)

    return call(
        lay,
        body,
        state,
        [("vmem", info)] + [("vmem", grads) for *_, grads in received],
        [],
        name="deposit_patches",
    )[0]


def split_rows(lay, state, owners, others, taken=None):
    rows = lay.rows // (2 * owners)
    pieces = 2 * owners * lay.layers * lay.blocks
    half = pltpu.VMEM((2, lay.layers, owners, rows, lay.width), F32)
    aside = [pltpu.HBM((taken[1] - taken[0], lay.pixels), F32)] if taken else []

    def body(state, target, *refs):
        sems = refs[-1]
        core = lax.axis_index("lat")
        core = 1 - core if others else core
        copies = []
        for owner in range(owners):
            for part in range(2):
                for layer in range(lay.layers):
                    for block in range(lay.blocks):
                        start = lay.total(part, layer, block, lay.tall + (2 * owner + core) * rows)
                        copies.append(
                            pltpu.make_async_copy(
                                state.at[pl.ds(pl.multiple_of(start, 8), rows), :],
                                target.at[part, layer, owner, :, pl.ds(block * lay.pixels, lay.pixels)],
                                sems.at[len(copies)],
                            )
                        )
        if taken:
            rest = state.at[pl.ds(taken[0], taken[1] - taken[0]), :]
            copies.append(pltpu.make_async_copy(rest, refs[0], sems.at[pieces]))
        for copy in copies:
            copy.start()
        for copy in copies:
            copy.wait()

    return pl.pallas_call(
        body,
        in_specs=[VMEM],
        out_specs=[VMEM] + [HBM] * len(aside),
        out_shape=[half, *aside],
        scratch_shapes=[pltpu.SemaphoreType.DMA((pieces + 1,))],
        compiler_params=pltpu.CompilerParams(vmem_limit_bytes=SCOPED),
        cost_estimate=pl.CostEstimate(flops=1000, bytes_accessed=1000, transcendentals=0),
        name="split_rows",
    )(in_vmem(state))


def add_up(a, b):
    pieces = [(i, j) for i in range(a.shape[0]) for j in range(a.shape[1])]

    def body(a, b, out, total, sems):
        copies = []
        for n, (i, j) in enumerate(pieces):
            total[i, j] = a[i, j] + b[i, j]
            copies.append(pltpu.make_async_copy(total.at[i, j], out.at[i, j], sems.at[n]))
            copies[-1].start()
        for copy in copies:
            copy.wait()

    return pl.pallas_call(
        body,
        in_specs=[VMEM, VMEM],
        out_specs=HBM,
        out_shape=pltpu.HBM(a.shape, F32),
        scratch_shapes=[pltpu.VMEM(a.shape, F32), pltpu.SemaphoreType.DMA((len(pieces),))],
        compiler_params=pltpu.CompilerParams(vmem_limit_bytes=SCOPED),
        name="add_up",
    )(in_vmem(a), in_vmem(b))


def swap(shard, axis):
    return lax.ppermute(shard, axis, [(0, 1), (1, 0)])


def sort_probes(lay, early, positions, indices):
    n = lay.probes
    total = 4 * n

    def body(listed, *refs):
        *scans, info, positions, sem = refs
        copy = pltpu.make_async_copy(listed, positions, sem)
        copy.start()
        copy.wait()
        lat, side = lax.axis_index("lat"), lax.axis_index("probe")
        lane = lax.broadcasted_iota(jnp.int32, (1, 128), 1)
        at = lax.broadcasted_iota(jnp.int32, (total, 128), 0)
        across = jnp.full((1, 128), jnp.iinfo(jnp.int32).max, jnp.int32)
        down = jnp.zeros((total, 128), jnp.int32)
        for which, scan in enumerate(scans):
            owner = (side ^ (which % 2)) * 2 + (lat ^ (which // 2))
            for i in range(n):
                place = scan[i]
                key = lay.pack(positions[0, place], positions[1, place], owner * n + i)
                across = jnp.where(lane == which * n + i, key, across)
                down = jnp.where(at == which * n + i, key, down)
        rank = jnp.sum((across < down).astype(jnp.int32), axis=1, keepdims=True)
        whose = lane // n
        order = 2 * (lane % n) + jnp.where(whose == 2, 1 - lat, lat)
        wanted = jnp.where(jnp.where(whose == 1, 1 - side, side) == 0, 2 * n - 1 - order, 2 * n + order)
        reach = 2 * early * lay.count
        wanted = jnp.where(lane == 3 * n, 2 * n - 1 - reach, wanted)
        wanted = jnp.where(lane == 3 * n + 1, 2 * n + reach, wanted)
        wanted = jnp.where(lane > 3 * n + 1, -1, wanted)
        info[...] = jnp.sum(jnp.where(rank == wanted, down, 0), axis=0, keepdims=True)

    return pl.pallas_call(
        body,
        in_specs=[HBM] + [SMEM] * 4,
        out_specs=VMEM,
        out_shape=pltpu.VMEM((1, 128), jnp.int32),
        scratch_shapes=[pltpu.SMEM(positions.T.shape, jnp.int32), pltpu.SemaphoreType.DMA(())],
        compiler_params=pltpu.CompilerParams(vmem_limit_bytes=SCOPED),
        name="sort_probes",
    )(in_hbm(positions.T), *indices)


def bring(x):
    def body(x, out, sem):
        copy = pltpu.make_async_copy(x, out, sem)
        copy.start()
        copy.wait()

    return pl.pallas_call(
        body,
        in_specs=[HBM],
        out_specs=VMEM,
        out_shape=pltpu.VMEM(x.shape, x.dtype),
        scratch_shapes=[pltpu.SemaphoreType.DMA(())],
        compiler_params=pltpu.CompilerParams(vmem_limit_bytes=SCOPED),
        cost_estimate=pl.CostEstimate(flops=1000, bytes_accessed=1000, transcendentals=0),
        name="bring",
    )(in_hbm(x))


def local(specimen, illumination, positions, scan_index, frames):
    pixels = illumination.shape[-1]
    _, layers, half, width = specimen.shape
    height = 2 * half
    tables = jnp.asarray(make_tables(pixels))
    sections = lax.axis_size("depth")
    owners = lax.axis_size("probe")
    paired = owners == 2 and lax.axis_size("groups") <= 2
    probes = scan_index.size
    count = 2 if probes % 4 == 0 else 1
    lay = Layout(probes, count, layers, pixels, half if paired else height, height, width)
    early = lay.groups // 2

    everyone = mine = None
    if paired:
        scan = scan_index.reshape(-1)
        beside = swap(scan, "lat")
        half_rows, beside = lax.optimization_barrier((specimen, beside))
        other = swap(half_rows, "lat")
        indices = [scan, swap(scan, "probe"), beside, swap(beside, "probe")]
        measured, *indices[1:] = lax.optimization_barrier((frames, *indices[1:]))
        end = sections - 1
        ends = [(2 * end, 2 * end + 1), (2 * end + 1, 2 * end)]
        mine = lax.ppermute(measured, ("depth", "probe"), ends)
        info = sort_probes(lay, early, positions, indices)
        everyone = swap(info, "groups") if lax.axis_size("groups") == 2 else info
    else:
        other = swap(specimen, "lat")
        corners = positions[scan_index.reshape(-1)]
        info = lay.pack(corners[:, 0], corners[:, 1], jnp.arange(probes, dtype=jnp.int32))
        info = everyone = jnp.pad(info, (0, 3 * probes))[None]
    state = cut_patches(lay, info, specimen, other, None, 0, count, from_hbm=True)
    def busy(tick, source, by):
        delay = source if by > 0 else 2 * (sections - 1) - source
        return 0 <= tick - delay < lay.groups

    def pass_on(wave, tick, by):
        pairs = [
            (source, source + by)
            for source in range(sections)
            if 0 <= source + by < sections and busy(tick, source, by)
        ]
        return lax.ppermute(wave, "depth", pairs) if pairs else None

    def grads_of(state, begin, end):
        begin, end = lay.grads_of(begin, end)
        return lax.slice_in_dim(state, begin, end)

    fill = sections - 1
    parts = [(0, early // 2), (early // 2, early)] if paired else []
    crossing = {}
    down = up = None
    def upto(group):
        early_sections = min(group, lay.groups) * count
        return lambda section: jnp.where(section < 2, early_sections, probes)

    cuts = {0: (count, upto(3)), 2: (upto(3), upto(5)), 3: (upto(5), probes)}
    last_tick = lay.groups + 2 * fill - 1
    for tick in range(lay.groups + 2 * fill):
        own = None
        if paired and tick == fill - 1:
            down, mine, everyone = lax.optimization_barrier((down, mine, everyone))
            crossed = [lax.ppermute(x, ("depth", "lat"), ends) for x in (frames, mine)]
        if tick < lay.groups + fill:
            start_wave = illumination if tick < lay.groups else None
            state, own = run_forward(lay, tick, sections, tables, state, down, start_wave)
            if tick == 0:
                own, specimen = lax.optimization_barrier((own, specimen))
                brought = bring(specimen)
            down = pass_on(own, tick, 1)
            if tick in cuts:
                state = cut_patches(lay, info, brought, other, state, *cuts[tick])
            if tick == 0:
                state = clear_total(lay, state)
            if tick == fill - 1:
                pools = [frames, mine, *crossed] if paired else [frames]
                state, late = place_frames(lay, sections, info, everyone, pools, state)
        if tick >= fill:
            state, *rising = run_backward(lay, tick, sections, tables, state, up, own, tick < last_tick)
            up = pass_on(rising[0], tick, -1) if rising else None
            received = crossing.pop(tick, [])
            for begin, end in parts:
                if tick == end - 1 + 2 * fill:
                    due = min(tick + CROSSING, last_tick - 1)
                    crossing.setdefault(due, []).append((begin, 1, swap(grads_of(state, begin, end), "probe")))
            state = deposit(lay, tick, sections, info, received, state)
    if not paired:
        send, = split_rows(lay, state, owners, True)
        keep, = split_rows(lay, state, owners, False)
        return lax.psum_scatter(keep + swap(send, "lat"), "probe", scatter_dimension=2, tiled=False)

    send, = split_rows(lay, state, 1, True)
    send, state = lax.optimization_barrier((send, state))
    received = swap(send, "lat")
    keep, late_grads = split_rows(lay, state, 1, False, lay.grads_of(early, lay.groups))

    def as_they_are(keep, received, grads):
        return add_up(keep, received)

    def with_partners(keep, received, grads):
        sums = Layout(probes, count, layers, pixels, half, height, width, only_sums=True)
        state = clear_total(sums, None)
        state = deposit(sums, None, sections, info, [(early, 1, swap(grads, "probe"))], state)
        send, = split_rows(sums, state, 1, True)
        more, = split_rows(sums, state, 1, False)
        return add_up(keep + more, received + swap(send, "lat"))

    result = lax.cond(late[0, 0] > 0, with_partners, as_they_are, keep, received, late_grads)
    return result[:, :, 0]


def solution(mesh):
    return jax.shard_map(
        local,
        mesh=mesh,
        in_specs=(
            P(None, ("groups", "depth"), "lat", None),
            P(),
            P("groups", None),
            P("groups", ("probe", "lat")),
            P("groups", ("probe", "lat"), None, None),
        ),
        out_specs=P(None, ("groups", "depth"), ("probe", "lat"), None),
        check_vma=False,
    )
```

```python
import functools
import math

import jax
import jax.numpy as jnp
import ml_dtypes
import numpy as np
from jax import lax
from jax.experimental import pallas as pl
from jax.experimental.pallas import tpu as pltpu
from jax.sharding import PartitionSpec as P

FRESNEL = 8.0
SCOPED = 8 << 20
CROSSING = 3
F32 = jnp.float32
BF16 = jnp.bfloat16
HBM = pl.BlockSpec(memory_space=pl.ANY)
VMEM = pl.BlockSpec(memory_space=pltpu.VMEM)
SMEM = pl.BlockSpec(memory_space=pltpu.SMEM)


def in_hbm(x):
    return pltpu.with_memory_space_constraint(x, pltpu.HBM)


def in_vmem(x):
    return pltpu.with_memory_space_constraint(x, pltpu.VMEM)


def real_blocks(matrix):
    real, imag = matrix.real, matrix.imag
    left = np.block([[real, -imag], [imag, real]])
    right = np.block([[real, imag], [-imag, real]])
    return np.stack([left, right])


@functools.lru_cache(maxsize=None)
def make_tables(pixels):
    index = np.arange(pixels)
    freq = np.where(index < pixels // 2, index, index - pixels) / pixels
    spread = index[:, None] - index[None, :]
    phase = 2.0 * math.pi * freq * spread[:, :, None] - math.pi * FRESNEL * freq * freq
    propagator = np.mean(np.exp(1j * phase), axis=-1)
    turns = index[:, None] * index[None, :] % pixels
    fourier = np.exp(-2j * math.pi * turns / pixels) / math.sqrt(pixels)
    blocks = np.stack([real_blocks(propagator), real_blocks(fourier)]).astype(np.float32)
    high = blocks.astype(ml_dtypes.bfloat16)
    low = (blocks - high.astype(np.float32)).astype(ml_dtypes.bfloat16)
    return np.stack([high, low], axis=2)


def halves(x):
    high = x.astype(BF16)
    return high, (x - high.astype(F32)).astype(BF16)


def dot(a, b):
    return jnp.dot(a, b, preferred_element_type=F32)


def transform(left, right, fields):
    size = fields[0][0].shape[0]
    mids = []
    for high, low in [halves(jnp.concatenate(field, axis=0)) for field in fields]:
        both = dot(left[0], jnp.concatenate([high, low], axis=1))
        mids.append(both[:, :size] + (both[:, size:] + dot(left[1], high)))
    outs = []
    for high, low in [halves(jnp.concatenate([mid[:size], mid[size:]], axis=1)) for mid in mids]:
        both = dot(jnp.concatenate([high, low], axis=0), right[0])
        outs.append(both[:size] + (both[size:] + dot(high, right[1])))
    return [(out[:, :size], out[:, size:]) for out in outs]


def times(a, b):
    return a[0] * b[0] - a[1] * b[1], a[0] * b[1] + a[1] * b[0]


def times_conj(a, b):
    return a[0] * b[0] + a[1] * b[1], a[1] * b[0] - a[0] * b[1]


class Layout:
    def __init__(self, probes, count, layers, pixels, rows, height, width, only_sums=False):
        self.probes, self.count, self.layers, self.pixels = probes, count, layers, pixels
        self.groups = probes // count
        self.tall = pixels + 8
        self.rows, self.height, self.width = rows, height, width
        self.blocks = width // pixels
        self.deep = rows + 2 * self.tall
        self.column_bits = (width - 1).bit_length()
        self.name_bits = (4 * probes - 1).bit_length()
        self.stack = probes * layers * 2 * pixels
        self.seen_from = self.stack
        self.grads_from = 2 * self.stack
        self.frames_from = 3 * self.stack
        self.total_from = 0 if only_sums else self.frames_from + probes * pixels
        self.shape = (self.total_from + 2 * layers * self.blocks * self.deep, pixels)

    def stacked(self, group, i, layer, part):
        probe = group * self.count + i
        return ((probe * self.layers + layer) * 2 + part) * self.pixels

    def tile(self, start):
        return pl.ds(pl.multiple_of(start, 8), self.pixels)

    def patch(self, group, i, layer, part):
        return self.tile(self.stacked(group, i, layer, part))

    def seen(self, group, i, layer, part):
        return self.tile(self.seen_from + self.stacked(group, i, layer, part))

    def grad(self, group, i, layer, part):
        return self.tile(self.grads_from + self.stacked(group, i, layer, part))

    def grads_of(self, begin, end):
        each = self.stack // self.groups
        return self.grads_from + begin * each, self.grads_from + end * each

    def frame(self, group, i):
        return self.tile(self.frames_from + (group * self.count + i) * self.pixels)

    def total(self, part, layer, block, row):
        block = (part * self.layers + layer) * self.blocks + block
        return self.total_from + block * self.deep + row

    def pack(self, row, column, name):
        return (((row << self.column_bits) + column) << self.name_bits) + name

    def row(self, key):
        return key >> (self.column_bits + self.name_bits)

    def window(self, info, probe, whose=0):
        lane = lax.broadcasted_iota(jnp.int32, info.shape, 1)
        key = jnp.sum(jnp.where(lane == probe + whose * self.probes, info[...], 0))
        row = self.row(key)
        column = (key >> self.name_bits) & ((1 << self.column_bits) - 1)
        row0 = jnp.minimum(row // 8 * 8, self.height - self.tall)
        block = jnp.minimum(column // self.pixels, self.blocks - 2)
        return row0, row - row0, block, column - block * self.pixels


def call(lay, body, state, before, outs, scratch=(), flag=False, flops=1000, moved=1000, name=None):
    spaces = {"hbm": (HBM, in_hbm), "vmem": (VMEM, in_vmem), "smem": (SMEM, lambda x: x)}
    specs = [spaces[kind][0] for kind, _ in before]
    operands = [spaces[kind][1](x) for kind, x in before]
    at = len(before)
    aliases = {}
    if state is not None:
        specs.append(VMEM)
        operands.append(in_vmem(state))
        aliases = {at: 0}

    def kernel(*refs):
        body(*refs[:at], *refs[at + len(aliases) :])

    return pl.pallas_call(
        kernel,
        in_specs=specs,
        out_specs=[VMEM] * (1 + len(outs) + flag),
        out_shape=[pltpu.VMEM(shape, F32) for shape in (lay.shape, *outs)]
        + [pltpu.VMEM((1, 128), jnp.int32)] * flag,
        scratch_shapes=list(scratch),
        input_output_aliases=aliases,
        compiler_params=pltpu.CompilerParams(vmem_limit_bytes=SCOPED),
        cost_estimate=pl.CostEstimate(flops=flops, bytes_accessed=moved, transcendentals=0),
        name=name,
    )(*operands)


def clear_total(lay, state):
    start = lay.total_from

    def body(state):
        state[pl.ds(start, lay.shape[0] - start), :] = jnp.zeros((lay.shape[0] - start, lay.pixels), F32)

    return call(lay, body, state, [], [], name="clear_total")[0]


def place_frames(lay, sections, info, everyone, pools, state):
    def body(info, everyone, *refs):
        *pools, state, late, sems = refs
        nearest = 3 * lay.probes
        reach = jnp.bool_(False)
        for ref in (info, everyone):
            reach |= lay.row(ref[0, nearest]) + lay.pixels > lay.rows
            reach |= lay.row(ref[0, nearest + 1]) < lay.rows
        late[...] = jnp.full(late.shape, reach.astype(jnp.int32), jnp.int32)
        lat, side = lax.axis_index("lat"), lax.axis_index("probe")

        @pl.when(lax.axis_index("depth") == sections - 1)
        def _():
            for act in ("start", "wait"):
                for probe in range(lay.probes):
                    name = info[0, probe] & ((1 << lay.name_bits) - 1)
                    owner = name // lay.probes
                    slot = name % lay.probes
                    if len(pools) > 1:
                        slot += ((owner // 2) ^ side) * lay.probes + ((owner % 2) ^ lat) * 2 * lay.probes
                    first = 0
                    for pool in pools:
                        size = pool.shape[0] // lay.pixels

                        @pl.when((slot >= first) & (slot < first + size))
                        def _(pool=pool, first=first, probe=probe, slot=slot):
                            copy = pltpu.make_async_copy(
                                pool.at[lay.tile((slot - first) * lay.pixels), :],
                                state.at[lay.frame(0, probe), :],
                                sems.at[probe],
                            )
                            getattr(copy, act)()

                        first += size

    pools = [pool.reshape((-1, lay.pixels)) for pool in pools]
    pools = [("hbm", pools[0]), *(("vmem", pool) for pool in pools[1:])]
    return call(
        lay,
        body,
        state,
        [("smem", info), ("smem", everyone), *pools],
        [],
        flag=True,
        scratch=[pltpu.SemaphoreType.DMA((lay.probes,))],
        name="place_frames",
    )


def cut_patches(lay, info, own, other, state, begin, end, from_hbm=False):
    half = own.shape[2]
    tall, pixels = lay.tall, lay.pixels

    def one(probe, info, own, other, state, window, sem):
        row0, down, block, shift = lay.window(info, probe)
        own_top = lax.axis_index("lat") == 0
        near_at = pl.ds(pl.multiple_of(block * pixels, pixels), pixels)
        far_at = pl.ds(pl.multiple_of((block + 1) * pixels, pixels), pixels)
        for source, is_top in ((own, own_top), (other, jnp.logical_not(own_top))):
            start = jnp.clip(row0 - jnp.where(is_top, 0, half), 0, half - tall)
            to = pl.ds(pl.multiple_of(jnp.where(is_top, 0, tall), 8), tall)
            rows = pl.ds(pl.multiple_of(start, 8), tall)

            @pl.when(jnp.where(is_top, row0 < half, row0 + tall > half))
            def _(source=source, rows=rows, to=to):
                if source is own and from_hbm:
                    both = pl.ds(pl.multiple_of(block * pixels, pixels), 2 * pixels)
                    copy = pltpu.make_async_copy(source.at[:, :, rows, both], window.at[:, :, to, :], sem)
                    copy.start()
                    copy.wait()
                    return
                for part in range(2):
                    for layer in range(lay.layers):
                        window[part, layer, to, 0:pixels] = source[part, layer, rows, near_at]
                        window[part, layer, to, pixels : 2 * pixels] = source[part, layer, rows, far_at]

        offset = jnp.where(row0 < half, jnp.maximum(row0 - (half - tall), 0), tall)
        rows = pl.ds(pl.multiple_of(offset, 8), tall)
        turn = (pixels - shift) % pixels
        lane = lax.broadcasted_iota(jnp.int32, (tall, pixels), 1)
        for part in range(2):
            for layer in range(lay.layers):
                near = pltpu.roll(window[part, layer, rows, 0:pixels], turn, 1)
                far = pltpu.roll(window[part, layer, rows, pixels : 2 * pixels], turn, 1)
                patch = jnp.where(lane < pixels - shift, near, far)
                patch = pltpu.roll(patch, (tall - down) % tall, 0)[:pixels]
                state[lay.patch(0, probe, layer, part), :] = patch

    def body(info, *refs):
        section = lax.axis_index("depth")
        bounds = [x(section) if callable(x) else x for x in (begin, end)]
        lax.fori_loop(*bounds, lambda probe, _: one(probe, info, *refs) or 0, 0)

    return call(
        lay,
        body,
        state,
        [("vmem", info), ("hbm" if from_hbm else "vmem", own), ("vmem", other)],
        [],
        scratch=[pltpu.VMEM((2, lay.layers, 2 * tall, 2 * pixels), F32), pltpu.SemaphoreType.DMA(())],
        name="cut_patches",
    )[0]


def section_cost(lay):
    size = lay.count * lay.pixels**2
    return dict(flops=lay.layers * 2 * 3 * 8 * size * lay.pixels, moved=(lay.layers * 2 + 4) * 8 * size)


def pair(ref, at):
    return ref[at(0), :], ref[at(1), :]


def run_forward(lay, tick, sections, tables, state, arrived, start_wave):
    def body(tables, *refs):
        arrived_ref = refs[0] if arrived is not None else None
        start_ref = refs[-3] if start_wave is not None else None
        state, leave = refs[-2:]
        section = lax.axis_index("depth")
        group = tick - section
        final = (section == sections - 1).astype(jnp.int32)

        @pl.when((group >= 0) & (group < lay.groups))
        def _():
            wave = []
            for i in range(lay.count):
                if arrived is None:
                    wave.append((start_ref[0], start_ref[1]))
                elif start_wave is None:
                    wave.append((arrived_ref[i, 0], arrived_ref[i, 1]))
                else:
                    wave.append(
                        tuple(jnp.where(section == 0, start_ref[p], arrived_ref[i, p]) for p in range(2))
                    )
            for layer in range(lay.layers):
                chi = []
                for i in range(lay.count):
                    for part in range(2):
                        state[lay.seen(group, i, layer, part), :] = wave[i][part]
                    chi.append(times(pair(state, functools.partial(lay.patch, group, i, layer)), wave[i]))
                at = final if layer == lay.layers - 1 else 0
                wave = transform((tables[at, 0, 0], tables[at, 0, 1]), (tables[at, 1, 0], tables[at, 1, 1]), chi)
            for i in range(lay.count):
                real, imag = wave[i]
                misfit = real * real + imag * imag - state[lay.frame(group, i), :]
                factor = jnp.where(final == 1, misfit, 1.0)
                leave[i, 0] = real * factor
                leave[i, 1] = imag * factor

    waves = [("vmem", x) for x in (arrived, start_wave) if x is not None]
    return call(
        lay,
        body,
        state,
        [("vmem", tables), *waves],
        [(lay.count, 2, lay.pixels, lay.pixels)],
        name="forward_section",
        **section_cost(lay),
    )


def run_backward(lay, tick, sections, tables, state, arrived, own, passes_on=True):
    def body(tables, *refs):
        arrived_ref = refs[0] if arrived is not None else None
        own_ref = refs[1 if arrived is not None else 0] if own is not None else None
        state, leave = refs[-2:] if passes_on else (refs[-1], None)
        section = lax.axis_index("depth")
        group = tick - (2 * (sections - 1) - section)
        final = (section == sections - 1).astype(jnp.int32)

        @pl.when((group >= 0) & (group < lay.groups))
        def _():
            wave = []
            for i in range(lay.count):
                if arrived is None:
                    wave.append((own_ref[i, 0], own_ref[i, 1]))
                elif own is None:
                    wave.append((arrived_ref[i, 0], arrived_ref[i, 1]))
                else:
                    wave.append(
                        tuple(jnp.where(final == 1, own_ref[i, p], arrived_ref[i, p]) for p in range(2))
                    )
            for layer in reversed(range(lay.layers)):
                at = final if layer == lay.layers - 1 else 0
                chi = transform((tables[at, 1, 0], tables[at, 1, 1]), (tables[at, 0, 0], tables[at, 0, 1]), wave)
                wave = []
                for i in range(lay.count):
                    real, imag = times_conj(chi[i], pair(state, functools.partial(lay.seen, group, i, layer)))
                    state[lay.grad(group, i, layer, 0), :] = real
                    state[lay.grad(group, i, layer, 1), :] = imag
                    wave.append(times_conj(chi[i], pair(state, functools.partial(lay.patch, group, i, layer))))
            for i in range(lay.count if passes_on else 0):
                leave[i, 0] = wave[i][0]
                leave[i, 1] = wave[i][1]

    waves = [("vmem", x) for x in (arrived, own) if x is not None]
    return call(
        lay,
        body,
        state,
        [("vmem", tables), *waves],
        [(lay.count, 2, lay.pixels, lay.pixels)] * passes_on,
        name="backward_section",
        **section_cost(lay),
    )


def deposit(lay, tick, sections, info, received, state):
    pixels, tall = lay.pixels, lay.tall

    def body(info, *refs):
        state = refs[-1]
        lane = lax.broadcasted_iota(jnp.int32, (tall, pixels), 1)
        blank = jnp.zeros((8, pixels), F32)
        base = lax.axis_index("probe") * lay.rows if lay.rows < lay.height else 0

        def add(probe, whose, active, load):
            row0, down, block, shift = lay.window(info, probe, whose)
            start = row0 - base + tall

            @pl.when(active & (start > 0) & (start < lay.rows + tall))
            def _():
                for layer in range(lay.layers):
                    for part in range(2):
                        padded = jnp.concatenate([load(layer, part), blank], axis=0)
                        turned = pltpu.roll(pltpu.roll(padded, down, 0), shift % pixels, 1)
                        near = pl.ds(pl.multiple_of(lay.total(part, layer, block, start), 8), tall)
                        far = pl.ds(pl.multiple_of(lay.total(part, layer, block + 1, start), 8), tall)
                        state[near, :] += jnp.where(lane >= shift, turned, 0.0)
                        state[far, :] += jnp.where(lane >= shift, 0.0, turned)

        if tick is not None:
            group = tick - (2 * (sections - 1) - lax.axis_index("depth"))
            active = (group >= 0) & (group < lay.groups)
            group = jnp.clip(group, 0, lay.groups - 1)
            for i in range(lay.count):
                add(
                    group * lay.count + i,
                    0,
                    active,
                    lambda layer, part, i=i: state[lay.grad(group, i, layer, part), :],
                )
        for ref, (first, whose, grads) in zip(refs, received):

            def one(i, _, ref=ref, first=first, whose=whose):
                add(
                    first * lay.count + i,
                    whose,
                    True,
                    lambda layer, part: ref[lay.patch(0, i, layer, part), :],
                )
                return 0

            lax.fori_loop(0, grads.shape[0] // (lay.layers * 2 * pixels), one, 0)

    return call(
        lay,
        body,
        state,
        [("vmem", info)] + [("vmem", grads) for *_, grads in received],
        [],
        name="deposit_patches",
    )[0]


def split_rows(lay, state, owners, others, taken=None):
    rows = lay.rows // (2 * owners)
    pieces = 2 * owners * lay.layers * lay.blocks
    half = pltpu.VMEM((2, lay.layers, owners, rows, lay.width), F32)
    aside = [pltpu.HBM((taken[1] - taken[0], lay.pixels), F32)] if taken else []

    def body(state, target, *refs):
        sems = refs[-1]
        core = lax.axis_index("lat")
        core = 1 - core if others else core
        copies = []
        for owner in range(owners):
            for part in range(2):
                for layer in range(lay.layers):
                    for block in range(lay.blocks):
                        start = lay.total(part, layer, block, lay.tall + (2 * owner + core) * rows)
                        copies.append(
                            pltpu.make_async_copy(
                                state.at[pl.ds(pl.multiple_of(start, 8), rows), :],
                                target.at[part, layer, owner, :, pl.ds(block * lay.pixels, lay.pixels)],
                                sems.at[len(copies)],
                            )
                        )
        if taken:
            rest = state.at[pl.ds(taken[0], taken[1] - taken[0]), :]
            copies.append(pltpu.make_async_copy(rest, refs[0], sems.at[pieces]))
        for copy in copies:
            copy.start()
        for copy in copies:
            copy.wait()

    return pl.pallas_call(
        body,
        in_specs=[VMEM],
        out_specs=[VMEM] + [HBM] * len(aside),
        out_shape=[half, *aside],
        scratch_shapes=[pltpu.SemaphoreType.DMA((pieces + 1,))],
        compiler_params=pltpu.CompilerParams(vmem_limit_bytes=SCOPED),
        cost_estimate=pl.CostEstimate(flops=1000, bytes_accessed=1000, transcendentals=0),
        name="split_rows",
    )(in_vmem(state))


def add_up(a, b):
    pieces = [(i, j) for i in range(a.shape[0]) for j in range(a.shape[1])]

    def body(a, b, out, total, sems):
        copies = []
        for n, (i, j) in enumerate(pieces):
            total[i, j] = a[i, j] + b[i, j]
            copies.append(pltpu.make_async_copy(total.at[i, j], out.at[i, j], sems.at[n]))
            copies[-1].start()
        for copy in copies:
            copy.wait()

    return pl.pallas_call(
        body,
        in_specs=[VMEM, VMEM],
        out_specs=HBM,
        out_shape=pltpu.HBM(a.shape, F32),
        scratch_shapes=[pltpu.VMEM(a.shape, F32), pltpu.SemaphoreType.DMA((len(pieces),))],
        compiler_params=pltpu.CompilerParams(vmem_limit_bytes=SCOPED),
        name="add_up",
    )(in_vmem(a), in_vmem(b))


def swap(shard, axis):
    return lax.ppermute(shard, axis, [(0, 1), (1, 0)])


def sort_probes(lay, early, positions, indices):
    n = lay.probes
    total = 4 * n

    def body(listed, scan, *refs):
        *scans, info, positions, mine, sems = refs
        copies = [
            pltpu.make_async_copy(listed, positions, sems.at[0]),
            pltpu.make_async_copy(scan, mine, sems.at[1]),
        ]
        for copy in copies:
            copy.start()
        for copy in copies:
            copy.wait()
        scans = [mine.at[0], *scans]
        lat, side = lax.axis_index("lat"), lax.axis_index("probe")
        lane = lax.broadcasted_iota(jnp.int32, (1, 128), 1)
        at = lax.broadcasted_iota(jnp.int32, (total, 128), 0)
        across = jnp.full((1, 128), jnp.iinfo(jnp.int32).max, jnp.int32)
        down = jnp.zeros((total, 128), jnp.int32)
        for which, scan in enumerate(scans):
            owner = (side ^ (which % 2)) * 2 + (lat ^ (which // 2))
            for i in range(n):
                place = scan[i]
                key = lay.pack(positions[0, place], positions[1, place], owner * n + i)
                across = jnp.where(lane == which * n + i, key, across)
                down = jnp.where(at == which * n + i, key, down)
        rank = jnp.sum((across < down).astype(jnp.int32), axis=1, keepdims=True)
        whose = lane // n
        order = 2 * (lane % n) + jnp.where(whose == 2, 1 - lat, lat)
        wanted = jnp.where(jnp.where(whose == 1, 1 - side, side) == 0, 2 * n - 1 - order, 2 * n + order)
        reach = 2 * early * lay.count
        wanted = jnp.where(lane == 3 * n, 2 * n - 1 - reach, wanted)
        wanted = jnp.where(lane == 3 * n + 1, 2 * n + reach, wanted)
        wanted = jnp.where(lane > 3 * n + 1, -1, wanted)
        info[...] = jnp.sum(jnp.where(rank == wanted, down, 0), axis=0, keepdims=True)

    return pl.pallas_call(
        body,
        in_specs=[HBM] * 2 + [SMEM] * 3,
        out_specs=VMEM,
        out_shape=pltpu.VMEM((1, 128), jnp.int32),
        scratch_shapes=[
            pltpu.SMEM(positions.T.shape, jnp.int32),
            pltpu.SMEM((1, n), jnp.int32),
            pltpu.SemaphoreType.DMA((2,)),
        ],
        compiler_params=pltpu.CompilerParams(vmem_limit_bytes=SCOPED),
        name="sort_probes",
    )(in_hbm(positions.T), in_hbm(indices[0].reshape((1, n))), *indices[1:])


def bring(x):
    def body(x, out, sem):
        copy = pltpu.make_async_copy(x, out, sem)
        copy.start()
        copy.wait()

    return pl.pallas_call(
        body,
        in_specs=[HBM],
        out_specs=VMEM,
        out_shape=pltpu.VMEM(x.shape, x.dtype),
        scratch_shapes=[pltpu.SemaphoreType.DMA(())],
        compiler_params=pltpu.CompilerParams(vmem_limit_bytes=SCOPED),
        cost_estimate=pl.CostEstimate(flops=1000, bytes_accessed=1000, transcendentals=0),
        name="bring",
    )(in_hbm(x))


def local(specimen, illumination, positions, scan_index, frames):
    pixels = illumination.shape[-1]
    _, layers, half, width = specimen.shape
    height = 2 * half
    tables = jnp.asarray(make_tables(pixels))
    sections = lax.axis_size("depth")
    owners = lax.axis_size("probe")
    paired = owners == 2 and lax.axis_size("groups") <= 2
    probes = scan_index.size
    count = 2 if probes % 4 == 0 else 1
    lay = Layout(probes, count, layers, pixels, half if paired else height, height, width)
    early = lay.groups // 2

    everyone = mine = None
    if paired:
        scan = scan_index.reshape(-1)
        beside = swap(scan, "lat")
        half_rows, beside = lax.optimization_barrier((specimen, beside))
        other = swap(half_rows, "lat")
        indices = [scan, swap(scan, "probe"), beside, swap(beside, "probe")]
        measured, *indices[1:] = lax.optimization_barrier((frames, *indices[1:]))
        end = sections - 1
        ends = [(2 * end, 2 * end + 1), (2 * end + 1, 2 * end)]
        mine = lax.ppermute(measured, ("depth", "probe"), ends)
        info = sort_probes(lay, early, positions, indices)
        everyone = swap(info, "groups") if lax.axis_size("groups") == 2 else info
    else:
        other = swap(specimen, "lat")
        corners = positions[scan_index.reshape(-1)]
        info = lay.pack(corners[:, 0], corners[:, 1], jnp.arange(probes, dtype=jnp.int32))
        info = everyone = jnp.pad(info, (0, 3 * probes))[None]
    state = cut_patches(lay, info, specimen, other, None, 0, count, from_hbm=True)
    def busy(tick, source, by):
        delay = source if by > 0 else 2 * (sections - 1) - source
        return 0 <= tick - delay < lay.groups

    def pass_on(wave, tick, by):
        pairs = [
            (source, source + by)
            for source in range(sections)
            if 0 <= source + by < sections and busy(tick, source, by)
        ]
        return lax.ppermute(wave, "depth", pairs) if pairs else None

    def grads_of(state, begin, end):
        begin, end = lay.grads_of(begin, end)
        return lax.slice_in_dim(state, begin, end)

    fill = sections - 1
    parts = [(0, early // 2), (early // 2, early)] if paired else []
    crossing = {}
    down = up = None
    def upto(group):
        early_sections = min(group, lay.groups) * count
        return lambda section: jnp.where(section < 2, early_sections, probes)

    cuts = {0: (count, upto(3)), 2: (upto(3), upto(5)), 3: (upto(5), probes)}
    last_tick = lay.groups + 2 * fill - 1
    for tick in range(lay.groups + 2 * fill):
        own = None
        if paired and tick == fill - 1:
            down, mine, everyone = lax.optimization_barrier((down, mine, everyone))
            crossed = [lax.ppermute(x, ("depth", "lat"), ends) for x in (frames, mine)]
        if tick < lay.groups + fill:
            start_wave = illumination if tick < lay.groups else None
            state, own = run_forward(lay, tick, sections, tables, state, down, start_wave)
            if tick == 0:
                own, specimen = lax.optimization_barrier((own, specimen))
                brought = bring(specimen)
            down = pass_on(own, tick, 1)
            if tick in cuts:
                state = cut_patches(lay, info, brought, other, state, *cuts[tick])
            if tick == 0:
                state = clear_total(lay, state)
            if tick == fill - 1:
                pools = [frames, mine, *crossed] if paired else [frames]
                state, late = place_frames(lay, sections, info, everyone, pools, state)
        if tick >= fill:
            state, *rising = run_backward(lay, tick, sections, tables, state, up, own, tick < last_tick)
            up = pass_on(rising[0], tick, -1) if rising else None
            received = crossing.pop(tick, [])
            for begin, end in parts:
                if tick == end - 1 + 2 * fill:
                    due = min(tick + CROSSING, last_tick - 1)
                    crossing.setdefault(due, []).append((begin, 1, swap(grads_of(state, begin, end), "probe")))
            state = deposit(lay, tick, sections, info, received, state)
    if not paired:
        send, = split_rows(lay, state, owners, True)
        keep, = split_rows(lay, state, owners, False)
        return lax.psum_scatter(keep + swap(send, "lat"), "probe", scatter_dimension=2, tiled=False)

    send, = split_rows(lay, state, 1, True)
    send, state = lax.optimization_barrier((send, state))
    received = swap(send, "lat")
    keep, late_grads = split_rows(lay, state, 1, False, lay.grads_of(early, lay.groups))

    def as_they_are(keep, received, grads):
        return add_up(keep, received)

    def with_partners(keep, received, grads):
        sums = Layout(probes, count, layers, pixels, half, height, width, only_sums=True)
        state = clear_total(sums, None)
        state = deposit(sums, None, sections, info, [(early, 1, swap(grads, "probe"))], state)
        send, = split_rows(sums, state, 1, True)
        more, = split_rows(sums, state, 1, False)
        return add_up(keep + more, received + swap(send, "lat"))

    result = lax.cond(late[0, 0] > 0, with_partners, as_they_are, keep, received, late_grads)
    return result[:, :, 0]


def solution(mesh):
    return jax.shard_map(
        local,
        mesh=mesh,
        in_specs=(
            P(None, ("groups", "depth"), "lat", None),
            P(),
            P("groups", None),
            P("groups", ("probe", "lat")),
            P("groups", ("probe", "lat"), None, None),
        ),
        out_specs=P(None, ("groups", "depth"), ("probe", "lat"), None),
        check_vma=False,
    )
```

```python
import functools
import math

import jax
import jax.numpy as jnp
import ml_dtypes
import numpy as np
from jax import lax
from jax.experimental import pallas as pl
from jax.experimental.pallas import tpu as pltpu
from jax.sharding import PartitionSpec as P

FRESNEL = 8.0
SCOPED = 8 << 20
CROSSING = 3
F32 = jnp.float32
BF16 = jnp.bfloat16
HBM = pl.BlockSpec(memory_space=pl.ANY)
VMEM = pl.BlockSpec(memory_space=pltpu.VMEM)
SMEM = pl.BlockSpec(memory_space=pltpu.SMEM)


def in_hbm(x):
    return pltpu.with_memory_space_constraint(x, pltpu.HBM)


def in_vmem(x):
    return pltpu.with_memory_space_constraint(x, pltpu.VMEM)


def real_blocks(matrix):
    real, imag = matrix.real, matrix.imag
    left = np.block([[real, -imag], [imag, real]])
    right = np.block([[real, imag], [-imag, real]])
    return np.stack([left, right])


@functools.lru_cache(maxsize=None)
def make_tables(pixels):
    index = np.arange(pixels)
    freq = np.where(index < pixels // 2, index, index - pixels) / pixels
    spread = index[:, None] - index[None, :]
    phase = 2.0 * math.pi * freq * spread[:, :, None] - math.pi * FRESNEL * freq * freq
    propagator = np.mean(np.exp(1j * phase), axis=-1)
    turns = index[:, None] * index[None, :] % pixels
    fourier = np.exp(-2j * math.pi * turns / pixels) / math.sqrt(pixels)
    blocks = np.stack([real_blocks(propagator), real_blocks(fourier)]).astype(np.float32)
    high = blocks.astype(ml_dtypes.bfloat16)
    low = (blocks - high.astype(np.float32)).astype(ml_dtypes.bfloat16)
    return np.stack([high, low], axis=2)


def halves(x):
    high = x.astype(BF16)
    return high, (x - high.astype(F32)).astype(BF16)


def dot(a, b):
    return jnp.dot(a, b, preferred_element_type=F32)


def transform(left, right, fields):
    size = fields[0][0].shape[0]
    mids = []
    for high, low in [halves(jnp.concatenate(field, axis=0)) for field in fields]:
        both = dot(left[0], jnp.concatenate([high, low], axis=1))
        mids.append(both[:, :size] + (both[:, size:] + dot(left[1], high)))
    outs = []
    for high, low in [halves(jnp.concatenate([mid[:size], mid[size:]], axis=1)) for mid in mids]:
        both = dot(jnp.concatenate([high, low], axis=0), right[0])
        outs.append(both[:size] + (both[size:] + dot(high, right[1])))
    return [(out[:, :size], out[:, size:]) for out in outs]


def times(a, b):
    return a[0] * b[0] - a[1] * b[1], a[0] * b[1] + a[1] * b[0]


def times_conj(a, b):
    return a[0] * b[0] + a[1] * b[1], a[1] * b[0] - a[0] * b[1]


class Layout:
    def __init__(self, probes, count, layers, pixels, rows, height, width, only_sums=False):
        self.probes, self.count, self.layers, self.pixels = probes, count, layers, pixels
        self.groups = probes // count
        self.tall = pixels + 8
        self.rows, self.height, self.width = rows, height, width
        self.blocks = width // pixels
        self.deep = rows + 2 * self.tall
        self.column_bits = (width - 1).bit_length()
        self.name_bits = (4 * probes - 1).bit_length()
        self.stack = probes * layers * 2 * pixels
        self.seen_from = self.stack
        self.grads_from = 2 * self.stack
        self.frames_from = 3 * self.stack
        self.total_from = 0 if only_sums else self.frames_from + probes * pixels
        self.shape = (self.total_from + 2 * layers * self.blocks * self.deep, pixels)

    def stacked(self, group, i, layer, part):
        probe = group * self.count + i
        return ((probe * self.layers + layer) * 2 + part) * self.pixels

    def tile(self, start):
        return pl.ds(pl.multiple_of(start, 8), self.pixels)

    def patch(self, group, i, layer, part):
        return self.tile(self.stacked(group, i, layer, part))

    def seen(self, group, i, layer, part):
        return self.tile(self.seen_from + self.stacked(group, i, layer, part))

    def grad(self, group, i, layer, part):
        return self.tile(self.grads_from + self.stacked(group, i, layer, part))

    def grads_of(self, begin, end):
        each = self.stack // self.groups
        return self.grads_from + begin * each, self.grads_from + end * each

    def frame(self, group, i):
        return self.tile(self.frames_from + (group * self.count + i) * self.pixels)

    def total(self, part, layer, block, row):
        block = (part * self.layers + layer) * self.blocks + block
        return self.total_from + block * self.deep + row

    def pack(self, row, column, name):
        return (((row << self.column_bits) + column) << self.name_bits) + name

    def row(self, key):
        return key >> (self.column_bits + self.name_bits)

    def window(self, info, probe, whose=0):
        lane = lax.broadcasted_iota(jnp.int32, info.shape, 1)
        key = jnp.sum(jnp.where(lane == probe + whose * self.probes, info[...], 0))
        row = self.row(key)
        column = (key >> self.name_bits) & ((1 << self.column_bits) - 1)
        row0 = jnp.minimum(row // 8 * 8, self.height - self.tall)
        block = jnp.minimum(column // self.pixels, self.blocks - 2)
        return row0, row - row0, block, column - block * self.pixels


def call(lay, body, state, before, outs, scratch=(), flag=False, flops=1000, moved=1000, name=None):
    spaces = {"hbm": (HBM, in_hbm), "vmem": (VMEM, in_vmem), "smem": (SMEM, lambda x: x)}
    specs = [spaces[kind][0] for kind, _ in before]
    operands = [spaces[kind][1](x) for kind, x in before]
    at = len(before)
    aliases = {}
    if state is not None:
        specs.append(VMEM)
        operands.append(in_vmem(state))
        aliases = {at: 0}

    def kernel(*refs):
        body(*refs[:at], *refs[at + len(aliases) :])

    return pl.pallas_call(
        kernel,
        in_specs=specs,
        out_specs=[VMEM] * (1 + len(outs) + flag),
        out_shape=[pltpu.VMEM(shape, F32) for shape in (lay.shape, *outs)]
        + [pltpu.VMEM((1, 128), jnp.int32)] * flag,
        scratch_shapes=list(scratch),
        input_output_aliases=aliases,
        compiler_params=pltpu.CompilerParams(vmem_limit_bytes=SCOPED),
        cost_estimate=pl.CostEstimate(flops=flops, bytes_accessed=moved, transcendentals=0),
        name=name,
    )(*operands)


def clear_total(lay, state):
    start = lay.total_from

    def body(state):
        state[pl.ds(start, lay.shape[0] - start), :] = jnp.zeros((lay.shape[0] - start, lay.pixels), F32)

    return call(lay, body, state, [], [], name="clear_total")[0]


def place_frames(lay, sections, info, everyone, pools, state):
    def body(info, everyone, *refs):
        *pools, state, late, sems = refs
        nearest = 3 * lay.probes
        reach = jnp.bool_(False)
        for ref in (info, everyone):
            reach |= lay.row(ref[0, nearest]) + lay.pixels > lay.rows
            reach |= lay.row(ref[0, nearest + 1]) < lay.rows
        late[...] = jnp.full(late.shape, reach.astype(jnp.int32), jnp.int32)
        lat, side = lax.axis_index("lat"), lax.axis_index("probe")

        @pl.when(lax.axis_index("depth") == sections - 1)
        def _():
            for act in ("start", "wait"):
                for probe in range(lay.probes):
                    name = info[0, probe] & ((1 << lay.name_bits) - 1)
                    owner = name // lay.probes
                    slot = name % lay.probes
                    if len(pools) > 1:
                        slot += ((owner // 2) ^ side) * lay.probes + ((owner % 2) ^ lat) * 2 * lay.probes
                    first = 0
                    for pool in pools:
                        size = pool.shape[0] // lay.pixels

                        @pl.when((slot >= first) & (slot < first + size))
                        def _(pool=pool, first=first, probe=probe, slot=slot):
                            copy = pltpu.make_async_copy(
                                pool.at[lay.tile((slot - first) * lay.pixels), :],
                                state.at[lay.frame(0, probe), :],
                                sems.at[probe],
                            )
                            getattr(copy, act)()

                        first += size

    pools = [pool.reshape((-1, lay.pixels)) for pool in pools]
    pools = [("hbm", pools[0]), *(("vmem", pool) for pool in pools[1:])]
    return call(
        lay,
        body,
        state,
        [("smem", info), ("smem", everyone), *pools],
        [],
        flag=True,
        scratch=[pltpu.SemaphoreType.DMA((lay.probes,))],
        name="place_frames",
    )


def cut_patches(lay, info, own, other, state, begin, end, from_hbm=False):
    half = own.shape[2]
    tall, pixels = lay.tall, lay.pixels

    def one(probe, info, own, other, state, window, sem):
        row0, down, block, shift = lay.window(info, probe)
        own_top = lax.axis_index("lat") == 0
        near_at = pl.ds(pl.multiple_of(block * pixels, pixels), pixels)
        far_at = pl.ds(pl.multiple_of((block + 1) * pixels, pixels), pixels)
        for source, is_top in ((own, own_top), (other, jnp.logical_not(own_top))):
            start = jnp.clip(row0 - jnp.where(is_top, 0, half), 0, half - tall)
            to = pl.ds(pl.multiple_of(jnp.where(is_top, 0, tall), 8), tall)
            rows = pl.ds(pl.multiple_of(start, 8), tall)

            @pl.when(jnp.where(is_top, row0 < half, row0 + tall > half))
            def _(source=source, rows=rows, to=to):
                if source is own and from_hbm:
                    both = pl.ds(pl.multiple_of(block * pixels, pixels), 2 * pixels)
                    copy = pltpu.make_async_copy(source.at[:, :, rows, both], window.at[:, :, to, :], sem)
                    copy.start()
                    copy.wait()
                    return
                for part in range(2):
                    for layer in range(lay.layers):
                        window[part, layer, to, 0:pixels] = source[part, layer, rows, near_at]
                        window[part, layer, to, pixels : 2 * pixels] = source[part, layer, rows, far_at]

        offset = jnp.where(row0 < half, jnp.maximum(row0 - (half - tall), 0), tall)
        rows = pl.ds(pl.multiple_of(offset, 8), tall)
        turn = (pixels - shift) % pixels
        lane = lax.broadcasted_iota(jnp.int32, (tall, pixels), 1)
        for part in range(2):
            for layer in range(lay.layers):
                near = pltpu.roll(window[part, layer, rows, 0:pixels], turn, 1)
                far = pltpu.roll(window[part, layer, rows, pixels : 2 * pixels], turn, 1)
                patch = jnp.where(lane < pixels - shift, near, far)
                patch = pltpu.roll(patch, (tall - down) % tall, 0)[:pixels]
                state[lay.patch(0, probe, layer, part), :] = patch

    def body(info, *refs):
        section = lax.axis_index("depth")
        bounds = [x(section) if callable(x) else x for x in (begin, end)]
        lax.fori_loop(*bounds, lambda probe, _: one(probe, info, *refs) or 0, 0)

    return call(
        lay,
        body,
        state,
        [("vmem", info), ("hbm" if from_hbm else "vmem", own), ("vmem", other)],
        [],
        scratch=[pltpu.VMEM((2, lay.layers, 2 * tall, 2 * pixels), F32), pltpu.SemaphoreType.DMA(())],
        name="cut_patches",
    )[0]


def section_cost(lay):
    size = lay.count * lay.pixels**2
    return dict(flops=lay.layers * 2 * 3 * 8 * size * lay.pixels, moved=(lay.layers * 2 + 4) * 8 * size)


def pair(ref, at):
    return ref[at(0), :], ref[at(1), :]


def run_forward(lay, tick, sections, tables, state, arrived, start_wave):
    def body(tables, *refs):
        arrived_ref = refs[0] if arrived is not None else None
        start_ref = refs[-3] if start_wave is not None else None
        state, leave = refs[-2:]
        section = lax.axis_index("depth")
        group = tick - section
        final = (section == sections - 1).astype(jnp.int32)

        @pl.when((group >= 0) & (group < lay.groups))
        def _():
            wave = []
            for i in range(lay.count):
                if arrived is None:
                    wave.append((start_ref[0], start_ref[1]))
                elif start_wave is None:
                    wave.append((arrived_ref[i, 0], arrived_ref[i, 1]))
                else:
                    wave.append(
                        tuple(jnp.where(section == 0, start_ref[p], arrived_ref[i, p]) for p in range(2))
                    )
            for layer in range(lay.layers):
                chi = []
                for i in range(lay.count):
                    for part in range(2):
                        state[lay.seen(group, i, layer, part), :] = wave[i][part]
                    chi.append(times(pair(state, functools.partial(lay.patch, group, i, layer)), wave[i]))
                at = final if layer == lay.layers - 1 else 0
                wave = transform((tables[at, 0, 0], tables[at, 0, 1]), (tables[at, 1, 0], tables[at, 1, 1]), chi)
            for i in range(lay.count):
                real, imag = wave[i]
                misfit = real * real + imag * imag - state[lay.frame(group, i), :]
                factor = jnp.where(final == 1, misfit, 1.0)
                leave[i, 0] = real * factor
                leave[i, 1] = imag * factor

    waves = [("vmem", x) for x in (arrived, start_wave) if x is not None]
    return call(
        lay,
        body,
        state,
        [("vmem", tables), *waves],
        [(lay.count, 2, lay.pixels, lay.pixels)],
        name="forward_section",
        **section_cost(lay),
    )


def run_backward(lay, tick, sections, tables, state, arrived, own, passes_on=True):
    def body(tables, *refs):
        arrived_ref = refs[0] if arrived is not None else None
        own_ref = refs[1 if arrived is not None else 0] if own is not None else None
        state, leave = refs[-2:] if passes_on else (refs[-1], None)
        section = lax.axis_index("depth")
        group = tick - (2 * (sections - 1) - section)
        final = (section == sections - 1).astype(jnp.int32)

        @pl.when((group >= 0) & (group < lay.groups))
        def _():
            wave = []
            for i in range(lay.count):
                if arrived is None:
                    wave.append((own_ref[i, 0], own_ref[i, 1]))
                elif own is None:
                    wave.append((arrived_ref[i, 0], arrived_ref[i, 1]))
                else:
                    wave.append(
                        tuple(jnp.where(final == 1, own_ref[i, p], arrived_ref[i, p]) for p in range(2))
                    )
            for layer in reversed(range(lay.layers)):
                at = final if layer == lay.layers - 1 else 0
                chi = transform((tables[at, 1, 0], tables[at, 1, 1]), (tables[at, 0, 0], tables[at, 0, 1]), wave)
                wave = []
                for i in range(lay.count):
                    real, imag = times_conj(chi[i], pair(state, functools.partial(lay.seen, group, i, layer)))
                    state[lay.grad(group, i, layer, 0), :] = real
                    state[lay.grad(group, i, layer, 1), :] = imag
                    wave.append(times_conj(chi[i], pair(state, functools.partial(lay.patch, group, i, layer))))
            for i in range(lay.count if passes_on else 0):
                leave[i, 0] = wave[i][0]
                leave[i, 1] = wave[i][1]

    waves = [("vmem", x) for x in (arrived, own) if x is not None]
    return call(
        lay,
        body,
        state,
        [("vmem", tables), *waves],
        [(lay.count, 2, lay.pixels, lay.pixels)] * passes_on,
        name="backward_section",
        **section_cost(lay),
    )


def deposit(lay, tick, sections, info, received, state):
    pixels, tall = lay.pixels, lay.tall

    def body(info, *refs):
        state = refs[-1]
        lane = lax.broadcasted_iota(jnp.int32, (tall, pixels), 1)
        blank = jnp.zeros((8, pixels), F32)
        base = lax.axis_index("probe") * lay.rows if lay.rows < lay.height else 0

        def add(probe, whose, active, load):
            row0, down, block, shift = lay.window(info, probe, whose)
            start = row0 - base + tall

            @pl.when(active & (start > 0) & (start < lay.rows + tall))
            def _():
                for layer in range(lay.layers):
                    for part in range(2):
                        padded = jnp.concatenate([load(layer, part), blank], axis=0)
                        turned = pltpu.roll(pltpu.roll(padded, down, 0), shift % pixels, 1)
                        near = pl.ds(pl.multiple_of(lay.total(part, layer, block, start), 8), tall)
                        far = pl.ds(pl.multiple_of(lay.total(part, layer, block + 1, start), 8), tall)
                        state[near, :] += jnp.where(lane >= shift, turned, 0.0)
                        state[far, :] += jnp.where(lane >= shift, 0.0, turned)

        if tick is not None:
            group = tick - (2 * (sections - 1) - lax.axis_index("depth"))
            active = (group >= 0) & (group < lay.groups)
            group = jnp.clip(group, 0, lay.groups - 1)
            for i in range(lay.count):
                add(
                    group * lay.count + i,
                    0,
                    active,
                    lambda layer, part, i=i: state[lay.grad(group, i, layer, part), :],
                )
        for ref, (first, whose, grads) in zip(refs, received):

            def one(i, _, ref=ref, first=first, whose=whose):
                add(
                    first * lay.count + i,
                    whose,
                    True,
                    lambda layer, part: ref[lay.patch(0, i, layer, part), :],
                )
                return 0

            lax.fori_loop(0, grads.shape[0] // (lay.layers * 2 * pixels), one, 0)

    return call(
        lay,
        body,
        state,
        [("vmem", info)] + [("vmem", grads) for *_, grads in received],
        [],
        name="deposit_patches",
    )[0]


def split_rows(lay, state, owners, others, taken=None):
    rows = lay.rows // (2 * owners)
    pieces = 2 * owners * lay.layers * lay.blocks
    half = pltpu.VMEM((2, lay.layers, owners, rows, lay.width), F32)
    aside = [pltpu.HBM((taken[1] - taken[0], lay.pixels), F32)] if taken else []

    def body(state, target, *refs):
        sems = refs[-1]
        core = lax.axis_index("lat")
        core = 1 - core if others else core
        copies = []
        for owner in range(owners):
            for part in range(2):
                for layer in range(lay.layers):
                    for block in range(lay.blocks):
                        start = lay.total(part, layer, block, lay.tall + (2 * owner + core) * rows)
                        copies.append(
                            pltpu.make_async_copy(
                                state.at[pl.ds(pl.multiple_of(start, 8), rows), :],
                                target.at[part, layer, owner, :, pl.ds(block * lay.pixels, lay.pixels)],
                                sems.at[len(copies)],
                            )
                        )
        if taken:
            rest = state.at[pl.ds(taken[0], taken[1] - taken[0]), :]
            copies.append(pltpu.make_async_copy(rest, refs[0], sems.at[pieces]))
        for copy in copies:
            copy.start()
        for copy in copies:
            copy.wait()

    return pl.pallas_call(
        body,
        in_specs=[VMEM],
        out_specs=[VMEM] + [HBM] * len(aside),
        out_shape=[half, *aside],
        scratch_shapes=[pltpu.SemaphoreType.DMA((pieces + 1,))],
        compiler_params=pltpu.CompilerParams(vmem_limit_bytes=SCOPED),
        cost_estimate=pl.CostEstimate(flops=1000, bytes_accessed=1000, transcendentals=0),
        name="split_rows",
    )(in_vmem(state))


def add_up(a, b):
    pieces = [(i, j) for i in range(a.shape[0]) for j in range(a.shape[1])]

    def body(a, b, out, total, sems):
        copies = []
        for n, (i, j) in enumerate(pieces):
            total[i, j] = a[i, j] + b[i, j]
            copies.append(pltpu.make_async_copy(total.at[i, j], out.at[i, j], sems.at[n]))
            copies[-1].start()
        for copy in copies:
            copy.wait()

    return pl.pallas_call(
        body,
        in_specs=[VMEM, VMEM],
        out_specs=HBM,
        out_shape=pltpu.HBM(a.shape, F32),
        scratch_shapes=[pltpu.VMEM(a.shape, F32), pltpu.SemaphoreType.DMA((len(pieces),))],
        compiler_params=pltpu.CompilerParams(vmem_limit_bytes=SCOPED),
        name="add_up",
    )(in_vmem(a), in_vmem(b))


def swap(shard, axis):
    return lax.ppermute(shard, axis, [(0, 1), (1, 0)])


def sort_probes(lay, early, positions, indices):
    n = lay.probes
    total = 4 * n

    def body(listed, scan, *refs):
        *scans, info, positions, mine, sems = refs
        copies = [
            pltpu.make_async_copy(listed, positions, sems.at[0]),
            pltpu.make_async_copy(scan, mine, sems.at[1]),
        ]
        for copy in copies:
            copy.start()
        for copy in copies:
            copy.wait()
        scans = [mine.at[0], *scans]
        lat, side = lax.axis_index("lat"), lax.axis_index("probe")
        lane = lax.broadcasted_iota(jnp.int32, (1, 128), 1)
        at = lax.broadcasted_iota(jnp.int32, (total, 128), 0)
        across = jnp.full((1, 128), jnp.iinfo(jnp.int32).max, jnp.int32)
        down = jnp.zeros((total, 128), jnp.int32)
        for which, scan in enumerate(scans):
            owner = (side ^ (which % 2)) * 2 + (lat ^ (which // 2))
            for i in range(n):
                place = scan[i]
                key = lay.pack(positions[0, place], positions[1, place], owner * n + i)
                across = jnp.where(lane == which * n + i, key, across)
                down = jnp.where(at == which * n + i, key, down)
        rank = jnp.sum((across < down).astype(jnp.int32), axis=1, keepdims=True)
        whose = lane // n
        order = 2 * (lane % n) + jnp.where(whose == 2, 1 - lat, lat)
        wanted = jnp.where(jnp.where(whose == 1, 1 - side, side) == 0, 2 * n - 1 - order, 2 * n + order)
        reach = 2 * early * lay.count
        wanted = jnp.where(lane == 3 * n, 2 * n - 1 - reach, wanted)
        wanted = jnp.where(lane == 3 * n + 1, 2 * n + reach, wanted)
        wanted = jnp.where(lane > 3 * n + 1, -1, wanted)
        info[...] = jnp.sum(jnp.where(rank == wanted, down, 0), axis=0, keepdims=True)

    return pl.pallas_call(
        body,
        in_specs=[HBM] * 2 + [SMEM] * 3,
        out_specs=VMEM,
        out_shape=pltpu.VMEM((1, 128), jnp.int32),
        scratch_shapes=[
            pltpu.SMEM(positions.T.shape, jnp.int32),
            pltpu.SMEM((1, n), jnp.int32),
            pltpu.SemaphoreType.DMA((2,)),
        ],
        compiler_params=pltpu.CompilerParams(vmem_limit_bytes=SCOPED),
        name="sort_probes",
    )(in_hbm(positions.T), in_hbm(indices[0].reshape((1, n))), *indices[1:])


def bring(x):
    def body(x, out, sem):
        copy = pltpu.make_async_copy(x, out, sem)
        copy.start()
        copy.wait()

    return pl.pallas_call(
        body,
        in_specs=[HBM],
        out_specs=VMEM,
        out_shape=pltpu.VMEM(x.shape, x.dtype),
        scratch_shapes=[pltpu.SemaphoreType.DMA(())],
        compiler_params=pltpu.CompilerParams(vmem_limit_bytes=SCOPED),
        cost_estimate=pl.CostEstimate(flops=1000, bytes_accessed=1000, transcendentals=0),
        name="bring",
    )(in_hbm(x))


def local(specimen, illumination, positions, scan_index, frames):
    pixels = illumination.shape[-1]
    _, layers, half, width = specimen.shape
    height = 2 * half
    tables = jnp.asarray(make_tables(pixels))
    sections = lax.axis_size("depth")
    owners = lax.axis_size("probe")
    paired = owners == 2 and lax.axis_size("groups") <= 2
    probes = scan_index.size
    count = 2 if probes % 4 == 0 else 1
    lay = Layout(probes, count, layers, pixels, half if paired else height, height, width)
    early = lay.groups // 2

    everyone = mine = None
    if paired:
        scan = scan_index.reshape(-1)
        beside = swap(scan, "lat")
        half_rows, beside = lax.optimization_barrier((specimen, beside))
        other = swap(half_rows, "lat")
        indices = [scan, swap(scan, "probe"), beside, swap(beside, "probe")]
        measured, *indices[1:] = lax.optimization_barrier((frames, *indices[1:]))
        end = sections - 1
        ends = [(2 * end, 2 * end + 1), (2 * end + 1, 2 * end)]
        mine = lax.ppermute(measured, ("depth", "probe"), ends)
        info = sort_probes(lay, early, positions, indices)
        everyone = swap(info, "groups") if lax.axis_size("groups") == 2 else info
    else:
        other = swap(specimen, "lat")
        corners = positions[scan_index.reshape(-1)]
        info = lay.pack(corners[:, 0], corners[:, 1], jnp.arange(probes, dtype=jnp.int32))
        info = everyone = jnp.pad(info, (0, 3 * probes))[None]
    state = cut_patches(lay, info, specimen, other, None, 0, count, from_hbm=True)
    def busy(tick, source, by):
        delay = source if by > 0 else 2 * (sections - 1) - source
        return 0 <= tick - delay < lay.groups

    def pass_on(wave, tick, by):
        pairs = [
            (source, source + by)
            for source in range(sections)
            if 0 <= source + by < sections and busy(tick, source, by)
        ]
        return lax.ppermute(wave, "depth", pairs) if pairs else None

    def grads_of(state, begin, end):
        begin, end = lay.grads_of(begin, end)
        return lax.slice_in_dim(state, begin, end)

    fill = sections - 1
    parts = [(0, early // 2), (early // 2, early)] if paired else []
    crossing = {}
    down = up = None
    def upto(group):
        early_sections = min(group, lay.groups) * count
        return lambda section: jnp.where(section < 2, early_sections, probes)

    cuts = {0: (count, upto(3)), 1: (upto(3), upto(5)), 3: (upto(5), probes)}
    last_tick = lay.groups + 2 * fill - 1
    for tick in range(lay.groups + 2 * fill):
        own = None
        if tick == fill:
            pools = [frames]
            if paired:
                down, mine, everyone = lax.optimization_barrier((down, mine, everyone))
                pools += [mine, *(lax.ppermute(x, ("depth", "lat"), ends) for x in (frames, mine))]
            state, late = place_frames(lay, sections, info, everyone, pools, state)
        if tick < lay.groups + fill:
            start_wave = illumination if tick < lay.groups else None
            state, own = run_forward(lay, tick, sections, tables, state, down, start_wave)
            if tick == 0:
                own, specimen = lax.optimization_barrier((own, specimen))
                brought = bring(specimen)
            down = pass_on(own, tick, 1)
            if tick in cuts:
                state = cut_patches(lay, info, brought, other, state, *cuts[tick])
            if tick == 0:
                state = clear_total(lay, state)
        if tick >= fill:
            state, *rising = run_backward(lay, tick, sections, tables, state, up, own, tick < last_tick)
            up = pass_on(rising[0], tick, -1) if rising else None
            received = crossing.pop(tick, [])
            for begin, end in parts:
                if tick == end - 1 + 2 * fill:
                    due = min(tick + CROSSING, last_tick - 1)
                    crossing.setdefault(due, []).append((begin, 1, swap(grads_of(state, begin, end), "probe")))
            state = deposit(lay, tick, sections, info, received, state)
    if not paired:
        send, = split_rows(lay, state, owners, True)
        keep, = split_rows(lay, state, owners, False)
        return lax.psum_scatter(keep + swap(send, "lat"), "probe", scatter_dimension=2, tiled=False)

    send, = split_rows(lay, state, 1, True)
    send, state = lax.optimization_barrier((send, state))
    received = swap(send, "lat")
    keep, late_grads = split_rows(lay, state, 1, False, lay.grads_of(early, lay.groups))

    def as_they_are(keep, received, grads):
        return add_up(keep, received)

    def with_partners(keep, received, grads):
        sums = Layout(probes, count, layers, pixels, half, height, width, only_sums=True)
        state = clear_total(sums, None)
        state = deposit(sums, None, sections, info, [(early, 1, swap(grads, "probe"))], state)
        send, = split_rows(sums, state, 1, True)
        more, = split_rows(sums, state, 1, False)
        return add_up(keep + more, received + swap(send, "lat"))

    result = lax.cond(late[0, 0] > 0, with_partners, as_they_are, keep, received, late_grads)
    return result[:, :, 0]


def solution(mesh):
    return jax.shard_map(
        local,
        mesh=mesh,
        in_specs=(
            P(None, ("groups", "depth"), "lat", None),
            P(),
            P("groups", None),
            P("groups", ("probe", "lat")),
            P("groups", ("probe", "lat"), None, None),
        ),
        out_specs=P(None, ("groups", "depth"), ("probe", "lat"), None),
        check_vma=False,
    )
```

```python
import functools
import math

import jax
import jax.numpy as jnp
import ml_dtypes
import numpy as np
from jax import lax
from jax.experimental import pallas as pl
from jax.experimental.pallas import tpu as pltpu
from jax.sharding import PartitionSpec as P

FRESNEL = 8.0
SCOPED = 8 << 20
CROSSING = 3
F32 = jnp.float32
BF16 = jnp.bfloat16
HBM = pl.BlockSpec(memory_space=pl.ANY)
VMEM = pl.BlockSpec(memory_space=pltpu.VMEM)
SMEM = pl.BlockSpec(memory_space=pltpu.SMEM)


def in_hbm(x):
    return pltpu.with_memory_space_constraint(x, pltpu.HBM)


def in_vmem(x):
    return pltpu.with_memory_space_constraint(x, pltpu.VMEM)


def real_blocks(matrix):
    real, imag = matrix.real, matrix.imag
    left = np.block([[real, -imag], [imag, real]])
    right = np.block([[real, imag], [-imag, real]])
    return np.stack([left, right])


@functools.lru_cache(maxsize=None)
def make_tables(pixels):
    index = np.arange(pixels)
    freq = np.where(index < pixels // 2, index, index - pixels) / pixels
    spread = index[:, None] - index[None, :]
    phase = 2.0 * math.pi * freq * spread[:, :, None] - math.pi * FRESNEL * freq * freq
    propagator = np.mean(np.exp(1j * phase), axis=-1)
    turns = index[:, None] * index[None, :] % pixels
    fourier = np.exp(-2j * math.pi * turns / pixels) / math.sqrt(pixels)
    blocks = np.stack([real_blocks(propagator), real_blocks(fourier)]).astype(np.float32)
    high = blocks.astype(ml_dtypes.bfloat16)
    low = (blocks - high.astype(np.float32)).astype(ml_dtypes.bfloat16)
    return np.stack([high, low], axis=2)


def halves(x):
    high = x.astype(BF16)
    return high, (x - high.astype(F32)).astype(BF16)


def dot(a, b):
    return jnp.dot(a, b, preferred_element_type=F32)


def transform(left, right, fields):
    size = fields[0][0].shape[0]
    mids = []
    for high, low in [halves(jnp.concatenate(field, axis=0)) for field in fields]:
        both = dot(left[0], jnp.concatenate([high, low], axis=1))
        mids.append(both[:, :size] + (both[:, size:] + dot(left[1], high)))
    outs = []
    for high, low in [halves(jnp.concatenate([mid[:size], mid[size:]], axis=1)) for mid in mids]:
        both = dot(jnp.concatenate([high, low], axis=0), right[0])
        outs.append(both[:size] + (both[size:] + dot(high, right[1])))
    return [(out[:, :size], out[:, size:]) for out in outs]


def times(a, b):
    return a[0] * b[0] - a[1] * b[1], a[0] * b[1] + a[1] * b[0]


def times_conj(a, b):
    return a[0] * b[0] + a[1] * b[1], a[1] * b[0] - a[0] * b[1]


class Layout:
    def __init__(self, probes, count, layers, pixels, rows, height, width, only_sums=False):
        self.probes, self.count, self.layers, self.pixels = probes, count, layers, pixels
        self.groups = probes // count
        self.tall = pixels + 8
        self.rows, self.height, self.width = rows, height, width
        self.blocks = width // pixels
        self.deep = rows + 2 * self.tall
        self.column_bits = (width - 1).bit_length()
        self.name_bits = (4 * probes - 1).bit_length()
        self.stack = probes * layers * 2 * pixels
        self.seen_from = self.stack
        self.grads_from = 2 * self.stack
        self.frames_from = 3 * self.stack
        self.total_from = 0 if only_sums else self.frames_from + probes * pixels
        self.shape = (self.total_from + 2 * layers * self.blocks * self.deep, pixels)

    def stacked(self, group, i, layer, part):
        probe = group * self.count + i
        return ((probe * self.layers + layer) * 2 + part) * self.pixels

    def tile(self, start):
        return pl.ds(pl.multiple_of(start, 8), self.pixels)

    def patch(self, group, i, layer, part):
        return self.tile(self.stacked(group, i, layer, part))

    def seen(self, group, i, layer, part):
        return self.tile(self.seen_from + self.stacked(group, i, layer, part))

    def grad(self, group, i, layer, part):
        return self.tile(self.grads_from + self.stacked(group, i, layer, part))

    def grads_of(self, begin, end):
        each = self.stack // self.groups
        return self.grads_from + begin * each, self.grads_from + end * each

    def frame(self, group, i):
        return self.tile(self.frames_from + (group * self.count + i) * self.pixels)

    def total(self, part, layer, block, row):
        block = (part * self.layers + layer) * self.blocks + block
        return self.total_from + block * self.deep + row

    def pack(self, row, column, name):
        return (((row << self.column_bits) + column) << self.name_bits) + name

    def row(self, key):
        return key >> (self.column_bits + self.name_bits)

    def window(self, info, probe, whose=0):
        lane = lax.broadcasted_iota(jnp.int32, info.shape, 1)
        key = jnp.sum(jnp.where(lane == probe + whose * self.probes, info[...], 0))
        row = self.row(key)
        column = (key >> self.name_bits) & ((1 << self.column_bits) - 1)
        row0 = jnp.minimum(row // 8 * 8, self.height - self.tall)
        block = jnp.minimum(column // self.pixels, self.blocks - 2)
        return row0, row - row0, block, column - block * self.pixels


def call(lay, body, state, before, outs, scratch=(), flag=False, flops=1000, moved=1000, name=None):
    spaces = {"hbm": (HBM, in_hbm), "vmem": (VMEM, in_vmem), "smem": (SMEM, lambda x: x)}
    specs = [spaces[kind][0] for kind, _ in before]
    operands = [spaces[kind][1](x) for kind, x in before]
    at = len(before)
    aliases = {}
    if state is not None:
        specs.append(VMEM)
        operands.append(in_vmem(state))
        aliases = {at: 0}

    def kernel(*refs):
        body(*refs[:at], *refs[at + len(aliases) :])

    return pl.pallas_call(
        kernel,
        in_specs=specs,
        out_specs=[VMEM] * (1 + len(outs) + flag),
        out_shape=[pltpu.VMEM(shape, F32) for shape in (lay.shape, *outs)]
        + [pltpu.VMEM((1, 128), jnp.int32)] * flag,
        scratch_shapes=list(scratch),
        input_output_aliases=aliases,
        compiler_params=pltpu.CompilerParams(vmem_limit_bytes=SCOPED),
        cost_estimate=pl.CostEstimate(flops=flops, bytes_accessed=moved, transcendentals=0),
        name=name,
    )(*operands)


def clear_total(lay, state):
    start = lay.total_from

    def body(state):
        state[pl.ds(start, lay.shape[0] - start), :] = jnp.zeros((lay.shape[0] - start, lay.pixels), F32)

    return call(lay, body, state, [], [], name="clear_total")[0]


def place_frames(lay, sections, info, everyone, pools, state):
    def body(info, everyone, *refs):
        *pools, state, late, sems = refs
        nearest = 3 * lay.probes
        reach = jnp.bool_(False)
        for ref in (info, everyone):
            reach |= lay.row(ref[0, nearest]) + lay.pixels > lay.rows
            reach |= lay.row(ref[0, nearest + 1]) < lay.rows
        late[...] = jnp.full(late.shape, reach.astype(jnp.int32), jnp.int32)
        lat, side = lax.axis_index("lat"), lax.axis_index("probe")

        @pl.when(lax.axis_index("depth") == sections - 1)
        def _():
            for act in ("start", "wait"):
                for probe in range(lay.probes):
                    name = info[0, probe] & ((1 << lay.name_bits) - 1)
                    owner = name // lay.probes
                    slot = name % lay.probes
                    if len(pools) > 1:
                        slot += ((owner // 2) ^ side) * lay.probes + ((owner % 2) ^ lat) * 2 * lay.probes
                    first = 0
                    for pool in pools:
                        size = pool.shape[0] // lay.pixels

                        @pl.when((slot >= first) & (slot < first + size))
                        def _(pool=pool, first=first, probe=probe, slot=slot):
                            copy = pltpu.make_async_copy(
                                pool.at[lay.tile((slot - first) * lay.pixels), :],
                                state.at[lay.frame(0, probe), :],
                                sems.at[probe],
                            )
                            getattr(copy, act)()

                        first += size

    pools = [pool.reshape((-1, lay.pixels)) for pool in pools]
    pools = [("hbm", pools[0]), *(("vmem", pool) for pool in pools[1:])]
    return call(
        lay,
        body,
        state,
        [("smem", info), ("smem", everyone), *pools],
        [],
        flag=True,
        scratch=[pltpu.SemaphoreType.DMA((lay.probes,))],
        name="place_frames",
    )


def cut_patches(lay, info, own, other, state, begin, end, from_hbm=False):
    half = own.shape[2]
    tall, pixels = lay.tall, lay.pixels

    def one(probe, info, own, other, state, window, sem):
        row0, down, block, shift = lay.window(info, probe)
        own_top = lax.axis_index("lat") == 0
        near_at = pl.ds(pl.multiple_of(block * pixels, pixels), pixels)
        far_at = pl.ds(pl.multiple_of((block + 1) * pixels, pixels), pixels)
        for source, is_top in ((own, own_top), (other, jnp.logical_not(own_top))):
            start = jnp.clip(row0 - jnp.where(is_top, 0, half), 0, half - tall)
            to = pl.ds(pl.multiple_of(jnp.where(is_top, 0, tall), 8), tall)
            rows = pl.ds(pl.multiple_of(start, 8), tall)

            @pl.when(jnp.where(is_top, row0 < half, row0 + tall > half))
            def _(source=source, rows=rows, to=to):
                if source is own and from_hbm:
                    both = pl.ds(pl.multiple_of(block * pixels, pixels), 2 * pixels)
                    copy = pltpu.make_async_copy(source.at[:, :, rows, both], window.at[:, :, to, :], sem)
                    copy.start()
                    copy.wait()
                    return
                for part in range(2):
                    for layer in range(lay.layers):
                        window[part, layer, to, 0:pixels] = source[part, layer, rows, near_at]
                        window[part, layer, to, pixels : 2 * pixels] = source[part, layer, rows, far_at]

        offset = jnp.where(row0 < half, jnp.maximum(row0 - (half - tall), 0), tall)
        rows = pl.ds(pl.multiple_of(offset, 8), tall)
        turn = (pixels - shift) % pixels
        lane = lax.broadcasted_iota(jnp.int32, (tall, pixels), 1)
        for part in range(2):
            for layer in range(lay.layers):
                near = pltpu.roll(window[part, layer, rows, 0:pixels], turn, 1)
                far = pltpu.roll(window[part, layer, rows, pixels : 2 * pixels], turn, 1)
                patch = jnp.where(lane < pixels - shift, near, far)
                patch = pltpu.roll(patch, (tall - down) % tall, 0)[:pixels]
                state[lay.patch(0, probe, layer, part), :] = patch

    def body(info, *refs):
        section = lax.axis_index("depth")
        bounds = [x(section) if callable(x) else x for x in (begin, end)]
        lax.fori_loop(*bounds, lambda probe, _: one(probe, info, *refs) or 0, 0)

    return call(
        lay,
        body,
        state,
        [("vmem", info), ("hbm" if from_hbm else "vmem", own), ("vmem", other)],
        [],
        scratch=[pltpu.VMEM((2, lay.layers, 2 * tall, 2 * pixels), F32), pltpu.SemaphoreType.DMA(())],
        name="cut_patches",
    )[0]


def section_cost(lay):
    size = lay.count * lay.pixels**2
    return dict(flops=lay.layers * 2 * 3 * 8 * size * lay.pixels, moved=(lay.layers * 2 + 4) * 8 * size)


def pair(ref, at):
    return ref[at(0), :], ref[at(1), :]


def run_forward(lay, tick, sections, tables, state, arrived, start_wave):
    def body(tables, *refs):
        arrived_ref = refs[0] if arrived is not None else None
        start_ref = refs[-3] if start_wave is not None else None
        state, leave = refs[-2:]
        section = lax.axis_index("depth")
        group = tick - section
        final = (section == sections - 1).astype(jnp.int32)

        @pl.when((group >= 0) & (group < lay.groups))
        def _():
            wave = []
            for i in range(lay.count):
                if arrived is None:
                    wave.append((start_ref[0], start_ref[1]))
                elif start_wave is None:
                    wave.append((arrived_ref[i, 0], arrived_ref[i, 1]))
                else:
                    wave.append(
                        tuple(jnp.where(section == 0, start_ref[p], arrived_ref[i, p]) for p in range(2))
                    )
            for layer in range(lay.layers):
                chi = []
                for i in range(lay.count):
                    for part in range(2):
                        state[lay.seen(group, i, layer, part), :] = wave[i][part]
                    chi.append(times(pair(state, functools.partial(lay.patch, group, i, layer)), wave[i]))
                at = final if layer == lay.layers - 1 else 0
                wave = transform((tables[at, 0, 0], tables[at, 0, 1]), (tables[at, 1, 0], tables[at, 1, 1]), chi)
            for i in range(lay.count):
                real, imag = wave[i]
                misfit = real * real + imag * imag - state[lay.frame(group, i), :]
                factor = jnp.where(final == 1, misfit, 1.0)
                leave[i, 0] = real * factor
                leave[i, 1] = imag * factor

    waves = [("vmem", x) for x in (arrived, start_wave) if x is not None]
    return call(
        lay,
        body,
        state,
        [("vmem", tables), *waves],
        [(lay.count, 2, lay.pixels, lay.pixels)],
        name="forward_section",
        **section_cost(lay),
    )


def run_backward(lay, tick, sections, tables, state, arrived, own, passes_on=True):
    def body(tables, *refs):
        arrived_ref = refs[0] if arrived is not None else None
        own_ref = refs[1 if arrived is not None else 0] if own is not None else None
        state, leave = refs[-2:] if passes_on else (refs[-1], None)
        section = lax.axis_index("depth")
        group = tick - (2 * (sections - 1) - section)
        final = (section == sections - 1).astype(jnp.int32)

        @pl.when((group >= 0) & (group < lay.groups))
        def _():
            wave = []
            for i in range(lay.count):
                if arrived is None:
                    wave.append((own_ref[i, 0], own_ref[i, 1]))
                elif own is None:
                    wave.append((arrived_ref[i, 0], arrived_ref[i, 1]))
                else:
                    wave.append(
                        tuple(jnp.where(final == 1, own_ref[i, p], arrived_ref[i, p]) for p in range(2))
                    )
            for layer in reversed(range(lay.layers)):
                at = final if layer == lay.layers - 1 else 0
                chi = transform((tables[at, 1, 0], tables[at, 1, 1]), (tables[at, 0, 0], tables[at, 0, 1]), wave)
                wave = []
                for i in range(lay.count):
                    real, imag = times_conj(chi[i], pair(state, functools.partial(lay.seen, group, i, layer)))
                    state[lay.grad(group, i, layer, 0), :] = real
                    state[lay.grad(group, i, layer, 1), :] = imag
                    wave.append(times_conj(chi[i], pair(state, functools.partial(lay.patch, group, i, layer))))
            for i in range(lay.count if passes_on else 0):
                leave[i, 0] = wave[i][0]
                leave[i, 1] = wave[i][1]

    waves = [("vmem", x) for x in (arrived, own) if x is not None]
    return call(
        lay,
        body,
        state,
        [("vmem", tables), *waves],
        [(lay.count, 2, lay.pixels, lay.pixels)] * passes_on,
        name="backward_section",
        **section_cost(lay),
    )


def deposit(lay, tick, sections, info, received, state):
    pixels, tall = lay.pixels, lay.tall

    def body(info, *refs):
        state = refs[-1]
        lane = lax.broadcasted_iota(jnp.int32, (tall, pixels), 1)
        blank = jnp.zeros((8, pixels), F32)
        base = lax.axis_index("probe") * lay.rows if lay.rows < lay.height else 0

        def add(probe, whose, active, load):
            row0, down, block, shift = lay.window(info, probe, whose)
            start = row0 - base + tall

            @pl.when(active & (start > 0) & (start < lay.rows + tall))
            def _():
                for layer in range(lay.layers):
                    for part in range(2):
                        padded = jnp.concatenate([load(layer, part), blank], axis=0)
                        turned = pltpu.roll(pltpu.roll(padded, down, 0), shift % pixels, 1)
                        near = pl.ds(pl.multiple_of(lay.total(part, layer, block, start), 8), tall)
                        far = pl.ds(pl.multiple_of(lay.total(part, layer, block + 1, start), 8), tall)
                        state[near, :] += jnp.where(lane >= shift, turned, 0.0)
                        state[far, :] += jnp.where(lane >= shift, 0.0, turned)

        if tick is not None:
            group = tick - (2 * (sections - 1) - lax.axis_index("depth"))
            active = (group >= 0) & (group < lay.groups)
            group = jnp.clip(group, 0, lay.groups - 1)
            for i in range(lay.count):
                add(
                    group * lay.count + i,
                    0,
                    active,
                    lambda layer, part, i=i: state[lay.grad(group, i, layer, part), :],
                )
        for ref, (first, whose, grads) in zip(refs, received):

            def one(i, _, ref=ref, first=first, whose=whose):
                add(
                    first * lay.count + i,
                    whose,
                    True,
                    lambda layer, part: ref[lay.patch(0, i, layer, part), :],
                )
                return 0

            lax.fori_loop(0, grads.shape[0] // (lay.layers * 2 * pixels), one, 0)

    return call(
        lay,
        body,
        state,
        [("vmem", info)] + [("vmem", grads) for *_, grads in received],
        [],
        name="deposit_patches",
    )[0]


def split_rows(lay, state, owners, others, taken=None):
    rows = lay.rows // (2 * owners)
    pieces = 2 * owners * lay.layers * lay.blocks
    half = pltpu.VMEM((2, lay.layers, owners, rows, lay.width), F32)
    aside = [pltpu.HBM((taken[1] - taken[0], lay.pixels), F32)] if taken else []

    def body(state, target, *refs):
        sems = refs[-1]
        core = lax.axis_index("lat")
        core = 1 - core if others else core
        copies = []
        for owner in range(owners):
            for part in range(2):
                for layer in range(lay.layers):
                    for block in range(lay.blocks):
                        start = lay.total(part, layer, block, lay.tall + (2 * owner + core) * rows)
                        copies.append(
                            pltpu.make_async_copy(
                                state.at[pl.ds(pl.multiple_of(start, 8), rows), :],
                                target.at[part, layer, owner, :, pl.ds(block * lay.pixels, lay.pixels)],
                                sems.at[len(copies)],
                            )
                        )
        if taken:
            rest = state.at[pl.ds(taken[0], taken[1] - taken[0]), :]
            copies.append(pltpu.make_async_copy(rest, refs[0], sems.at[pieces]))
        for copy in copies:
            copy.start()
        for copy in copies:
            copy.wait()

    return pl.pallas_call(
        body,
        in_specs=[VMEM],
        out_specs=[VMEM] + [HBM] * len(aside),
        out_shape=[half, *aside],
        scratch_shapes=[pltpu.SemaphoreType.DMA((pieces + 1,))],
        compiler_params=pltpu.CompilerParams(vmem_limit_bytes=SCOPED),
        cost_estimate=pl.CostEstimate(flops=1000, bytes_accessed=1000, transcendentals=0),
        name="split_rows",
    )(in_vmem(state))


def add_up(a, b):
    pieces = [(i, j) for i in range(a.shape[0]) for j in range(a.shape[1])]

    def body(a, b, out, total, sems):
        copies = []
        for n, (i, j) in enumerate(pieces):
            total[i, j] = a[i, j] + b[i, j]
            copies.append(pltpu.make_async_copy(total.at[i, j], out.at[i, j], sems.at[n]))
            copies[-1].start()
        for copy in copies:
            copy.wait()

    return pl.pallas_call(
        body,
        in_specs=[VMEM, VMEM],
        out_specs=HBM,
        out_shape=pltpu.HBM(a.shape, F32),
        scratch_shapes=[pltpu.VMEM(a.shape, F32), pltpu.SemaphoreType.DMA((len(pieces),))],
        compiler_params=pltpu.CompilerParams(vmem_limit_bytes=SCOPED),
        name="add_up",
    )(in_vmem(a), in_vmem(b))


def swap(shard, axis):
    return lax.ppermute(shard, axis, [(0, 1), (1, 0)])


def sort_probes(lay, early, positions, indices):
    n = lay.probes
    total = 4 * n

    def body(listed, scan, *refs):
        *scans, info, positions, mine, sems = refs
        copies = [
            pltpu.make_async_copy(listed, positions, sems.at[0]),
            pltpu.make_async_copy(scan, mine, sems.at[1]),
        ]
        for copy in copies:
            copy.start()
        for copy in copies:
            copy.wait()
        across_probe, beside = scans
        scans = [
            lambda i: mine[0, i],
            lambda i: across_probe[i],
            lambda i: beside[i],
            lambda i: across_probe[n + i],
        ]
        lat, side = lax.axis_index("lat"), lax.axis_index("probe")
        lane = lax.broadcasted_iota(jnp.int32, (1, 128), 1)
        at = lax.broadcasted_iota(jnp.int32, (total, 128), 0)
        across = jnp.full((1, 128), jnp.iinfo(jnp.int32).max, jnp.int32)
        down = jnp.zeros((total, 128), jnp.int32)
        for which, scan in enumerate(scans):
            owner = (side ^ (which % 2)) * 2 + (lat ^ (which // 2))
            for i in range(n):
                place = scan(i)
                key = lay.pack(positions[0, place], positions[1, place], owner * n + i)
                across = jnp.where(lane == which * n + i, key, across)
                down = jnp.where(at == which * n + i, key, down)
        rank = jnp.sum((across < down).astype(jnp.int32), axis=1, keepdims=True)
        whose = lane // n
        order = 2 * (lane % n) + jnp.where(whose == 2, 1 - lat, lat)
        wanted = jnp.where(jnp.where(whose == 1, 1 - side, side) == 0, 2 * n - 1 - order, 2 * n + order)
        reach = 2 * early * lay.count
        wanted = jnp.where(lane == 3 * n, 2 * n - 1 - reach, wanted)
        wanted = jnp.where(lane == 3 * n + 1, 2 * n + reach, wanted)
        wanted = jnp.where(lane > 3 * n + 1, -1, wanted)
        info[...] = jnp.sum(jnp.where(rank == wanted, down, 0), axis=0, keepdims=True)

    return pl.pallas_call(
        body,
        in_specs=[HBM] * 2 + [SMEM] * 2,
        out_specs=VMEM,
        out_shape=pltpu.VMEM((1, 128), jnp.int32),
        scratch_shapes=[
            pltpu.SMEM(positions.T.shape, jnp.int32),
            pltpu.SMEM((1, n), jnp.int32),
            pltpu.SemaphoreType.DMA((2,)),
        ],
        compiler_params=pltpu.CompilerParams(vmem_limit_bytes=SCOPED),
        name="sort_probes",
    )(in_hbm(positions.T), in_hbm(indices[0].reshape((1, n))), *indices[1:])


def bring(x):
    def body(x, out, sem):
        copy = pltpu.make_async_copy(x, out, sem)
        copy.start()
        copy.wait()

    return pl.pallas_call(
        body,
        in_specs=[HBM],
        out_specs=VMEM,
        out_shape=pltpu.VMEM(x.shape, x.dtype),
        scratch_shapes=[pltpu.SemaphoreType.DMA(())],
        compiler_params=pltpu.CompilerParams(vmem_limit_bytes=SCOPED),
        cost_estimate=pl.CostEstimate(flops=1000, bytes_accessed=1000, transcendentals=0),
        name="bring",
    )(in_hbm(x))


def local(specimen, illumination, positions, scan_index, frames):
    pixels = illumination.shape[-1]
    _, layers, half, width = specimen.shape
    height = 2 * half
    tables = jnp.asarray(make_tables(pixels))
    sections = lax.axis_size("depth")
    owners = lax.axis_size("probe")
    paired = owners == 2 and lax.axis_size("groups") <= 2
    probes = scan_index.size
    count = 2 if probes % 4 == 0 else 1
    lay = Layout(probes, count, layers, pixels, half if paired else height, height, width)
    early = lay.groups // 2

    everyone = mine = None
    if paired:
        scan = scan_index.reshape(-1)
        beside = swap(scan, "lat")
        half_rows, beside = lax.optimization_barrier((specimen, beside))
        other = swap(half_rows, "lat")
        indices = [scan, swap(jnp.concatenate([scan, beside]), "probe"), beside]
        measured, indices[1] = lax.optimization_barrier((frames, indices[1]))
        end = sections - 1
        ends = [(2 * end, 2 * end + 1), (2 * end + 1, 2 * end)]
        mine = lax.ppermute(measured, ("depth", "probe"), ends)
        info = sort_probes(lay, early, positions, indices)
        everyone = swap(info, "groups") if lax.axis_size("groups") == 2 else info
    else:
        other = swap(specimen, "lat")
        corners = positions[scan_index.reshape(-1)]
        info = lay.pack(corners[:, 0], corners[:, 1], jnp.arange(probes, dtype=jnp.int32))
        info = everyone = jnp.pad(info, (0, 3 * probes))[None]
    state = cut_patches(lay, info, specimen, other, None, 0, count, from_hbm=True)
    def busy(tick, source, by):
        delay = source if by > 0 else 2 * (sections - 1) - source
        return 0 <= tick - delay < lay.groups

    def pass_on(wave, tick, by):
        pairs = [
            (source, source + by)
            for source in range(sections)
            if 0 <= source + by < sections and busy(tick, source, by)
        ]
        return lax.ppermute(wave, "depth", pairs) if pairs else None

    def grads_of(state, begin, end):
        begin, end = lay.grads_of(begin, end)
        return lax.slice_in_dim(state, begin, end)

    fill = sections - 1
    parts = [(0, early // 2), (early // 2, early)] if paired else []
    crossing = {}
    down = up = None
    def upto(group):
        early_sections = min(group, lay.groups) * count
        return lambda section: jnp.where(section < 2, early_sections, probes)

    cuts = {0: (count, upto(3)), 2: (upto(3), upto(5)), 3: (upto(5), probes)}
    last_tick = lay.groups + 2 * fill - 1
    for tick in range(lay.groups + 2 * fill):
        own = None
        if paired and tick == fill - 1:
            down, mine, everyone = lax.optimization_barrier((down, mine, everyone))
            crossed = [lax.ppermute(x, ("depth", "lat"), ends) for x in (frames, mine)]
        if tick < lay.groups + fill:
            start_wave = illumination if tick < lay.groups else None
            state, own = run_forward(lay, tick, sections, tables, state, down, start_wave)
            if tick == 0:
                own, specimen = lax.optimization_barrier((own, specimen))
                brought = bring(specimen)
            down = pass_on(own, tick, 1)
            if tick in cuts:
                state = cut_patches(lay, info, brought, other, state, *cuts[tick])
            if tick == 0:
                state = clear_total(lay, state)
            if tick == fill - 1:
                pools = [frames, mine, *crossed] if paired else [frames]
                state, late = place_frames(lay, sections, info, everyone, pools, state)
        if tick >= fill:
            state, *rising = run_backward(lay, tick, sections, tables, state, up, own, tick < last_tick)
            up = pass_on(rising[0], tick, -1) if rising else None
            received = crossing.pop(tick, [])
            for begin, end in parts:
                if tick == end - 1 + 2 * fill:
                    due = min(tick + CROSSING, last_tick - 1)
                    crossing.setdefault(due, []).append((begin, 1, swap(grads_of(state, begin, end), "probe")))
            state = deposit(lay, tick, sections, info, received, state)
    if not paired:
        send, = split_rows(lay, state, owners, True)
        keep, = split_rows(lay, state, owners, False)
        return lax.psum_scatter(keep + swap(send, "lat"), "probe", scatter_dimension=2, tiled=False)

    send, = split_rows(lay, state, 1, True)
    send, state = lax.optimization_barrier((send, state))
    received = swap(send, "lat")
    keep, late_grads = split_rows(lay, state, 1, False, lay.grads_of(early, lay.groups))

    def as_they_are(keep, received, grads):
        return add_up(keep, received)

    def with_partners(keep, received, grads):
        sums = Layout(probes, count, layers, pixels, half, height, width, only_sums=True)
        state = clear_total(sums, None)
        state = deposit(sums, None, sections, info, [(early, 1, swap(grads, "probe"))], state)
        send, = split_rows(sums, state, 1, True)
        more, = split_rows(sums, state, 1, False)
        return add_up(keep + more, received + swap(send, "lat"))

    result = lax.cond(late[0, 0] > 0, with_partners, as_they_are, keep, received, late_grads)
    return result[:, :, 0]


def solution(mesh):
    return jax.shard_map(
        local,
        mesh=mesh,
        in_specs=(
            P(None, ("groups", "depth"), "lat", None),
            P(),
            P("groups", None),
            P("groups", ("probe", "lat")),
            P("groups", ("probe", "lat"), None, None),
        ),
        out_specs=P(None, ("groups", "depth"), ("probe", "lat"), None),
        check_vma=False,
    )
```
